32 devices in a mesh: ctx: 8 (over z, y), head: 4 (over x, core).
Axes of the slice: x: 2, y: 2, z: 4, core: 2. Of those that a mesh axis runs over, the one named last changes fastest.
Arguments:
- queries: bfloat16 [8192, 32, 128], P('ctx', 'head'), may hold values from -16 to 16
- keys: bfloat16 [8192, 32, 128], P('ctx', 'head'), may hold values from -16 to 16
- values: bfloat16 [8192, 32, 128], P('ctx', 'head'), may hold values from -6 to 6
- out_grad: bfloat16 [8192, 4096], P('ctx'), may hold values from -6 to 6
- wo: bfloat16 [4096, 4096], P('head', 'ctx'), may hold values from -0.125 to 0.125
Outputs:
- layer_out: bfloat16 [8192, 4096], P('ctx', 'head')
- queries_gradient: bfloat16 [8192, 32, 128], P('ctx', 'head')
- keys_gradient: bfloat16 [8192, 32, 128], P('ctx', 'head')
- values_gradient: bfloat16 [8192, 32, 128], P('ctx', 'head')
- proj_grad: bfloat16 [4096, 4096], P('head', 'ctx')
The draws below stay inside these ranges and needn't reach their ends.
All inputs are finite; a program needn't handle non-finite values.
Results may differ from the reference program's by a relative error of at most 0.015.
Values may be sent and summed in bfloat16 or wider, within the bound.
No kernel may reach another device: no remote copies, remote signals or barrier semaphores. Data moves between devices by JAX's collectives and lax.ppermute only.
A program may use at most 128 MiB of HBM per device.

```python
import jax
import jax.numpy as jnp
from jax import lax

D = 4096
H = 32
HS = 128
C = 512
R = 16
L = 8192


def draw_queries(key, part):
    shape = (R * C, H, HS)
    result = jnp.clip(jax.random.normal(jax.random.fold_in(key, 21), shape, jnp.float32), -6.0, 6.0)
    return result.astype(jnp.bfloat16)


def draw_keys(key, part):
    shape = (R * C, H, HS)
    result = jnp.clip(jax.random.normal(jax.random.fold_in(key, 22), shape, jnp.float32), -6.0, 6.0)
    return result.astype(jnp.bfloat16)


def strengthened(drawn, rng, source, target, shards_of, factor):
    def block_of(dim):
        return (jnp.arange(drawn.shape[dim]) // (drawn.shape[dim] // shards_of)).reshape((-1,) + (1,) * (drawn.ndim - 1 - dim))

    near = jax.random.permutation(rng, shards_of)[block_of(target)]
    other_side = (block_of(target) + shards_of // 2) % shards_of
    return jnp.where((block_of(source) == near) | (block_of(source) == other_side), factor * drawn, drawn)


def block_levels(own_key, extent, pieces, low, high):
    def one(dim, parts):
        heights = jax.random.uniform(jax.random.fold_in(jax.random.fold_in(own_key, 6), dim), (parts,), jnp.float32, low / len(pieces), high / len(pieces))
        return jnp.repeat(jnp.exp(heights), extent[dim] // parts).reshape((-1,) + (1,) * (len(extent) - dim - 1))

    factor_of = one(*pieces[0])
    for cut in pieces[1:]:
        factor_of = factor_of * one(*cut)
    return factor_of


def centred(key, shape, width, reach, cuts=(), kind=jnp.bfloat16):
    level = block_levels(key, shape, cuts, -0.22, 0.18) if cuts else 1.0
    values = jax.random.normal(key, shape, jnp.float32) * width * level
    return jnp.minimum(jnp.maximum(values, -reach), reach).astype(kind)


def gaussian_with(stream_key, extent, scale, reach, shards, heavy, kind=jnp.bfloat16):
    drawn = scale * jax.random.normal(stream_key, extent, jnp.float32)
    if shards:
        drawn = drawn * block_levels(stream_key, extent, shards, -0.22, 0.18)
    return jnp.clip(strengthened(drawn, jax.random.fold_in(stream_key, 3), *heavy), -reach, reach).astype(kind)


def setup_inputs(seed: int = 0) -> dict:
    key_list = jax.random.split(jax.random.key(seed), 6)
    return {
        "queries": draw_queries(jax.random.fold_in(key_list[5], 71), 0),
        "keys": draw_keys(jax.random.fold_in(key_list[5], 71), 0),
        "values": centred(key_list[2], (L, H, HS), 1.0, 6.0, ((0, 8), (1, 4))),
        "out_grad": gaussian_with(key_list[3], (L, D), 1.0, 6.0, ((0, 8),), (0, 1, 8, 2.0)),
        "wo": gaussian_with(key_list[4], (H * HS, D), (H * HS) ** -0.5, 0.125, ((0, 4), (1, 8)), (0, 1, 8, 2.0)),
    }


def attend(block_queries, block_keys, block_values, block_gradient):
    scale_factor = HS ** -0.5
    length = block_queries.shape[1]
    places = jnp.arange(length)
    visible = places[:, None] >= places[None, :]
    wide_queries = block_queries.astype(jnp.float32)
    wide_keys = block_keys.astype(jnp.float32)
    wide_values = block_values.astype(jnp.float32)
    wide_gradient = block_gradient.astype(jnp.float32)
    score_matrix = jnp.einsum("osl,ocl->osc", wide_queries, wide_keys) * scale_factor
    score_matrix = jnp.where(visible[None], score_matrix, -jnp.inf)
    highest = jnp.max(score_matrix, axis=-1, keepdims=True)
    lifted = jnp.exp(score_matrix - highest)
    weights = lifted / jnp.sum(lifted, axis=-1, keepdims=True)
    rounded_scores = weights.astype(jnp.bfloat16).astype(jnp.float32)
    attended_values = jnp.einsum("rti,ric->rtc", rounded_scores, wide_values).astype(jnp.bfloat16)
    probability_gradient = jnp.einsum("osl,ocl->osc", wide_gradient, wide_values)
    score_grad = weights * (probability_gradient - jnp.sum(weights * probability_gradient, axis=-1, keepdims=True))
    scores_lowered = score_grad.astype(jnp.bfloat16).astype(jnp.float32)
    queries_gradient = (jnp.einsum("rti,ric->rtc", scores_lowered, wide_keys) * scale_factor).astype(jnp.bfloat16)
    keys_gradient = (jnp.einsum("hfa,hfz->haz", scores_lowered, wide_queries) * scale_factor).astype(jnp.bfloat16)
    values_gradient = jnp.einsum("hfa,hfz->haz", rounded_scores, wide_gradient).astype(jnp.bfloat16)
    return attended_values, queries_gradient, keys_gradient, values_gradient


def row_heads(grids):
    moved = tuple(tensor[:, :, :, 0].transpose(0, 2, 1, 3) for tensor in grids)

    def one_row(row_items):
        return attend(row_items[0], row_items[1], row_items[2], row_items[3])

    results = lax.map(one_row, moved)
    return tuple(tensor.transpose(0, 2, 1, 3) for tensor in results)


def strided_heads(grids):
    half = H // 2
    moved = tuple(tensor[:, :, :, 1].transpose(1, 2, 0, 3).reshape(C * half, R, HS) for tensor in grids)
    results = attend(moved[0], moved[1], moved[2], moved[3])
    return tuple(tensor.reshape(C, half, R, HS).transpose(2, 0, 1, 3) for tensor in results)


def reference(queries, keys, values, out_grad, wo):
    attn_grad = jnp.dot(out_grad, wo.T, preferred_element_type=jnp.float32).astype(jnp.bfloat16)
    attn_grad = attn_grad.reshape(R * C, H, HS)
    grids = tuple(tensor.reshape(R, C, H // 2, 2, HS) for tensor in (queries, keys, values, attn_grad))
    row_parts = row_heads(grids)
    col_parts = strided_heads(grids)
    joined = tuple(jnp.stack([row_parts[index], col_parts[index]], axis=3).reshape(R * C, H, HS) for index in range(4))
    flat_attn = joined[0].reshape(R * C, H * HS)
    layer_out = jnp.dot(flat_attn, wo, preferred_element_type=jnp.float32).astype(jnp.bfloat16)
    proj_grad = jnp.dot(flat_attn.T, out_grad, preferred_element_type=jnp.float32).astype(jnp.bfloat16)
    return layer_out, joined[1], joined[2], joined[3], proj_grad
```

```python
import functools

import jax
import jax.numpy as jnp
from jax import lax
from jax.experimental import pallas as pl
from jax.experimental.pallas import tpu as pltpu
from jax.sharding import PartitionSpec as P

C = 512
LANE = 16
VMEM = pl.BlockSpec(memory_space=pltpu.VMEM)
BF16 = jnp.bfloat16
F32 = jnp.float32


def params(mib):
    return pltpu.CompilerParams(vmem_limit_bytes=mib * 1024 * 1024)


def dot(a, b, dims):
    return lax.dot_general(a, b, (dims, ((), ())), preferred_element_type=F32)


def softmax(scores):
    highest = jnp.max(scores, axis=-1, keepdims=True)
    lifted = jnp.exp(scores - highest)
    return lifted * (1.0 / jnp.sum(lifted, axis=-1, keepdims=True))


def split_kernel(n, rows, me, q_ref, k_ref, v_ref, *rest):
    chunks, row_refs, wide = rest[:n], rest[n : n + 3], rest[n + 3]
    step, row = pl.program_id(0), pl.program_id(1)
    width, heads, _ = q_ref.shape
    for array, ref in enumerate((q_ref, k_ref, v_ref)):
        wide[array] = ref[...].astype(F32).reshape(width * heads, ref.shape[2])
    for array in range(3):
        for head in range(heads // 2):
            even = wide[array, pl.ds(2 * head, width, stride=heads), :]
            row_refs[array][head] = even.astype(BF16)
    for d in range(n):

        @pl.when(step == d)
        def _():
            for array in range(3):
                for head in range(heads // 2):
                    odd = wide[array, pl.ds(2 * head + 1, width, stride=heads), :]
                    chunks[d][array, head, row] = odd.astype(BF16)


def split_inputs(me, queries, keys, values, n):
    tokens, heads, dim = queries.shape
    rows, width, half = tokens // C, C // n, heads // 2
    block = pl.BlockSpec((width, heads, dim), lambda d, r, me: (r * n + (me[0] ^ d), 0, 0))
    chunk = jax.ShapeDtypeStruct((3, half, rows, width, dim), BF16)
    by_head = jax.ShapeDtypeStruct((half, tokens, dim), BF16)
    out = pl.pallas_call(
        functools.partial(split_kernel, n, rows),
        grid_spec=pltpu.PrefetchScalarGridSpec(
            num_scalar_prefetch=1,
            grid=(n, rows),
            in_specs=[block] * 3,
            out_specs=[pl.BlockSpec(chunk.shape, lambda d, r, me: (0, 0, 0, 0, 0))] * n
            + [pl.BlockSpec((half, width, dim), lambda d, r, me: (0, r * n + (me[0] ^ d), 0))] * 3,
            scratch_shapes=[pltpu.VMEM((3, width * heads, dim), F32)],
        ),
        out_shape=[chunk] * n + [by_head] * 3,
        compiler_params=params(40),
        name="split_inputs",
    )(me, queries, keys, values)
    return out[:n], out[n:]


def join_kernel(n, rows, me, *refs):
    chunks, row_refs, outs, wide = refs[:n], refs[n : n + 3], refs[n + 3 : n + 6], refs[n + 6]
    step, row = pl.program_id(0), pl.program_id(1)
    width, heads, dim = outs[0].shape
    for d in range(n):

        @pl.when(step == d)
        def _():
            for array in range(3):
                for head in range(heads // 2):
                    wide[array, pl.ds(2 * head + 1, width, stride=heads), :] = chunks[d][array, head, row].astype(F32)

    for array in range(3):
        for head in range(heads // 2):
            wide[array, pl.ds(2 * head, width, stride=heads), :] = row_refs[array][head].astype(F32)
        outs[array][...] = wide[array].reshape(width, heads, dim).astype(BF16)


def join_gradients(me, chunks, by_head, n):
    _, half, rows, width, dim = chunks[0].shape
    tokens, heads = by_head[0].shape[1], 2 * half
    whole = jax.ShapeDtypeStruct((tokens, heads, dim), BF16)
    return pl.pallas_call(
        functools.partial(join_kernel, n, rows),
        grid_spec=pltpu.PrefetchScalarGridSpec(
            num_scalar_prefetch=1,
            grid=(n, rows),
            in_specs=[pl.BlockSpec(chunks[0].shape, lambda d, r, me: (0, 0, 0, 0, 0))] * n
            + [pl.BlockSpec((half, width, dim), lambda d, r, me: (0, r * n + (me[0] ^ d), 0))] * 3,
            out_specs=[pl.BlockSpec((width, heads, dim), lambda d, r, me: (r * n + (me[0] ^ d), 0, 0))] * 3,
            scratch_shapes=[pltpu.VMEM((3, width * heads, dim), F32)],
        ),
        out_shape=[whole] * 3,
        compiler_params=params(40),
        name="join_gradients",
    )(me, *chunks, *by_head)


def deal_kernel(n, me, flat_ref, *chunks):
    half, rows, width, dim = chunks[0].shape
    for d in range(n):
        column = pl.multiple_of((me[0] ^ d) * width, width)
        for row in range(rows):
            for head in range(half):
                chunks[d][head, row] = flat_ref[pl.ds(row * C + column, width), head * dim : (head + 1) * dim]


def deal(me, flat, n, dim):
    tokens, span = flat.shape
    chunk = jax.ShapeDtypeStruct((span // dim, tokens // C, C // n, dim), BF16)
    return pl.pallas_call(
        functools.partial(deal_kernel, n),
        in_specs=[pl.BlockSpec(memory_space=pltpu.SMEM), VMEM],
        out_specs=[VMEM] * n,
        out_shape=[chunk] * n,
        compiler_params=params(16),
        name="deal",
    )(me, flat)


def collect_kernel(n, me, *refs):
    chunks, flat_ref = refs[:n], refs[n]
    half, rows, width, dim = chunks[0].shape
    for d in range(n):
        column = pl.multiple_of((me[0] ^ d) * width, width)
        for row in range(rows):
            for head in range(half):
                flat_ref[pl.ds(row * C + column, width), head * dim : (head + 1) * dim] = chunks[d][head, row]


def collect(me, chunks, n):
    half, rows, width, dim = chunks[0].shape
    return pl.pallas_call(
        functools.partial(collect_kernel, n),
        in_specs=[pl.BlockSpec(memory_space=pltpu.SMEM)] + [VMEM] * n,
        out_specs=VMEM,
        out_shape=jax.ShapeDtypeStruct((rows * C, half * dim), BF16),
        compiler_params=params(16),
        name="collect",
    )(me, *chunks)


def row_blocks(length):
    step = length // 2
    return [(start, step) for start in range(0, length, step)]


def row_probs(q, k, start, step, scale):
    scores = dot(q, k, ((1,), (1,))) * scale
    place = lax.broadcasted_iota(jnp.int32, scores.shape, 0) + start
    seen = lax.broadcasted_iota(jnp.int32, scores.shape, 1)
    return softmax(jnp.where(place >= seen, scores, -jnp.inf))


def row_forward_kernel(scale, q_ref, k_ref, v_ref, o_ref):
    for start, step in row_blocks(q_ref.shape[0]):
        stop = start + step
        probs = row_probs(q_ref[start:stop], k_ref[:stop], start, step, scale)
        o_ref[start:stop] = dot(probs.astype(BF16), v_ref[:stop], ((1,), (0,))).astype(BF16)


def row_forward(q, k, v):
    half, tokens, dim = q.shape
    by_head = pl.BlockSpec((pl.squeezed, C, dim), lambda r, h: (h, r, 0))
    return pl.pallas_call(
        functools.partial(row_forward_kernel, dim**-0.5),
        grid=(tokens // C, half),
        in_specs=[by_head] * 3,
        out_specs=pl.BlockSpec((C, dim), lambda r, h: (r, h)),
        out_shape=jax.ShapeDtypeStruct((tokens, half * dim), BF16),
        compiler_params=params(24),
        cost_estimate=pl.CostEstimate(
            flops=4 * tokens * C * half * dim, bytes_accessed=8 * tokens * half * dim, transcendentals=tokens * C * half
        ),
        name="row_forward",
    )(q, k, v)


def row_backward_kernel(scale, q_ref, k_ref, v_ref, g_ref, dq_ref, dk_ref, dv_ref, k_sum, v_sum):
    k_sum[...] = jnp.zeros_like(k_sum)
    v_sum[...] = jnp.zeros_like(v_sum)
    for start, step in row_blocks(q_ref.shape[0]):
        stop = start + step
        q, k, grad = q_ref[start:stop], k_ref[:stop], g_ref[start:stop]
        probs = row_probs(q, k, start, step, scale)
        prob_grad = dot(grad, v_ref[:stop], ((1,), (1,)))
        inner = jnp.sum(probs * prob_grad, axis=-1, keepdims=True)
        score_low = (probs * (prob_grad - inner)).astype(BF16)
        dq_ref[start:stop] = (dot(score_low, k, ((1,), (0,))) * scale).astype(BF16)
        k_sum[:stop] += dot(score_low, q, ((0,), (0,)))
        v_sum[:stop] += dot(probs.astype(BF16), grad, ((0,), (0,)))
    dk_ref[...] = (k_sum[...] * scale).astype(BF16)
    dv_ref[...] = v_sum[...].astype(BF16)


def row_backward(q, k, v, grad):
    half, tokens, dim = q.shape
    by_head = pl.BlockSpec((pl.squeezed, C, dim), lambda r, h: (h, r, 0))
    return pl.pallas_call(
        functools.partial(row_backward_kernel, dim**-0.5),
        grid=(tokens // C, half),
        in_specs=[by_head] * 3 + [pl.BlockSpec((C, dim), lambda r, h: (r, h))],
        out_specs=[by_head] * 3,
        out_shape=[jax.ShapeDtypeStruct(q.shape, BF16)] * 3,
        scratch_shapes=[pltpu.VMEM((C, dim), F32)] * 2,
        compiler_params=params(32),
        cost_estimate=pl.CostEstimate(
            flops=10 * tokens * C * half * dim, bytes_accessed=14 * tokens * half * dim, transcendentals=tokens * C * half
        ),
        name="row_backward",
    )(q, k, v, grad)


def column_mask(me, n, rows):
    size = n * rows * LANE

    def parts(axis):
        place = lax.broadcasted_iota(jnp.int32, (size, size), axis)
        line, column = place // LANE, place % LANE
        return ((line // rows) ^ me) * rows + line % rows, column

    row_q, column_q = parts(0)
    row_k, column_k = parts(1)
    return (column_q == column_k) & (row_q >= row_k)


def gathered(chunks, index, at):
    rows, dim = chunks[0].shape[-3], chunks[0].shape[-1]
    return jnp.concatenate(
        [chunk[(*index, row, pl.ds(at, LANE), slice(None))] for chunk in chunks for row in range(rows)], axis=0
    )


def scattered(chunks, index, at, value):
    rows = chunks[0].shape[-3]
    for d, chunk in enumerate(chunks):
        for row in range(rows):
            line = d * rows + row
            chunk[(*index, row, pl.ds(at, LANE), slice(None))] = value[line * LANE : (line + 1) * LANE]


def column_probs(bias, q, k, scale):
    return softmax(dot(q, k, ((1,), (1,))) * scale + bias[...])


def column_forward_kernel(n, scale, me, *refs):
    chunks, outs, bias = refs[:n], refs[n : 2 * n], refs[2 * n]
    _, half, rows, width, _ = chunks[0].shape
    bias[...] = jnp.where(column_mask(me[0], n, rows), 0.0, -jnp.inf)
    blocks = width // LANE

    @pl.loop(0, half * blocks)
    def _(step):
        head, at = step // blocks, pl.multiple_of(step % blocks * LANE, LANE)
        q, k, v = (gathered(chunks, (array, head), at) for array in range(3))
        probs = column_probs(bias, q, k, scale)
        scattered(outs, (head,), at, dot(probs.astype(BF16), v, ((1,), (0,))).astype(BF16))


def column_forward(me, chunks, n):
    _, half, rows, width, dim = chunks[0].shape
    size = n * rows * LANE
    return pl.pallas_call(
        functools.partial(column_forward_kernel, n, dim**-0.5),
        in_specs=[pl.BlockSpec(memory_space=pltpu.SMEM)] + [VMEM] * n,
        out_specs=[VMEM] * n,
        out_shape=[jax.ShapeDtypeStruct((half, rows, width, dim), BF16)] * n,
        scratch_shapes=[pltpu.VMEM((size, size), F32)],
        compiler_params=params(24),
        cost_estimate=pl.CostEstimate(
            flops=4 * size * size * dim * half * width // LANE,
            bytes_accessed=8 * n * half * rows * width * dim,
            transcendentals=size * size * half * width // LANE,
        ),
        name="column_forward",
    )(me, *chunks)


def column_backward_kernel(n, scale, me, *refs):
    chunks, grads, outs, bias = refs[:n], refs[n : 2 * n], refs[2 * n : 3 * n], refs[3 * n]
    _, half, rows, width, _ = chunks[0].shape
    bias[...] = jnp.where(column_mask(me[0], n, rows), 0.0, -jnp.inf)
    blocks = width // LANE

    @pl.loop(0, half * blocks)
    def _(step):
        head, at = step // blocks, pl.multiple_of(step % blocks * LANE, LANE)
        q, k, v = (gathered(chunks, (array, head), at) for array in range(3))
        grad = gathered(grads, (head,), at)
        probs = column_probs(bias, q, k, scale)
        prob_grad = dot(grad, v, ((1,), (1,)))
        inner = jnp.sum(probs * prob_grad, axis=-1, keepdims=True)
        score_low = (probs * (prob_grad - inner)).astype(BF16)
        scattered(outs, (0, head), at, (dot(score_low, k, ((1,), (0,))) * scale).astype(BF16))
        scattered(outs, (1, head), at, (dot(score_low, q, ((0,), (0,))) * scale).astype(BF16))
        scattered(outs, (2, head), at, dot(probs.astype(BF16), grad, ((0,), (0,))).astype(BF16))


def column_backward(me, chunks, grads, n):
    _, half, rows, width, dim = chunks[0].shape
    size = n * rows * LANE
    return pl.pallas_call(
        functools.partial(column_backward_kernel, n, dim**-0.5),
        in_specs=[pl.BlockSpec(memory_space=pltpu.SMEM)] + [VMEM] * (2 * n),
        out_specs=[VMEM] * n,
        out_shape=[jax.ShapeDtypeStruct(chunks[0].shape, BF16)] * n,
        scratch_shapes=[pltpu.VMEM((size, size), F32)],
        compiler_params=params(24),
        cost_estimate=pl.CostEstimate(
            flops=10 * size * size * dim * half * width // LANE,
            bytes_accessed=14 * n * half * rows * width * dim,
            transcendentals=size * size * half * width // LANE,
        ),
        name="column_backward",
    )(me, *chunks, *grads)


def swap(chunks, n):
    return [chunks[0]] + [
        lax.ppermute(chunks[d], "ctx", [(place, place ^ d) for place in range(n)]) for d in range(1, n)
    ]


def on_device(queries, keys, values, out_grad, wo, *, n):
    tokens, heads, dim = queries.shape
    half, model = heads // 2, out_grad.shape[1]
    me = lax.axis_index("ctx").astype(jnp.int32).reshape(1)
    chunks, by_head = split_inputs(me, queries, keys, values, n)
    chunks = swap(chunks, n)
    wo_pairs = wo.reshape(half, 2, dim, wo.shape[1])

    def weight(kind):
        part = wo_pairs[:, kind].reshape(half * dim, wo.shape[1])
        return lax.all_gather(part, "ctx", axis=1, tiled=True)

    wo_column, wo_row = weight(1), weight(0)
    grad_column = dot(out_grad, wo_column, ((1,), (1,))).astype(BF16)
    grads = swap(deal(me, grad_column, n, dim), n)

    row_out = row_forward(*by_head)
    proj_row = dot(row_out, out_grad, ((0,), (0,))).astype(BF16)
    proj_row = lax.psum_scatter(proj_row, "ctx", scatter_dimension=1, tiled=True)

    column_out = collect(me, swap(column_forward(me, chunks, n), n), n)
    proj_column = dot(column_out, out_grad, ((0,), (0,))).astype(BF16)
    proj_column = lax.psum_scatter(proj_column, "ctx", scatter_dimension=1, tiled=True)

    partial_out = dot(row_out, wo_row, ((1,), (0,))) + dot(column_out, wo_column, ((1,), (0,)))
    layer_out = lax.psum_scatter(partial_out.astype(BF16), "head", scatter_dimension=1, tiled=True)

    grad_row = dot(out_grad, wo_row, ((1,), (1,))).astype(BF16)
    row_grads = row_backward(*by_head, grad_row)
    column_grads = swap(column_backward(me, chunks, grads, n), n)
    gradients = join_gradients(me, column_grads, row_grads, n)

    shape = (half, dim, proj_row.shape[1])
    proj_grad = jnp.stack([proj_row.reshape(shape), proj_column.reshape(shape)], axis=1)
    return (layer_out, *gradients, proj_grad.reshape(heads * dim, shape[2]))


def solution(mesh):
    in_specs = (
        P("ctx", "head", None),
        P("ctx", "head", None),
        P("ctx", "head", None),
        P("ctx", None),
        P("head", "ctx"),
    )
    out_specs = (
        P("ctx", "head"),
        P("ctx", "head", None),
        P("ctx", "head", None),
        P("ctx", "head", None),
        P("head", "ctx"),
    )
    return jax.shard_map(
        functools.partial(on_device, n=mesh.shape["ctx"]),
        mesh=mesh,
        in_specs=in_specs,
        out_specs=out_specs,
        check_vma=False,
    )
```

```python
import functools

import jax
import jax.numpy as jnp
from jax import lax
from jax.experimental import pallas as pl
from jax.experimental.pallas import tpu as pltpu
from jax.sharding import PartitionSpec as P

C = 512
LANE = 16
VMEM = pl.BlockSpec(memory_space=pltpu.VMEM)
BF16 = jnp.bfloat16
F32 = jnp.float32


def params(mib):
    return pltpu.CompilerParams(vmem_limit_bytes=mib * 1024 * 1024)


def dot(a, b, dims):
    return lax.dot_general(a, b, (dims, ((), ())), preferred_element_type=F32)


def softmax(scores):
    highest = jnp.max(scores, axis=-1, keepdims=True)
    lifted = jnp.exp(scores - highest)
    return lifted * (1.0 / jnp.sum(lifted, axis=-1, keepdims=True))


def split_kernel(n, rows, me, q_ref, k_ref, v_ref, *rest):
    chunks, row_refs, wide = rest[:n], rest[n : n + 3], rest[n + 3]
    step, row = pl.program_id(0), pl.program_id(1)
    width, heads, _ = q_ref.shape
    for array, ref in enumerate((q_ref, k_ref, v_ref)):
        wide[array] = ref[...].astype(F32).reshape(width * heads, ref.shape[2])
    for array in range(3):
        for head in range(heads // 2):
            even = wide[array, pl.ds(2 * head, width, stride=heads), :]
            row_refs[array][head] = even.astype(BF16)
    for d in range(n):

        @pl.when(step == d)
        def _():
            for array in range(3):
                for head in range(heads // 2):
                    odd = wide[array, pl.ds(2 * head + 1, width, stride=heads), :]
                    chunks[d][array, head, row] = odd.astype(BF16)


def split_inputs(me, queries, keys, values, n):
    tokens, heads, dim = queries.shape
    rows, width, half = tokens // C, C // n, heads // 2
    block = pl.BlockSpec((width, heads, dim), lambda d, r, me: (r * n + (me[0] ^ d), 0, 0))
    chunk = jax.ShapeDtypeStruct((3, half, rows, width, dim), BF16)
    by_head = jax.ShapeDtypeStruct((half, tokens, dim), BF16)
    out = pl.pallas_call(
        functools.partial(split_kernel, n, rows),
        grid_spec=pltpu.PrefetchScalarGridSpec(
            num_scalar_prefetch=1,
            grid=(n, rows),
            in_specs=[block] * 3,
            out_specs=[pl.BlockSpec(chunk.shape, lambda d, r, me: (0, 0, 0, 0, 0))] * n
            + [pl.BlockSpec((half, width, dim), lambda d, r, me: (0, r * n + (me[0] ^ d), 0))] * 3,
            scratch_shapes=[pltpu.VMEM((3, width * heads, dim), F32)],
        ),
        out_shape=[chunk] * n + [by_head] * 3,
        compiler_params=params(40),
        name="split_inputs",
    )(me, queries, keys, values)
    return out[:n], out[n:]


def join_kernel(n, rows, me, *refs):
    chunks, row_refs, outs, wide = refs[:n], refs[n : n + 3], refs[n + 3 : n + 6], refs[n + 6]
    step, row = pl.program_id(0), pl.program_id(1)
    width, heads, dim = outs[0].shape
    for d in range(n):

        @pl.when(step == d)
        def _():
            for array in range(3):
                for head in range(heads // 2):
                    wide[array, pl.ds(2 * head + 1, width, stride=heads), :] = chunks[d][array, head, row].astype(F32)

    for array in range(3):
        for head in range(heads // 2):
            wide[array, pl.ds(2 * head, width, stride=heads), :] = row_refs[array][head].astype(F32)
        outs[array][...] = wide[array].reshape(width, heads, dim).astype(BF16)


def join_gradients(me, chunks, by_head, n):
    _, half, rows, width, dim = chunks[0].shape
    tokens, heads = by_head[0].shape[1], 2 * half
    whole = jax.ShapeDtypeStruct((tokens, heads, dim), BF16)
    return pl.pallas_call(
        functools.partial(join_kernel, n, rows),
        grid_spec=pltpu.PrefetchScalarGridSpec(
            num_scalar_prefetch=1,
            grid=(n, rows),
            in_specs=[pl.BlockSpec(chunks[0].shape, lambda d, r, me: (0, 0, 0, 0, 0))] * n
            + [pl.BlockSpec((half, width, dim), lambda d, r, me: (0, r * n + (me[0] ^ d), 0))] * 3,
            out_specs=[pl.BlockSpec((width, heads, dim), lambda d, r, me: (r * n + (me[0] ^ d), 0, 0))] * 3,
            scratch_shapes=[pltpu.VMEM((3, width * heads, dim), F32)],
        ),
        out_shape=[whole] * 3,
        compiler_params=params(40),
        name="join_gradients",
    )(me, *chunks, *by_head)


def collect_kernel(n, me, row_ref, *refs):
    chunks, flat_ref, both_ref = refs[:n], refs[n], refs[n + 1]
    half, rows, width, dim = chunks[0].shape
    for head in range(half):
        both_ref[:, 2 * head * dim : (2 * head + 1) * dim] = row_ref[:, head * dim : (head + 1) * dim]
    for d in range(n):
        column = pl.multiple_of((me[0] ^ d) * width, width)
        for row in range(rows):
            for head in range(half):
                part = chunks[d][head, row]
                flat_ref[pl.ds(row * C + column, width), head * dim : (head + 1) * dim] = part
                both_ref[pl.ds(row * C + column, width), (2 * head + 1) * dim : (2 * head + 2) * dim] = part


def collect(me, row_out, chunks, n):
    half, rows, width, dim = chunks[0].shape
    return pl.pallas_call(
        functools.partial(collect_kernel, n),
        in_specs=[pl.BlockSpec(memory_space=pltpu.SMEM)] + [VMEM] * (n + 1),
        out_specs=[VMEM] * 2,
        out_shape=[
            jax.ShapeDtypeStruct((rows * C, half * dim), BF16),
            jax.ShapeDtypeStruct((rows * C, 2 * half * dim), BF16),
        ],
        compiler_params=params(24),
        name="collect",
    )(me, row_out, *chunks)


def attn_grad_kernel(n, dim, me, ids, grad_ref, *refs):
    blocks, row_ref, chunks = refs[:n], refs[n], refs[n + 1 : 2 * n + 1]
    weight, total, sem = refs[2 * n + 1 :]
    step = pl.program_id(0)
    half, rows, width, _ = chunks[0].shape
    tokens = grad_ref.shape[0]
    tile = tokens // 4

    @pl.when(step == 0)
    def _():
        for d in range(n):
            pltpu.make_async_copy(blocks[d], weight.at[ids[d]], sem.at[ids[d]]).start()
        total[...] = jnp.zeros_like(total)

    pltpu.make_async_copy(blocks[0], weight.at[step], sem.at[step]).wait()

    @pl.loop(0, tokens, step=tile)
    def _(at):
        at = pl.multiple_of(at, tile)
        total[pl.ds(at, tile)] += dot(grad_ref[pl.ds(at, tile)], weight[step], ((1,), (1,)))

    @pl.when(step == n - 1)
    def _():
        for head in range(half):
            row_ref[:, head * dim : (head + 1) * dim] = total[:, 2 * head * dim : (2 * head + 1) * dim].astype(BF16)
            for d in range(n):
                column = pl.multiple_of((me[0] ^ d) * width, width)
                for row in range(rows):
                    part = total[pl.ds(row * C + column, width), (2 * head + 1) * dim : (2 * head + 2) * dim]
                    chunks[d][head, row] = part.astype(BF16)


def attn_grad(me, ids, out_grad, blocks, dim):
    n, (span, depth) = len(blocks), blocks[0].shape
    tokens, half = out_grad.shape[0], span // dim // 2
    chunk = jax.ShapeDtypeStruct((half, tokens // C, C // n, dim), BF16)
    out = pl.pallas_call(
        functools.partial(attn_grad_kernel, n, dim),
        grid_spec=pltpu.PrefetchScalarGridSpec(
            num_scalar_prefetch=2,
            grid=(n,),
            in_specs=[pl.BlockSpec((tokens, depth), lambda b, me, ids: (0, b))] + [pl.BlockSpec(memory_space=pl.ANY)] * n,
            out_specs=[pl.BlockSpec((tokens, half * dim), lambda b, me, ids: (0, 0))]
            + [pl.BlockSpec(chunk.shape, lambda b, me, ids: (0, 0, 0, 0))] * n,
            scratch_shapes=[
                pltpu.VMEM((n, span, depth), BF16),
                pltpu.VMEM((tokens, span), F32),
                pltpu.SemaphoreType.DMA((n,)),
            ],
        ),
        out_shape=[jax.ShapeDtypeStruct((tokens, half * dim), BF16)] + [chunk] * n,
        compiler_params=params(40),
        cost_estimate=pl.CostEstimate(
            flops=2 * tokens * span * depth * n,
            bytes_accessed=2 * n * depth * (tokens + span) + 2 * tokens * span,
            transcendentals=0,
        ),
        name="attn_grad",
    )(me, ids, out_grad, *blocks)
    return out[0], out[1:]


def layer_kernel(n, count, adds, ids, wanted, flat_ref, *refs):
    blocks, extra, out_ref = refs[:n], refs[n : n + adds], refs[n + adds]
    weight, sem = refs[n + adds + 1 :]
    step = pl.program_id(0)
    tokens = flat_ref.shape[0]
    tile = tokens // 4

    @pl.when(step == 0)
    def _():
        for s in range(count):
            for d in range(n):

                @pl.when(ids[d] == wanted[s])
                def _():
                    pltpu.make_async_copy(blocks[d], weight.at[s], sem.at[s]).start()

    pltpu.make_async_copy(blocks[0], weight.at[step], sem.at[step]).wait()

    @pl.loop(0, tokens, step=tile)
    def _(at):
        at = pl.multiple_of(at, tile)
        value = dot(flat_ref[pl.ds(at, tile)], weight[step], ((1,), (0,)))
        for ref in extra:
            value = value + ref[pl.ds(at, tile)].astype(F32)
        out_ref[pl.ds(at, tile)] = value.astype(BF16)


def layer_part(ids, flat, blocks, wanted, extra, first):
    n, (span, depth) = len(blocks), blocks[0].shape
    tokens, count = flat.shape[0], wanted.shape[0]
    by_column = pl.BlockSpec((tokens, depth), lambda s, ids, wanted: (0, s))
    return pl.pallas_call(
        functools.partial(layer_kernel, n, count, len(extra)),
        grid_spec=pltpu.PrefetchScalarGridSpec(
            num_scalar_prefetch=2,
            grid=(count,),
            in_specs=[pl.BlockSpec((tokens, span), lambda s, ids, wanted: (0, 0))]
            + [pl.BlockSpec(memory_space=pl.ANY)] * n
            + [pl.BlockSpec((tokens, depth), functools.partial(lambda f, s, ids, wanted: (0, s + f), f)) for f in first],
            out_specs=by_column,
            scratch_shapes=[pltpu.VMEM((count, span, depth), BF16), pltpu.SemaphoreType.DMA((count,))],
        ),
        out_shape=jax.ShapeDtypeStruct((tokens, count * depth), BF16),
        compiler_params=params(32),
        cost_estimate=pl.CostEstimate(
            flops=2 * tokens * span * depth * count,
            bytes_accessed=2 * (count * depth * (tokens + span) + tokens * span),
            transcendentals=0,
        ),
        name="layer_part",
    )(ids, wanted, flat, *blocks, *extra)


def row_blocks(length):
    step = length // 2
    return [(start, step) for start in range(0, length, step)]


def row_probs(q, k, start, step, scale):
    scores = dot(q, k, ((1,), (1,))) * scale
    place = lax.broadcasted_iota(jnp.int32, scores.shape, 0) + start
    seen = lax.broadcasted_iota(jnp.int32, scores.shape, 1)
    return softmax(jnp.where(place >= seen, scores, -jnp.inf))


def row_forward_kernel(scale, q_ref, k_ref, v_ref, o_ref):
    for start, step in row_blocks(q_ref.shape[0]):
        stop = start + step
        probs = row_probs(q_ref[start:stop], k_ref[:stop], start, step, scale)
        o_ref[start:stop] = dot(probs.astype(BF16), v_ref[:stop], ((1,), (0,))).astype(BF16)


def row_forward(q, k, v):
    half, tokens, dim = q.shape
    by_head = pl.BlockSpec((pl.squeezed, C, dim), lambda r, h: (h, r, 0))
    return pl.pallas_call(
        functools.partial(row_forward_kernel, dim**-0.5),
        grid=(tokens // C, half),
        in_specs=[by_head] * 3,
        out_specs=pl.BlockSpec((C, dim), lambda r, h: (r, h)),
        out_shape=jax.ShapeDtypeStruct((tokens, half * dim), BF16),
        compiler_params=params(24),
        cost_estimate=pl.CostEstimate(
            flops=4 * tokens * C * half * dim, bytes_accessed=8 * tokens * half * dim, transcendentals=tokens * C * half
        ),
        name="row_forward",
    )(q, k, v)


def row_backward_kernel(scale, q_ref, k_ref, v_ref, g_ref, dq_ref, dk_ref, dv_ref, k_sum, v_sum):
    k_sum[...] = jnp.zeros_like(k_sum)
    v_sum[...] = jnp.zeros_like(v_sum)
    for start, step in row_blocks(q_ref.shape[0]):
        stop = start + step
        q, k, grad = q_ref[start:stop], k_ref[:stop], g_ref[start:stop]
        probs = row_probs(q, k, start, step, scale)
        prob_grad = dot(grad, v_ref[:stop], ((1,), (1,)))
        inner = jnp.sum(probs * prob_grad, axis=-1, keepdims=True)
        score_low = (probs * (prob_grad - inner)).astype(BF16)
        dq_ref[start:stop] = (dot(score_low, k, ((1,), (0,))) * scale).astype(BF16)
        k_sum[:stop] += dot(score_low, q, ((0,), (0,)))
        v_sum[:stop] += dot(probs.astype(BF16), grad, ((0,), (0,)))
    dk_ref[...] = (k_sum[...] * scale).astype(BF16)
    dv_ref[...] = v_sum[...].astype(BF16)


def row_backward(q, k, v, grad):
    half, tokens, dim = q.shape
    by_head = pl.BlockSpec((pl.squeezed, C, dim), lambda r, h: (h, r, 0))
    return pl.pallas_call(
        functools.partial(row_backward_kernel, dim**-0.5),
        grid=(tokens // C, half),
        in_specs=[by_head] * 3 + [pl.BlockSpec((C, dim), lambda r, h: (r, h))],
        out_specs=[by_head] * 3,
        out_shape=[jax.ShapeDtypeStruct(q.shape, BF16)] * 3,
        scratch_shapes=[pltpu.VMEM((C, dim), F32)] * 2,
        compiler_params=params(32),
        cost_estimate=pl.CostEstimate(
            flops=10 * tokens * C * half * dim, bytes_accessed=14 * tokens * half * dim, transcendentals=tokens * C * half
        ),
        name="row_backward",
    )(q, k, v, grad)


def column_mask(me, n, rows):
    size = n * rows * LANE

    def parts(axis):
        place = lax.broadcasted_iota(jnp.int32, (size, size), axis)
        line, column = place // LANE, place % LANE
        return ((line // rows) ^ me) * rows + line % rows, column

    row_q, column_q = parts(0)
    row_k, column_k = parts(1)
    return (column_q == column_k) & (row_q >= row_k)


def gathered(chunks, index, at):
    rows, dim = chunks[0].shape[-3], chunks[0].shape[-1]
    return jnp.concatenate(
        [chunk[(*index, row, pl.ds(at, LANE), slice(None))] for chunk in chunks for row in range(rows)], axis=0
    )


def scattered(chunks, index, at, value):
    rows = chunks[0].shape[-3]
    for d, chunk in enumerate(chunks):
        for row in range(rows):
            line = d * rows + row
            chunk[(*index, row, pl.ds(at, LANE), slice(None))] = value[line * LANE : (line + 1) * LANE]


def column_probs(bias, q, k, scale):
    return softmax(dot(q, k, ((1,), (1,))) * scale + bias[...])


def column_forward_kernel(n, scale, me, *refs):
    chunks, outs, bias = refs[:n], refs[n : 2 * n], refs[2 * n]
    _, half, rows, width, _ = chunks[0].shape
    bias[...] = jnp.where(column_mask(me[0], n, rows), 0.0, -jnp.inf)
    blocks = width // LANE

    @pl.loop(0, half * blocks)
    def _(step):
        head, at = step // blocks, pl.multiple_of(step % blocks * LANE, LANE)
        q, k, v = (gathered(chunks, (array, head), at) for array in range(3))
        probs = column_probs(bias, q, k, scale)
        scattered(outs, (head,), at, dot(probs.astype(BF16), v, ((1,), (0,))).astype(BF16))


def column_forward(me, chunks, n):
    _, half, rows, width, dim = chunks[0].shape
    size = n * rows * LANE
    return pl.pallas_call(
        functools.partial(column_forward_kernel, n, dim**-0.5),
        in_specs=[pl.BlockSpec(memory_space=pltpu.SMEM)] + [VMEM] * n,
        out_specs=[VMEM] * n,
        out_shape=[jax.ShapeDtypeStruct((half, rows, width, dim), BF16)] * n,
        scratch_shapes=[pltpu.VMEM((size, size), F32)],
        compiler_params=params(24),
        cost_estimate=pl.CostEstimate(
            flops=4 * size * size * dim * half * width // LANE,
            bytes_accessed=8 * n * half * rows * width * dim,
            transcendentals=size * size * half * width // LANE,
        ),
        name="column_forward",
    )(me, *chunks)


def column_backward_kernel(n, scale, me, *refs):
    chunks, grads, outs, bias = refs[:n], refs[n : 2 * n], refs[2 * n : 3 * n], refs[3 * n]
    _, half, rows, width, _ = chunks[0].shape
    bias[...] = jnp.where(column_mask(me[0], n, rows), 0.0, -jnp.inf)
    blocks = width // LANE

    @pl.loop(0, half * blocks)
    def _(step):
        head, at = step // blocks, pl.multiple_of(step % blocks * LANE, LANE)
        q, k, v = (gathered(chunks, (array, head), at) for array in range(3))
        grad = gathered(grads, (head,), at)
        probs = column_probs(bias, q, k, scale)
        prob_grad = dot(grad, v, ((1,), (1,)))
        inner = jnp.sum(probs * prob_grad, axis=-1, keepdims=True)
        score_low = (probs * (prob_grad - inner)).astype(BF16)
        scattered(outs, (0, head), at, (dot(score_low, k, ((1,), (0,))) * scale).astype(BF16))
        scattered(outs, (1, head), at, (dot(score_low, q, ((0,), (0,))) * scale).astype(BF16))
        scattered(outs, (2, head), at, dot(probs.astype(BF16), grad, ((0,), (0,))).astype(BF16))


def column_backward(me, chunks, grads, n):
    _, half, rows, width, dim = chunks[0].shape
    size = n * rows * LANE
    return pl.pallas_call(
        functools.partial(column_backward_kernel, n, dim**-0.5),
        in_specs=[pl.BlockSpec(memory_space=pltpu.SMEM)] + [VMEM] * (2 * n),
        out_specs=[VMEM] * n,
        out_shape=[jax.ShapeDtypeStruct(chunks[0].shape, BF16)] * n,
        scratch_shapes=[pltpu.VMEM((size, size), F32)],
        compiler_params=params(24),
        cost_estimate=pl.CostEstimate(
            flops=10 * size * size * dim * half * width // LANE,
            bytes_accessed=14 * n * half * rows * width * dim,
            transcendentals=size * size * half * width // LANE,
        ),
        name="column_backward",
    )(me, *chunks, *grads)


def swap(chunks, n):
    order = [d for pair in zip(range(n // 2, n), range(n // 2)) for d in pair if d]
    out = list(chunks)
    for d in order:
        out[d] = lax.ppermute(chunks[d], "ctx", [(place, place ^ d) for place in range(n)])
    return out


def gather_weight(me, wo, n):
    inner = n // 4
    line = me[0] // inner

    def along(pairs, block):
        return lax.ppermute(block, "ctx", [(a * inner + y, b * inner + y) for a, b in pairs for y in range(inner)])

    middle = (line == 1) | (line == 2)
    pair, cross, outward = [(0, 1), (1, 0), (2, 3), (3, 2)], [(1, 2), (2, 1)], [(1, 0), (2, 3)]
    near = along(pair, wo)
    cross_own = along(cross, wo)
    cross_near = along(cross, near)
    far_own = jnp.where(middle, cross_own, along(outward, cross_own))
    far_near = jnp.where(middle, cross_near, along(outward, cross_near))
    upper = line < 2
    lines = [line, line ^ 1, jnp.where(upper, 2, 1), jnp.where(upper, 3, 0)]
    blocks, ids = [], []
    for block, owner in zip((wo, near, far_own, far_near), lines):
        for e in range(inner):
            if e:
                blocks.append(lax.ppermute(block, "ctx", [(place, place ^ e) for place in range(n)]))
            else:
                blocks.append(block)
            ids.append(owner * inner + (me[0] % inner ^ e))
    return blocks, jnp.stack(ids).astype(jnp.int32)


def scatter_layer(ids, flat, blocks, heads_n):
    mine = lax.axis_index("head").astype(jnp.int32)
    per = len(blocks) // heads_n

    def wanted(offsets):
        return jnp.stack([(mine ^ g) * per + b for g in offsets for b in range(per)]).astype(jnp.int32)

    def move(part, g):
        return lax.ppermute(part, "head", [(place, place ^ g) for place in range(heads_n)])

    even = list(range(0, heads_n, 2))
    near = move(layer_part(ids, flat, blocks, wanted([g + 1 for g in even]), [], []), 1)
    far = [move(layer_part(ids, flat, blocks, wanted([g]), [near], [g // 2 * per]), g) for g in even[1:]]
    return layer_part(ids, flat, blocks, wanted([0]), [near] + far, [0] * (1 + len(far)))


def on_device(queries, keys, values, out_grad, wo, *, n, heads_n):
    tokens, heads, dim = queries.shape
    half = heads // 2
    me = lax.axis_index("ctx").astype(jnp.int32).reshape(1)
    chunks, by_head = split_inputs(me, queries, keys, values, n)
    chunks = swap(chunks, n)
    blocks, ids = gather_weight(me, wo, n)

    row_out = row_forward(*by_head)
    proj_row = dot(row_out, out_grad, ((0,), (0,))).astype(BF16)
    proj_row = lax.psum_scatter(proj_row, "ctx", scatter_dimension=1, tiled=True)

    grad_row, grads = attn_grad(me, ids, out_grad, blocks, dim)
    grads = swap(grads, n)
    column_out, flat = collect(me, row_out, swap(column_forward(me, chunks, n), n), n)
    column_out, proj_row = lax.optimization_barrier((column_out, proj_row))
    proj_column = dot(column_out, out_grad, ((0,), (0,))).astype(BF16)
    proj_column = lax.psum_scatter(proj_column, "ctx", scatter_dimension=1, tiled=True)

    layer_out = scatter_layer(ids, flat, blocks, heads_n)
    column_grads = swap(column_backward(me, chunks, grads, n), n)
    row_grads = row_backward(*by_head, grad_row)
    gradients = join_gradients(me, column_grads, row_grads, n)

    shape = (half, dim, proj_row.shape[1])
    proj_grad = jnp.stack([proj_row.reshape(shape), proj_column.reshape(shape)], axis=1)
    return (layer_out, *gradients, proj_grad.reshape(heads * dim, shape[2]))


def solution(mesh):
    in_specs = (
        P("ctx", "head", None),
        P("ctx", "head", None),
        P("ctx", "head", None),
        P("ctx", None),
        P("head", "ctx"),
    )
    out_specs = (
        P("ctx", "head"),
        P("ctx", "head", None),
        P("ctx", "head", None),
        P("ctx", "head", None),
        P("head", "ctx"),
    )
    return jax.shard_map(
        functools.partial(on_device, n=mesh.shape["ctx"], heads_n=mesh.shape["head"]),
        mesh=mesh,
        in_specs=in_specs,
        out_specs=out_specs,
        check_vma=False,
    )
```

```python
import functools

import jax
import jax.numpy as jnp
from jax import lax
from jax.experimental import pallas as pl
from jax.experimental.pallas import tpu as pltpu
from jax.sharding import PartitionSpec as P

C = 512
LANE = 16
VMEM = pl.BlockSpec(memory_space=pltpu.VMEM)
BF16 = jnp.bfloat16
F32 = jnp.float32


def params(mib):
    return pltpu.CompilerParams(vmem_limit_bytes=mib * 1024 * 1024)


def dot(a, b, dims):
    return lax.dot_general(a, b, (dims, ((), ())), preferred_element_type=F32)


def softmax(scores):
    highest = jnp.max(scores, axis=-1, keepdims=True)
    lifted = jnp.exp(scores - highest)
    return lifted * (1.0 / jnp.sum(lifted, axis=-1, keepdims=True))


def split_kernel(n, rows, me, q_ref, k_ref, v_ref, *rest):
    chunks, row_refs, wide = rest[:n], rest[n : n + 3], rest[n + 3]
    step, row = pl.program_id(0), pl.program_id(1)
    width, heads, _ = q_ref.shape
    for array, ref in enumerate((q_ref, k_ref, v_ref)):
        wide[array] = ref[...].astype(F32).reshape(width * heads, ref.shape[2])
    for array in range(3):
        for head in range(heads // 2):
            even = wide[array, pl.ds(2 * head, width, stride=heads), :]
            row_refs[array][head] = even.astype(BF16)
    for d in range(n):

        @pl.when(step == d)
        def _():
            for array in range(3):
                for head in range(heads // 2):
                    odd = wide[array, pl.ds(2 * head + 1, width, stride=heads), :]
                    chunks[d][array, head, row] = odd.astype(BF16)


def split_inputs(me, queries, keys, values, n):
    tokens, heads, dim = queries.shape
    rows, width, half = tokens // C, C // n, heads // 2
    block = pl.BlockSpec((width, heads, dim), lambda d, r, me: (r * n + (me[0] ^ d), 0, 0))
    chunk = jax.ShapeDtypeStruct((3, half, rows, width, dim), BF16)
    by_head = jax.ShapeDtypeStruct((half, tokens, dim), BF16)
    out = pl.pallas_call(
        functools.partial(split_kernel, n, rows),
        grid_spec=pltpu.PrefetchScalarGridSpec(
            num_scalar_prefetch=1,
            grid=(n, rows),
            in_specs=[block] * 3,
            out_specs=[pl.BlockSpec(chunk.shape, lambda d, r, me: (0, 0, 0, 0, 0))] * n
            + [pl.BlockSpec((half, width, dim), lambda d, r, me: (0, r * n + (me[0] ^ d), 0))] * 3,
            scratch_shapes=[pltpu.VMEM((3, width * heads, dim), F32)],
        ),
        out_shape=[chunk] * n + [by_head] * 3,
        compiler_params=params(40),
        name="split_inputs",
    )(me, queries, keys, values)
    return out[:n], out[n:]


def join_kernel(n, rows, me, *refs):
    chunks, row_refs, outs, wide = refs[:n], refs[n : n + 3], refs[n + 3 : n + 6], refs[n + 6]
    step, row = pl.program_id(0), pl.program_id(1)
    width, heads, dim = outs[0].shape
    for d in range(n):

        @pl.when(step == d)
        def _():
            for array in range(3):
                for head in range(heads // 2):
                    wide[array, pl.ds(2 * head + 1, width, stride=heads), :] = chunks[d][array, head, row].astype(F32)

    for array in range(3):
        for head in range(heads // 2):
            wide[array, pl.ds(2 * head, width, stride=heads), :] = row_refs[array][head].astype(F32)
        outs[array][...] = wide[array].reshape(width, heads, dim).astype(BF16)


def join_gradients(me, chunks, by_head, n):
    _, half, rows, width, dim = chunks[0].shape
    tokens, heads = by_head[0].shape[1], 2 * half
    whole = jax.ShapeDtypeStruct((tokens, heads, dim), BF16)
    return pl.pallas_call(
        functools.partial(join_kernel, n, rows),
        grid_spec=pltpu.PrefetchScalarGridSpec(
            num_scalar_prefetch=1,
            grid=(n, rows),
            in_specs=[pl.BlockSpec(chunks[0].shape, lambda d, r, me: (0, 0, 0, 0, 0))] * n
            + [pl.BlockSpec((half, width, dim), lambda d, r, me: (0, r * n + (me[0] ^ d), 0))] * 3,
            out_specs=[pl.BlockSpec((width, heads, dim), lambda d, r, me: (r * n + (me[0] ^ d), 0, 0))] * 3,
            scratch_shapes=[pltpu.VMEM((3, width * heads, dim), F32)],
        ),
        out_shape=[whole] * 3,
        compiler_params=params(40),
        name="join_gradients",
    )(me, *chunks, *by_head)


def collect_kernel(n, me, row_ref, *refs):
    chunks, flat_ref, both_ref = refs[:n], refs[n], refs[n + 1]
    half, rows, width, dim = chunks[0].shape
    for head in range(half):
        both_ref[:, 2 * head * dim : (2 * head + 1) * dim] = row_ref[:, head * dim : (head + 1) * dim]
    for d in range(n):
        column = pl.multiple_of((me[0] ^ d) * width, width)
        for row in range(rows):
            for head in range(half):
                part = chunks[d][head, row]
                flat_ref[pl.ds(row * C + column, width), head * dim : (head + 1) * dim] = part
                both_ref[pl.ds(row * C + column, width), (2 * head + 1) * dim : (2 * head + 2) * dim] = part


def collect(me, row_out, chunks, n):
    half, rows, width, dim = chunks[0].shape
    return pl.pallas_call(
        functools.partial(collect_kernel, n),
        in_specs=[pl.BlockSpec(memory_space=pltpu.SMEM)] + [VMEM] * (n + 1),
        out_specs=[VMEM] * 2,
        out_shape=[
            jax.ShapeDtypeStruct((rows * C, half * dim), BF16),
            jax.ShapeDtypeStruct((rows * C, 2 * half * dim), BF16),
        ],
        compiler_params=params(24),
        name="collect",
    )(me, row_out, *chunks)


def attn_grad_kernel(n, dim, me, ids, grad_ref, *refs):
    blocks, row_ref, chunks = refs[:n], refs[n], refs[n + 1 : 2 * n + 1]
    weight, total, sem = refs[2 * n + 1 :]
    step = pl.program_id(0)
    half, rows, width, _ = chunks[0].shape
    tokens = grad_ref.shape[0]
    tile = tokens // 4

    @pl.when(step == 0)
    def _():
        for d in range(n):
            pltpu.make_async_copy(blocks[d], weight.at[ids[d]], sem.at[ids[d]]).start()
        total[...] = jnp.zeros_like(total)

    pltpu.make_async_copy(blocks[0], weight.at[step], sem.at[step]).wait()

    @pl.loop(0, tokens, step=tile)
    def _(at):
        at = pl.multiple_of(at, tile)
        total[pl.ds(at, tile)] += dot(grad_ref[pl.ds(at, tile)], weight[step], ((1,), (1,)))

    @pl.when(step == n - 1)
    def _():
        for head in range(half):
            row_ref[:, head * dim : (head + 1) * dim] = total[:, 2 * head * dim : (2 * head + 1) * dim].astype(BF16)
            for d in range(n):
                column = pl.multiple_of((me[0] ^ d) * width, width)
                for row in range(rows):
                    part = total[pl.ds(row * C + column, width), (2 * head + 1) * dim : (2 * head + 2) * dim]
                    chunks[d][head, row] = part.astype(BF16)


def attn_grad(me, ids, out_grad, blocks, dim):
    n, (span, depth) = len(blocks), blocks[0].shape
    tokens, half = out_grad.shape[0], span // dim // 2
    chunk = jax.ShapeDtypeStruct((half, tokens // C, C // n, dim), BF16)
    out = pl.pallas_call(
        functools.partial(attn_grad_kernel, n, dim),
        grid_spec=pltpu.PrefetchScalarGridSpec(
            num_scalar_prefetch=2,
            grid=(n,),
            in_specs=[pl.BlockSpec((tokens, depth), lambda b, me, ids: (0, b))] + [pl.BlockSpec(memory_space=pl.ANY)] * n,
            out_specs=[pl.BlockSpec((tokens, half * dim), lambda b, me, ids: (0, 0))]
            + [pl.BlockSpec(chunk.shape, lambda b, me, ids: (0, 0, 0, 0))] * n,
            scratch_shapes=[
                pltpu.VMEM((n, span, depth), BF16),
                pltpu.VMEM((tokens, span), F32),
                pltpu.SemaphoreType.DMA((n,)),
            ],
        ),
        out_shape=[jax.ShapeDtypeStruct((tokens, half * dim), BF16)] + [chunk] * n,
        compiler_params=params(40),
        cost_estimate=pl.CostEstimate(
            flops=2 * tokens * span * depth * n,
            bytes_accessed=2 * n * depth * (tokens + span) + 2 * tokens * span,
            transcendentals=0,
        ),
        name="attn_grad",
    )(me, ids, out_grad, *blocks)
    return out[0], out[1:]


def layer_kernel(n, count, adds, ids, wanted, flat_ref, *refs):
    blocks, extra, out_ref = refs[:n], refs[n : n + adds], refs[n + adds]
    weight, sem = refs[n + adds + 1 :]
    step = pl.program_id(0)
    tokens = flat_ref.shape[0]
    tile = tokens // 4

    @pl.when(step == 0)
    def _():
        for s in range(count):
            for d in range(n):

                @pl.when(ids[d] == wanted[s])
                def _():
                    pltpu.make_async_copy(blocks[d], weight.at[s], sem.at[s]).start()

    pltpu.make_async_copy(blocks[0], weight.at[step], sem.at[step]).wait()

    @pl.loop(0, tokens, step=tile)
    def _(at):
        at = pl.multiple_of(at, tile)
        value = dot(flat_ref[pl.ds(at, tile)], weight[step], ((1,), (0,)))
        for ref in extra:
            value = value + ref[pl.ds(at, tile)].astype(F32)
        out_ref[pl.ds(at, tile)] = value.astype(BF16)


def layer_part(ids, flat, blocks, wanted, extra, first):
    n, (span, depth) = len(blocks), blocks[0].shape
    tokens, count = flat.shape[0], wanted.shape[0]
    by_column = pl.BlockSpec((tokens, depth), lambda s, ids, wanted: (0, s))
    return pl.pallas_call(
        functools.partial(layer_kernel, n, count, len(extra)),
        grid_spec=pltpu.PrefetchScalarGridSpec(
            num_scalar_prefetch=2,
            grid=(count,),
            in_specs=[pl.BlockSpec((tokens, span), lambda s, ids, wanted: (0, 0))]
            + [pl.BlockSpec(memory_space=pl.ANY)] * n
            + [pl.BlockSpec((tokens, depth), functools.partial(lambda f, s, ids, wanted: (0, s + f), f)) for f in first],
            out_specs=by_column,
            scratch_shapes=[pltpu.VMEM((count, span, depth), BF16), pltpu.SemaphoreType.DMA((count,))],
        ),
        out_shape=jax.ShapeDtypeStruct((tokens, count * depth), BF16),
        compiler_params=params(32),
        cost_estimate=pl.CostEstimate(
            flops=2 * tokens * span * depth * count,
            bytes_accessed=2 * (count * depth * (tokens + span) + tokens * span),
            transcendentals=0,
        ),
        name="layer_part",
    )(ids, wanted, flat, *blocks, *extra)


def proj_kernel(lead, adds, dim, order, flat_ref, grad_ref, *refs):
    extra, outs, turned = refs[:adds], refs[adds:-1], refs[-1]
    step = pl.program_id(0)
    span = flat_ref.shape[1]

    @pl.when(step == 0)
    def _():
        for at in range(0, span, dim):
            turned[at : at + dim] = flat_ref[:, at : at + dim].T

    def value(at):
        out = dot(turned[at : at + dim], grad_ref[...], ((1,), (0,)))
        for ref in extra:
            out = out + ref[at : at + dim].astype(F32)
        return out.astype(BF16)

    @pl.when(step < lead)
    def _():
        for at in range(0, span, dim):
            outs[0][at : at + dim] = value(at)

    @pl.when(step >= lead)
    def _():
        for at in range(0, span, dim):
            outs[-1][at : at + dim] = value(at)


def proj_part(order, flat, out_grad, extra, depth, dim, lead):
    tokens, span = flat.shape
    count = order.shape[0]
    sizes = [size for size in (lead, count - lead) if size]
    places = [lambda s, order: (jnp.minimum(s, lead - 1), 0, 0), lambda s, order: (jnp.maximum(s - lead, 0), 0, 0)]
    return pl.pallas_call(
        functools.partial(proj_kernel, lead, len(extra), dim),
        grid_spec=pltpu.PrefetchScalarGridSpec(
            num_scalar_prefetch=1,
            grid=(count,),
            in_specs=[
                pl.BlockSpec((tokens, span), lambda s, order: (0, 0)),
                pl.BlockSpec((tokens, depth), lambda s, order: (0, order[s])),
            ]
            + [pl.BlockSpec((pl.squeezed, span, depth), lambda s, order: (s, 0, 0))] * len(extra),
            out_specs=[pl.BlockSpec((pl.squeezed, span, depth), place) for place in places[-len(sizes) :]],
            scratch_shapes=[pltpu.VMEM((span, tokens), BF16)],
        ),
        out_shape=[jax.ShapeDtypeStruct((size, span, depth), BF16) for size in sizes],
        compiler_params=params(24),
        cost_estimate=pl.CostEstimate(
            flops=2 * tokens * span * depth * count,
            bytes_accessed=2 * (count * depth * (tokens + span * (1 + len(extra))) + tokens * span),
            transcendentals=0,
        ),
        name="proj_part",
    )(order, flat, out_grad, *extra)


def row_blocks(length):
    step = length // 2
    return [(start, step) for start in range(0, length, step)]


def row_probs(q, k, start, step, scale):
    scores = dot(q, k, ((1,), (1,))) * scale
    place = lax.broadcasted_iota(jnp.int32, scores.shape, 0) + start
    seen = lax.broadcasted_iota(jnp.int32, scores.shape, 1)
    return softmax(jnp.where(place >= seen, scores, -jnp.inf))


def row_forward_kernel(scale, q_ref, k_ref, v_ref, o_ref):
    for start, step in row_blocks(q_ref.shape[0]):
        stop = start + step
        probs = row_probs(q_ref[start:stop], k_ref[:stop], start, step, scale)
        o_ref[start:stop] = dot(probs.astype(BF16), v_ref[:stop], ((1,), (0,))).astype(BF16)


def row_forward(q, k, v):
    half, tokens, dim = q.shape
    by_head = pl.BlockSpec((pl.squeezed, C, dim), lambda r, h: (h, r, 0))
    return pl.pallas_call(
        functools.partial(row_forward_kernel, dim**-0.5),
        grid=(tokens // C, half),
        in_specs=[by_head] * 3,
        out_specs=pl.BlockSpec((C, dim), lambda r, h: (r, h)),
        out_shape=jax.ShapeDtypeStruct((tokens, half * dim), BF16),
        compiler_params=params(24),
        cost_estimate=pl.CostEstimate(
            flops=4 * tokens * C * half * dim, bytes_accessed=8 * tokens * half * dim, transcendentals=tokens * C * half
        ),
        name="row_forward",
    )(q, k, v)


def row_backward_kernel(scale, q_ref, k_ref, v_ref, g_ref, dq_ref, dk_ref, dv_ref, k_sum, v_sum):
    k_sum[...] = jnp.zeros_like(k_sum)
    v_sum[...] = jnp.zeros_like(v_sum)
    for start, step in row_blocks(q_ref.shape[0]):
        stop = start + step
        q, k, grad = q_ref[start:stop], k_ref[:stop], g_ref[start:stop]
        probs = row_probs(q, k, start, step, scale)
        prob_grad = dot(grad, v_ref[:stop], ((1,), (1,)))
        inner = jnp.sum(probs * prob_grad, axis=-1, keepdims=True)
        score_low = (probs * (prob_grad - inner)).astype(BF16)
        dq_ref[start:stop] = (dot(score_low, k, ((1,), (0,))) * scale).astype(BF16)
        k_sum[:stop] += dot(score_low, q, ((0,), (0,)))
        v_sum[:stop] += dot(probs.astype(BF16), grad, ((0,), (0,)))
    dk_ref[...] = (k_sum[...] * scale).astype(BF16)
    dv_ref[...] = v_sum[...].astype(BF16)


def row_backward(q, k, v, grad):
    half, tokens, dim = q.shape
    by_head = pl.BlockSpec((pl.squeezed, C, dim), lambda r, h: (h, r, 0))
    return pl.pallas_call(
        functools.partial(row_backward_kernel, dim**-0.5),
        grid=(tokens // C, half),
        in_specs=[by_head] * 3 + [pl.BlockSpec((C, dim), lambda r, h: (r, h))],
        out_specs=[by_head] * 3,
        out_shape=[jax.ShapeDtypeStruct(q.shape, BF16)] * 3,
        scratch_shapes=[pltpu.VMEM((C, dim), F32)] * 2,
        compiler_params=params(32),
        cost_estimate=pl.CostEstimate(
            flops=10 * tokens * C * half * dim, bytes_accessed=14 * tokens * half * dim, transcendentals=tokens * C * half
        ),
        name="row_backward",
    )(q, k, v, grad)


def column_mask(me, n, rows):
    size = n * rows * LANE

    def parts(axis):
        place = lax.broadcasted_iota(jnp.int32, (size, size), axis)
        line, column = place // LANE, place % LANE
        return ((line // rows) ^ me) * rows + line % rows, column

    row_q, column_q = parts(0)
    row_k, column_k = parts(1)
    return (column_q == column_k) & (row_q >= row_k)


def gathered(chunks, index, at):
    rows, dim = chunks[0].shape[-3], chunks[0].shape[-1]
    return jnp.concatenate(
        [chunk[(*index, row, pl.ds(at, LANE), slice(None))] for chunk in chunks for row in range(rows)], axis=0
    )


def scattered(chunks, index, at, value):
    rows = chunks[0].shape[-3]
    for d, chunk in enumerate(chunks):
        for row in range(rows):
            line = d * rows + row
            chunk[(*index, row, pl.ds(at, LANE), slice(None))] = value[line * LANE : (line + 1) * LANE]


def column_probs(bias, q, k, scale):
    return softmax(dot(q, k, ((1,), (1,))) * scale + bias[...])


def column_forward_kernel(n, scale, me, *refs):
    chunks, outs, bias = refs[:n], refs[n : 2 * n], refs[2 * n]
    _, half, rows, width, _ = chunks[0].shape
    bias[...] = jnp.where(column_mask(me[0], n, rows), 0.0, -jnp.inf)
    blocks = width // LANE

    @pl.loop(0, half * blocks)
    def _(step):
        head, at = step // blocks, pl.multiple_of(step % blocks * LANE, LANE)
        q, k, v = (gathered(chunks, (array, head), at) for array in range(3))
        probs = column_probs(bias, q, k, scale)
        scattered(outs, (head,), at, dot(probs.astype(BF16), v, ((1,), (0,))).astype(BF16))


def column_forward(me, chunks, n):
    _, half, rows, width, dim = chunks[0].shape
    size = n * rows * LANE
    return pl.pallas_call(
        functools.partial(column_forward_kernel, n, dim**-0.5),
        in_specs=[pl.BlockSpec(memory_space=pltpu.SMEM)] + [VMEM] * n,
        out_specs=[VMEM] * n,
        out_shape=[jax.ShapeDtypeStruct((half, rows, width, dim), BF16)] * n,
        scratch_shapes=[pltpu.VMEM((size, size), F32)],
        compiler_params=params(24),
        cost_estimate=pl.CostEstimate(
            flops=4 * size * size * dim * half * width // LANE,
            bytes_accessed=8 * n * half * rows * width * dim,
            transcendentals=size * size * half * width // LANE,
        ),
        name="column_forward",
    )(me, *chunks)


def column_backward_kernel(n, scale, me, *refs):
    chunks, grads, outs, bias = refs[:n], refs[n : 2 * n], refs[2 * n : 3 * n], refs[3 * n]
    _, half, rows, width, _ = chunks[0].shape
    bias[...] = jnp.where(column_mask(me[0], n, rows), 0.0, -jnp.inf)
    blocks = width // LANE

    @pl.loop(0, half * blocks)
    def _(step):
        head, at = step // blocks, pl.multiple_of(step % blocks * LANE, LANE)
        q, k, v = (gathered(chunks, (array, head), at) for array in range(3))
        grad = gathered(grads, (head,), at)
        probs = column_probs(bias, q, k, scale)
        prob_grad = dot(grad, v, ((1,), (1,)))
        inner = jnp.sum(probs * prob_grad, axis=-1, keepdims=True)
        score_low = (probs * (prob_grad - inner)).astype(BF16)
        scattered(outs, (0, head), at, (dot(score_low, k, ((1,), (0,))) * scale).astype(BF16))
        scattered(outs, (1, head), at, (dot(score_low, q, ((0,), (0,))) * scale).astype(BF16))
        scattered(outs, (2, head), at, dot(probs.astype(BF16), grad, ((0,), (0,))).astype(BF16))


def column_backward(me, chunks, grads, n):
    _, half, rows, width, dim = chunks[0].shape
    size = n * rows * LANE
    return pl.pallas_call(
        functools.partial(column_backward_kernel, n, dim**-0.5),
        in_specs=[pl.BlockSpec(memory_space=pltpu.SMEM)] + [VMEM] * (2 * n),
        out_specs=[VMEM] * n,
        out_shape=[jax.ShapeDtypeStruct(chunks[0].shape, BF16)] * n,
        scratch_shapes=[pltpu.VMEM((size, size), F32)],
        compiler_params=params(24),
        cost_estimate=pl.CostEstimate(
            flops=10 * size * size * dim * half * width // LANE,
            bytes_accessed=14 * n * half * rows * width * dim,
            transcendentals=size * size * half * width // LANE,
        ),
        name="column_backward",
    )(me, *chunks, *grads)


PAIRS = [(0, 1), (1, 0), (2, 3), (3, 2)]
INWARD = [(0, 1), (3, 2)]
CROSS = [(1, 2), (2, 1)]
OUTWARD = [(1, 0), (2, 3)]


def after(value, *done):
    return lax.optimization_barrier((value, *done))[0]


class Links:
    def __init__(self, n, window):
        self.n, self.inner, self.window, self.sent = n, n // 4, window, []

    def send(self, value, pairs):
        if len(self.sent) >= self.window:
            value = after(value, self.sent[-self.window])
        out = lax.ppermute(value, "ctx", pairs)
        self.sent.append(out)
        return out

    def along(self, value, pairs):
        return self.send(value, [(a * self.inner + y, b * self.inner + y) for a, b in pairs for y in range(self.inner)])

    def flip(self, value, d):
        return self.send(value, [(place, place ^ d) for place in range(self.n)])

    def swap(self, chunks, order):
        out = list(chunks)
        for d in order:
            out[d] = self.flip(chunks[d], d)
        return out


def scatter_layer(ids, flat, blocks, heads_n):
    mine = lax.axis_index("head").astype(jnp.int32)
    per = len(blocks) // heads_n

    def wanted(offsets):
        return jnp.stack([(mine ^ g) * per + b for g in offsets for b in range(per)]).astype(jnp.int32)

    def move(part, g):
        return lax.ppermute(part, "head", [(place, place ^ g) for place in range(heads_n)])

    even = list(range(0, heads_n, 2))
    near = move(layer_part(ids, flat, blocks, wanted([g + 1 for g in even]), [], []), 1)
    far = [move(layer_part(ids, flat, blocks, wanted([g]), [near], [g // 2 * per]), g) for g in even[1:]]
    return layer_part(ids, flat, blocks, wanted([0]), [near] + far, [0] * (1 + len(far)))


def on_device(queries, keys, values, out_grad, wo, *, n, heads_n):
    tokens, heads, dim = queries.shape
    half, depth, inner = heads // 2, wo.shape[1], n // 4
    me = lax.axis_index("ctx").astype(jnp.int32).reshape(1)
    line, spot = me[0] // inner, me[0] % inner
    middle, upper = (line == 1) | (line == 2), line < 2
    far = [jnp.where(upper, 2, 1), jnp.where(upper, 3, 0)]
    links = Links(n, 5)
    wide = [d for d in range(n) if d >= 2 * inner]
    close = [d for d in range(1, n) if d < 2 * inner]
    order = [d for d in wide if d % inner == 0] + [d for d in close if d % inner == 0]
    order += [d for d in wide if d % inner] + [d for d in close if d % inner]

    def around(block):
        return [block if e == 0 else links.flip(block, e) for e in range(inner)]

    near = links.along(wo, PAIRS)
    cross_own = links.along(wo, CROSS)
    own_blocks = around(wo)
    chunks, by_head = split_inputs(me, queries, keys, values, n)
    sent = list(chunks)
    sent[order[0]] = links.flip(chunks[order[0]], order[0])
    cross_near = links.along(near, CROSS)
    near_blocks = around(near)
    far_own = jnp.where(middle, cross_own, links.along(cross_own, OUTWARD))
    far_near = jnp.where(middle, cross_near, links.along(cross_near, OUTWARD))
    far_own_blocks = around(far_own)
    far_near_blocks = around(far_near)
    for d in order[1:]:
        sent[d] = links.flip(chunks[d], d)
    chunks = sent
    blocks = own_blocks + near_blocks + far_own_blocks + far_near_blocks
    ids = [owner * inner + (spot ^ e) for owner in (line, line ^ 1, *far) for e in range(inner)]
    ids = jnp.stack(ids).astype(jnp.int32)

    def targets(e):
        return jnp.stack([owner * inner + (spot ^ e) for owner in (line ^ 1, *far, line)]).astype(jnp.int32)

    def within(flat):
        theirs = [links.flip(proj_part(targets(e), flat, out_grad, [], depth, dim, 0)[0], e) for e in range(1, inner)]
        return proj_part(targets(0), flat, out_grad, theirs, depth, dim, 3)

    def add(*terms):
        return sum(term.astype(F32) for term in terms).astype(BF16)

    row_out = row_forward(*(after(tensor, near) for tensor in by_head))
    row_lead, row_own = within(row_out)

    grad_row, grads = attn_grad(me, ids, out_grad, blocks, dim)
    grads = links.swap(grads, order)
    column_part = links.swap(column_forward(me, chunks, n), order)
    column_out, flat = collect(me, row_out, column_part, n)

    row_in = links.along(row_lead, INWARD)
    row_cross = links.along(add(row_lead[1:], row_in[1:]), CROSS)
    column_lead, column_own = within(column_out)
    gradients = column_backward(me, chunks, grads, n)
    column_in = links.along(column_lead, INWARD)
    column_grads = list(gradients)
    for d in order[: n // 2]:
        column_grads[d] = links.flip(gradients[d], d)
    column_cross = links.along(add(column_lead[1:], column_in[1:]), CROSS)
    row_back = links.along(add(row_lead[0], row_cross[1]), OUTWARD)
    for d in order[n // 2 :]:
        column_grads[d] = links.flip(gradients[d], d)
    column_back = links.along(add(column_lead[0], column_cross[1]), OUTWARD)

    layer_out = scatter_layer(ids, flat, blocks, heads_n)
    row_grads = row_backward(*by_head, grad_row)
    gradients = join_gradients(me, column_grads, row_grads, n)

    proj_row = add(row_own[0], row_in[0], row_cross[0], row_back)
    proj_column = add(column_own[0], column_in[0], column_cross[0], column_back)
    shape = (half, dim, depth)
    proj_grad = jnp.stack([proj_row.reshape(shape), proj_column.reshape(shape)], axis=1)
    return (layer_out, *gradients, proj_grad.reshape(heads * dim, depth))


def solution(mesh):
    in_specs = (
        P("ctx", "head", None),
        P("ctx", "head", None),
        P("ctx", "head", None),
        P("ctx", None),
        P("head", "ctx"),
    )
    out_specs = (
        P("ctx", "head"),
        P("ctx", "head", None),
        P("ctx", "head", None),
        P("ctx", "head", None),
        P("head", "ctx"),
    )
    return jax.shard_map(
        functools.partial(on_device, n=mesh.shape["ctx"], heads_n=mesh.shape["head"]),
        mesh=mesh,
        in_specs=in_specs,
        out_specs=out_specs,
        check_vma=False,
    )
```

```python
import functools

import jax
import jax.numpy as jnp
from jax import lax
from jax.experimental import pallas as pl
from jax.experimental.pallas import tpu as pltpu
from jax.sharding import PartitionSpec as P

C = 512
LANE = 16
VMEM = pl.BlockSpec(memory_space=pltpu.VMEM)
BF16 = jnp.bfloat16
F32 = jnp.float32


def params(mib):
    return pltpu.CompilerParams(vmem_limit_bytes=mib * 1024 * 1024)


def dot(a, b, dims):
    return lax.dot_general(a, b, (dims, ((), ())), preferred_element_type=F32)


def softmax(scores):
    highest = jnp.max(scores, axis=-1, keepdims=True)
    lifted = jnp.exp(scores - highest)
    return lifted * (1.0 / jnp.sum(lifted, axis=-1, keepdims=True))


def split_kernel(n, rows, me, q_ref, k_ref, v_ref, *rest):
    chunks, row_refs, wide = rest[:n], rest[n : n + 3], rest[n + 3]
    step, row = pl.program_id(0), pl.program_id(1)
    width, heads, _ = q_ref.shape
    for array, ref in enumerate((q_ref, k_ref, v_ref)):
        wide[array] = ref[...].astype(F32).reshape(width * heads, ref.shape[2])
    for array in range(3):
        for head in range(heads // 2):
            even = wide[array, pl.ds(2 * head, width, stride=heads), :]
            row_refs[array][head] = even.astype(BF16)
    for d in range(n):

        @pl.when(step == d)
        def _():
            for array in range(3):
                for head in range(heads // 2):
                    odd = wide[array, pl.ds(2 * head + 1, width, stride=heads), :]
                    chunks[d][array, head, row] = odd.astype(BF16)


def split_inputs(me, queries, keys, values, n):
    tokens, heads, dim = queries.shape
    rows, width, half = tokens // C, C // n, heads // 2
    block = pl.BlockSpec((width, heads, dim), lambda d, r, me: (r * n + (me[0] ^ d), 0, 0))
    chunk = jax.ShapeDtypeStruct((3, half, rows, width, dim), BF16)
    by_head = jax.ShapeDtypeStruct((half, tokens, dim), BF16)
    out = pl.pallas_call(
        functools.partial(split_kernel, n, rows),
        grid_spec=pltpu.PrefetchScalarGridSpec(
            num_scalar_prefetch=1,
            grid=(n, rows),
            in_specs=[block] * 3,
            out_specs=[pl.BlockSpec(chunk.shape, lambda d, r, me: (0, 0, 0, 0, 0))] * n
            + [pl.BlockSpec((half, width, dim), lambda d, r, me: (0, r * n + (me[0] ^ d), 0))] * 3,
            scratch_shapes=[pltpu.VMEM((3, width * heads, dim), F32)],
        ),
        out_shape=[chunk] * n + [by_head] * 3,
        compiler_params=params(60),
        name="split_inputs",
    )(me, queries, keys, values)
    return out[:n], out[n:]


def join_kernel(n, rows, me, *refs):
    chunks, row_refs, outs, wide = refs[:n], refs[n : n + 3], refs[n + 3 : n + 6], refs[n + 6]
    step, row = pl.program_id(0), pl.program_id(1)
    width, heads, dim = outs[0].shape
    for d in range(n):

        @pl.when(step == d)
        def _():
            for array in range(3):
                for head in range(heads // 2):
                    wide[array, pl.ds(2 * head + 1, width, stride=heads), :] = chunks[d][array, head, row].astype(F32)

    for array in range(3):
        for head in range(heads // 2):
            wide[array, pl.ds(2 * head, width, stride=heads), :] = row_refs[array][head].astype(F32)
        outs[array][...] = wide[array].reshape(width, heads, dim).astype(BF16)


def join_gradients(me, chunks, by_head, n):
    _, half, rows, width, dim = chunks[0].shape
    tokens, heads = by_head[0].shape[1], 2 * half
    whole = jax.ShapeDtypeStruct((tokens, heads, dim), BF16)
    return pl.pallas_call(
        functools.partial(join_kernel, n, rows),
        grid_spec=pltpu.PrefetchScalarGridSpec(
            num_scalar_prefetch=1,
            grid=(n, rows),
            in_specs=[pl.BlockSpec(chunks[0].shape, lambda d, r, me: (0, 0, 0, 0, 0))] * n
            + [pl.BlockSpec((half, width, dim), lambda d, r, me: (0, r * n + (me[0] ^ d), 0))] * 3,
            out_specs=[pl.BlockSpec((width, heads, dim), lambda d, r, me: (r * n + (me[0] ^ d), 0, 0))] * 3,
            scratch_shapes=[pltpu.VMEM((3, width * heads, dim), F32)],
        ),
        out_shape=[whole] * 3,
        compiler_params=params(60),
        name="join_gradients",
    )(me, *chunks, *by_head)


def collect_kernel(n, me, row_ref, *refs):
    chunks, flat_ref, both_ref = refs[:n], refs[n], refs[n + 1]
    half, rows, width, dim = chunks[0].shape
    for head in range(half):
        both_ref[:, 2 * head * dim : (2 * head + 1) * dim] = row_ref[:, head * dim : (head + 1) * dim]
    for d in range(n):
        column = pl.multiple_of((me[0] ^ d) * width, width)
        for row in range(rows):
            for head in range(half):
                part = chunks[d][head, row]
                flat_ref[pl.ds(row * C + column, width), head * dim : (head + 1) * dim] = part
                both_ref[pl.ds(row * C + column, width), (2 * head + 1) * dim : (2 * head + 2) * dim] = part


def collect(me, row_out, chunks, n):
    half, rows, width, dim = chunks[0].shape
    return pl.pallas_call(
        functools.partial(collect_kernel, n),
        in_specs=[pl.BlockSpec(memory_space=pltpu.SMEM)] + [VMEM] * (n + 1),
        out_specs=[VMEM] * 2,
        out_shape=[
            jax.ShapeDtypeStruct((rows * C, half * dim), BF16),
            jax.ShapeDtypeStruct((rows * C, 2 * half * dim), BF16),
        ],
        compiler_params=params(60),
        name="collect",
    )(me, row_out, *chunks)


def attn_grad_kernel(n, dim, me, ids, grad_ref, *refs):
    blocks, row_ref, chunks = refs[:n], refs[n], refs[n + 1 : 2 * n + 1]
    weight, total, sem = refs[2 * n + 1 :]
    step = pl.program_id(0)
    half, rows, width, _ = chunks[0].shape
    tokens = grad_ref.shape[0]
    tile = tokens // 4

    @pl.when(step == 0)
    def _():
        for d in range(n):
            pltpu.make_async_copy(blocks[d], weight.at[ids[d]], sem.at[ids[d]]).start()
        total[...] = jnp.zeros_like(total)

    pltpu.make_async_copy(blocks[0], weight.at[step], sem.at[step]).wait()

    @pl.loop(0, tokens, step=tile)
    def _(at):
        at = pl.multiple_of(at, tile)
        total[pl.ds(at, tile)] += dot(grad_ref[pl.ds(at, tile)], weight[step], ((1,), (1,)))

    @pl.when(step == n - 1)
    def _():
        for head in range(half):
            row_ref[:, head * dim : (head + 1) * dim] = total[:, 2 * head * dim : (2 * head + 1) * dim].astype(BF16)
            for d in range(n):
                column = pl.multiple_of((me[0] ^ d) * width, width)
                for row in range(rows):
                    part = total[pl.ds(row * C + column, width), (2 * head + 1) * dim : (2 * head + 2) * dim]
                    chunks[d][head, row] = part.astype(BF16)


def attn_grad(me, ids, out_grad, blocks, dim):
    n, (span, depth) = len(blocks), blocks[0].shape
    tokens, half = out_grad.shape[0], span // dim // 2
    chunk = jax.ShapeDtypeStruct((half, tokens // C, C // n, dim), BF16)
    out = pl.pallas_call(
        functools.partial(attn_grad_kernel, n, dim),
        grid_spec=pltpu.PrefetchScalarGridSpec(
            num_scalar_prefetch=2,
            grid=(n,),
            in_specs=[pl.BlockSpec((tokens, depth), lambda b, me, ids: (0, b))] + [pl.BlockSpec(memory_space=pl.ANY)] * n,
            out_specs=[pl.BlockSpec((tokens, half * dim), lambda b, me, ids: (0, 0))]
            + [pl.BlockSpec(chunk.shape, lambda b, me, ids: (0, 0, 0, 0))] * n,
            scratch_shapes=[
                pltpu.VMEM((n, span, depth), BF16),
                pltpu.VMEM((tokens, span), F32),
                pltpu.SemaphoreType.DMA((n,)),
            ],
        ),
        out_shape=[jax.ShapeDtypeStruct((tokens, half * dim), BF16)] + [chunk] * n,
        compiler_params=params(60),
        cost_estimate=pl.CostEstimate(
            flops=2 * tokens * span * depth * n,
            bytes_accessed=2 * n * depth * (tokens + span) + 2 * tokens * span,
            transcendentals=0,
        ),
        name="attn_grad",
    )(me, ids, out_grad, *blocks)
    return out[0], out[1:]


def layer_kernel(n, count, adds, ids, wanted, flat_ref, *refs):
    blocks, extra, out_ref = refs[:n], refs[n : n + adds], refs[n + adds]
    weight, sem = refs[n + adds + 1 :]
    step = pl.program_id(0)
    tokens = flat_ref.shape[0]
    tile = tokens // 4

    @pl.when(step == 0)
    def _():
        for s in range(count):
            for d in range(n):

                @pl.when(ids[d] == wanted[s])
                def _():
                    pltpu.make_async_copy(blocks[d], weight.at[s], sem.at[s]).start()

    pltpu.make_async_copy(blocks[0], weight.at[step], sem.at[step]).wait()

    @pl.loop(0, tokens, step=tile)
    def _(at):
        at = pl.multiple_of(at, tile)
        value = dot(flat_ref[pl.ds(at, tile)], weight[step], ((1,), (0,)))
        for ref in extra:
            value = value + ref[pl.ds(at, tile)].astype(F32)
        out_ref[pl.ds(at, tile)] = value.astype(BF16)


def layer_part(ids, flat, blocks, wanted, extra, first):
    n, (span, depth) = len(blocks), blocks[0].shape
    tokens, count = flat.shape[0], wanted.shape[0]
    by_column = pl.BlockSpec((tokens, depth), lambda s, ids, wanted: (0, s))
    return pl.pallas_call(
        functools.partial(layer_kernel, n, count, len(extra)),
        grid_spec=pltpu.PrefetchScalarGridSpec(
            num_scalar_prefetch=2,
            grid=(count,),
            in_specs=[pl.BlockSpec((tokens, span), lambda s, ids, wanted: (0, 0))]
            + [pl.BlockSpec(memory_space=pl.ANY)] * n
            + [pl.BlockSpec((tokens, depth), functools.partial(lambda f, s, ids, wanted: (0, s + f), f)) for f in first],
            out_specs=by_column,
            scratch_shapes=[pltpu.VMEM((count, span, depth), BF16), pltpu.SemaphoreType.DMA((count,))],
        ),
        out_shape=jax.ShapeDtypeStruct((tokens, count * depth), BF16),
        compiler_params=params(60),
        cost_estimate=pl.CostEstimate(
            flops=2 * tokens * span * depth * count,
            bytes_accessed=2 * (count * depth * (tokens + span) + tokens * span),
            transcendentals=0,
        ),
        name="layer_part",
    )(ids, wanted, flat, *blocks, *extra)


def proj_kernel(lead, adds, dim, order, flat_ref, grad_ref, *refs):
    extra, outs, turned = refs[:adds], refs[adds:-1], refs[-1]
    step = pl.program_id(0)
    span = flat_ref.shape[1]

    @pl.when(step == 0)
    def _():
        for at in range(0, span, dim):
            turned[at : at + dim] = flat_ref[:, at : at + dim].T

    def value(at):
        out = dot(turned[at : at + dim], grad_ref[...], ((1,), (0,)))
        for ref in extra:
            out = out + ref[at : at + dim].astype(F32)
        return out.astype(BF16)

    @pl.when(step < lead)
    def _():
        for at in range(0, span, dim):
            outs[0][at : at + dim] = value(at)

    @pl.when(step >= lead)
    def _():
        for at in range(0, span, dim):
            outs[-1][at : at + dim] = value(at)


def proj_part(order, flat, out_grad, extra, depth, dim, lead):
    tokens, span = flat.shape
    count = order.shape[0]
    sizes = [size for size in (lead, count - lead) if size]
    places = [lambda s, order: (jnp.minimum(s, lead - 1), 0, 0), lambda s, order: (jnp.maximum(s - lead, 0), 0, 0)]
    return pl.pallas_call(
        functools.partial(proj_kernel, lead, len(extra), dim),
        grid_spec=pltpu.PrefetchScalarGridSpec(
            num_scalar_prefetch=1,
            grid=(count,),
            in_specs=[
                pl.BlockSpec((tokens, span), lambda s, order: (0, 0)),
                pl.BlockSpec((tokens, depth), lambda s, order: (0, order[s])),
            ]
            + [pl.BlockSpec((pl.squeezed, span, depth), lambda s, order: (s, 0, 0))] * len(extra),
            out_specs=[pl.BlockSpec((pl.squeezed, span, depth), place) for place in places[-len(sizes) :]],
            scratch_shapes=[pltpu.VMEM((span, tokens), BF16)],
        ),
        out_shape=[jax.ShapeDtypeStruct((size, span, depth), BF16) for size in sizes],
        compiler_params=params(60),
        cost_estimate=pl.CostEstimate(
            flops=2 * tokens * span * depth * count,
            bytes_accessed=2 * (count * depth * (tokens + span * (1 + len(extra))) + tokens * span),
            transcendentals=0,
        ),
        name="proj_part",
    )(order, flat, out_grad, *extra)


def row_blocks(length):
    step = length // 2
    return [(start, step) for start in range(0, length, step)]


def row_probs(q, k, start, step, scale):
    scores = dot(q, k, ((1,), (1,))) * scale
    place = lax.broadcasted_iota(jnp.int32, scores.shape, 0) + start
    seen = lax.broadcasted_iota(jnp.int32, scores.shape, 1)
    return softmax(jnp.where(place >= seen, scores, -jnp.inf))


def row_forward_kernel(scale, q_ref, k_ref, v_ref, o_ref):
    for start, step in row_blocks(q_ref.shape[0]):
        stop = start + step
        probs = row_probs(q_ref[start:stop], k_ref[:stop], start, step, scale)
        o_ref[start:stop] = dot(probs.astype(BF16), v_ref[:stop], ((1,), (0,))).astype(BF16)


def row_forward(q, k, v):
    half, tokens, dim = q.shape
    by_head = pl.BlockSpec((pl.squeezed, C, dim), lambda r, h: (h, r, 0))
    return pl.pallas_call(
        functools.partial(row_forward_kernel, dim**-0.5),
        grid=(tokens // C, half),
        in_specs=[by_head] * 3,
        out_specs=pl.BlockSpec((C, dim), lambda r, h: (r, h)),
        out_shape=jax.ShapeDtypeStruct((tokens, half * dim), BF16),
        compiler_params=params(60),
        cost_estimate=pl.CostEstimate(
            flops=4 * tokens * C * half * dim, bytes_accessed=8 * tokens * half * dim, transcendentals=tokens * C * half
        ),
        name="row_forward",
    )(q, k, v)


def row_backward_kernel(scale, q_ref, k_ref, v_ref, g_ref, dq_ref, dk_ref, dv_ref, k_sum, v_sum):
    k_sum[...] = jnp.zeros_like(k_sum)
    v_sum[...] = jnp.zeros_like(v_sum)
    for start, step in row_blocks(q_ref.shape[0]):
        stop = start + step
        q, k, grad = q_ref[start:stop], k_ref[:stop], g_ref[start:stop]
        probs = row_probs(q, k, start, step, scale)
        prob_grad = dot(grad, v_ref[:stop], ((1,), (1,)))
        inner = jnp.sum(probs * prob_grad, axis=-1, keepdims=True)
        score_low = (probs * (prob_grad - inner)).astype(BF16)
        dq_ref[start:stop] = (dot(score_low, k, ((1,), (0,))) * scale).astype(BF16)
        k_sum[:stop] += dot(score_low, q, ((0,), (0,)))
        v_sum[:stop] += dot(probs.astype(BF16), grad, ((0,), (0,)))
    dk_ref[...] = (k_sum[...] * scale).astype(BF16)
    dv_ref[...] = v_sum[...].astype(BF16)


def row_backward(q, k, v, grad):
    half, tokens, dim = q.shape
    by_head = pl.BlockSpec((pl.squeezed, C, dim), lambda r, h: (h, r, 0))
    return pl.pallas_call(
        functools.partial(row_backward_kernel, dim**-0.5),
        grid=(tokens // C, half),
        in_specs=[by_head] * 3 + [pl.BlockSpec((C, dim), lambda r, h: (r, h))],
        out_specs=[by_head] * 3,
        out_shape=[jax.ShapeDtypeStruct(q.shape, BF16)] * 3,
        scratch_shapes=[pltpu.VMEM((C, dim), F32)] * 2,
        compiler_params=params(60),
        cost_estimate=pl.CostEstimate(
            flops=10 * tokens * C * half * dim, bytes_accessed=14 * tokens * half * dim, transcendentals=tokens * C * half
        ),
        name="row_backward",
    )(q, k, v, grad)


def column_mask(me, n, rows):
    size = n * rows * LANE

    def parts(axis):
        place = lax.broadcasted_iota(jnp.int32, (size, size), axis)
        line, column = place // LANE, place % LANE
        return ((line // rows) ^ me) * rows + line % rows, column

    row_q, column_q = parts(0)
    row_k, column_k = parts(1)
    return (column_q == column_k) & (row_q >= row_k)


def gathered(chunks, index, at):
    rows, dim = chunks[0].shape[-3], chunks[0].shape[-1]
    return jnp.concatenate(
        [chunk[(*index, row, pl.ds(at, LANE), slice(None))] for chunk in chunks for row in range(rows)], axis=0
    )


def scattered(chunks, index, at, value):
    rows = chunks[0].shape[-3]
    for d, chunk in enumerate(chunks):
        for row in range(rows):
            line = d * rows + row
            chunk[(*index, row, pl.ds(at, LANE), slice(None))] = value[line * LANE : (line + 1) * LANE]


def column_probs(bias, q, k, scale):
    return softmax(dot(q, k, ((1,), (1,))) * scale + bias[...])


def column_forward_kernel(n, scale, me, *refs):
    chunks, outs, bias = refs[:n], refs[n : 2 * n], refs[2 * n]
    _, half, rows, width, _ = chunks[0].shape
    bias[...] = jnp.where(column_mask(me[0], n, rows), 0.0, -jnp.inf)
    blocks = width // LANE

    @pl.loop(0, half * blocks)
    def _(step):
        head, at = step // blocks, pl.multiple_of(step % blocks * LANE, LANE)
        q, k, v = (gathered(chunks, (array, head), at) for array in range(3))
        probs = column_probs(bias, q, k, scale)
        scattered(outs, (head,), at, dot(probs.astype(BF16), v, ((1,), (0,))).astype(BF16))


def column_forward(me, chunks, n):
    _, half, rows, width, dim = chunks[0].shape
    size = n * rows * LANE
    return pl.pallas_call(
        functools.partial(column_forward_kernel, n, dim**-0.5),
        in_specs=[pl.BlockSpec(memory_space=pltpu.SMEM)] + [VMEM] * n,
        out_specs=[VMEM] * n,
        out_shape=[jax.ShapeDtypeStruct((half, rows, width, dim), BF16)] * n,
        scratch_shapes=[pltpu.VMEM((size, size), F32)],
        compiler_params=params(60),
        cost_estimate=pl.CostEstimate(
            flops=4 * size * size * dim * half * width // LANE,
            bytes_accessed=8 * n * half * rows * width * dim,
            transcendentals=size * size * half * width // LANE,
        ),
        name="column_forward",
    )(me, *chunks)


def column_backward_kernel(n, scale, me, *refs):
    chunks, grads, outs, bias = refs[:n], refs[n : 2 * n], refs[2 * n : 3 * n], refs[3 * n]
    _, half, rows, width, _ = chunks[0].shape
    bias[...] = jnp.where(column_mask(me[0], n, rows), 0.0, -jnp.inf)
    blocks = width // LANE

    @pl.loop(0, half * blocks)
    def _(step):
        head, at = step // blocks, pl.multiple_of(step % blocks * LANE, LANE)
        q, k, v = (gathered(chunks, (array, head), at) for array in range(3))
        grad = gathered(grads, (head,), at)
        probs = column_probs(bias, q, k, scale)
        prob_grad = dot(grad, v, ((1,), (1,)))
        inner = jnp.sum(probs * prob_grad, axis=-1, keepdims=True)
        score_low = (probs * (prob_grad - inner)).astype(BF16)
        scattered(outs, (0, head), at, (dot(score_low, k, ((1,), (0,))) * scale).astype(BF16))
        scattered(outs, (1, head), at, (dot(score_low, q, ((0,), (0,))) * scale).astype(BF16))
        scattered(outs, (2, head), at, dot(probs.astype(BF16), grad, ((0,), (0,))).astype(BF16))


def column_backward(me, chunks, grads, n):
    _, half, rows, width, dim = chunks[0].shape
    size = n * rows * LANE
    return pl.pallas_call(
        functools.partial(column_backward_kernel, n, dim**-0.5),
        in_specs=[pl.BlockSpec(memory_space=pltpu.SMEM)] + [VMEM] * (2 * n),
        out_specs=[VMEM] * n,
        out_shape=[jax.ShapeDtypeStruct(chunks[0].shape, BF16)] * n,
        scratch_shapes=[pltpu.VMEM((size, size), F32)],
        compiler_params=params(60),
        cost_estimate=pl.CostEstimate(
            flops=10 * size * size * dim * half * width // LANE,
            bytes_accessed=14 * n * half * rows * width * dim,
            transcendentals=size * size * half * width // LANE,
        ),
        name="column_backward",
    )(me, *chunks, *grads)


PAIRS = [(0, 1), (1, 0), (2, 3), (3, 2)]
INWARD = [(0, 1), (3, 2)]
CROSS = [(1, 2), (2, 1)]
OUTWARD = [(1, 0), (2, 3)]


def after(value, *done):
    return lax.optimization_barrier((value, *done))[0]


class Links:
    def __init__(self, n, window):
        self.n, self.inner, self.window, self.sent = n, n // 4, window, []

    def send(self, value, pairs):
        over = len(self.sent) - self.window + 1
        if over > 0:
            value = after(value, *self.sent[max(0, over - self.window) : over])
        out = lax.ppermute(value, "ctx", pairs)
        self.sent.append(out)
        return out

    def along(self, value, pairs):
        return self.send(value, [(a * self.inner + y, b * self.inner + y) for a, b in pairs for y in range(self.inner)])

    def flip(self, value, d):
        return self.send(value, [(place, place ^ d) for place in range(self.n)])

    def swap(self, chunks, order):
        out = list(chunks)
        for d in order:
            out[d] = self.flip(chunks[d], d)
        return out


def scatter_layer(ids, flat, blocks, heads_n):
    mine = lax.axis_index("head").astype(jnp.int32)
    per = len(blocks) // heads_n

    def wanted(offsets):
        return jnp.stack([(mine ^ g) * per + b for g in offsets for b in range(per)]).astype(jnp.int32)

    def move(part, g):
        return lax.ppermute(part, "head", [(place, place ^ g) for place in range(heads_n)])

    even = list(range(0, heads_n, 2))
    near = move(layer_part(ids, flat, blocks, wanted([g + 1 for g in even]), [], []), 1)
    far = [move(layer_part(ids, flat, blocks, wanted([g]), [near], [g // 2 * per]), g) for g in even[1:]]
    return layer_part(ids, flat, blocks, wanted([0]), [near] + far, [0] * (1 + len(far)))


def on_device(queries, keys, values, out_grad, wo, *, n, heads_n):
    tokens, heads, dim = queries.shape
    half, depth, inner = heads // 2, wo.shape[1], n // 4
    me = lax.axis_index("ctx").astype(jnp.int32).reshape(1)
    line, spot = me[0] // inner, me[0] % inner
    middle, upper = (line == 1) | (line == 2), line < 2
    far = [jnp.where(upper, 2, 1), jnp.where(upper, 3, 0)]
    links = Links(n, 5)
    wide = [d for d in range(n) if d >= 2 * inner]
    close = [d for d in range(1, n) if d < 2 * inner]
    order = [d for d in wide if d % inner == 0] + [d for d in close if d % inner == 0]
    order += [d for d in wide if d % inner] + [d for d in close if d % inner]

    def around(block):
        return [block if e == 0 else links.flip(block, e) for e in range(inner)]

    near = links.along(wo, PAIRS)
    cross_own = links.along(wo, CROSS)
    own_blocks = around(wo)
    chunks, by_head = split_inputs(me, queries, keys, values, n)
    sent = list(chunks)

    def deal(*which):
        for d in which:
            sent[d] = links.flip(chunks[d], d)

    deal(order[0])
    near_blocks = around(after(near, chunks[0]))
    deal(*order[1 : n // 4])
    cross_near = links.along(near, CROSS)
    far_own = jnp.where(middle, cross_own, links.along(cross_own, OUTWARD))
    deal(*order[n // 4 : n // 2])
    far_own_blocks = around(far_own)
    far_near = jnp.where(middle, cross_near, links.along(cross_near, OUTWARD))
    deal(*order[n // 2 :])
    far_near_blocks = around(far_near)
    chunks = sent
    blocks = own_blocks + near_blocks + far_own_blocks + far_near_blocks
    ids = [owner * inner + (spot ^ e) for owner in (line, line ^ 1, *far) for e in range(inner)]
    ids = jnp.stack(ids).astype(jnp.int32)

    def targets(owners, e):
        return jnp.stack([owner * inner + (spot ^ e) for owner in owners]).astype(jnp.int32)

    def exchanged(flat, owners):
        return [
            links.flip(proj_part(targets(owners, e), flat, out_grad, [], depth, dim, 0)[0], e) for e in range(1, inner)
        ]

    def summed(flat, owners, theirs, lead):
        return proj_part(targets(owners, 0), flat, out_grad, theirs, depth, dim, lead)

    def add(*terms):
        return sum(term.astype(F32) for term in terms).astype(BF16)

    close = [line ^ 1, line]
    row_out = row_forward(*(after(tensor, near) for tensor in by_head))
    row_far = exchanged(row_out, far)
    outs = column_forward(me, chunks, n)
    column_part = links.swap(outs, order)
    grad_row, grads = attn_grad(me, ids, after(out_grad, outs[0]), blocks, dim)
    grads = links.swap(grads, order)
    column_out, flat = collect(me, row_out, column_part, n)
    column_far = exchanged(column_out, far)
    (row_far,) = summed(row_out, far, row_far, 0)
    row_far_in = links.along(row_far, INWARD)
    gradients = column_backward(me, chunks, grads, n)
    column_grads = list(gradients)

    def give_back(*which):
        for d in which:
            column_grads[d] = links.flip(gradients[d], d)

    give_back(*order[: n // 4])
    (column_far,) = summed(column_out, far, column_far, 0)
    column_far_in = links.along(column_far, INWARD)
    column_close = exchanged(column_out, close)
    row_cross = links.along(add(row_far, row_far_in), CROSS)
    give_back(*order[n // 4 : n // 4 + 1])
    column_cross = links.along(add(column_far, column_far_in), CROSS)
    row_close = exchanged(row_out, close)
    column_near, column_own = summed(column_out, close, column_close, 1)
    column_near_in = links.along(column_near[0], INWARD)
    give_back(*order[n // 4 + 1 : n // 2 + 1])
    column_back = links.along(add(column_near[0], column_cross[1]), OUTWARD)
    row_near, row_own = summed(row_out, close, row_close, 1)
    row_near_in = links.along(row_near[0], INWARD)
    row_back = links.along(add(row_near[0], row_cross[1]), OUTWARD)
    give_back(*order[n // 2 + 1 :])

    layer_out = scatter_layer(ids, after(flat, gradients[0]), blocks, heads_n)
    row_grads = row_backward(*by_head, after(grad_row, gradients[0]))
    gradients = join_gradients(me, column_grads, row_grads, n)

    proj_row = add(row_own[0], row_near_in, row_cross[0], row_back)
    proj_column = add(column_own[0], column_near_in, column_cross[0], column_back)
    shape = (half, dim, depth)
    proj_grad = jnp.stack([proj_row.reshape(shape), proj_column.reshape(shape)], axis=1)
    return (layer_out, *gradients, proj_grad.reshape(heads * dim, depth))


def solution(mesh):
    in_specs = (
        P("ctx", "head", None),
        P("ctx", "head", None),
        P("ctx", "head", None),
        P("ctx", None),
        P("head", "ctx"),
    )
    out_specs = (
        P("ctx", "head"),
        P("ctx", "head", None),
        P("ctx", "head", None),
        P("ctx", "head", None),
        P("head", "ctx"),
    )
    return jax.shard_map(
        functools.partial(on_device, n=mesh.shape["ctx"], heads_n=mesh.shape["head"]),
        mesh=mesh,
        in_specs=in_specs,
        out_specs=out_specs,
        check_vma=False,
    )
```

```python
import functools

import jax
import jax.numpy as jnp
from jax import lax
from jax.experimental import pallas as pl
from jax.experimental.pallas import tpu as pltpu
from jax.sharding import PartitionSpec as P

C = 512
LANE = 16
VMEM = pl.BlockSpec(memory_space=pltpu.VMEM)
BF16 = jnp.bfloat16
F32 = jnp.float32


def params(mib):
    return pltpu.CompilerParams(vmem_limit_bytes=mib * 1024 * 1024)


def dot(a, b, dims):
    return lax.dot_general(a, b, (dims, ((), ())), preferred_element_type=F32)


def softmax(scores):
    highest = jnp.max(scores, axis=-1, keepdims=True)
    lifted = jnp.exp(scores - highest)
    return lifted * (1.0 / jnp.sum(lifted, axis=-1, keepdims=True))


def split_kernel(q_ref, k_ref, v_ref, chunk_ref, *rest):
    row_refs, wide = rest[:3], rest[3]
    n, width = chunk_ref.shape[0], chunk_ref.shape[3]
    span, heads, dim = q_ref.shape
    for array, ref in enumerate((q_ref, k_ref, v_ref)):
        wide[...] = ref[...].astype(F32).reshape(span * heads, dim)
        for head in range(heads // 2):
            row_refs[array][head] = wide[pl.ds(2 * head, span, stride=heads), :].astype(BF16)
            for d in range(n):
                odd = wide[pl.ds(d * width * heads + 2 * head + 1, width, stride=heads), :]
                chunk_ref[d, array, head] = odd.astype(BF16)


def split_inputs(queries, keys, values, n):
    tokens, heads, dim = queries.shape
    rows, width, half = tokens // C, C // n, heads // 2
    by_head = jax.ShapeDtypeStruct((half, tokens, dim), BF16)
    out = pl.pallas_call(
        split_kernel,
        grid=(rows,),
        in_specs=[pl.BlockSpec((C, heads, dim), lambda r: (r, 0, 0))] * 3,
        out_specs=[pl.BlockSpec((n, 3, half, pl.squeezed, width, dim), lambda r: (0, 0, 0, r, 0, 0))]
        + [pl.BlockSpec((half, C, dim), lambda r: (0, r, 0))] * 3,
        scratch_shapes=[pltpu.VMEM((C * heads, dim), F32)],
        out_shape=[jax.ShapeDtypeStruct((n, 3, half, rows, width, dim), BF16)] + [by_head] * 3,
        compiler_params=params(60),
        name="split_inputs",
    )(queries, keys, values)
    return out[0], out[1:]


def join_kernel(chunk_ref, *refs):
    row_refs, outs, wide = refs[:3], refs[3:6], refs[6]
    n, width = chunk_ref.shape[0], chunk_ref.shape[3]
    span, heads, dim = outs[0].shape
    for array in range(3):
        for head in range(heads // 2):
            wide[pl.ds(2 * head, span, stride=heads), :] = row_refs[array][head].astype(F32)
            for d in range(n):
                part = chunk_ref[d, array, head].astype(F32)
                wide[pl.ds(d * width * heads + 2 * head + 1, width, stride=heads), :] = part
        outs[array][...] = wide[...].reshape(span, heads, dim).astype(BF16)


def join_gradients(chunks, by_head):
    n, _, half, rows, width, dim = chunks.shape
    tokens, heads = by_head[0].shape[1], 2 * half
    return pl.pallas_call(
        join_kernel,
        grid=(rows,),
        in_specs=[pl.BlockSpec((n, 3, half, pl.squeezed, width, dim), lambda r: (0, 0, 0, r, 0, 0))]
        + [pl.BlockSpec((half, C, dim), lambda r: (0, r, 0))] * 3,
        out_specs=[pl.BlockSpec((C, heads, dim), lambda r: (r, 0, 0))] * 3,
        scratch_shapes=[pltpu.VMEM((C * heads, dim), F32)],
        out_shape=[jax.ShapeDtypeStruct((tokens, heads, dim), BF16)] * 3,
        compiler_params=params(60),
        name="join_gradients",
    )(chunks, *by_head)


def collect_kernel(row_ref, chunk_ref, flat_ref, both_ref):
    n, half, rows, width, dim = chunk_ref.shape
    for head in range(half):
        both_ref[:, 2 * head * dim : (2 * head + 1) * dim] = row_ref[:, head * dim : (head + 1) * dim]
        for d in range(n):
            for row in range(rows):
                part = chunk_ref[d, head, row]
                at = row * C + d * width
                flat_ref[at : at + width, head * dim : (head + 1) * dim] = part
                both_ref[at : at + width, (2 * head + 1) * dim : (2 * head + 2) * dim] = part


def collect(row_out, chunks):
    n, half, rows, width, dim = chunks.shape
    return pl.pallas_call(
        collect_kernel,
        in_specs=[VMEM] * 2,
        out_specs=[VMEM] * 2,
        out_shape=[
            jax.ShapeDtypeStruct((rows * C, half * dim), BF16),
            jax.ShapeDtypeStruct((rows * C, 2 * half * dim), BF16),
        ],
        compiler_params=params(24),
        name="collect",
    )(row_out, chunks)


def attn_grad_kernel(n, dim, ids, grad_ref, *refs):
    blocks, (row_ref, chunk_ref, weight, total, sem) = refs[:n], refs[n:]
    step = pl.program_id(0)
    _, half, rows, width, _ = chunk_ref.shape
    tokens = grad_ref.shape[0]
    tile = tokens // 4

    @pl.when(step == 0)
    def _():
        for d in range(n):
            pltpu.make_async_copy(blocks[d], weight.at[ids[d]], sem.at[ids[d]]).start()
        total[...] = jnp.zeros_like(total)

    pltpu.make_async_copy(blocks[0], weight.at[step], sem.at[step]).wait()

    @pl.loop(0, tokens, step=tile)
    def _(at):
        at = pl.multiple_of(at, tile)
        total[pl.ds(at, tile)] += dot(grad_ref[pl.ds(at, tile)], weight[step], ((1,), (1,)))

    @pl.when(step == n - 1)
    def _():
        for head in range(half):
            row_ref[:, head * dim : (head + 1) * dim] = total[:, 2 * head * dim : (2 * head + 1) * dim].astype(BF16)
            for d in range(n):
                for row in range(rows):
                    at = row * C + d * width
                    part = total[at : at + width, (2 * head + 1) * dim : (2 * head + 2) * dim]
                    chunk_ref[d, head, row] = part.astype(BF16)


def attn_grad(ids, out_grad, blocks, dim):
    n, (span, depth) = len(blocks), blocks[0].shape
    tokens, half = out_grad.shape[0], span // dim // 2
    chunk = jax.ShapeDtypeStruct((n, half, tokens // C, C // n, dim), BF16)
    return pl.pallas_call(
        functools.partial(attn_grad_kernel, n, dim),
        grid_spec=pltpu.PrefetchScalarGridSpec(
            num_scalar_prefetch=1,
            grid=(n,),
            in_specs=[pl.BlockSpec((tokens, depth), lambda b, ids: (0, b))] + [pl.BlockSpec(memory_space=pl.ANY)] * n,
            out_specs=[
                pl.BlockSpec((tokens, half * dim), lambda b, ids: (0, 0)),
                pl.BlockSpec(chunk.shape, lambda b, ids: (0, 0, 0, 0, 0)),
            ],
            scratch_shapes=[
                pltpu.VMEM((n, span, depth), BF16),
                pltpu.VMEM((tokens, span), F32),
                pltpu.SemaphoreType.DMA((n,)),
            ],
        ),
        out_shape=[jax.ShapeDtypeStruct((tokens, half * dim), BF16), chunk],
        compiler_params=params(60),
        cost_estimate=pl.CostEstimate(
            flops=2 * tokens * span * depth * n,
            bytes_accessed=2 * n * depth * (tokens + span) + 2 * tokens * span,
            transcendentals=0,
        ),
        name="attn_grad",
    )(ids, out_grad, *blocks)


def layer_kernel(n, count, adds, ids, wanted, flat_ref, *refs):
    blocks, extra, out_ref = refs[:n], refs[n : n + adds], refs[n + adds]
    weight, sem = refs[n + adds + 1 :]
    step = pl.program_id(0)
    tokens = flat_ref.shape[0]
    tile = tokens // 4

    @pl.when(step == 0)
    def _():
        for s in range(count):
            for d in range(n):

                @pl.when(ids[d] == wanted[s])
                def _():
                    pltpu.make_async_copy(blocks[d], weight.at[s], sem.at[s]).start()

    pltpu.make_async_copy(blocks[0], weight.at[step], sem.at[step]).wait()

    @pl.loop(0, tokens, step=tile)
    def _(at):
        at = pl.multiple_of(at, tile)
        value = dot(flat_ref[pl.ds(at, tile)], weight[step], ((1,), (0,)))
        for ref in extra:
            value = value + ref[pl.ds(at, tile)].astype(F32)
        out_ref[pl.ds(at, tile)] = value.astype(BF16)


def layer_part(ids, flat, blocks, wanted, extra, first):
    n, (span, depth) = len(blocks), blocks[0].shape
    tokens, count = flat.shape[0], wanted.shape[0]
    by_column = pl.BlockSpec((tokens, depth), lambda s, ids, wanted: (0, s))
    return pl.pallas_call(
        functools.partial(layer_kernel, n, count, len(extra)),
        grid_spec=pltpu.PrefetchScalarGridSpec(
            num_scalar_prefetch=2,
            grid=(count,),
            in_specs=[pl.BlockSpec((tokens, span), lambda s, ids, wanted: (0, 0))]
            + [pl.BlockSpec(memory_space=pl.ANY)] * n
            + [pl.BlockSpec((tokens, depth), functools.partial(lambda f, s, ids, wanted: (0, s + f), f)) for f in first],
            out_specs=by_column,
            scratch_shapes=[pltpu.VMEM((count, span, depth), BF16), pltpu.SemaphoreType.DMA((count,))],
        ),
        out_shape=jax.ShapeDtypeStruct((tokens, count * depth), BF16),
        compiler_params=params(60),
        cost_estimate=pl.CostEstimate(
            flops=2 * tokens * span * depth * count,
            bytes_accessed=2 * (count * depth * (tokens + span) + tokens * span),
            transcendentals=0,
        ),
        name="layer_part",
    )(ids, wanted, flat, *blocks, *extra)


def proj_kernel(lead, adds, dim, order, flat_ref, grad_ref, *refs):
    extra, outs, turned = refs[:adds], refs[adds:-1], refs[-1]
    step = pl.program_id(0)
    span = flat_ref.shape[1]

    @pl.when(step == 0)
    def _():
        for at in range(0, span, dim):
            turned[at : at + dim] = flat_ref[:, at : at + dim].T

    def value(at):
        out = dot(turned[at : at + dim], grad_ref[...], ((1,), (0,)))
        for ref in extra:
            out = out + ref[at : at + dim].astype(F32)
        return out.astype(BF16)

    @pl.when(step < lead)
    def _():
        for at in range(0, span, dim):
            outs[0][at : at + dim] = value(at)

    @pl.when(step >= lead)
    def _():
        for at in range(0, span, dim):
            outs[-1][at : at + dim] = value(at)


def proj_part(order, flat, out_grad, extra, depth, dim, lead):
    tokens, span = flat.shape
    count = order.shape[0]
    sizes = [size for size in (lead, count - lead) if size]
    places = [lambda s, order: (jnp.minimum(s, lead - 1), 0, 0), lambda s, order: (jnp.maximum(s - lead, 0), 0, 0)]
    return pl.pallas_call(
        functools.partial(proj_kernel, lead, len(extra), dim),
        grid_spec=pltpu.PrefetchScalarGridSpec(
            num_scalar_prefetch=1,
            grid=(count,),
            in_specs=[
                pl.BlockSpec((tokens, span), lambda s, order: (0, 0)),
                pl.BlockSpec((tokens, depth), lambda s, order: (0, order[s])),
            ]
            + [pl.BlockSpec((pl.squeezed, span, depth), lambda s, order: (s, 0, 0))] * len(extra),
            out_specs=[pl.BlockSpec((pl.squeezed, span, depth), place) for place in places[-len(sizes) :]],
            scratch_shapes=[pltpu.VMEM((span, tokens), BF16)],
        ),
        out_shape=[jax.ShapeDtypeStruct((size, span, depth), BF16) for size in sizes],
        compiler_params=params(60),
        cost_estimate=pl.CostEstimate(
            flops=2 * tokens * span * depth * count,
            bytes_accessed=2 * (count * depth * (tokens + span * (1 + len(extra))) + tokens * span),
            transcendentals=0,
        ),
        name="proj_part",
    )(order, flat, out_grad, *extra)


def row_blocks(length):
    step = length // 2
    return [(start, step) for start in range(0, length, step)]


def row_probs(q, k, start, step, scale):
    scores = dot(q, k, ((1,), (1,))) * scale
    place = lax.broadcasted_iota(jnp.int32, scores.shape, 0) + start
    seen = lax.broadcasted_iota(jnp.int32, scores.shape, 1)
    return softmax(jnp.where(place >= seen, scores, -jnp.inf))


def row_forward_kernel(scale, q_ref, k_ref, v_ref, o_ref):
    for start, step in row_blocks(q_ref.shape[0]):
        stop = start + step
        probs = row_probs(q_ref[start:stop], k_ref[:stop], start, step, scale)
        o_ref[start:stop] = dot(probs.astype(BF16), v_ref[:stop], ((1,), (0,))).astype(BF16)


def row_forward(q, k, v):
    half, tokens, dim = q.shape
    by_head = pl.BlockSpec((pl.squeezed, C, dim), lambda r, h: (h, r, 0))
    return pl.pallas_call(
        functools.partial(row_forward_kernel, dim**-0.5),
        grid=(tokens // C, half),
        in_specs=[by_head] * 3,
        out_specs=pl.BlockSpec((C, dim), lambda r, h: (r, h)),
        out_shape=jax.ShapeDtypeStruct((tokens, half * dim), BF16),
        compiler_params=params(60),
        cost_estimate=pl.CostEstimate(
            flops=4 * tokens * C * half * dim, bytes_accessed=8 * tokens * half * dim, transcendentals=tokens * C * half
        ),
        name="row_forward",
    )(q, k, v)


def row_backward_kernel(scale, q_ref, k_ref, v_ref, g_ref, dq_ref, dk_ref, dv_ref, k_sum, v_sum):
    k_sum[...] = jnp.zeros_like(k_sum)
    v_sum[...] = jnp.zeros_like(v_sum)
    for start, step in row_blocks(q_ref.shape[0]):
        stop = start + step
        q, k, grad = q_ref[start:stop], k_ref[:stop], g_ref[start:stop]
        probs = row_probs(q, k, start, step, scale)
        prob_grad = dot(grad, v_ref[:stop], ((1,), (1,)))
        inner = jnp.sum(probs * prob_grad, axis=-1, keepdims=True)
        score_low = (probs * (prob_grad - inner)).astype(BF16)
        dq_ref[start:stop] = (dot(score_low, k, ((1,), (0,))) * scale).astype(BF16)
        k_sum[:stop] += dot(score_low, q, ((0,), (0,)))
        v_sum[:stop] += dot(probs.astype(BF16), grad, ((0,), (0,)))
    dk_ref[...] = (k_sum[...] * scale).astype(BF16)
    dv_ref[...] = v_sum[...].astype(BF16)


def row_backward(q, k, v, grad):
    half, tokens, dim = q.shape
    by_head = pl.BlockSpec((pl.squeezed, C, dim), lambda r, h: (h, r, 0))
    return pl.pallas_call(
        functools.partial(row_backward_kernel, dim**-0.5),
        grid=(tokens // C, half),
        in_specs=[by_head] * 3 + [pl.BlockSpec((C, dim), lambda r, h: (r, h))],
        out_specs=[by_head] * 3,
        out_shape=[jax.ShapeDtypeStruct(q.shape, BF16)] * 3,
        scratch_shapes=[pltpu.VMEM((C, dim), F32)] * 2,
        compiler_params=params(60),
        cost_estimate=pl.CostEstimate(
            flops=10 * tokens * C * half * dim, bytes_accessed=14 * tokens * half * dim, transcendentals=tokens * C * half
        ),
        name="row_backward",
    )(q, k, v, grad)


def column_mask(size):
    def parts(axis):
        place = lax.broadcasted_iota(jnp.int32, (size, size), axis)
        return place // LANE, place % LANE

    row_q, column_q = parts(0)
    row_k, column_k = parts(1)
    return (column_q == column_k) & (row_q >= row_k)


def gathered(ref, index, at):
    n, rows = ref.shape[0], ref.shape[-3]
    return jnp.concatenate([ref[(d, *index, row, pl.ds(at, LANE))] for d in range(n) for row in range(rows)], axis=0)


def scattered(ref, index, at, value):
    n, rows = ref.shape[0], ref.shape[-3]
    for d in range(n):
        for row in range(rows):
            line = d * rows + row
            ref[(d, *index, row, pl.ds(at, LANE))] = value[line * LANE : (line + 1) * LANE]


def column_probs(bias, q, k, scale):
    return softmax(dot(q, k, ((1,), (1,))) * scale + bias[...])


def column_forward_kernel(scale, chunk_ref, out_ref, bias):
    half, width = chunk_ref.shape[2], chunk_ref.shape[4]
    bias[...] = jnp.where(column_mask(bias.shape[0]), 0.0, -jnp.inf)
    blocks = width // LANE

    @pl.loop(0, half * blocks)
    def _(step):
        head, at = step // blocks, pl.multiple_of(step % blocks * LANE, LANE)
        q, k, v = (gathered(chunk_ref, (array, head), at) for array in range(3))
        probs = column_probs(bias, q, k, scale)
        scattered(out_ref, (head,), at, dot(probs.astype(BF16), v, ((1,), (0,))).astype(BF16))


def column_forward(chunks):
    n, _, half, rows, width, dim = chunks.shape
    size = n * rows * LANE
    return pl.pallas_call(
        functools.partial(column_forward_kernel, dim**-0.5),
        in_specs=[VMEM],
        out_specs=VMEM,
        out_shape=jax.ShapeDtypeStruct((n, half, rows, width, dim), BF16),
        scratch_shapes=[pltpu.VMEM((size, size), F32)],
        compiler_params=params(24),
        cost_estimate=pl.CostEstimate(
            flops=4 * size * size * dim * half * width // LANE,
            bytes_accessed=8 * n * half * rows * width * dim,
            transcendentals=size * size * half * width // LANE,
        ),
        name="column_forward",
    )(chunks)


def column_backward_kernel(scale, chunk_ref, grad_ref, out_ref, bias):
    half, width = chunk_ref.shape[2], chunk_ref.shape[4]
    bias[...] = jnp.where(column_mask(bias.shape[0]), 0.0, -jnp.inf)
    blocks = width // LANE

    @pl.loop(0, half * blocks)
    def _(step):
        head, at = step // blocks, pl.multiple_of(step % blocks * LANE, LANE)
        q, k, v = (gathered(chunk_ref, (array, head), at) for array in range(3))
        grad = gathered(grad_ref, (head,), at)
        probs = column_probs(bias, q, k, scale)
        prob_grad = dot(grad, v, ((1,), (1,)))
        inner = jnp.sum(probs * prob_grad, axis=-1, keepdims=True)
        score_low = (probs * (prob_grad - inner)).astype(BF16)
        scattered(out_ref, (0, head), at, (dot(score_low, k, ((1,), (0,))) * scale).astype(BF16))
        scattered(out_ref, (1, head), at, (dot(score_low, q, ((0,), (0,))) * scale).astype(BF16))
        scattered(out_ref, (2, head), at, dot(probs.astype(BF16), grad, ((0,), (0,))).astype(BF16))


def column_backward(chunks, grads):
    n, _, half, rows, width, dim = chunks.shape
    size = n * rows * LANE
    return pl.pallas_call(
        functools.partial(column_backward_kernel, dim**-0.5),
        in_specs=[VMEM] * 2,
        out_specs=VMEM,
        out_shape=jax.ShapeDtypeStruct(chunks.shape, BF16),
        scratch_shapes=[pltpu.VMEM((size, size), F32)],
        compiler_params=params(24),
        cost_estimate=pl.CostEstimate(
            flops=10 * size * size * dim * half * width // LANE,
            bytes_accessed=14 * n * half * rows * width * dim,
            transcendentals=size * size * half * width // LANE,
        ),
        name="column_backward",
    )(chunks, grads)


PAIRS = [(0, 1), (1, 0), (2, 3), (3, 2)]
INWARD = [(0, 1), (3, 2)]
CROSS = [(1, 2), (2, 1)]
OUTWARD = [(1, 0), (2, 3)]


def after(value, *done):
    return lax.optimization_barrier((value, *done))[0]


class Links:
    def __init__(self, n, window):
        self.n, self.inner, self.window, self.sent = n, n // 4, window, []

    def send(self, value, pairs):
        over = len(self.sent) - self.window + 1
        if over > 0:
            value = after(value, *self.sent[max(0, over - self.window) : over])
        out = lax.ppermute(value, "ctx", pairs)
        self.sent.append(out)
        return out

    def along(self, value, pairs):
        return self.send(value, [(a * self.inner + y, b * self.inner + y) for a, b in pairs for y in range(self.inner)])

    def flip(self, value, d):
        return self.send(value, [(place, place ^ d) for place in range(self.n)])


def swap(chunks):
    return lax.all_to_all(chunks, "ctx", split_axis=0, concat_axis=0, tiled=True)


def scatter_layer(ids, flat, blocks, heads_n):
    mine = lax.axis_index("head").astype(jnp.int32)
    per = len(blocks) // heads_n

    def wanted(offsets):
        return jnp.stack([(mine ^ g) * per + b for g in offsets for b in range(per)]).astype(jnp.int32)

    def move(part, g):
        return lax.ppermute(part, "head", [(place, place ^ g) for place in range(heads_n)])

    even = list(range(0, heads_n, 2))
    near = move(layer_part(ids, flat, blocks, wanted([g + 1 for g in even]), [], []), 1)
    far = [move(layer_part(ids, flat, blocks, wanted([g]), [near], [g // 2 * per]), g) for g in even[1:]]
    return layer_part(ids, flat, blocks, wanted([0]), [near] + far, [0] * (1 + len(far)))


def on_device(queries, keys, values, out_grad, wo, *, n, heads_n):
    tokens, heads, dim = queries.shape
    half, depth, inner = heads // 2, wo.shape[1], n // 4
    me = lax.axis_index("ctx").astype(jnp.int32)
    line, spot = me // inner, me % inner
    middle, upper = (line == 1) | (line == 2), line < 2
    far, close = [jnp.where(upper, 2, 1), jnp.where(upper, 3, 0)], [line ^ 1, line]
    links = Links(n, 5)

    def around(block):
        return [block if e == 0 else links.flip(block, e) for e in range(inner)]

    near = links.along(wo, PAIRS)
    cross_own = links.along(wo, CROSS)
    own_blocks = around(wo)
    chunks, by_head = split_inputs(queries, keys, values, n)
    chunks, near = swap(chunks), after(near, chunks)
    near_blocks = around(near)
    cross_near = links.along(near, CROSS)
    far_own = jnp.where(middle, cross_own, links.along(cross_own, OUTWARD))
    far_own_blocks = around(far_own)
    far_near = jnp.where(middle, cross_near, links.along(cross_near, OUTWARD))
    far_near_blocks = around(far_near)
    blocks = own_blocks + near_blocks + far_own_blocks + far_near_blocks
    ids = [owner * inner + (spot ^ e) for owner in (line, line ^ 1, *far) for e in range(inner)]
    ids = jnp.stack(ids).astype(jnp.int32)

    def targets(owners, e):
        return jnp.stack([owner * inner + (spot ^ e) for owner in owners]).astype(jnp.int32)

    def exchanged(flat, owners):
        return [
            links.flip(proj_part(targets(owners, e), flat, out_grad, [], depth, dim, 0)[0], e) for e in range(1, inner)
        ]

    def summed(flat, owners, theirs, lead):
        return proj_part(targets(owners, 0), flat, out_grad, theirs, depth, dim, lead)

    def add(*terms):
        return sum(term.astype(F32) for term in terms).astype(BF16)

    row_out = row_forward(*(after(tensor, near) for tensor in by_head))
    row_far = exchanged(row_out, far)
    row_close = exchanged(row_out, close)

    outs = column_forward(chunks)
    column_part = swap(outs)
    grad_row, grads = attn_grad(ids, after(out_grad, outs), blocks, dim)
    grads = swap(after(grads, column_part))
    column_out, flat = collect(row_out, column_part)
    column_far = exchanged(column_out, far)
    column_close = exchanged(column_out, close)
    gradients = column_backward(chunks, grads)
    column_grads = swap(gradients)

    (row_far,) = summed(after(row_out, column_out), far, row_far, 0)
    row_far_in = links.along(row_far, INWARD)
    row_near, row_own = summed(after(row_out, column_out), close, row_close, 1)
    row_near_in = links.along(row_near[0], INWARD)
    (column_far,) = summed(after(column_out, gradients), far, column_far, 0)
    column_far_in = links.along(column_far, INWARD)
    row_cross = links.along(add(row_far, row_far_in), CROSS)
    column_near, column_own = summed(after(column_out, gradients), close, column_close, 1)
    column_near_in = links.along(column_near[0], INWARD)
    column_cross = links.along(add(column_far, column_far_in), CROSS)
    row_back = links.along(add(row_near[0], row_cross[1]), OUTWARD)
    column_back = links.along(add(column_near[0], column_cross[1]), OUTWARD)

    layer_out = scatter_layer(ids, after(flat, gradients), blocks, heads_n)
    row_grads = row_backward(*by_head, after(grad_row, gradients))
    gradients = join_gradients(column_grads, row_grads)

    proj_row = add(row_own[0], row_near_in, row_cross[0], row_back)
    proj_column = add(column_own[0], column_near_in, column_cross[0], column_back)
    shape = (half, dim, depth)
    proj_grad = jnp.stack([proj_row.reshape(shape), proj_column.reshape(shape)], axis=1)
    return (layer_out, *gradients, proj_grad.reshape(heads * dim, depth))


def solution(mesh):
    in_specs = (
        P("ctx", "head", None),
        P("ctx", "head", None),
        P("ctx", "head", None),
        P("ctx", None),
        P("head", "ctx"),
    )
    out_specs = (
        P("ctx", "head"),
        P("ctx", "head", None),
        P("ctx", "head", None),
        P("ctx", "head", None),
        P("head", "ctx"),
    )
    return jax.shard_map(
        functools.partial(on_device, n=mesh.shape["ctx"], heads_n=mesh.shape["head"]),
        mesh=mesh,
        in_specs=in_specs,
        out_specs=out_specs,
        check_vma=False,
    )
```

```python
import functools

import jax
import jax.numpy as jnp
from jax import lax
from jax.experimental import pallas as pl
from jax.experimental.pallas import tpu as pltpu
from jax.sharding import PartitionSpec as P

C = 512
LANE = 16
VMEM = pl.BlockSpec(memory_space=pltpu.VMEM)
BF16 = jnp.bfloat16
F32 = jnp.float32


def params(mib):
    return pltpu.CompilerParams(vmem_limit_bytes=mib * 1024 * 1024)


def dot(a, b, dims):
    return lax.dot_general(a, b, (dims, ((), ())), preferred_element_type=F32)


def softmax(scores):
    highest = jnp.max(scores, axis=-1, keepdims=True)
    lifted = jnp.exp(scores - highest)
    return lifted * (1.0 / jnp.sum(lifted, axis=-1, keepdims=True))


def split_kernel(q_ref, k_ref, v_ref, chunk_ref, *rest):
    row_refs, wide = rest[:3], rest[3]
    n, width = chunk_ref.shape[0], chunk_ref.shape[3]
    span, heads, dim = q_ref.shape
    for array, ref in enumerate((q_ref, k_ref, v_ref)):
        wide[...] = ref[...].astype(F32).reshape(span * heads, dim)
        for head in range(heads // 2):
            row_refs[array][head] = wide[pl.ds(2 * head, span, stride=heads), :].astype(BF16)
            for d in range(n):
                odd = wide[pl.ds(d * width * heads + 2 * head + 1, width, stride=heads), :]
                chunk_ref[d, array, head] = odd.astype(BF16)


def split_inputs(queries, keys, values, n):
    tokens, heads, dim = queries.shape
    rows, width, half = tokens // C, C // n, heads // 2
    by_head = jax.ShapeDtypeStruct((half, tokens, dim), BF16)
    out = pl.pallas_call(
        split_kernel,
        grid=(rows,),
        in_specs=[pl.BlockSpec((C, heads, dim), lambda r: (r, 0, 0))] * 3,
        out_specs=[pl.BlockSpec((n, 3, half, pl.squeezed, width, dim), lambda r: (0, 0, 0, r, 0, 0))]
        + [pl.BlockSpec((half, C, dim), lambda r: (0, r, 0))] * 3,
        scratch_shapes=[pltpu.VMEM((C * heads, dim), F32)],
        out_shape=[jax.ShapeDtypeStruct((n, 3, half, rows, width, dim), BF16)] + [by_head] * 3,
        compiler_params=params(60),
        name="split_inputs",
    )(queries, keys, values)
    return out[0], out[1:]


def join_kernel(chunk_ref, *refs):
    row_refs, outs, wide = refs[:3], refs[3:6], refs[6]
    n, width = chunk_ref.shape[0], chunk_ref.shape[3]
    span, heads, dim = outs[0].shape
    for array in range(3):
        for head in range(heads // 2):
            wide[pl.ds(2 * head, span, stride=heads), :] = row_refs[array][head].astype(F32)
            for d in range(n):
                part = chunk_ref[d, array, head].astype(F32)
                wide[pl.ds(d * width * heads + 2 * head + 1, width, stride=heads), :] = part
        outs[array][...] = wide[...].reshape(span, heads, dim).astype(BF16)


def join_gradients(chunks, by_head):
    n, _, half, rows, width, dim = chunks.shape
    tokens, heads = by_head[0].shape[1], 2 * half
    return pl.pallas_call(
        join_kernel,
        grid=(rows,),
        in_specs=[pl.BlockSpec((n, 3, half, pl.squeezed, width, dim), lambda r: (0, 0, 0, r, 0, 0))]
        + [pl.BlockSpec((half, C, dim), lambda r: (0, r, 0))] * 3,
        out_specs=[pl.BlockSpec((C, heads, dim), lambda r: (r, 0, 0))] * 3,
        scratch_shapes=[pltpu.VMEM((C * heads, dim), F32)],
        out_shape=[jax.ShapeDtypeStruct((tokens, heads, dim), BF16)] * 3,
        compiler_params=params(60),
        name="join_gradients",
    )(chunks, *by_head)


def collect_kernel(row_ref, chunk_ref, flat_ref, both_ref):
    n, half, rows, width, dim = chunk_ref.shape
    for head in range(half):
        both_ref[:, 2 * head * dim : (2 * head + 1) * dim] = row_ref[:, head * dim : (head + 1) * dim]
        for d in range(n):
            for row in range(rows):
                part = chunk_ref[d, head, row]
                at = row * C + d * width
                flat_ref[at : at + width, head * dim : (head + 1) * dim] = part
                both_ref[at : at + width, (2 * head + 1) * dim : (2 * head + 2) * dim] = part


def collect(row_out, chunks):
    n, half, rows, width, dim = chunks.shape
    return pl.pallas_call(
        collect_kernel,
        in_specs=[VMEM] * 2,
        out_specs=[VMEM] * 2,
        out_shape=[
            jax.ShapeDtypeStruct((rows * C, half * dim), BF16),
            jax.ShapeDtypeStruct((rows * C, 2 * half * dim), BF16),
        ],
        compiler_params=params(24),
        name="collect",
    )(row_out, chunks)


def attn_grad_kernel(n, dim, ids, grad_ref, *refs):
    blocks, (row_ref, chunk_ref, weight, total, sem) = refs[:n], refs[n:]
    step = pl.program_id(0)
    _, half, rows, width, _ = chunk_ref.shape
    tokens = grad_ref.shape[0]
    tile = tokens // 4

    @pl.when(step == 0)
    def _():
        for d in range(n):
            pltpu.make_async_copy(blocks[d], weight.at[ids[d]], sem.at[ids[d]]).start()
        total[...] = jnp.zeros_like(total)

    pltpu.make_async_copy(blocks[0], weight.at[step], sem.at[step]).wait()

    @pl.loop(0, tokens, step=tile)
    def _(at):
        at = pl.multiple_of(at, tile)
        total[pl.ds(at, tile)] += dot(grad_ref[pl.ds(at, tile)], weight[step], ((1,), (1,)))

    @pl.when(step == n - 1)
    def _():
        for head in range(half):
            row_ref[:, head * dim : (head + 1) * dim] = total[:, 2 * head * dim : (2 * head + 1) * dim].astype(BF16)
            for d in range(n):
                for row in range(rows):
                    at = row * C + d * width
                    part = total[at : at + width, (2 * head + 1) * dim : (2 * head + 2) * dim]
                    chunk_ref[d, head, row] = part.astype(BF16)


def attn_grad(ids, out_grad, blocks, dim):
    n, (span, depth) = len(blocks), blocks[0].shape
    tokens, half = out_grad.shape[0], span // dim // 2
    chunk = jax.ShapeDtypeStruct((n, half, tokens // C, C // n, dim), BF16)
    return pl.pallas_call(
        functools.partial(attn_grad_kernel, n, dim),
        grid_spec=pltpu.PrefetchScalarGridSpec(
            num_scalar_prefetch=1,
            grid=(n,),
            in_specs=[pl.BlockSpec((tokens, depth), lambda b, ids: (0, b))] + [pl.BlockSpec(memory_space=pl.ANY)] * n,
            out_specs=[
                pl.BlockSpec((tokens, half * dim), lambda b, ids: (0, 0)),
                pl.BlockSpec(chunk.shape, lambda b, ids: (0, 0, 0, 0, 0)),
            ],
            scratch_shapes=[
                pltpu.VMEM((n, span, depth), BF16),
                pltpu.VMEM((tokens, span), F32),
                pltpu.SemaphoreType.DMA((n,)),
            ],
        ),
        out_shape=[jax.ShapeDtypeStruct((tokens, half * dim), BF16), chunk],
        compiler_params=params(60),
        cost_estimate=pl.CostEstimate(
            flops=2 * tokens * span * depth * n,
            bytes_accessed=2 * n * depth * (tokens + span) + 2 * tokens * span,
            transcendentals=0,
        ),
        name="attn_grad",
    )(ids, out_grad, *blocks)


def layer_kernel(n, count, adds, ids, wanted, flat_ref, *refs):
    blocks, extra, out_ref = refs[:n], refs[n : n + adds], refs[n + adds]
    weight, sem = refs[n + adds + 1 :]
    step = pl.program_id(0)
    tokens = flat_ref.shape[0]
    tile = tokens // 4

    @pl.when(step == 0)
    def _():
        for s in range(count):
            for d in range(n):

                @pl.when(ids[d] == wanted[s])
                def _():
                    pltpu.make_async_copy(blocks[d], weight.at[s], sem.at[s]).start()

    pltpu.make_async_copy(blocks[0], weight.at[step], sem.at[step]).wait()

    @pl.loop(0, tokens, step=tile)
    def _(at):
        at = pl.multiple_of(at, tile)
        value = dot(flat_ref[pl.ds(at, tile)], weight[step], ((1,), (0,)))
        for ref in extra:
            value = value + ref[pl.ds(at, tile)].astype(F32)
        out_ref[pl.ds(at, tile)] = value.astype(BF16)


def layer_part(ids, flat, blocks, wanted, extra, first):
    n, (span, depth) = len(blocks), blocks[0].shape
    tokens, count = flat.shape[0], wanted.shape[0]
    by_column = pl.BlockSpec((tokens, depth), lambda s, ids, wanted: (0, s))
    return pl.pallas_call(
        functools.partial(layer_kernel, n, count, len(extra)),
        grid_spec=pltpu.PrefetchScalarGridSpec(
            num_scalar_prefetch=2,
            grid=(count,),
            in_specs=[pl.BlockSpec((tokens, span), lambda s, ids, wanted: (0, 0))]
            + [pl.BlockSpec(memory_space=pl.ANY)] * n
            + [pl.BlockSpec((tokens, depth), functools.partial(lambda f, s, ids, wanted: (0, s + f), f)) for f in first],
            out_specs=by_column,
            scratch_shapes=[pltpu.VMEM((count, span, depth), BF16), pltpu.SemaphoreType.DMA((count,))],
        ),
        out_shape=jax.ShapeDtypeStruct((tokens, count * depth), BF16),
        compiler_params=params(60),
        cost_estimate=pl.CostEstimate(
            flops=2 * tokens * span * depth * count,
            bytes_accessed=2 * (count * depth * (tokens + span) + tokens * span),
            transcendentals=0,
        ),
        name="layer_part",
    )(ids, wanted, flat, *blocks, *extra)


def proj_kernel(lead, adds, dim, order, flat_ref, grad_ref, *refs):
    extra, outs, turned = refs[:adds], refs[adds:-1], refs[-1]
    step = pl.program_id(0)
    span = flat_ref.shape[1]

    @pl.when(step == 0)
    def _():
        for at in range(0, span, dim):
            turned[at : at + dim] = flat_ref[:, at : at + dim].T

    def value(at):
        out = dot(turned[at : at + dim], grad_ref[...], ((1,), (0,)))
        for ref in extra:
            out = out + ref[at : at + dim].astype(F32)
        return out.astype(BF16)

    @pl.when(step < lead)
    def _():
        for at in range(0, span, dim):
            outs[0][at : at + dim] = value(at)

    @pl.when(step >= lead)
    def _():
        for at in range(0, span, dim):
            outs[-1][at : at + dim] = value(at)


def proj_part(order, flat, out_grad, extra, depth, dim, lead):
    tokens, span = flat.shape
    count = order.shape[0]
    sizes = [size for size in (lead, count - lead) if size]
    places = [lambda s, order: (jnp.minimum(s, lead - 1), 0, 0), lambda s, order: (jnp.maximum(s - lead, 0), 0, 0)]
    return pl.pallas_call(
        functools.partial(proj_kernel, lead, len(extra), dim),
        grid_spec=pltpu.PrefetchScalarGridSpec(
            num_scalar_prefetch=1,
            grid=(count,),
            in_specs=[
                pl.BlockSpec((tokens, span), lambda s, order: (0, 0)),
                pl.BlockSpec((tokens, depth), lambda s, order: (0, order[s])),
            ]
            + [pl.BlockSpec((pl.squeezed, span, depth), lambda s, order: (s, 0, 0))] * len(extra),
            out_specs=[pl.BlockSpec((pl.squeezed, span, depth), place) for place in places[-len(sizes) :]],
            scratch_shapes=[pltpu.VMEM((span, tokens), BF16)],
        ),
        out_shape=[jax.ShapeDtypeStruct((size, span, depth), BF16) for size in sizes],
        compiler_params=params(60),
        cost_estimate=pl.CostEstimate(
            flops=2 * tokens * span * depth * count,
            bytes_accessed=2 * (count * depth * (tokens + span * (1 + len(extra))) + tokens * span),
            transcendentals=0,
        ),
        name="proj_part",
    )(order, flat, out_grad, *extra)


def row_blocks(length):
    step = length // 2
    return [(start, step) for start in range(0, length, step)]


def row_probs(q, k, start, step, scale):
    scores = dot(q, k, ((1,), (1,))) * scale
    place = lax.broadcasted_iota(jnp.int32, scores.shape, 0) + start
    seen = lax.broadcasted_iota(jnp.int32, scores.shape, 1)
    return softmax(jnp.where(place >= seen, scores, -jnp.inf))


def row_forward_kernel(scale, q_ref, k_ref, v_ref, o_ref):
    for start, step in row_blocks(q_ref.shape[0]):
        stop = start + step
        probs = row_probs(q_ref[start:stop], k_ref[:stop], start, step, scale)
        o_ref[start:stop] = dot(probs.astype(BF16), v_ref[:stop], ((1,), (0,))).astype(BF16)


def row_forward(q, k, v):
    half, tokens, dim = q.shape
    by_head = pl.BlockSpec((pl.squeezed, C, dim), lambda r, h: (h, r, 0))
    return pl.pallas_call(
        functools.partial(row_forward_kernel, dim**-0.5),
        grid=(tokens // C, half),
        in_specs=[by_head] * 3,
        out_specs=pl.BlockSpec((C, dim), lambda r, h: (r, h)),
        out_shape=jax.ShapeDtypeStruct((tokens, half * dim), BF16),
        compiler_params=params(60),
        cost_estimate=pl.CostEstimate(
            flops=4 * tokens * C * half * dim, bytes_accessed=8 * tokens * half * dim, transcendentals=tokens * C * half
        ),
        name="row_forward",
    )(q, k, v)


def row_backward_kernel(scale, q_ref, k_ref, v_ref, g_ref, dq_ref, dk_ref, dv_ref, k_sum, v_sum):
    k_sum[...] = jnp.zeros_like(k_sum)
    v_sum[...] = jnp.zeros_like(v_sum)
    for start, step in row_blocks(q_ref.shape[0]):
        stop = start + step
        q, k, grad = q_ref[start:stop], k_ref[:stop], g_ref[start:stop]
        probs = row_probs(q, k, start, step, scale)
        prob_grad = dot(grad, v_ref[:stop], ((1,), (1,)))
        inner = jnp.sum(probs * prob_grad, axis=-1, keepdims=True)
        score_low = (probs * (prob_grad - inner)).astype(BF16)
        dq_ref[start:stop] = (dot(score_low, k, ((1,), (0,))) * scale).astype(BF16)
        k_sum[:stop] += dot(score_low, q, ((0,), (0,)))
        v_sum[:stop] += dot(probs.astype(BF16), grad, ((0,), (0,)))
    dk_ref[...] = (k_sum[...] * scale).astype(BF16)
    dv_ref[...] = v_sum[...].astype(BF16)


def row_backward(q, k, v, grad):
    half, tokens, dim = q.shape
    by_head = pl.BlockSpec((pl.squeezed, C, dim), lambda r, h: (h, r, 0))
    return pl.pallas_call(
        functools.partial(row_backward_kernel, dim**-0.5),
        grid=(tokens // C, half),
        in_specs=[by_head] * 3 + [pl.BlockSpec((C, dim), lambda r, h: (r, h))],
        out_specs=[by_head] * 3,
        out_shape=[jax.ShapeDtypeStruct(q.shape, BF16)] * 3,
        scratch_shapes=[pltpu.VMEM((C, dim), F32)] * 2,
        compiler_params=params(60),
        cost_estimate=pl.CostEstimate(
            flops=10 * tokens * C * half * dim, bytes_accessed=14 * tokens * half * dim, transcendentals=tokens * C * half
        ),
        name="row_backward",
    )(q, k, v, grad)


def column_mask(size):
    def parts(axis):
        place = lax.broadcasted_iota(jnp.int32, (size, size), axis)
        return place // LANE, place % LANE

    row_q, column_q = parts(0)
    row_k, column_k = parts(1)
    return (column_q == column_k) & (row_q >= row_k)


def gathered(ref, index, at):
    n, rows = ref.shape[0], ref.shape[-3]
    return jnp.concatenate([ref[(d, *index, row, pl.ds(at, LANE))] for d in range(n) for row in range(rows)], axis=0)


def scattered(ref, index, at, value):
    n, rows = ref.shape[0], ref.shape[-3]
    for d in range(n):
        for row in range(rows):
            line = d * rows + row
            ref[(d, *index, row, pl.ds(at, LANE))] = value[line * LANE : (line + 1) * LANE]


def column_probs(bias, q, k, scale):
    return softmax(dot(q, k, ((1,), (1,))) * scale + bias[...])


def column_forward_kernel(scale, chunk_ref, out_ref, bias):
    half, width = chunk_ref.shape[2], chunk_ref.shape[4]
    bias[...] = jnp.where(column_mask(bias.shape[0]), 0.0, -jnp.inf)
    blocks = width // LANE

    @pl.loop(0, half * blocks)
    def _(step):
        head, at = step // blocks, pl.multiple_of(step % blocks * LANE, LANE)
        q, k, v = (gathered(chunk_ref, (array, head), at) for array in range(3))
        probs = column_probs(bias, q, k, scale)
        scattered(out_ref, (head,), at, dot(probs.astype(BF16), v, ((1,), (0,))).astype(BF16))


def column_forward(chunks):
    n, _, half, rows, width, dim = chunks.shape
    size = n * rows * LANE
    return pl.pallas_call(
        functools.partial(column_forward_kernel, dim**-0.5),
        in_specs=[VMEM],
        out_specs=VMEM,
        out_shape=jax.ShapeDtypeStruct((n, half, rows, width, dim), BF16),
        scratch_shapes=[pltpu.VMEM((size, size), F32)],
        compiler_params=params(24),
        cost_estimate=pl.CostEstimate(
            flops=4 * size * size * dim * half * width // LANE,
            bytes_accessed=8 * n * half * rows * width * dim,
            transcendentals=size * size * half * width // LANE,
        ),
        name="column_forward",
    )(chunks)


def column_backward_kernel(scale, chunk_ref, grad_ref, out_ref, bias):
    half, width = chunk_ref.shape[2], chunk_ref.shape[4]
    bias[...] = jnp.where(column_mask(bias.shape[0]), 0.0, -jnp.inf)
    blocks = width // LANE

    @pl.loop(0, half * blocks)
    def _(step):
        head, at = step // blocks, pl.multiple_of(step % blocks * LANE, LANE)
        q, k, v = (gathered(chunk_ref, (array, head), at) for array in range(3))
        grad = gathered(grad_ref, (head,), at)
        probs = column_probs(bias, q, k, scale)
        prob_grad = dot(grad, v, ((1,), (1,)))
        inner = jnp.sum(probs * prob_grad, axis=-1, keepdims=True)
        score_low = (probs * (prob_grad - inner)).astype(BF16)
        scattered(out_ref, (0, head), at, (dot(score_low, k, ((1,), (0,))) * scale).astype(BF16))
        scattered(out_ref, (1, head), at, (dot(score_low, q, ((0,), (0,))) * scale).astype(BF16))
        scattered(out_ref, (2, head), at, dot(probs.astype(BF16), grad, ((0,), (0,))).astype(BF16))


def column_backward(chunks, grads):
    n, _, half, rows, width, dim = chunks.shape
    size = n * rows * LANE
    return pl.pallas_call(
        functools.partial(column_backward_kernel, dim**-0.5),
        in_specs=[VMEM] * 2,
        out_specs=VMEM,
        out_shape=jax.ShapeDtypeStruct(chunks.shape, BF16),
        scratch_shapes=[pltpu.VMEM((size, size), F32)],
        compiler_params=params(24),
        cost_estimate=pl.CostEstimate(
            flops=10 * size * size * dim * half * width // LANE,
            bytes_accessed=14 * n * half * rows * width * dim,
            transcendentals=size * size * half * width // LANE,
        ),
        name="column_backward",
    )(chunks, grads)


PAIRS = [(0, 1), (1, 0), (2, 3), (3, 2)]
INWARD = [(0, 1), (3, 2)]
CROSS = [(1, 2), (2, 1)]
OUTWARD = [(1, 0), (2, 3)]


def after(value, *done):
    return lax.optimization_barrier((value, *done))[0]


class Links:
    def __init__(self, n, window):
        self.n, self.inner, self.window, self.sent = n, n // 4, window, []

    def send(self, value, pairs):
        over = len(self.sent) - self.window + 1
        if over > 0:
            value = after(value, *self.sent[max(0, over - self.window) : over])
        out = lax.ppermute(value, "ctx", pairs)
        self.sent.append(out)
        return out

    def along(self, value, pairs):
        return self.send(value, [(a * self.inner + y, b * self.inner + y) for a, b in pairs for y in range(self.inner)])

    def flip(self, value, d):
        return self.send(value, [(place, place ^ d) for place in range(self.n)])


def swap(chunks):
    return lax.all_to_all(chunks, "ctx", split_axis=0, concat_axis=0, tiled=True)


def scatter_layer(ids, flat, blocks, heads_n):
    mine = lax.axis_index("head").astype(jnp.int32)
    per = len(blocks) // heads_n

    def wanted(offsets):
        return jnp.stack([(mine ^ g) * per + b for g in offsets for b in range(per)]).astype(jnp.int32)

    def move(part, g):
        return lax.ppermute(part, "head", [(place, place ^ g) for place in range(heads_n)])

    even = list(range(0, heads_n, 2))
    near = move(layer_part(ids, flat, blocks, wanted([g + 1 for g in even]), [], []), 1)
    far = [move(layer_part(ids, flat, blocks, wanted([g]), [near], [g // 2 * per]), g) for g in even[1:]]
    return layer_part(ids, flat, blocks, wanted([0]), [near] + far, [0] * (1 + len(far)))


def on_device(queries, keys, values, out_grad, wo, *, n, heads_n):
    tokens, heads, dim = queries.shape
    half, depth, inner = heads // 2, wo.shape[1], n // 4
    me = lax.axis_index("ctx").astype(jnp.int32)
    line, spot = me // inner, me % inner
    middle, upper = (line == 1) | (line == 2), line < 2
    far, close = [jnp.where(upper, 2, 1), jnp.where(upper, 3, 0)], [line ^ 1, line]
    links = Links(n, 5)

    def around(block):
        return [block if e == 0 else links.flip(block, e) for e in range(inner)]

    near = links.along(wo, PAIRS)
    cross_own = links.along(wo, CROSS)
    own_blocks = around(wo)
    chunks, by_head = split_inputs(queries, keys, values, n)
    chunks = swap(after(chunks, near, cross_own, *own_blocks[1:]))
    near_blocks = around(near)
    cross_near = links.along(near, CROSS)
    far_own = jnp.where(middle, cross_own, links.along(cross_own, OUTWARD))
    far_own_blocks = around(far_own)
    far_near = jnp.where(middle, cross_near, links.along(cross_near, OUTWARD))
    far_near_blocks = around(far_near)
    blocks = own_blocks + near_blocks + far_own_blocks + far_near_blocks
    ids = [owner * inner + (spot ^ e) for owner in (line, line ^ 1, *far) for e in range(inner)]
    ids = jnp.stack(ids).astype(jnp.int32)

    def targets(owners, e):
        return jnp.stack([owner * inner + (spot ^ e) for owner in owners]).astype(jnp.int32)

    def leaving(flat, owners):
        return [proj_part(targets(owners, e), flat, out_grad, [], depth, dim, 0)[0] for e in range(1, inner)]

    def exchanged(parts):
        return [links.flip(part, e + 1) for e, part in enumerate(parts)]

    def summed(flat, owners, theirs, lead):
        return proj_part(targets(owners, 0), flat, out_grad, theirs, depth, dim, lead)

    def add(*terms):
        return sum(term.astype(F32) for term in terms).astype(BF16)

    row_out = row_forward(*(after(tensor, near, cross_own) for tensor in by_head))
    row_far, row_close = leaving(row_out, far), leaving(row_out, close)
    outs = column_forward(after(chunks, *row_far, *row_close))
    row_far, row_close = exchanged(row_far), exchanged(row_close)

    column_part = swap(outs)
    grad_row, grads = attn_grad(ids, after(out_grad, outs), blocks, dim)
    grads = swap(after(grads, column_part))
    column_out, flat = collect(row_out, column_part)
    column_far, column_close = leaving(column_out, far), leaving(column_out, close)
    gradients = column_backward(chunks, after(grads, *column_far, *column_close, *row_far))
    column_far, column_close = exchanged(column_far), exchanged(column_close)
    column_grads = swap(gradients)

    later = after(row_out, gradients, *row_close)
    (row_far,) = summed(later, far, row_far, 0)
    row_far_in = links.along(row_far, INWARD)
    row_near, row_own = summed(later, close, row_close, 1)
    row_near_in = links.along(row_near[0], INWARD)
    (column_far,) = summed(column_out, far, column_far, 0)
    column_far_in = links.along(column_far, INWARD)
    row_cross = links.along(add(row_far, row_far_in), CROSS)
    flat = after(flat, column_far)
    column_near, column_own = summed(column_out, close, column_close, 1)
    column_near_in = links.along(column_near[0], INWARD)
    column_cross = links.along(add(column_far, column_far_in), CROSS)
    row_back = links.along(add(row_near[0], row_cross[1]), OUTWARD)
    column_back = links.along(add(column_near[0], column_cross[1]), OUTWARD)

    layer_out = scatter_layer(ids, flat, blocks, heads_n)
    row_grads = row_backward(*by_head, after(grad_row, gradients))
    gradients = join_gradients(column_grads, row_grads)

    proj_row = add(row_own[0], row_near_in, row_cross[0], row_back)
    proj_column = add(column_own[0], column_near_in, column_cross[0], column_back)
    shape = (half, dim, depth)
    proj_grad = jnp.stack([proj_row.reshape(shape), proj_column.reshape(shape)], axis=1)
    return (layer_out, *gradients, proj_grad.reshape(heads * dim, depth))


def solution(mesh):
    in_specs = (
        P("ctx", "head", None),
        P("ctx", "head", None),
        P("ctx", "head", None),
        P("ctx", None),
        P("head", "ctx"),
    )
    out_specs = (
        P("ctx", "head"),
        P("ctx", "head", None),
        P("ctx", "head", None),
        P("ctx", "head", None),
        P("head", "ctx"),
    )
    return jax.shard_map(
        functools.partial(on_device, n=mesh.shape["ctx"], heads_n=mesh.shape["head"]),
        mesh=mesh,
        in_specs=in_specs,
        out_specs=out_specs,
        check_vma=False,
    )
```

```python
import functools

import jax
import jax.numpy as jnp
from jax import lax
from jax.experimental import pallas as pl
from jax.experimental.pallas import tpu as pltpu
from jax.sharding import PartitionSpec as P

C = 512
LANE = 16
VMEM = pl.BlockSpec(memory_space=pltpu.VMEM)
BF16 = jnp.bfloat16
F32 = jnp.float32


def params(mib):
    return pltpu.CompilerParams(vmem_limit_bytes=mib * 1024 * 1024)


def dot(a, b, dims):
    return lax.dot_general(a, b, (dims, ((), ())), preferred_element_type=F32)


def softmax(scores):
    highest = jnp.max(scores, axis=-1, keepdims=True)
    lifted = jnp.exp(scores - highest)
    return lifted * (1.0 / jnp.sum(lifted, axis=-1, keepdims=True))


def split_kernel(q_ref, k_ref, v_ref, chunk_ref, *rest):
    row_refs, wide = rest[:3], rest[3]
    n, width = chunk_ref.shape[0], chunk_ref.shape[3]
    span, heads, dim = q_ref.shape
    for array, ref in enumerate((q_ref, k_ref, v_ref)):
        wide[...] = ref[...].astype(F32).reshape(span * heads, dim)
        for head in range(heads // 2):
            row_refs[array][head] = wide[pl.ds(2 * head, span, stride=heads), :].astype(BF16)
            for d in range(n):
                odd = wide[pl.ds(d * width * heads + 2 * head + 1, width, stride=heads), :]
                chunk_ref[d, array, head] = odd.astype(BF16)


def split_inputs(queries, keys, values, n):
    tokens, heads, dim = queries.shape
    rows, width, half = tokens // C, C // n, heads // 2
    by_head = jax.ShapeDtypeStruct((half, tokens, dim), BF16)
    out = pl.pallas_call(
        split_kernel,
        grid=(rows,),
        in_specs=[pl.BlockSpec((C, heads, dim), lambda r: (r, 0, 0))] * 3,
        out_specs=[pl.BlockSpec((n, 3, half, pl.squeezed, width, dim), lambda r: (0, 0, 0, r, 0, 0))]
        + [pl.BlockSpec((half, C, dim), lambda r: (0, r, 0))] * 3,
        scratch_shapes=[pltpu.VMEM((C * heads, dim), F32)],
        out_shape=[jax.ShapeDtypeStruct((n, 3, half, rows, width, dim), BF16)] + [by_head] * 3,
        compiler_params=params(60),
        name="split_inputs",
    )(queries, keys, values)
    return out[0], out[1:]


def join_kernel(chunk_ref, *refs):
    row_refs, outs, wide = refs[:3], refs[3:6], refs[6]
    n, width = chunk_ref.shape[0], chunk_ref.shape[3]
    span, heads, dim = outs[0].shape
    for array in range(3):
        for head in range(heads // 2):
            wide[pl.ds(2 * head, span, stride=heads), :] = row_refs[array][head].astype(F32)
            for d in range(n):
                part = chunk_ref[d, array, head].astype(F32)
                wide[pl.ds(d * width * heads + 2 * head + 1, width, stride=heads), :] = part
        outs[array][...] = wide[...].reshape(span, heads, dim).astype(BF16)


def join_gradients(chunks, by_head):
    n, _, half, rows, width, dim = chunks.shape
    tokens, heads = by_head[0].shape[1], 2 * half
    return pl.pallas_call(
        join_kernel,
        grid=(rows,),
        in_specs=[pl.BlockSpec((n, 3, half, pl.squeezed, width, dim), lambda r: (0, 0, 0, r, 0, 0))]
        + [pl.BlockSpec((half, C, dim), lambda r: (0, r, 0))] * 3,
        out_specs=[pl.BlockSpec((C, heads, dim), lambda r: (r, 0, 0))] * 3,
        scratch_shapes=[pltpu.VMEM((C * heads, dim), F32)],
        out_shape=[jax.ShapeDtypeStruct((tokens, heads, dim), BF16)] * 3,
        compiler_params=params(60),
        name="join_gradients",
    )(chunks, *by_head)


def collect_kernel(row_ref, chunk_ref, flat_ref, both_ref):
    n, half, rows, width, dim = chunk_ref.shape
    for head in range(half):
        both_ref[:, 2 * head * dim : (2 * head + 1) * dim] = row_ref[:, head * dim : (head + 1) * dim]
        for d in range(n):
            for row in range(rows):
                part = chunk_ref[d, head, row]
                at = row * C + d * width
                flat_ref[at : at + width, head * dim : (head + 1) * dim] = part
                both_ref[at : at + width, (2 * head + 1) * dim : (2 * head + 2) * dim] = part


def collect(row_out, chunks):
    n, half, rows, width, dim = chunks.shape
    return pl.pallas_call(
        collect_kernel,
        in_specs=[VMEM] * 2,
        out_specs=[VMEM] * 2,
        out_shape=[
            jax.ShapeDtypeStruct((rows * C, half * dim), BF16),
            jax.ShapeDtypeStruct((rows * C, 2 * half * dim), BF16),
        ],
        compiler_params=params(24),
        name="collect",
    )(row_out, chunks)


def attn_grad_kernel(n, dim, ids, grad_ref, *refs):
    blocks, (row_ref, chunk_ref, weight, total, sem) = refs[:n], refs[n:]
    step = pl.program_id(0)
    _, half, rows, width, _ = chunk_ref.shape
    tokens = grad_ref.shape[0]
    tile = tokens // 4

    @pl.when(step == 0)
    def _():
        for d in range(n):
            pltpu.make_async_copy(blocks[d], weight.at[ids[d]], sem.at[ids[d]]).start()
        total[...] = jnp.zeros_like(total)

    pltpu.make_async_copy(blocks[0], weight.at[step], sem.at[step]).wait()

    @pl.loop(0, tokens, step=tile)
    def _(at):
        at = pl.multiple_of(at, tile)
        total[pl.ds(at, tile)] += dot(grad_ref[pl.ds(at, tile)], weight[step], ((1,), (1,)))

    @pl.when(step == n - 1)
    def _():
        for head in range(half):
            row_ref[:, head * dim : (head + 1) * dim] = total[:, 2 * head * dim : (2 * head + 1) * dim].astype(BF16)
            for d in range(n):
                for row in range(rows):
                    at = row * C + d * width
                    part = total[at : at + width, (2 * head + 1) * dim : (2 * head + 2) * dim]
                    chunk_ref[d, head, row] = part.astype(BF16)


def attn_grad(ids, out_grad, blocks, dim):
    n, (span, depth) = len(blocks), blocks[0].shape
    tokens, half = out_grad.shape[0], span // dim // 2
    chunk = jax.ShapeDtypeStruct((n, half, tokens // C, C // n, dim), BF16)
    return pl.pallas_call(
        functools.partial(attn_grad_kernel, n, dim),
        grid_spec=pltpu.PrefetchScalarGridSpec(
            num_scalar_prefetch=1,
            grid=(n,),
            in_specs=[pl.BlockSpec((tokens, depth), lambda b, ids: (0, b))] + [pl.BlockSpec(memory_space=pl.ANY)] * n,
            out_specs=[
                pl.BlockSpec((tokens, half * dim), lambda b, ids: (0, 0)),
                pl.BlockSpec(chunk.shape, lambda b, ids: (0, 0, 0, 0, 0)),
            ],
            scratch_shapes=[
                pltpu.VMEM((n, span, depth), BF16),
                pltpu.VMEM((tokens, span), F32),
                pltpu.SemaphoreType.DMA((n,)),
            ],
        ),
        out_shape=[jax.ShapeDtypeStruct((tokens, half * dim), BF16), chunk],
        compiler_params=params(60),
        cost_estimate=pl.CostEstimate(
            flops=2 * tokens * span * depth * n,
            bytes_accessed=2 * n * depth * (tokens + span) + 2 * tokens * span,
            transcendentals=0,
        ),
        name="attn_grad",
    )(ids, out_grad, *blocks)


def layer_kernel(n, count, adds, ids, wanted, flat_ref, *refs):
    blocks, extra, out_ref = refs[:n], refs[n : n + adds], refs[n + adds]
    weight, sem = refs[n + adds + 1 :]
    step = pl.program_id(0)
    tokens = flat_ref.shape[0]
    tile = tokens // 4

    @pl.when(step == 0)
    def _():
        for s in range(count):
            for d in range(n):

                @pl.when(ids[d] == wanted[s])
                def _():
                    pltpu.make_async_copy(blocks[d], weight.at[s], sem.at[s]).start()

    pltpu.make_async_copy(blocks[0], weight.at[step], sem.at[step]).wait()

    @pl.loop(0, tokens, step=tile)
    def _(at):
        at = pl.multiple_of(at, tile)
        value = dot(flat_ref[pl.ds(at, tile)], weight[step], ((1,), (0,)))
        for ref in extra:
            value = value + ref[pl.ds(at, tile)].astype(F32)
        out_ref[pl.ds(at, tile)] = value.astype(BF16)


def layer_part(ids, flat, blocks, wanted, extra, first):
    n, (span, depth) = len(blocks), blocks[0].shape
    tokens, count = flat.shape[0], wanted.shape[0]
    by_column = pl.BlockSpec((tokens, depth), lambda s, ids, wanted: (0, s))
    return pl.pallas_call(
        functools.partial(layer_kernel, n, count, len(extra)),
        grid_spec=pltpu.PrefetchScalarGridSpec(
            num_scalar_prefetch=2,
            grid=(count,),
            in_specs=[pl.BlockSpec((tokens, span), lambda s, ids, wanted: (0, 0))]
            + [pl.BlockSpec(memory_space=pl.ANY)] * n
            + [pl.BlockSpec((tokens, depth), functools.partial(lambda f, s, ids, wanted: (0, s + f), f)) for f in first],
            out_specs=by_column,
            scratch_shapes=[pltpu.VMEM((count, span, depth), BF16), pltpu.SemaphoreType.DMA((count,))],
        ),
        out_shape=jax.ShapeDtypeStruct((tokens, count * depth), BF16),
        compiler_params=params(60),
        cost_estimate=pl.CostEstimate(
            flops=2 * tokens * span * depth * count,
            bytes_accessed=2 * (count * depth * (tokens + span) + tokens * span),
            transcendentals=0,
        ),
        name="layer_part",
    )(ids, wanted, flat, *blocks, *extra)


def proj_kernel(lead, adds, dim, order, flat_ref, grad_ref, *refs):
    extra, outs, turned = refs[:adds], refs[adds:-1], refs[-1]
    step = pl.program_id(0)
    span = flat_ref.shape[1]

    @pl.when(step == 0)
    def _():
        for at in range(0, span, dim):
            turned[at : at + dim] = flat_ref[:, at : at + dim].T

    def value(at):
        out = dot(turned[at : at + dim], grad_ref[...], ((1,), (0,)))
        for ref in extra:
            out = out + ref[at : at + dim].astype(F32)
        return out.astype(BF16)

    @pl.when(step < lead)
    def _():
        for at in range(0, span, dim):
            outs[0][at : at + dim] = value(at)

    @pl.when(step >= lead)
    def _():
        for at in range(0, span, dim):
            outs[-1][at : at + dim] = value(at)


def proj_part(order, flat, out_grad, extra, depth, dim, lead):
    tokens, span = flat.shape
    count = order.shape[0]
    sizes = [size for size in (lead, count - lead) if size]
    places = [lambda s, order: (jnp.minimum(s, lead - 1), 0, 0), lambda s, order: (jnp.maximum(s - lead, 0), 0, 0)]
    return pl.pallas_call(
        functools.partial(proj_kernel, lead, len(extra), dim),
        grid_spec=pltpu.PrefetchScalarGridSpec(
            num_scalar_prefetch=1,
            grid=(count,),
            in_specs=[
                pl.BlockSpec((tokens, span), lambda s, order: (0, 0)),
                pl.BlockSpec((tokens, depth), lambda s, order: (0, order[s])),
            ]
            + [pl.BlockSpec((pl.squeezed, span, depth), lambda s, order: (s, 0, 0))] * len(extra),
            out_specs=[pl.BlockSpec((pl.squeezed, span, depth), place) for place in places[-len(sizes) :]],
            scratch_shapes=[pltpu.VMEM((span, tokens), BF16)],
        ),
        out_shape=[jax.ShapeDtypeStruct((size, span, depth), BF16) for size in sizes],
        compiler_params=params(60),
        cost_estimate=pl.CostEstimate(
            flops=2 * tokens * span * depth * count,
            bytes_accessed=2 * (count * depth * (tokens + span * (1 + len(extra))) + tokens * span),
            transcendentals=0,
        ),
        name="proj_part",
    )(order, flat, out_grad, *extra)


def row_blocks(length):
    step = length // 2
    return [(start, step) for start in range(0, length, step)]


def row_probs(q, k, start, step, scale):
    scores = dot(q, k, ((1,), (1,))) * scale
    place = lax.broadcasted_iota(jnp.int32, scores.shape, 0) + start
    seen = lax.broadcasted_iota(jnp.int32, scores.shape, 1)
    return softmax(jnp.where(place >= seen, scores, -jnp.inf))


def row_forward_kernel(scale, q_ref, k_ref, v_ref, o_ref):
    for start, step in row_blocks(q_ref.shape[0]):
        stop = start + step
        probs = row_probs(q_ref[start:stop], k_ref[:stop], start, step, scale)
        o_ref[start:stop] = dot(probs.astype(BF16), v_ref[:stop], ((1,), (0,))).astype(BF16)


def row_forward(q, k, v):
    half, tokens, dim = q.shape
    by_head = pl.BlockSpec((pl.squeezed, C, dim), lambda r, h: (h, r, 0))
    return pl.pallas_call(
        functools.partial(row_forward_kernel, dim**-0.5),
        grid=(tokens // C, half),
        in_specs=[by_head] * 3,
        out_specs=pl.BlockSpec((C, dim), lambda r, h: (r, h)),
        out_shape=jax.ShapeDtypeStruct((tokens, half * dim), BF16),
        compiler_params=params(60),
        cost_estimate=pl.CostEstimate(
            flops=4 * tokens * C * half * dim, bytes_accessed=8 * tokens * half * dim, transcendentals=tokens * C * half
        ),
        name="row_forward",
    )(q, k, v)


def row_backward_kernel(scale, q_ref, k_ref, v_ref, g_ref, dq_ref, dk_ref, dv_ref, k_sum, v_sum):
    k_sum[...] = jnp.zeros_like(k_sum)
    v_sum[...] = jnp.zeros_like(v_sum)
    for start, step in row_blocks(q_ref.shape[0]):
        stop = start + step
        q, k, grad = q_ref[start:stop], k_ref[:stop], g_ref[start:stop]
        probs = row_probs(q, k, start, step, scale)
        prob_grad = dot(grad, v_ref[:stop], ((1,), (1,)))
        inner = jnp.sum(probs * prob_grad, axis=-1, keepdims=True)
        score_low = (probs * (prob_grad - inner)).astype(BF16)
        dq_ref[start:stop] = (dot(score_low, k, ((1,), (0,))) * scale).astype(BF16)
        k_sum[:stop] += dot(score_low, q, ((0,), (0,)))
        v_sum[:stop] += dot(probs.astype(BF16), grad, ((0,), (0,)))
    dk_ref[...] = (k_sum[...] * scale).astype(BF16)
    dv_ref[...] = v_sum[...].astype(BF16)


def row_backward(q, k, v, grad):
    half, tokens, dim = q.shape
    by_head = pl.BlockSpec((pl.squeezed, C, dim), lambda r, h: (h, r, 0))
    return pl.pallas_call(
        functools.partial(row_backward_kernel, dim**-0.5),
        grid=(tokens // C, half),
        in_specs=[by_head] * 3 + [pl.BlockSpec((C, dim), lambda r, h: (r, h))],
        out_specs=[by_head] * 3,
        out_shape=[jax.ShapeDtypeStruct(q.shape, BF16)] * 3,
        scratch_shapes=[pltpu.VMEM((C, dim), F32)] * 2,
        compiler_params=params(60),
        cost_estimate=pl.CostEstimate(
            flops=10 * tokens * C * half * dim, bytes_accessed=14 * tokens * half * dim, transcendentals=tokens * C * half
        ),
        name="row_backward",
    )(q, k, v, grad)


def column_mask(size):
    def parts(axis):
        place = lax.broadcasted_iota(jnp.int32, (size, size), axis)
        return place // LANE, place % LANE

    row_q, column_q = parts(0)
    row_k, column_k = parts(1)
    return (column_q == column_k) & (row_q >= row_k)


def gathered(ref, index, at):
    n, rows = ref.shape[0], ref.shape[-3]
    return jnp.concatenate([ref[(d, *index, row, pl.ds(at, LANE))] for d in range(n) for row in range(rows)], axis=0)


def scattered(ref, index, at, value):
    n, rows = ref.shape[0], ref.shape[-3]
    for d in range(n):
        for row in range(rows):
            line = d * rows + row
            ref[(d, *index, row, pl.ds(at, LANE))] = value[line * LANE : (line + 1) * LANE]


def column_probs(bias, q, k, scale):
    return softmax(dot(q, k, ((1,), (1,))) * scale + bias[...])


def column_forward_kernel(scale, chunk_ref, out_ref, bias):
    half, width = chunk_ref.shape[2], chunk_ref.shape[4]
    bias[...] = jnp.where(column_mask(bias.shape[0]), 0.0, -jnp.inf)
    blocks = width // LANE

    @pl.loop(0, half * blocks)
    def _(step):
        head, at = step // blocks, pl.multiple_of(step % blocks * LANE, LANE)
        q, k, v = (gathered(chunk_ref, (array, head), at) for array in range(3))
        probs = column_probs(bias, q, k, scale)
        scattered(out_ref, (head,), at, dot(probs.astype(BF16), v, ((1,), (0,))).astype(BF16))


def column_forward(chunks):
    n, _, half, rows, width, dim = chunks.shape
    size = n * rows * LANE
    return pl.pallas_call(
        functools.partial(column_forward_kernel, dim**-0.5),
        in_specs=[VMEM],
        out_specs=VMEM,
        out_shape=jax.ShapeDtypeStruct((n, half, rows, width, dim), BF16),
        scratch_shapes=[pltpu.VMEM((size, size), F32)],
        compiler_params=params(24),
        cost_estimate=pl.CostEstimate(
            flops=4 * size * size * dim * half * width // LANE,
            bytes_accessed=8 * n * half * rows * width * dim,
            transcendentals=size * size * half * width // LANE,
        ),
        name="column_forward",
    )(chunks)


def column_backward_kernel(scale, chunk_ref, grad_ref, out_ref, bias):
    half, width = chunk_ref.shape[2], chunk_ref.shape[4]
    bias[...] = jnp.where(column_mask(bias.shape[0]), 0.0, -jnp.inf)
    blocks = width // LANE

    @pl.loop(0, half * blocks)
    def _(step):
        head, at = step // blocks, pl.multiple_of(step % blocks * LANE, LANE)
        q, k, v = (gathered(chunk_ref, (array, head), at) for array in range(3))
        grad = gathered(grad_ref, (head,), at)
        probs = column_probs(bias, q, k, scale)
        prob_grad = dot(grad, v, ((1,), (1,)))
        inner = jnp.sum(probs * prob_grad, axis=-1, keepdims=True)
        score_low = (probs * (prob_grad - inner)).astype(BF16)
        scattered(out_ref, (0, head), at, (dot(score_low, k, ((1,), (0,))) * scale).astype(BF16))
        scattered(out_ref, (1, head), at, (dot(score_low, q, ((0,), (0,))) * scale).astype(BF16))
        scattered(out_ref, (2, head), at, dot(probs.astype(BF16), grad, ((0,), (0,))).astype(BF16))


def column_backward(chunks, grads):
    n, _, half, rows, width, dim = chunks.shape
    size = n * rows * LANE
    return pl.pallas_call(
        functools.partial(column_backward_kernel, dim**-0.5),
        in_specs=[VMEM] * 2,
        out_specs=VMEM,
        out_shape=jax.ShapeDtypeStruct(chunks.shape, BF16),
        scratch_shapes=[pltpu.VMEM((size, size), F32)],
        compiler_params=params(24),
        cost_estimate=pl.CostEstimate(
            flops=10 * size * size * dim * half * width // LANE,
            bytes_accessed=14 * n * half * rows * width * dim,
            transcendentals=size * size * half * width // LANE,
        ),
        name="column_backward",
    )(chunks, grads)


PAIRS = [(0, 1), (1, 0), (2, 3), (3, 2)]
INWARD = [(0, 1), (3, 2)]
CROSS = [(1, 2), (2, 1)]
OUTWARD = [(1, 0), (2, 3)]


def after(value, *done):
    return lax.optimization_barrier((value, *done))[0]


class Links:
    def __init__(self, n, window):
        self.n, self.inner, self.window, self.sent = n, n // 4, window, []

    def send(self, value, pairs):
        over = len(self.sent) - self.window + 1
        if over > 0:
            value = after(value, *self.sent[max(0, over - self.window) : over])
        out = lax.ppermute(value, "ctx", pairs)
        self.sent.append(out)
        return out

    def along(self, value, pairs):
        return self.send(value, [(a * self.inner + y, b * self.inner + y) for a, b in pairs for y in range(self.inner)])

    def flip(self, value, d):
        return self.send(value, [(place, place ^ d) for place in range(self.n)])


def swap(chunks):
    return lax.all_to_all(chunks, "ctx", split_axis=0, concat_axis=0, tiled=True)


class LayerSum:
    def __init__(self, ids, flat, blocks, heads_n):
        self.ids, self.flat, self.blocks, self.heads_n = ids, flat, blocks, heads_n
        self.mine = lax.axis_index("head").astype(jnp.int32)
        self.per = len(blocks) // heads_n
        self.even = list(range(0, heads_n, 2))

    def part(self, offsets, extra, first):
        wanted = [(self.mine ^ g) * self.per + b for g in offsets for b in range(self.per)]
        wanted = jnp.stack(wanted).astype(jnp.int32)
        return layer_part(self.ids, self.flat, self.blocks, wanted, extra, first)

    def move(self, part, g):
        return lax.ppermute(part, "head", [(place, place ^ g) for place in range(self.heads_n)])

    def start(self):
        self.first = self.part([g + 1 for g in self.even], [], [])
        self.near = self.move(self.first, 1)

    def turn(self, done):
        self.flat = after(self.flat, done)
        self.far = [self.move(self.part([g], [self.near], [g // 2 * self.per]), g) for g in self.even[1:]]

    def finish(self):
        return self.part([0], [self.near] + self.far, [0] * (1 + len(self.far)))


def on_device(queries, keys, values, out_grad, wo, *, n, heads_n):
    tokens, heads, dim = queries.shape
    half, depth, inner = heads // 2, wo.shape[1], n // 4
    me = lax.axis_index("ctx").astype(jnp.int32)
    line, spot = me // inner, me % inner
    middle, upper = (line == 1) | (line == 2), line < 2
    far, close = [jnp.where(upper, 2, 1), jnp.where(upper, 3, 0)], [line ^ 1, line]
    links = Links(n, 5)

    def around(block):
        return [block if e == 0 else links.flip(block, e) for e in range(inner)]

    def targets(owners, e):
        return jnp.stack([owner * inner + (spot ^ e) for owner in owners]).astype(jnp.int32)

    def leaving(flat, owners):
        return [proj_part(targets(owners, e), flat, out_grad, [], depth, dim, 0)[0] for e in range(1, inner)]

    def exchanged(parts):
        return [links.flip(part, e + 1) for e, part in enumerate(parts)]

    def summed(flat, owners, theirs, lead):
        return proj_part(targets(owners, 0), flat, out_grad, theirs, depth, dim, lead)

    def add(*terms):
        return sum(term.astype(F32) for term in terms).astype(BF16)

    everyone = [line ^ 1, *far, line]
    near = links.along(wo, PAIRS)
    cross_own = links.along(wo, CROSS)
    own_blocks = around(wo)
    chunks, by_head = split_inputs(queries, keys, values, n)
    row_out = row_forward(*by_head)
    row_theirs = leaving(row_out, everyone)
    near = after(near, chunks)
    near_blocks = around(near)
    cross_near = links.along(near, CROSS)
    out_own = links.along(cross_own, OUTWARD)
    chunks = swap(after(chunks, *near_blocks, cross_near, out_own, *row_theirs))
    far_own = jnp.where(middle, cross_own, out_own)
    far_own_blocks = around(far_own)
    far_near = jnp.where(middle, cross_near, links.along(cross_near, OUTWARD))
    far_near_blocks = around(far_near)
    blocks = own_blocks + near_blocks + far_own_blocks + far_near_blocks
    ids = [owner * inner + (spot ^ e) for owner in (line, line ^ 1, *far) for e in range(inner)]
    ids = jnp.stack(ids).astype(jnp.int32)

    row_theirs = exchanged(row_theirs)
    outs = column_forward(after(chunks, *far_own_blocks))
    column_part = swap(outs)
    grad_row, grads = attn_grad(ids, after(out_grad, outs), blocks, dim)
    grads = swap(after(grads, column_part, *row_theirs))
    column_out, flat = collect(row_out, column_part)
    column_far, column_close = leaving(column_out, far), leaving(column_out, close)
    layer = LayerSum(ids, flat, blocks, heads_n)
    layer.start()
    gradients = column_backward(chunks, after(grads, *column_far, *column_close, layer.first))
    column_far, column_close = exchanged(column_far), exchanged(column_close)
    column_grads = swap(gradients)

    row_lead, row_own = summed(after(row_out, gradients), everyone, row_theirs, 3)
    row_in = links.along(row_lead, INWARD)
    layer.turn(gradients)
    (column_far,) = summed(after(column_out, gradients), far, column_far, 0)
    column_far_in = links.along(column_far, INWARD)
    row_grads = row_backward(*by_head, after(grad_row, column_far))
    column_near, column_own = summed(after(column_out, gradients), close, column_close, 1)
    row_cross = links.along(add(row_lead[1:], row_in[1:]), CROSS)
    column_cross = links.along(add(column_far, after(column_far_in, row_grads[0])), CROSS)
    column_near_in = links.along(column_near[0], INWARD)
    row_back = links.along(add(row_lead[0], row_cross[1]), OUTWARD)
    column_back = links.along(add(column_near[0], column_cross[1]), OUTWARD)

    gradients = join_gradients(column_grads, row_grads)
    proj_row = add(row_own[0], row_in[0], row_cross[0], row_back)
    proj_column = add(column_own[0], column_near_in, column_cross[0], column_back)
    shape = (half, dim, depth)
    proj_grad = jnp.stack([proj_row.reshape(shape), proj_column.reshape(shape)], axis=1)
    return (layer.finish(), *gradients, proj_grad.reshape(heads * dim, depth))


def solution(mesh):
    in_specs = (
        P("ctx", "head", None),
        P("ctx", "head", None),
        P("ctx", "head", None),
        P("ctx", None),
        P("head", "ctx"),
    )
    out_specs = (
        P("ctx", "head"),
        P("ctx", "head", None),
        P("ctx", "head", None),
        P("ctx", "head", None),
        P("head", "ctx"),
    )
    return jax.shard_map(
        functools.partial(on_device, n=mesh.shape["ctx"], heads_n=mesh.shape["head"]),
        mesh=mesh,
        in_specs=in_specs,
        out_specs=out_specs,
        check_vma=False,
    )
```

```python
import functools

import jax
import jax.numpy as jnp
from jax import lax
from jax.experimental import pallas as pl
from jax.experimental.pallas import tpu as pltpu
from jax.sharding import PartitionSpec as P

C = 512
LANE = 16
VMEM = pl.BlockSpec(memory_space=pltpu.VMEM)
BF16 = jnp.bfloat16
F32 = jnp.float32


def params(mib):
    return pltpu.CompilerParams(vmem_limit_bytes=mib * 1024 * 1024)


def dot(a, b, dims):
    return lax.dot_general(a, b, (dims, ((), ())), preferred_element_type=F32)


def softmax(scores):
    highest = jnp.max(scores, axis=-1, keepdims=True)
    lifted = jnp.exp(scores - highest)
    return lifted * (1.0 / jnp.sum(lifted, axis=-1, keepdims=True))


def split_kernel(q_ref, k_ref, v_ref, chunk_ref, *rest):
    row_refs, wide = rest[:3], rest[3]
    n, width = chunk_ref.shape[0], chunk_ref.shape[3]
    span, heads, dim = q_ref.shape
    for array, ref in enumerate((q_ref, k_ref, v_ref)):
        wide[...] = ref[...].astype(F32).reshape(span * heads, dim)
        for head in range(heads // 2):
            row_refs[array][head] = wide[pl.ds(2 * head, span, stride=heads), :].astype(BF16)
            for d in range(n):
                odd = wide[pl.ds(d * width * heads + 2 * head + 1, width, stride=heads), :]
                chunk_ref[d, array, head] = odd.astype(BF16)


def split_inputs(queries, keys, values, n):
    tokens, heads, dim = queries.shape
    rows, width, half = tokens // C, C // n, heads // 2
    by_head = jax.ShapeDtypeStruct((half, tokens, dim), BF16)
    out = pl.pallas_call(
        split_kernel,
        grid=(rows,),
        in_specs=[pl.BlockSpec((C, heads, dim), lambda r: (r, 0, 0))] * 3,
        out_specs=[pl.BlockSpec((n, 3, half, pl.squeezed, width, dim), lambda r: (0, 0, 0, r, 0, 0))]
        + [pl.BlockSpec((half, C, dim), lambda r: (0, r, 0))] * 3,
        scratch_shapes=[pltpu.VMEM((C * heads, dim), F32)],
        out_shape=[jax.ShapeDtypeStruct((n, 3, half, rows, width, dim), BF16)] + [by_head] * 3,
        compiler_params=params(60),
        name="split_inputs",
    )(queries, keys, values)
    return out[0], out[1:]


def join_kernel(chunk_ref, *refs):
    row_refs, outs, wide = refs[:3], refs[3:6], refs[6]
    n, width = chunk_ref.shape[0], chunk_ref.shape[3]
    span, heads, dim = outs[0].shape
    for array in range(3):
        for head in range(heads // 2):
            wide[pl.ds(2 * head, span, stride=heads), :] = row_refs[array][head].astype(F32)
            for d in range(n):
                part = chunk_ref[d, array, head].astype(F32)
                wide[pl.ds(d * width * heads + 2 * head + 1, width, stride=heads), :] = part
        outs[array][...] = wide[...].reshape(span, heads, dim).astype(BF16)


def join_gradients(chunks, by_head):
    n, _, half, rows, width, dim = chunks.shape
    tokens, heads = by_head[0].shape[1], 2 * half
    return pl.pallas_call(
        join_kernel,
        grid=(rows,),
        in_specs=[pl.BlockSpec((n, 3, half, pl.squeezed, width, dim), lambda r: (0, 0, 0, r, 0, 0))]
        + [pl.BlockSpec((half, C, dim), lambda r: (0, r, 0))] * 3,
        out_specs=[pl.BlockSpec((C, heads, dim), lambda r: (r, 0, 0))] * 3,
        scratch_shapes=[pltpu.VMEM((C * heads, dim), F32)],
        out_shape=[jax.ShapeDtypeStruct((tokens, heads, dim), BF16)] * 3,
        compiler_params=params(60),
        name="join_gradients",
    )(chunks, *by_head)


def collect_kernel(row_ref, chunk_ref, flat_ref, both_ref):
    n, half, rows, width, dim = chunk_ref.shape
    for head in range(half):
        both_ref[:, 2 * head * dim : (2 * head + 1) * dim] = row_ref[:, head * dim : (head + 1) * dim]
        for d in range(n):
            for row in range(rows):
                part = chunk_ref[d, head, row]
                at = row * C + d * width
                flat_ref[at : at + width, head * dim : (head + 1) * dim] = part
                both_ref[at : at + width, (2 * head + 1) * dim : (2 * head + 2) * dim] = part


def collect(row_out, chunks):
    n, half, rows, width, dim = chunks.shape
    return pl.pallas_call(
        collect_kernel,
        in_specs=[VMEM] * 2,
        out_specs=[VMEM] * 2,
        out_shape=[
            jax.ShapeDtypeStruct((rows * C, half * dim), BF16),
            jax.ShapeDtypeStruct((rows * C, 2 * half * dim), BF16),
        ],
        compiler_params=params(24),
        name="collect",
    )(row_out, chunks)


def attn_grad_kernel(n, dim, ids, grad_ref, *refs):
    blocks, (row_ref, chunk_ref, weight, total, sem) = refs[:n], refs[n:]
    step = pl.program_id(0)
    _, half, rows, width, _ = chunk_ref.shape
    tokens = grad_ref.shape[0]
    tile = tokens // 4

    @pl.when(step == 0)
    def _():
        for d in range(n):
            pltpu.make_async_copy(blocks[d], weight.at[ids[d]], sem.at[ids[d]]).start()
        total[...] = jnp.zeros_like(total)

    pltpu.make_async_copy(blocks[0], weight.at[step], sem.at[step]).wait()

    @pl.loop(0, tokens, step=tile)
    def _(at):
        at = pl.multiple_of(at, tile)
        total[pl.ds(at, tile)] += dot(grad_ref[pl.ds(at, tile)], weight[step], ((1,), (1,)))

    @pl.when(step == n - 1)
    def _():
        for head in range(half):
            row_ref[:, head * dim : (head + 1) * dim] = total[:, 2 * head * dim : (2 * head + 1) * dim].astype(BF16)
            for d in range(n):
                for row in range(rows):
                    at = row * C + d * width
                    part = total[at : at + width, (2 * head + 1) * dim : (2 * head + 2) * dim]
                    chunk_ref[d, head, row] = part.astype(BF16)


def attn_grad(ids, out_grad, blocks, dim):
    n, (span, depth) = len(blocks), blocks[0].shape
    tokens, half = out_grad.shape[0], span // dim // 2
    chunk = jax.ShapeDtypeStruct((n, half, tokens // C, C // n, dim), BF16)
    return pl.pallas_call(
        functools.partial(attn_grad_kernel, n, dim),
        grid_spec=pltpu.PrefetchScalarGridSpec(
            num_scalar_prefetch=1,
            grid=(n,),
            in_specs=[pl.BlockSpec((tokens, depth), lambda b, ids: (0, b))] + [pl.BlockSpec(memory_space=pl.ANY)] * n,
            out_specs=[
                pl.BlockSpec((tokens, half * dim), lambda b, ids: (0, 0)),
                pl.BlockSpec(chunk.shape, lambda b, ids: (0, 0, 0, 0, 0)),
            ],
            scratch_shapes=[
                pltpu.VMEM((n, span, depth), BF16),
                pltpu.VMEM((tokens, span), F32),
                pltpu.SemaphoreType.DMA((n,)),
            ],
        ),
        out_shape=[jax.ShapeDtypeStruct((tokens, half * dim), BF16), chunk],
        compiler_params=params(60),
        cost_estimate=pl.CostEstimate(
            flops=2 * tokens * span * depth * n,
            bytes_accessed=2 * n * depth * (tokens + span) + 2 * tokens * span,
            transcendentals=0,
        ),
        name="attn_grad",
    )(ids, out_grad, *blocks)


def layer_kernel(n, count, adds, ids, wanted, flat_ref, *refs):
    blocks, extra, out_ref = refs[:n], refs[n : n + adds], refs[n + adds]
    weight, sem = refs[n + adds + 1 :]
    step = pl.program_id(0)
    tokens = flat_ref.shape[0]
    tile = tokens // 4

    @pl.when(step == 0)
    def _():
        for s in range(count):
            for d in range(n):

                @pl.when(ids[d] == wanted[s])
                def _():
                    pltpu.make_async_copy(blocks[d], weight.at[s], sem.at[s]).start()

    pltpu.make_async_copy(blocks[0], weight.at[step], sem.at[step]).wait()

    @pl.loop(0, tokens, step=tile)
    def _(at):
        at = pl.multiple_of(at, tile)
        value = dot(flat_ref[pl.ds(at, tile)], weight[step], ((1,), (0,)))
        for ref in extra:
            value = value + ref[pl.ds(at, tile)].astype(F32)
        out_ref[pl.ds(at, tile)] = value.astype(BF16)


def layer_part(ids, flat, blocks, wanted, extra, first):
    n, (span, depth) = len(blocks), blocks[0].shape
    tokens, count = flat.shape[0], wanted.shape[0]
    by_column = pl.BlockSpec((tokens, depth), lambda s, ids, wanted: (0, s))
    return pl.pallas_call(
        functools.partial(layer_kernel, n, count, len(extra)),
        grid_spec=pltpu.PrefetchScalarGridSpec(
            num_scalar_prefetch=2,
            grid=(count,),
            in_specs=[pl.BlockSpec((tokens, span), lambda s, ids, wanted: (0, 0))]
            + [pl.BlockSpec(memory_space=pl.ANY)] * n
            + [pl.BlockSpec((tokens, depth), functools.partial(lambda f, s, ids, wanted: (0, s + f), f)) for f in first],
            out_specs=by_column,
            scratch_shapes=[pltpu.VMEM((count, span, depth), BF16), pltpu.SemaphoreType.DMA((count,))],
        ),
        out_shape=jax.ShapeDtypeStruct((tokens, count * depth), BF16),
        compiler_params=params(60),
        cost_estimate=pl.CostEstimate(
            flops=2 * tokens * span * depth * count,
            bytes_accessed=2 * (count * depth * (tokens + span) + tokens * span),
            transcendentals=0,
        ),
        name="layer_part",
    )(ids, wanted, flat, *blocks, *extra)


def proj_kernel(lead, adds, dim, order, flat_ref, grad_ref, *refs):
    extra, outs, turned = refs[:adds], refs[adds:-1], refs[-1]
    step = pl.program_id(0)
    span = flat_ref.shape[1]

    @pl.when(step == 0)
    def _():
        for at in range(0, span, dim):
            turned[at : at + dim] = flat_ref[:, at : at + dim].T

    def value(at):
        out = dot(turned[at : at + dim], grad_ref[...], ((1,), (0,)))
        for ref in extra:
            out = out + ref[at : at + dim].astype(F32)
        return out.astype(BF16)

    @pl.when(step < lead)
    def _():
        for at in range(0, span, dim):
            outs[0][at : at + dim] = value(at)

    @pl.when(step >= lead)
    def _():
        for at in range(0, span, dim):
            outs[-1][at : at + dim] = value(at)


def proj_part(order, flat, out_grad, extra, depth, dim, lead):
    tokens, span = flat.shape
    count = order.shape[0]
    sizes = [size for size in (lead, count - lead) if size]
    places = [lambda s, order: (jnp.minimum(s, lead - 1), 0, 0), lambda s, order: (jnp.maximum(s - lead, 0), 0, 0)]
    return pl.pallas_call(
        functools.partial(proj_kernel, lead, len(extra), dim),
        grid_spec=pltpu.PrefetchScalarGridSpec(
            num_scalar_prefetch=1,
            grid=(count,),
            in_specs=[
                pl.BlockSpec((tokens, span), lambda s, order: (0, 0)),
                pl.BlockSpec((tokens, depth), lambda s, order: (0, order[s])),
            ]
            + [pl.BlockSpec((pl.squeezed, span, depth), lambda s, order: (s, 0, 0))] * len(extra),
            out_specs=[pl.BlockSpec((pl.squeezed, span, depth), place) for place in places[-len(sizes) :]],
            scratch_shapes=[pltpu.VMEM((span, tokens), BF16)],
        ),
        out_shape=[jax.ShapeDtypeStruct((size, span, depth), BF16) for size in sizes],
        compiler_params=params(60),
        cost_estimate=pl.CostEstimate(
            flops=2 * tokens * span * depth * count,
            bytes_accessed=2 * (count * depth * (tokens + span * (1 + len(extra))) + tokens * span),
            transcendentals=0,
        ),
        name="proj_part",
    )(order, flat, out_grad, *extra)


def row_blocks(length):
    step = length // 2
    return [(start, step) for start in range(0, length, step)]


def row_probs(q, k, start, step, scale):
    scores = dot(q, k, ((1,), (1,))) * scale
    place = lax.broadcasted_iota(jnp.int32, scores.shape, 0) + start
    seen = lax.broadcasted_iota(jnp.int32, scores.shape, 1)
    return softmax(jnp.where(place >= seen, scores, -jnp.inf))


def row_forward_kernel(scale, q_ref, k_ref, v_ref, o_ref):
    for start, step in row_blocks(q_ref.shape[0]):
        stop = start + step
        probs = row_probs(q_ref[start:stop], k_ref[:stop], start, step, scale)
        o_ref[start:stop] = dot(probs.astype(BF16), v_ref[:stop], ((1,), (0,))).astype(BF16)


def row_forward(q, k, v):
    half, tokens, dim = q.shape
    by_head = pl.BlockSpec((pl.squeezed, C, dim), lambda r, h: (h, r, 0))
    return pl.pallas_call(
        functools.partial(row_forward_kernel, dim**-0.5),
        grid=(tokens // C, half),
        in_specs=[by_head] * 3,
        out_specs=pl.BlockSpec((C, dim), lambda r, h: (r, h)),
        out_shape=jax.ShapeDtypeStruct((tokens, half * dim), BF16),
        compiler_params=params(60),
        cost_estimate=pl.CostEstimate(
            flops=4 * tokens * C * half * dim, bytes_accessed=8 * tokens * half * dim, transcendentals=tokens * C * half
        ),
        name="row_forward",
    )(q, k, v)


def row_backward_kernel(scale, q_ref, k_ref, v_ref, g_ref, dq_ref, dk_ref, dv_ref, k_sum, v_sum):
    k_sum[...] = jnp.zeros_like(k_sum)
    v_sum[...] = jnp.zeros_like(v_sum)
    for start, step in row_blocks(q_ref.shape[0]):
        stop = start + step
        q, k, grad = q_ref[start:stop], k_ref[:stop], g_ref[start:stop]
        probs = row_probs(q, k, start, step, scale)
        prob_grad = dot(grad, v_ref[:stop], ((1,), (1,)))
        inner = jnp.sum(probs * prob_grad, axis=-1, keepdims=True)
        score_low = (probs * (prob_grad - inner)).astype(BF16)
        dq_ref[start:stop] = (dot(score_low, k, ((1,), (0,))) * scale).astype(BF16)
        k_sum[:stop] += dot(score_low, q, ((0,), (0,)))
        v_sum[:stop] += dot(probs.astype(BF16), grad, ((0,), (0,)))
    dk_ref[...] = (k_sum[...] * scale).astype(BF16)
    dv_ref[...] = v_sum[...].astype(BF16)


def row_backward(q, k, v, grad):
    half, tokens, dim = q.shape
    by_head = pl.BlockSpec((pl.squeezed, C, dim), lambda r, h: (h, r, 0))
    return pl.pallas_call(
        functools.partial(row_backward_kernel, dim**-0.5),
        grid=(tokens // C, half),
        in_specs=[by_head] * 3 + [pl.BlockSpec((C, dim), lambda r, h: (r, h))],
        out_specs=[by_head] * 3,
        out_shape=[jax.ShapeDtypeStruct(q.shape, BF16)] * 3,
        scratch_shapes=[pltpu.VMEM((C, dim), F32)] * 2,
        compiler_params=params(60),
        cost_estimate=pl.CostEstimate(
            flops=10 * tokens * C * half * dim, bytes_accessed=14 * tokens * half * dim, transcendentals=tokens * C * half
        ),
        name="row_backward",
    )(q, k, v, grad)


def column_mask(size):
    def parts(axis):
        place = lax.broadcasted_iota(jnp.int32, (size, size), axis)
        return place // LANE, place % LANE

    row_q, column_q = parts(0)
    row_k, column_k = parts(1)
    return (column_q == column_k) & (row_q >= row_k)


def gathered(ref, index, at):
    n, rows = ref.shape[0], ref.shape[-3]
    return jnp.concatenate([ref[(d, *index, row, pl.ds(at, LANE))] for d in range(n) for row in range(rows)], axis=0)


def scattered(ref, index, at, value):
    n, rows = ref.shape[0], ref.shape[-3]
    for d in range(n):
        for row in range(rows):
            line = d * rows + row
            ref[(d, *index, row, pl.ds(at, LANE))] = value[line * LANE : (line + 1) * LANE]


def column_probs(bias, q, k, scale):
    return softmax(dot(q, k, ((1,), (1,))) * scale + bias[...])


def column_forward_kernel(scale, chunk_ref, out_ref, bias):
    half, width = chunk_ref.shape[2], chunk_ref.shape[4]
    bias[...] = jnp.where(column_mask(bias.shape[0]), 0.0, -jnp.inf)
    blocks = width // LANE

    @pl.loop(0, half * blocks)
    def _(step):
        head, at = step // blocks, pl.multiple_of(step % blocks * LANE, LANE)
        q, k, v = (gathered(chunk_ref, (array, head), at) for array in range(3))
        probs = column_probs(bias, q, k, scale)
        scattered(out_ref, (head,), at, dot(probs.astype(BF16), v, ((1,), (0,))).astype(BF16))


def column_forward(chunks):
    n, _, half, rows, width, dim = chunks.shape
    size = n * rows * LANE
    return pl.pallas_call(
        functools.partial(column_forward_kernel, dim**-0.5),
        in_specs=[VMEM],
        out_specs=VMEM,
        out_shape=jax.ShapeDtypeStruct((n, half, rows, width, dim), BF16),
        scratch_shapes=[pltpu.VMEM((size, size), F32)],
        compiler_params=params(24),
        cost_estimate=pl.CostEstimate(
            flops=4 * size * size * dim * half * width // LANE,
            bytes_accessed=8 * n * half * rows * width * dim,
            transcendentals=size * size * half * width // LANE,
        ),
        name="column_forward",
    )(chunks)


def column_backward_kernel(scale, chunk_ref, grad_ref, out_ref, bias):
    half, width = chunk_ref.shape[2], chunk_ref.shape[4]
    bias[...] = jnp.where(column_mask(bias.shape[0]), 0.0, -jnp.inf)
    blocks = width // LANE

    @pl.loop(0, half * blocks)
    def _(step):
        head, at = step // blocks, pl.multiple_of(step % blocks * LANE, LANE)
        q, k, v = (gathered(chunk_ref, (array, head), at) for array in range(3))
        grad = gathered(grad_ref, (head,), at)
        probs = column_probs(bias, q, k, scale)
        prob_grad = dot(grad, v, ((1,), (1,)))
        inner = jnp.sum(probs * prob_grad, axis=-1, keepdims=True)
        score_low = (probs * (prob_grad - inner)).astype(BF16)
        scattered(out_ref, (0, head), at, (dot(score_low, k, ((1,), (0,))) * scale).astype(BF16))
        scattered(out_ref, (1, head), at, (dot(score_low, q, ((0,), (0,))) * scale).astype(BF16))
        scattered(out_ref, (2, head), at, dot(probs.astype(BF16), grad, ((0,), (0,))).astype(BF16))


def column_backward(chunks, grads):
    n, _, half, rows, width, dim = chunks.shape
    size = n * rows * LANE
    return pl.pallas_call(
        functools.partial(column_backward_kernel, dim**-0.5),
        in_specs=[VMEM] * 2,
        out_specs=VMEM,
        out_shape=jax.ShapeDtypeStruct(chunks.shape, BF16),
        scratch_shapes=[pltpu.VMEM((size, size), F32)],
        compiler_params=params(24),
        cost_estimate=pl.CostEstimate(
            flops=10 * size * size * dim * half * width // LANE,
            bytes_accessed=14 * n * half * rows * width * dim,
            transcendentals=size * size * half * width // LANE,
        ),
        name="column_backward",
    )(chunks, grads)


PAIRS = [(0, 1), (1, 0), (2, 3), (3, 2)]
INWARD = [(0, 1), (3, 2)]
CROSS = [(1, 2), (2, 1)]
OUTWARD = [(1, 0), (2, 3)]


def after(value, *done):
    return lax.optimization_barrier((value, *done))[0]


class Links:
    def __init__(self, n, window):
        self.n, self.inner, self.window, self.sent = n, n // 4, window, []

    def send(self, value, pairs):
        over = len(self.sent) - self.window + 1
        if over > 0:
            value = after(value, *self.sent[max(0, over - self.window) : over])
        out = lax.ppermute(value, "ctx", pairs)
        self.sent.append(out)
        return out

    def along(self, value, pairs):
        return self.send(value, [(a * self.inner + y, b * self.inner + y) for a, b in pairs for y in range(self.inner)])

    def flip(self, value, d):
        return self.send(value, [(place, place ^ d) for place in range(self.n)])


def swap(chunks):
    return lax.all_to_all(chunks, "ctx", split_axis=0, concat_axis=0, tiled=True)


class LayerSum:
    def __init__(self, ids, flat, blocks, heads_n):
        self.ids, self.flat, self.blocks, self.heads_n = ids, flat, blocks, heads_n
        self.mine = lax.axis_index("head").astype(jnp.int32)
        self.per = len(blocks) // heads_n
        self.even = list(range(0, heads_n, 2))

    def part(self, offsets, extra, first):
        wanted = [(self.mine ^ g) * self.per + b for g in offsets for b in range(self.per)]
        wanted = jnp.stack(wanted).astype(jnp.int32)
        return layer_part(self.ids, self.flat, self.blocks, wanted, extra, first)

    def move(self, part, g):
        return lax.ppermute(part, "head", [(place, place ^ g) for place in range(self.heads_n)])

    def start(self):
        self.first = self.part([g + 1 for g in self.even], [], [])
        self.near = self.move(self.first, 1)

    def turn(self, done):
        self.flat = after(self.flat, done)
        self.parts = [self.part([g], [self.near], [g // 2 * self.per]) for g in self.even[1:]]
        self.far = [self.move(part, g) for part, g in zip(self.parts, self.even[1:])]

    def finish(self):
        return self.part([0], [self.near] + self.far, [0] * (1 + len(self.far)))


def on_device(queries, keys, values, out_grad, wo, *, n, heads_n):
    tokens, heads, dim = queries.shape
    half, depth, inner = heads // 2, wo.shape[1], n // 4
    me = lax.axis_index("ctx").astype(jnp.int32)
    line, spot = me // inner, me % inner
    middle, upper = (line == 1) | (line == 2), line < 2
    far, close = [jnp.where(upper, 2, 1), jnp.where(upper, 3, 0)], [line ^ 1, line]
    links = Links(n, 5)

    def around(block):
        return [block if e == 0 else links.flip(block, e) for e in range(inner)]

    def targets(owners, e):
        return jnp.stack([owner * inner + (spot ^ e) for owner in owners]).astype(jnp.int32)

    def leaving(flat, owners):
        return [proj_part(targets(owners, e), flat, out_grad, [], depth, dim, 0)[0] for e in range(1, inner)]

    def exchanged(parts):
        return [links.flip(part, e + 1) for e, part in enumerate(parts)]

    def summed(flat, owners, theirs, lead):
        return proj_part(targets(owners, 0), flat, out_grad, theirs, depth, dim, lead)

    def add(*terms):
        return sum(term.astype(F32) for term in terms).astype(BF16)

    near = links.along(wo, PAIRS)
    cross_own = links.along(wo, CROSS)
    own_blocks = around(wo)
    chunks, by_head = split_inputs(queries, keys, values, n)
    row_out = row_forward(*by_head)
    row_far, row_close = leaving(row_out, far), leaving(row_out, close)
    near = after(near, chunks, *own_blocks[1:])
    near_blocks = around(near)
    cross_near = links.along(near, CROSS)
    out_own = links.along(cross_own, OUTWARD)
    chunks = swap(after(chunks, *near_blocks, cross_near, out_own, *row_far, *row_close))
    out_near = links.along(cross_near, OUTWARD)
    far_own = jnp.where(middle, cross_own, out_own)
    far_own_blocks = around(far_own)
    far_near = jnp.where(middle, cross_near, out_near)
    far_near_blocks = around(far_near)
    blocks = own_blocks + near_blocks + far_own_blocks + far_near_blocks
    ids = [owner * inner + (spot ^ e) for owner in (line, line ^ 1, *far) for e in range(inner)]
    ids = jnp.stack(ids).astype(jnp.int32)

    outs = column_forward(after(chunks, *far_own_blocks))
    column_part = swap(outs)
    grad_row, grads = attn_grad(ids, after(out_grad, outs), blocks, dim)
    row_far = exchanged([after(part, *far_near_blocks) for part in row_far])
    row_close = exchanged(row_close)
    grads = swap(after(grads, column_part, *row_far))
    (row_far,) = summed(after(row_out, outs), far, row_far, 0)
    row_far_in = links.along(row_far, INWARD)
    column_out, flat = collect(row_out, column_part)
    column_far, column_close = leaving(column_out, far), leaving(column_out, close)
    column_far = exchanged(column_far)
    layer = LayerSum(ids, flat, blocks, heads_n)
    layer.start()
    gradients = column_backward(chunks, after(grads, *column_close, row_far, layer.first))
    column_grads = swap(after(gradients, *column_far, row_far_in, *row_close))

    column_close = exchanged(column_close)
    row_cross = links.along(add(row_far, row_far_in), CROSS)
    row_near, row_own = summed(after(row_out, gradients), close, row_close, 1)
    row_near_in = links.along(row_near[0], INWARD)
    (column_far,) = summed(after(column_out, gradients), far, column_far, 0)
    column_far_in = links.along(column_far, INWARD)
    layer.turn(gradients)
    row_grads = row_backward(*by_head, after(grad_row, column_far))
    column_near, column_own = summed(after(column_out, *layer.parts), close, column_close, 1)
    column_near_in = links.along(column_near[0], INWARD)
    column_cross = links.along(add(column_far, after(column_far_in, row_grads[0])), CROSS)
    row_back = links.along(add(row_near[0], row_cross[1]), OUTWARD)
    column_back = links.along(add(column_near[0], column_cross[1]), OUTWARD)

    gradients = join_gradients(column_grads, row_grads)
    proj_row = add(row_own[0], row_near_in, row_cross[0], row_back)
    proj_column = add(column_own[0], column_near_in, column_cross[0], column_back)
    shape = (half, dim, depth)
    proj_grad = jnp.stack([proj_row.reshape(shape), proj_column.reshape(shape)], axis=1)
    return (layer.finish(), *gradients, proj_grad.reshape(heads * dim, depth))


def solution(mesh):
    in_specs = (
        P("ctx", "head", None),
        P("ctx", "head", None),
        P("ctx", "head", None),
        P("ctx", None),
        P("head", "ctx"),
    )
    out_specs = (
        P("ctx", "head"),
        P("ctx", "head", None),
        P("ctx", "head", None),
        P("ctx", "head", None),
        P("head", "ctx"),
    )
    return jax.shard_map(
        functools.partial(on_device, n=mesh.shape["ctx"], heads_n=mesh.shape["head"]),
        mesh=mesh,
        in_specs=in_specs,
        out_specs=out_specs,
        check_vma=False,
    )
```

```python
import functools

import jax
import jax.numpy as jnp
from jax import lax
from jax.experimental import pallas as pl
from jax.experimental.pallas import tpu as pltpu
from jax.sharding import PartitionSpec as P

C = 512
LANE = 16
VMEM = pl.BlockSpec(memory_space=pltpu.VMEM)
BF16 = jnp.bfloat16
F32 = jnp.float32


def params(mib):
    return pltpu.CompilerParams(vmem_limit_bytes=mib * 1024 * 1024)


def dot(a, b, dims):
    return lax.dot_general(a, b, (dims, ((), ())), preferred_element_type=F32)


def softmax(scores):
    highest = jnp.max(scores, axis=-1, keepdims=True)
    lifted = jnp.exp(scores - highest)
    return lifted * (1.0 / jnp.sum(lifted, axis=-1, keepdims=True))


def split_kernel(q_ref, k_ref, v_ref, chunk_ref, *rest):
    row_refs, wide = rest[:3], rest[3]
    n, width = chunk_ref.shape[0], chunk_ref.shape[3]
    span, heads, dim = q_ref.shape
    for array, ref in enumerate((q_ref, k_ref, v_ref)):
        wide[...] = ref[...].astype(F32).reshape(span * heads, dim)
        for head in range(heads // 2):
            row_refs[array][head] = wide[pl.ds(2 * head, span, stride=heads), :].astype(BF16)
            for d in range(n):
                odd = wide[pl.ds(d * width * heads + 2 * head + 1, width, stride=heads), :]
                chunk_ref[d, array, head] = odd.astype(BF16)


def split_inputs(queries, keys, values, n):
    tokens, heads, dim = queries.shape
    rows, width, half = tokens // C, C // n, heads // 2
    by_head = jax.ShapeDtypeStruct((half, tokens, dim), BF16)
    out = pl.pallas_call(
        split_kernel,
        grid=(rows,),
        in_specs=[pl.BlockSpec((C, heads, dim), lambda r: (r, 0, 0))] * 3,
        out_specs=[pl.BlockSpec((n, 3, half, pl.squeezed, width, dim), lambda r: (0, 0, 0, r, 0, 0))]
        + [pl.BlockSpec((half, C, dim), lambda r: (0, r, 0))] * 3,
        scratch_shapes=[pltpu.VMEM((C * heads, dim), F32)],
        out_shape=[jax.ShapeDtypeStruct((n, 3, half, rows, width, dim), BF16)] + [by_head] * 3,
        compiler_params=params(60),
        name="split_inputs",
    )(queries, keys, values)
    return out[0], out[1:]


def join_kernel(query_ref, rest_ref, *refs):
    row_refs, outs, wide = refs[:3], refs[3:6], refs[6]
    n, width = query_ref.shape[0], query_ref.shape[3]
    span, heads, dim = outs[0].shape
    for array in range(3):
        for head in range(heads // 2):
            wide[pl.ds(2 * head, span, stride=heads), :] = row_refs[array][head].astype(F32)
            for d in range(n):
                part = (query_ref if array == 0 else rest_ref)[d, max(array - 1, 0), head].astype(F32)
                wide[pl.ds(d * width * heads + 2 * head + 1, width, stride=heads), :] = part
        outs[array][...] = wide[...].reshape(span, heads, dim).astype(BF16)


def join_gradients(chunks, by_head):
    n, _, half, rows, width, dim = chunks[0].shape
    tokens, heads = by_head[0].shape[1], 2 * half
    return pl.pallas_call(
        join_kernel,
        grid=(rows,),
        in_specs=[pl.BlockSpec((n, k, half, pl.squeezed, width, dim), lambda r: (0, 0, 0, r, 0, 0)) for k in (1, 2)]
        + [pl.BlockSpec((half, C, dim), lambda r: (0, r, 0))] * 3,
        out_specs=[pl.BlockSpec((C, heads, dim), lambda r: (r, 0, 0))] * 3,
        scratch_shapes=[pltpu.VMEM((C * heads, dim), F32)],
        out_shape=[jax.ShapeDtypeStruct((tokens, heads, dim), BF16)] * 3,
        compiler_params=params(60),
        name="join_gradients",
    )(*chunks, *by_head)


def collect_kernel(row_ref, chunk_ref, flat_ref, both_ref):
    n, half, rows, width, dim = chunk_ref.shape
    for head in range(half):
        both_ref[:, 2 * head * dim : (2 * head + 1) * dim] = row_ref[:, head * dim : (head + 1) * dim]
        for d in range(n):
            for row in range(rows):
                part = chunk_ref[d, head, row]
                at = row * C + d * width
                flat_ref[at : at + width, head * dim : (head + 1) * dim] = part
                both_ref[at : at + width, (2 * head + 1) * dim : (2 * head + 2) * dim] = part


def collect(row_out, chunks):
    n, half, rows, width, dim = chunks.shape
    return pl.pallas_call(
        collect_kernel,
        in_specs=[VMEM] * 2,
        out_specs=[VMEM] * 2,
        out_shape=[
            jax.ShapeDtypeStruct((rows * C, half * dim), BF16),
            jax.ShapeDtypeStruct((rows * C, 2 * half * dim), BF16),
        ],
        compiler_params=params(24),
        name="collect",
    )(row_out, chunks)


def attn_grad_kernel(n, dim, last, ids, grad_ref, *refs):
    blocks, refs = refs[:n], refs[n:]
    step = pl.program_id(0)
    if last:
        so_far, row_ref, chunk_ref, weight, sem, total = refs
    else:
        total, weight, sem = refs
    tokens = grad_ref.shape[0]
    tile = tokens // 4

    @pl.when(step == 0)
    def _():
        for d in range(n):
            pltpu.make_async_copy(blocks[d], weight.at[d], sem.at[d]).start()
        total[...] = so_far[...] if last else jnp.zeros_like(total)

    pltpu.make_async_copy(blocks[0], weight.at[step], sem.at[step]).wait()

    @pl.loop(0, tokens, step=tile)
    def _(at):
        at = pl.multiple_of(at, tile)
        total[pl.ds(at, tile)] += dot(grad_ref[pl.ds(at, tile)], weight[step], ((1,), (1,)))

    if last:

        @pl.when(step == n - 1)
        def _():
            places, half, rows, width, _ = chunk_ref.shape
            for head in range(half):
                row_ref[:, head * dim : (head + 1) * dim] = total[:, 2 * head * dim : (2 * head + 1) * dim].astype(BF16)
                for d in range(places):
                    for row in range(rows):
                        at = row * C + d * width
                        part = total[at : at + width, (2 * head + 1) * dim : (2 * head + 2) * dim]
                        chunk_ref[d, head, row] = part.astype(BF16)


def attn_grad(ids, out_grad, blocks, so_far, dim):
    m, (span, depth), last = len(blocks), blocks[0].shape, so_far is not None
    tokens, model = out_grad.shape
    n, half = model // depth, span // dim // 2
    total = jax.ShapeDtypeStruct((tokens, span), F32)
    whole = pl.BlockSpec((tokens, span), lambda b, ids: (0, 0))
    chunk = jax.ShapeDtypeStruct((n, half, tokens // C, C // n, dim), BF16)
    scratch = [pltpu.VMEM((m, span, depth), BF16), pltpu.SemaphoreType.DMA((m,))]
    return pl.pallas_call(
        functools.partial(attn_grad_kernel, m, dim, last),
        grid_spec=pltpu.PrefetchScalarGridSpec(
            num_scalar_prefetch=1,
            grid=(m,),
            in_specs=[pl.BlockSpec((tokens, depth), lambda b, ids: (0, ids[b]))]
            + [pl.BlockSpec(memory_space=pl.ANY)] * m
            + [whole] * last,
            out_specs=[
                pl.BlockSpec((tokens, half * dim), lambda b, ids: (0, 0)),
                pl.BlockSpec(chunk.shape, lambda b, ids: (0, 0, 0, 0, 0)),
            ]
            if last
            else whole,
            scratch_shapes=scratch + [pltpu.VMEM(total.shape, F32)] * last,
        ),
        out_shape=[jax.ShapeDtypeStruct((tokens, half * dim), BF16), chunk] if last else total,
        compiler_params=params(60),
        cost_estimate=pl.CostEstimate(
            flops=2 * tokens * span * depth * m,
            bytes_accessed=2 * m * depth * (tokens + span) + 4 * tokens * span,
            transcendentals=0,
        ),
        name="attn_grad",
    )(ids, out_grad, *blocks, *([so_far] if last else []))


def layer_kernel(n, count, adds, ids, wanted, flat_ref, *refs):
    blocks, extra, out_ref = refs[:n], refs[n : n + adds], refs[n + adds]
    weight, sem = refs[n + adds + 1 :]
    step = pl.program_id(0)
    tokens = flat_ref.shape[0]
    tile = tokens // 4

    @pl.when(step == 0)
    def _():
        for s in range(count):
            for d in range(n):

                @pl.when(ids[d] == wanted[s])
                def _():
                    pltpu.make_async_copy(blocks[d], weight.at[s], sem.at[s]).start()

    pltpu.make_async_copy(blocks[0], weight.at[step], sem.at[step]).wait()

    @pl.loop(0, tokens, step=tile)
    def _(at):
        at = pl.multiple_of(at, tile)
        value = dot(flat_ref[pl.ds(at, tile)], weight[step], ((1,), (0,)))
        for ref in extra:
            value = value + ref[pl.ds(at, tile)].astype(F32)
        out_ref[pl.ds(at, tile)] = value.astype(BF16)


def layer_part(ids, flat, blocks, wanted, extra, first):
    n, (span, depth) = len(blocks), blocks[0].shape
    tokens, count = flat.shape[0], wanted.shape[0]
    by_column = pl.BlockSpec((tokens, depth), lambda s, ids, wanted: (0, s))
    return pl.pallas_call(
        functools.partial(layer_kernel, n, count, len(extra)),
        grid_spec=pltpu.PrefetchScalarGridSpec(
            num_scalar_prefetch=2,
            grid=(count,),
            in_specs=[pl.BlockSpec((tokens, span), lambda s, ids, wanted: (0, 0))]
            + [pl.BlockSpec(memory_space=pl.ANY)] * n
            + [pl.BlockSpec((tokens, depth), functools.partial(lambda f, s, ids, wanted: (0, s + f), f)) for f in first],
            out_specs=by_column,
            scratch_shapes=[pltpu.VMEM((count, span, depth), BF16), pltpu.SemaphoreType.DMA((count,))],
        ),
        out_shape=jax.ShapeDtypeStruct((tokens, count * depth), BF16),
        compiler_params=params(60),
        cost_estimate=pl.CostEstimate(
            flops=2 * tokens * span * depth * count,
            bytes_accessed=2 * (count * depth * (tokens + span) + tokens * span),
            transcendentals=0,
        ),
        name="layer_part",
    )(ids, wanted, flat, *blocks, *extra)


def proj_kernel(lead, adds, dim, order, flat_ref, grad_ref, *refs):
    extra, outs, turned = refs[:adds], refs[adds:-1], refs[-1]
    step = pl.program_id(0)
    span = flat_ref.shape[1]

    @pl.when(step == 0)
    def _():
        for at in range(0, span, dim):
            turned[at : at + dim] = flat_ref[:, at : at + dim].T

    def value(at):
        out = dot(turned[at : at + dim], grad_ref[...], ((1,), (0,)))
        for ref in extra:
            out = out + ref[at : at + dim].astype(F32)
        return out.astype(BF16)

    @pl.when(step < lead)
    def _():
        for at in range(0, span, dim):
            outs[0][at : at + dim] = value(at)

    @pl.when(step >= lead)
    def _():
        for at in range(0, span, dim):
            outs[-1][at : at + dim] = value(at)


def proj_part(order, flat, out_grad, extra, depth, dim, lead):
    tokens, span = flat.shape
    count = order.shape[0]
    sizes = [size for size in (lead, count - lead) if size]
    places = [lambda s, order: (jnp.minimum(s, lead - 1), 0, 0), lambda s, order: (jnp.maximum(s - lead, 0), 0, 0)]
    return pl.pallas_call(
        functools.partial(proj_kernel, lead, len(extra), dim),
        grid_spec=pltpu.PrefetchScalarGridSpec(
            num_scalar_prefetch=1,
            grid=(count,),
            in_specs=[
                pl.BlockSpec((tokens, span), lambda s, order: (0, 0)),
                pl.BlockSpec((tokens, depth), lambda s, order: (0, order[s])),
            ]
            + [pl.BlockSpec((pl.squeezed, span, depth), lambda s, order: (s, 0, 0))] * len(extra),
            out_specs=[pl.BlockSpec((pl.squeezed, span, depth), place) for place in places[-len(sizes) :]],
            scratch_shapes=[pltpu.VMEM((span, tokens), BF16)],
        ),
        out_shape=[jax.ShapeDtypeStruct((size, span, depth), BF16) for size in sizes],
        compiler_params=params(60),
        cost_estimate=pl.CostEstimate(
            flops=2 * tokens * span * depth * count,
            bytes_accessed=2 * (count * depth * (tokens + span * (1 + len(extra))) + tokens * span),
            transcendentals=0,
        ),
        name="proj_part",
    )(order, flat, out_grad, *extra)


def row_blocks(length):
    step = length // 2
    return [(start, step) for start in range(0, length, step)]


def row_probs(q, k, start, step, scale):
    scores = dot(q, k, ((1,), (1,))) * scale
    place = lax.broadcasted_iota(jnp.int32, scores.shape, 0) + start
    seen = lax.broadcasted_iota(jnp.int32, scores.shape, 1)
    return softmax(jnp.where(place >= seen, scores, -jnp.inf))


def row_forward_kernel(scale, q_ref, k_ref, v_ref, o_ref):
    for start, step in row_blocks(q_ref.shape[0]):
        stop = start + step
        probs = row_probs(q_ref[start:stop], k_ref[:stop], start, step, scale)
        o_ref[start:stop] = dot(probs.astype(BF16), v_ref[:stop], ((1,), (0,))).astype(BF16)


def row_forward(q, k, v):
    half, tokens, dim = q.shape
    by_head = pl.BlockSpec((pl.squeezed, C, dim), lambda r, h: (h, r, 0))
    return pl.pallas_call(
        functools.partial(row_forward_kernel, dim**-0.5),
        grid=(tokens // C, half),
        in_specs=[by_head] * 3,
        out_specs=pl.BlockSpec((C, dim), lambda r, h: (r, h)),
        out_shape=jax.ShapeDtypeStruct((tokens, half * dim), BF16),
        compiler_params=params(60),
        cost_estimate=pl.CostEstimate(
            flops=4 * tokens * C * half * dim, bytes_accessed=8 * tokens * half * dim, transcendentals=tokens * C * half
        ),
        name="row_forward",
    )(q, k, v)


def row_backward_kernel(scale, q_ref, k_ref, v_ref, g_ref, dq_ref, dk_ref, dv_ref, k_sum, v_sum):
    k_sum[...] = jnp.zeros_like(k_sum)
    v_sum[...] = jnp.zeros_like(v_sum)
    for start, step in row_blocks(q_ref.shape[0]):
        stop = start + step
        q, k, grad = q_ref[start:stop], k_ref[:stop], g_ref[start:stop]
        probs = row_probs(q, k, start, step, scale)
        prob_grad = dot(grad, v_ref[:stop], ((1,), (1,)))
        inner = jnp.sum(probs * prob_grad, axis=-1, keepdims=True)
        score_low = (probs * (prob_grad - inner)).astype(BF16)
        dq_ref[start:stop] = (dot(score_low, k, ((1,), (0,))) * scale).astype(BF16)
        k_sum[:stop] += dot(score_low, q, ((0,), (0,)))
        v_sum[:stop] += dot(probs.astype(BF16), grad, ((0,), (0,)))
    dk_ref[...] = (k_sum[...] * scale).astype(BF16)
    dv_ref[...] = v_sum[...].astype(BF16)


def row_backward(q, k, v, grad):
    half, tokens, dim = q.shape
    by_head = pl.BlockSpec((pl.squeezed, C, dim), lambda r, h: (h, r, 0))
    return pl.pallas_call(
        functools.partial(row_backward_kernel, dim**-0.5),
        grid=(tokens // C, half),
        in_specs=[by_head] * 3 + [pl.BlockSpec((C, dim), lambda r, h: (r, h))],
        out_specs=[by_head] * 3,
        out_shape=[jax.ShapeDtypeStruct(q.shape, BF16)] * 3,
        scratch_shapes=[pltpu.VMEM((C, dim), F32)] * 2,
        compiler_params=params(60),
        cost_estimate=pl.CostEstimate(
            flops=10 * tokens * C * half * dim, bytes_accessed=14 * tokens * half * dim, transcendentals=tokens * C * half
        ),
        name="row_backward",
    )(q, k, v, grad)


def column_mask(size):
    def parts(axis):
        place = lax.broadcasted_iota(jnp.int32, (size, size), axis)
        return place // LANE, place % LANE

    row_q, column_q = parts(0)
    row_k, column_k = parts(1)
    return (column_q == column_k) & (row_q >= row_k)


def gathered(ref, index, at):
    n, rows = ref.shape[0], ref.shape[-3]
    return jnp.concatenate([ref[(d, *index, row, pl.ds(at, LANE))] for d in range(n) for row in range(rows)], axis=0)


def scattered(ref, index, at, value):
    n, rows = ref.shape[0], ref.shape[-3]
    for d in range(n):
        for row in range(rows):
            line = d * rows + row
            ref[(d, *index, row, pl.ds(at, LANE))] = value[line * LANE : (line + 1) * LANE]


def column_probs(bias, q, k, scale):
    return softmax(dot(q, k, ((1,), (1,))) * scale + bias[...])


def column_forward_kernel(scale, chunk_ref, out_ref, bias):
    half, width = chunk_ref.shape[2], chunk_ref.shape[4]
    bias[...] = jnp.where(column_mask(bias.shape[0]), 0.0, -jnp.inf)
    blocks = width // LANE

    @pl.loop(0, half * blocks)
    def _(step):
        head, at = step // blocks, pl.multiple_of(step % blocks * LANE, LANE)
        q, k, v = (gathered(chunk_ref, (array, head), at) for array in range(3))
        probs = column_probs(bias, q, k, scale)
        scattered(out_ref, (head,), at, dot(probs.astype(BF16), v, ((1,), (0,))).astype(BF16))


def column_forward(chunks):
    n, _, half, rows, width, dim = chunks.shape
    size = n * rows * LANE
    return pl.pallas_call(
        functools.partial(column_forward_kernel, dim**-0.5),
        in_specs=[VMEM],
        out_specs=VMEM,
        out_shape=jax.ShapeDtypeStruct((n, half, rows, width, dim), BF16),
        scratch_shapes=[pltpu.VMEM((size, size), F32)],
        compiler_params=params(24),
        cost_estimate=pl.CostEstimate(
            flops=4 * size * size * dim * half * width // LANE,
            bytes_accessed=8 * n * half * rows * width * dim,
            transcendentals=size * size * half * width // LANE,
        ),
        name="column_forward",
    )(chunks)


def column_backward_kernel(scale, chunk_ref, grad_ref, query_ref, rest_ref, bias):
    half, width = chunk_ref.shape[2], chunk_ref.shape[4]
    bias[...] = jnp.where(column_mask(bias.shape[0]), 0.0, -jnp.inf)
    blocks = width // LANE

    @pl.loop(0, half * blocks)
    def _(step):
        head, at = step // blocks, pl.multiple_of(step % blocks * LANE, LANE)
        q, k, v = (gathered(chunk_ref, (array, head), at) for array in range(3))
        grad = gathered(grad_ref, (head,), at)
        probs = column_probs(bias, q, k, scale)
        prob_grad = dot(grad, v, ((1,), (1,)))
        inner = jnp.sum(probs * prob_grad, axis=-1, keepdims=True)
        score_low = (probs * (prob_grad - inner)).astype(BF16)
        scattered(query_ref, (0, head), at, (dot(score_low, k, ((1,), (0,))) * scale).astype(BF16))
        scattered(rest_ref, (0, head), at, (dot(score_low, q, ((0,), (0,))) * scale).astype(BF16))
        scattered(rest_ref, (1, head), at, dot(probs.astype(BF16), grad, ((0,), (0,))).astype(BF16))


def column_backward(chunks, grads):
    n, _, half, rows, width, dim = chunks.shape
    size = n * rows * LANE
    return pl.pallas_call(
        functools.partial(column_backward_kernel, dim**-0.5),
        in_specs=[VMEM] * 2,
        out_specs=[VMEM] * 2,
        out_shape=[jax.ShapeDtypeStruct((n, k, half, rows, width, dim), BF16) for k in (1, 2)],
        scratch_shapes=[pltpu.VMEM((size, size), F32)],
        compiler_params=params(24),
        cost_estimate=pl.CostEstimate(
            flops=10 * size * size * dim * half * width // LANE,
            bytes_accessed=14 * n * half * rows * width * dim,
            transcendentals=size * size * half * width // LANE,
        ),
        name="column_backward",
    )(chunks, grads)


PAIRS = [(0, 1), (1, 0), (2, 3), (3, 2)]
INWARD = [(0, 1), (3, 2)]
CROSS = [(1, 2), (2, 1)]
OUTWARD = [(1, 0), (2, 3)]


def after(value, *done):
    return lax.optimization_barrier((value, *done))[0]


class Links:
    def __init__(self, n, window):
        self.n, self.inner, self.window, self.sent = n, n // 4, window, []

    def send(self, value, pairs):
        over = len(self.sent) - self.window + 1
        if over > 0:
            value = after(value, *self.sent[max(0, over - self.window) : over])
        out = lax.ppermute(value, "ctx", pairs)
        self.sent.append(out)
        return out

    def along(self, value, pairs):
        return self.send(value, [(a * self.inner + y, b * self.inner + y) for a, b in pairs for y in range(self.inner)])

    def flip(self, value, d):
        return self.send(value, [(place, place ^ d) for place in range(self.n)])


def swap(chunks):
    return lax.all_to_all(chunks, "ctx", split_axis=0, concat_axis=0, tiled=True)


class LayerSum:
    def __init__(self, ids, flat, blocks, heads_n):
        self.ids, self.flat, self.blocks, self.heads_n = ids, flat, blocks, heads_n
        self.mine = lax.axis_index("head").astype(jnp.int32)
        self.per = len(blocks) // heads_n
        self.even = list(range(0, heads_n, 2))

    def part(self, offsets, extra, first):
        wanted = [(self.mine ^ g) * self.per + b for g in offsets for b in range(self.per)]
        wanted = jnp.stack(wanted).astype(jnp.int32)
        return layer_part(self.ids, self.flat, self.blocks, wanted, extra, first)

    def move(self, part, g):
        return lax.ppermute(part, "head", [(place, place ^ g) for place in range(self.heads_n)])

    def start(self):
        self.first = self.part([g + 1 for g in self.even], [], [])
        self.near = self.move(self.first, 1)

    def turn(self, done):
        self.flat = after(self.flat, done)
        self.parts = [self.part([g], [self.near], [g // 2 * self.per]) for g in self.even[1:]]
        self.far = [self.move(part, g) for part, g in zip(self.parts, self.even[1:])]

    def finish(self):
        return self.part([0], [self.near] + self.far, [0] * (1 + len(self.far)))


def on_device(queries, keys, values, out_grad, wo, *, n, heads_n):
    tokens, heads, dim = queries.shape
    half, depth, inner = heads // 2, wo.shape[1], n // 4
    me = lax.axis_index("ctx").astype(jnp.int32)
    line, spot = me // inner, me % inner
    middle, upper = (line == 1) | (line == 2), line < 2
    far, close = [jnp.where(upper, 2, 1), jnp.where(upper, 3, 0)], [line ^ 1, line]
    links = Links(n, 5)

    def around(block):
        return [block if e == 0 else links.flip(block, e) for e in range(inner)]

    def targets(owners, e):
        return jnp.stack([owner * inner + (spot ^ e) for owner in owners]).astype(jnp.int32)

    def leaving(flat, owners):
        return [proj_part(targets(owners, e), flat, out_grad, [], depth, dim, 0)[0] for e in range(1, inner)]

    def exchanged(parts):
        return [links.flip(part, e + 1) for e, part in enumerate(parts)]

    def summed(flat, owners, theirs, lead):
        return proj_part(targets(owners, 0), flat, out_grad, theirs, depth, dim, lead)

    def add(*terms):
        return sum(term.astype(F32) for term in terms).astype(BF16)

    near = links.along(wo, PAIRS)
    cross_own = links.along(wo, CROSS)
    own_blocks = around(wo)
    chunks, by_head = split_inputs(queries, keys, values, n)
    row_out = row_forward(*by_head)
    row_far, row_close = leaving(row_out, far), leaving(row_out, close)
    near = after(near, chunks, *own_blocks[1:])
    near_blocks = around(near)
    cross_near = links.along(near, CROSS)
    out_own = links.along(cross_own, OUTWARD)
    chunks = swap(after(chunks, *near_blocks, cross_near, out_own, *row_far, *row_close))
    out_near = links.along(cross_near, OUTWARD)
    far_own = jnp.where(middle, cross_own, out_own)
    far_own_blocks = around(far_own)
    far_near = jnp.where(middle, cross_near, out_near)
    far_near_blocks = around(far_near)
    blocks = own_blocks + near_blocks + far_own_blocks + far_near_blocks
    ids = [owner * inner + (spot ^ e) for owner in (line, line ^ 1, *far) for e in range(inner)]
    ids = jnp.stack(ids).astype(jnp.int32)
    early = n - inner

    outs = column_forward(after(chunks, *far_own_blocks))
    column_part = swap(outs)
    so_far = attn_grad(ids[:early], after(out_grad, outs), blocks[:early], None, dim)
    grad_row, grads = attn_grad(ids[early:], out_grad, blocks[early:], so_far, dim)
    row_far = exchanged([after(part, *far_near_blocks) for part in row_far])
    row_close = exchanged(row_close)
    grads = swap(after(grads, column_part, *row_far))
    (row_far,) = summed(after(row_out, outs), far, row_far, 0)
    row_far_in = links.along(row_far, INWARD)
    column_out, flat = collect(row_out, after(column_part, row_far))
    column_far, column_close = leaving(column_out, far), leaving(column_out, close)
    column_far = exchanged(column_far)
    grad_query, grad_rest = column_backward(chunks, after(grads, *column_close, row_far))
    grad_query = swap(after(grad_query, *column_far))

    layer = LayerSum(ids, after(flat, grad_rest), blocks, heads_n)
    (column_far,) = summed(after(column_out, grad_rest), far, column_far, 0)
    column_far_in = links.along(column_far, INWARD)
    row_cross = links.along(add(row_far, after(row_far_in, grad_rest)), CROSS)
    column_close = exchanged(column_close)
    row_near, row_own = summed(after(row_out, grad_rest), close, row_close, 1)
    row_near_in = links.along(row_near[0], INWARD)
    layer.start()
    grad_rest = swap(after(grad_rest, grad_query, column_far_in, row_cross, layer.first))
    column_cross = links.along(add(column_far, column_far_in), CROSS)
    layer.turn(layer.near)
    row_grads = row_backward(*by_head, after(grad_row, column_far_in))
    column_near, column_own = summed(after(column_out, *layer.parts), close, column_close, 1)
    column_near_in = links.along(column_near[0], INWARD)
    column_cross = after(column_cross, row_grads[0])
    row_back = links.along(add(row_near[0], row_cross[1]), OUTWARD)
    column_back = links.along(add(column_near[0], column_cross[1]), OUTWARD)

    gradients = join_gradients([grad_query, grad_rest], row_grads)
    proj_row = add(row_own[0], row_near_in, row_cross[0], row_back)
    proj_column = add(column_own[0], column_near_in, column_cross[0], column_back)
    shape = (half, dim, depth)
    proj_grad = jnp.stack([proj_row.reshape(shape), proj_column.reshape(shape)], axis=1)
    return (layer.finish(), *gradients, proj_grad.reshape(heads * dim, depth))


def solution(mesh):
    in_specs = (
        P("ctx", "head", None),
        P("ctx", "head", None),
        P("ctx", "head", None),
        P("ctx", None),
        P("head", "ctx"),
    )
    out_specs = (
        P("ctx", "head"),
        P("ctx", "head", None),
        P("ctx", "head", None),
        P("ctx", "head", None),
        P("head", "ctx"),
    )
    return jax.shard_map(
        functools.partial(on_device, n=mesh.shape["ctx"], heads_n=mesh.shape["head"]),
        mesh=mesh,
        in_specs=in_specs,
        out_specs=out_specs,
        check_vma=False,
    )
```

```python
import functools

import jax
import jax.numpy as jnp
from jax import lax
from jax.experimental import pallas as pl
from jax.experimental.pallas import tpu as pltpu
from jax.sharding import PartitionSpec as P

C = 512
LANE = 16
VMEM = pl.BlockSpec(memory_space=pltpu.VMEM)
BF16 = jnp.bfloat16
F32 = jnp.float32


def params(mib):
    return pltpu.CompilerParams(vmem_limit_bytes=mib * 1024 * 1024)


def dot(a, b, dims):
    return lax.dot_general(a, b, (dims, ((), ())), preferred_element_type=F32)


def softmax(scores):
    highest = jnp.max(scores, axis=-1, keepdims=True)
    lifted = jnp.exp(scores - highest)
    return lifted * (1.0 / jnp.sum(lifted, axis=-1, keepdims=True))


def split_kernel(q_ref, k_ref, v_ref, chunk_ref, *rest):
    row_refs, wide = rest[:3], rest[3]
    n, width = chunk_ref.shape[0], chunk_ref.shape[3]
    span, heads, dim = q_ref.shape
    for array, ref in enumerate((q_ref, k_ref, v_ref)):
        wide[...] = ref[...].astype(F32).reshape(span * heads, dim)
        for head in range(heads // 2):
            row_refs[array][head] = wide[pl.ds(2 * head, span, stride=heads), :].astype(BF16)
            for d in range(n):
                odd = wide[pl.ds(d * width * heads + 2 * head + 1, width, stride=heads), :]
                chunk_ref[d, array, head] = odd.astype(BF16)


def split_inputs(queries, keys, values, n):
    tokens, heads, dim = queries.shape
    rows, width, half = tokens // C, C // n, heads // 2
    by_head = jax.ShapeDtypeStruct((half, tokens, dim), BF16)
    out = pl.pallas_call(
        split_kernel,
        grid=(rows,),
        in_specs=[pl.BlockSpec((C, heads, dim), lambda r: (r, 0, 0))] * 3,
        out_specs=[pl.BlockSpec((n, 3, half, pl.squeezed, width, dim), lambda r: (0, 0, 0, r, 0, 0))]
        + [pl.BlockSpec((half, C, dim), lambda r: (0, r, 0))] * 3,
        scratch_shapes=[pltpu.VMEM((C * heads, dim), F32)],
        out_shape=[jax.ShapeDtypeStruct((n, 3, half, rows, width, dim), BF16)] + [by_head] * 3,
        compiler_params=params(60),
        name="split_inputs",
    )(queries, keys, values)
    return out[0], out[1:]


def join_kernel(chunk_ref, *refs):
    row_refs, outs, wide = refs[:3], refs[3:6], refs[6]
    n, width = chunk_ref.shape[0], chunk_ref.shape[3]
    span, heads, dim = outs[0].shape
    for array in range(3):
        for head in range(heads // 2):
            wide[pl.ds(2 * head, span, stride=heads), :] = row_refs[array][head].astype(F32)
            for d in range(n):
                part = chunk_ref[d, array, head].astype(F32)
                wide[pl.ds(d * width * heads + 2 * head + 1, width, stride=heads), :] = part
        outs[array][...] = wide[...].reshape(span, heads, dim).astype(BF16)


def join_gradients(chunks, by_head):
    n, _, half, rows, width, dim = chunks.shape
    tokens, heads = by_head[0].shape[1], 2 * half
    return pl.pallas_call(
        join_kernel,
        grid=(rows,),
        in_specs=[pl.BlockSpec((n, 3, half, pl.squeezed, width, dim), lambda r: (0, 0, 0, r, 0, 0))]
        + [pl.BlockSpec((half, C, dim), lambda r: (0, r, 0))] * 3,
        out_specs=[pl.BlockSpec((C, heads, dim), lambda r: (r, 0, 0))] * 3,
        scratch_shapes=[pltpu.VMEM((C * heads, dim), F32)],
        out_shape=[jax.ShapeDtypeStruct((tokens, heads, dim), BF16)] * 3,
        compiler_params=params(60),
        name="join_gradients",
    )(chunks, *by_head)


def collect_kernel(row_ref, chunk_ref, flat_ref, both_ref):
    n, half, rows, width, dim = chunk_ref.shape
    for head in range(half):
        both_ref[:, 2 * head * dim : (2 * head + 1) * dim] = row_ref[:, head * dim : (head + 1) * dim]
        for d in range(n):
            for row in range(rows):
                part = chunk_ref[d, head, row]
                at = row * C + d * width
                flat_ref[at : at + width, head * dim : (head + 1) * dim] = part
                both_ref[at : at + width, (2 * head + 1) * dim : (2 * head + 2) * dim] = part


def collect(row_out, chunks):
    n, half, rows, width, dim = chunks.shape
    return pl.pallas_call(
        collect_kernel,
        in_specs=[VMEM] * 2,
        out_specs=[VMEM] * 2,
        out_shape=[
            jax.ShapeDtypeStruct((rows * C, half * dim), BF16),
            jax.ShapeDtypeStruct((rows * C, 2 * half * dim), BF16),
        ],
        compiler_params=params(24),
        name="collect",
    )(row_out, chunks)


def attn_grad_kernel(n, dim, last, ids, grad_ref, *refs):
    blocks, refs = refs[:n], refs[n:]
    step = pl.program_id(0)
    if last:
        so_far, row_ref, chunk_ref, weight, sem, total = refs
    else:
        total, weight, sem = refs
    tokens = grad_ref.shape[0]
    tile = tokens // 4

    @pl.when(step == 0)
    def _():
        for d in range(n):
            pltpu.make_async_copy(blocks[d], weight.at[d], sem.at[d]).start()
        total[...] = so_far[...] if last else jnp.zeros_like(total)

    pltpu.make_async_copy(blocks[0], weight.at[step], sem.at[step]).wait()

    @pl.loop(0, tokens, step=tile)
    def _(at):
        at = pl.multiple_of(at, tile)
        total[pl.ds(at, tile)] += dot(grad_ref[pl.ds(at, tile)], weight[step], ((1,), (1,)))

    if last:

        @pl.when(step == n - 1)
        def _():
            places, half, rows, width, _ = chunk_ref.shape
            for head in range(half):
                row_ref[:, head * dim : (head + 1) * dim] = total[:, 2 * head * dim : (2 * head + 1) * dim].astype(BF16)
                for d in range(places):
                    for row in range(rows):
                        at = row * C + d * width
                        part = total[at : at + width, (2 * head + 1) * dim : (2 * head + 2) * dim]
                        chunk_ref[d, head, row] = part.astype(BF16)


def attn_grad(ids, out_grad, blocks, so_far, dim):
    m, (span, depth), last = len(blocks), blocks[0].shape, so_far is not None
    tokens, model = out_grad.shape
    n, half = model // depth, span // dim // 2
    total = jax.ShapeDtypeStruct((tokens, span), F32)
    whole = pl.BlockSpec((tokens, span), lambda b, ids: (0, 0))
    chunk = jax.ShapeDtypeStruct((n, half, tokens // C, C // n, dim), BF16)
    scratch = [pltpu.VMEM((m, span, depth), BF16), pltpu.SemaphoreType.DMA((m,))]
    return pl.pallas_call(
        functools.partial(attn_grad_kernel, m, dim, last),
        grid_spec=pltpu.PrefetchScalarGridSpec(
            num_scalar_prefetch=1,
            grid=(m,),
            in_specs=[pl.BlockSpec((tokens, depth), lambda b, ids: (0, ids[b]))]
            + [pl.BlockSpec(memory_space=pl.ANY)] * m
            + [whole] * last,
            out_specs=[
                pl.BlockSpec((tokens, half * dim), lambda b, ids: (0, 0)),
                pl.BlockSpec(chunk.shape, lambda b, ids: (0, 0, 0, 0, 0)),
            ]
            if last
            else whole,
            scratch_shapes=scratch + [pltpu.VMEM(total.shape, F32)] * last,
        ),
        out_shape=[jax.ShapeDtypeStruct((tokens, half * dim), BF16), chunk] if last else total,
        compiler_params=params(60),
        cost_estimate=pl.CostEstimate(
            flops=2 * tokens * span * depth * m,
            bytes_accessed=2 * m * depth * (tokens + span) + 4 * tokens * span,
            transcendentals=0,
        ),
        name="attn_grad",
    )(ids, out_grad, *blocks, *([so_far] if last else []))


def layer_kernel(n, count, adds, ids, wanted, flat_ref, *refs):
    blocks, extra, out_ref = refs[:n], refs[n : n + adds], refs[n + adds]
    weight, sem = refs[n + adds + 1 :]
    step = pl.program_id(0)
    tokens = flat_ref.shape[0]
    tile = tokens // 4

    @pl.when(step == 0)
    def _():
        for s in range(count):
            for d in range(n):

                @pl.when(ids[d] == wanted[s])
                def _():
                    pltpu.make_async_copy(blocks[d], weight.at[s], sem.at[s]).start()

    pltpu.make_async_copy(blocks[0], weight.at[step], sem.at[step]).wait()

    @pl.loop(0, tokens, step=tile)
    def _(at):
        at = pl.multiple_of(at, tile)
        value = dot(flat_ref[pl.ds(at, tile)], weight[step], ((1,), (0,)))
        for ref in extra:
            value = value + ref[pl.ds(at, tile)].astype(F32)
        out_ref[pl.ds(at, tile)] = value.astype(BF16)


def layer_part(ids, flat, blocks, wanted, extra, first):
    n, (span, depth) = len(blocks), blocks[0].shape
    tokens, count = flat.shape[0], wanted.shape[0]
    by_column = pl.BlockSpec((tokens, depth), lambda s, ids, wanted: (0, s))
    return pl.pallas_call(
        functools.partial(layer_kernel, n, count, len(extra)),
        grid_spec=pltpu.PrefetchScalarGridSpec(
            num_scalar_prefetch=2,
            grid=(count,),
            in_specs=[pl.BlockSpec((tokens, span), lambda s, ids, wanted: (0, 0))]
            + [pl.BlockSpec(memory_space=pl.ANY)] * n
            + [pl.BlockSpec((tokens, depth), functools.partial(lambda f, s, ids, wanted: (0, s + f), f)) for f in first],
            out_specs=by_column,
            scratch_shapes=[pltpu.VMEM((count, span, depth), BF16), pltpu.SemaphoreType.DMA((count,))],
        ),
        out_shape=jax.ShapeDtypeStruct((tokens, count * depth), BF16),
        compiler_params=params(60),
        cost_estimate=pl.CostEstimate(
            flops=2 * tokens * span * depth * count,
            bytes_accessed=2 * (count * depth * (tokens + span) + tokens * span),
            transcendentals=0,
        ),
        name="layer_part",
    )(ids, wanted, flat, *blocks, *extra)


def proj_kernel(lead, adds, dim, order, flat_ref, grad_ref, *refs):
    extra, outs, turned = refs[:adds], refs[adds:-1], refs[-1]
    step = pl.program_id(0)
    span = flat_ref.shape[1]

    @pl.when(step == 0)
    def _():
        for at in range(0, span, dim):
            turned[at : at + dim] = flat_ref[:, at : at + dim].T

    def value(at):
        out = dot(turned[at : at + dim], grad_ref[...], ((1,), (0,)))
        for ref in extra:
            out = out + ref[at : at + dim].astype(F32)
        return out.astype(BF16)

    @pl.when(step < lead)
    def _():
        for at in range(0, span, dim):
            outs[0][at : at + dim] = value(at)

    @pl.when(step >= lead)
    def _():
        for at in range(0, span, dim):
            outs[-1][at : at + dim] = value(at)


def proj_part(order, flat, out_grad, extra, depth, dim, lead):
    tokens, span = flat.shape
    count = order.shape[0]
    sizes = [size for size in (lead, count - lead) if size]
    places = [lambda s, order: (jnp.minimum(s, lead - 1), 0, 0), lambda s, order: (jnp.maximum(s - lead, 0), 0, 0)]
    return pl.pallas_call(
        functools.partial(proj_kernel, lead, len(extra), dim),
        grid_spec=pltpu.PrefetchScalarGridSpec(
            num_scalar_prefetch=1,
            grid=(count,),
            in_specs=[
                pl.BlockSpec((tokens, span), lambda s, order: (0, 0)),
                pl.BlockSpec((tokens, depth), lambda s, order: (0, order[s])),
            ]
            + [pl.BlockSpec((pl.squeezed, span, depth), lambda s, order: (s, 0, 0))] * len(extra),
            out_specs=[pl.BlockSpec((pl.squeezed, span, depth), place) for place in places[-len(sizes) :]],
            scratch_shapes=[pltpu.VMEM((span, tokens), BF16)],
        ),
        out_shape=[jax.ShapeDtypeStruct((size, span, depth), BF16) for size in sizes],
        compiler_params=params(60),
        cost_estimate=pl.CostEstimate(
            flops=2 * tokens * span * depth * count,
            bytes_accessed=2 * (count * depth * (tokens + span * (1 + len(extra))) + tokens * span),
            transcendentals=0,
        ),
        name="proj_part",
    )(order, flat, out_grad, *extra)


def row_blocks(length):
    step = length // 2
    return [(start, step) for start in range(0, length, step)]


def row_probs(q, k, start, step, scale):
    scores = dot(q, k, ((1,), (1,))) * scale
    place = lax.broadcasted_iota(jnp.int32, scores.shape, 0) + start
    seen = lax.broadcasted_iota(jnp.int32, scores.shape, 1)
    return softmax(jnp.where(place >= seen, scores, -jnp.inf))


def row_forward_kernel(scale, q_ref, k_ref, v_ref, o_ref):
    for start, step in row_blocks(q_ref.shape[0]):
        stop = start + step
        probs = row_probs(q_ref[start:stop], k_ref[:stop], start, step, scale)
        o_ref[start:stop] = dot(probs.astype(BF16), v_ref[:stop], ((1,), (0,))).astype(BF16)


def row_forward(q, k, v):
    half, tokens, dim = q.shape
    by_head = pl.BlockSpec((pl.squeezed, C, dim), lambda r, h: (h, r, 0))
    return pl.pallas_call(
        functools.partial(row_forward_kernel, dim**-0.5),
        grid=(tokens // C, half),
        in_specs=[by_head] * 3,
        out_specs=pl.BlockSpec((C, dim), lambda r, h: (r, h)),
        out_shape=jax.ShapeDtypeStruct((tokens, half * dim), BF16),
        compiler_params=params(60),
        cost_estimate=pl.CostEstimate(
            flops=4 * tokens * C * half * dim, bytes_accessed=8 * tokens * half * dim, transcendentals=tokens * C * half
        ),
        name="row_forward",
    )(q, k, v)


def row_backward_kernel(scale, q_ref, k_ref, v_ref, g_ref, dq_ref, dk_ref, dv_ref, k_sum, v_sum):
    k_sum[...] = jnp.zeros_like(k_sum)
    v_sum[...] = jnp.zeros_like(v_sum)
    for start, step in row_blocks(q_ref.shape[0]):
        stop = start + step
        q, k, grad = q_ref[start:stop], k_ref[:stop], g_ref[start:stop]
        probs = row_probs(q, k, start, step, scale)
        prob_grad = dot(grad, v_ref[:stop], ((1,), (1,)))
        inner = jnp.sum(probs * prob_grad, axis=-1, keepdims=True)
        score_low = (probs * (prob_grad - inner)).astype(BF16)
        dq_ref[start:stop] = (dot(score_low, k, ((1,), (0,))) * scale).astype(BF16)
        k_sum[:stop] += dot(score_low, q, ((0,), (0,)))
        v_sum[:stop] += dot(probs.astype(BF16), grad, ((0,), (0,)))
    dk_ref[...] = (k_sum[...] * scale).astype(BF16)
    dv_ref[...] = v_sum[...].astype(BF16)


def row_backward(q, k, v, grad):
    half, tokens, dim = q.shape
    by_head = pl.BlockSpec((pl.squeezed, C, dim), lambda r, h: (h, r, 0))
    return pl.pallas_call(
        functools.partial(row_backward_kernel, dim**-0.5),
        grid=(tokens // C, half),
        in_specs=[by_head] * 3 + [pl.BlockSpec((C, dim), lambda r, h: (r, h))],
        out_specs=[by_head] * 3,
        out_shape=[jax.ShapeDtypeStruct(q.shape, BF16)] * 3,
        scratch_shapes=[pltpu.VMEM((C, dim), F32)] * 2,
        compiler_params=params(60),
        cost_estimate=pl.CostEstimate(
            flops=10 * tokens * C * half * dim, bytes_accessed=14 * tokens * half * dim, transcendentals=tokens * C * half
        ),
        name="row_backward",
    )(q, k, v, grad)


def column_mask(size):
    def parts(axis):
        place = lax.broadcasted_iota(jnp.int32, (size, size), axis)
        return place // LANE, place % LANE

    row_q, column_q = parts(0)
    row_k, column_k = parts(1)
    return (column_q == column_k) & (row_q >= row_k)


def gathered(ref, index, at):
    n, rows = ref.shape[0], ref.shape[-3]
    return jnp.concatenate([ref[(d, *index, row, pl.ds(at, LANE))] for d in range(n) for row in range(rows)], axis=0)


def scattered(ref, index, at, value):
    n, rows = ref.shape[0], ref.shape[-3]
    for d in range(n):
        for row in range(rows):
            line = d * rows + row
            ref[(d, *index, row, pl.ds(at, LANE))] = value[line * LANE : (line + 1) * LANE]


def column_probs(bias, q, k, scale):
    return softmax(dot(q, k, ((1,), (1,))) * scale + bias[...])


def column_forward_kernel(scale, chunk_ref, out_ref, bias):
    half, width = chunk_ref.shape[2], chunk_ref.shape[4]
    bias[...] = jnp.where(column_mask(bias.shape[0]), 0.0, -jnp.inf)
    blocks = width // LANE

    @pl.loop(0, half * blocks)
    def _(step):
        head, at = step // blocks, pl.multiple_of(step % blocks * LANE, LANE)
        q, k, v = (gathered(chunk_ref, (array, head), at) for array in range(3))
        probs = column_probs(bias, q, k, scale)
        scattered(out_ref, (head,), at, dot(probs.astype(BF16), v, ((1,), (0,))).astype(BF16))


def column_forward(chunks):
    n, _, half, rows, width, dim = chunks.shape
    size = n * rows * LANE
    return pl.pallas_call(
        functools.partial(column_forward_kernel, dim**-0.5),
        in_specs=[VMEM],
        out_specs=VMEM,
        out_shape=jax.ShapeDtypeStruct((n, half, rows, width, dim), BF16),
        scratch_shapes=[pltpu.VMEM((size, size), F32)],
        compiler_params=params(24),
        cost_estimate=pl.CostEstimate(
            flops=4 * size * size * dim * half * width // LANE,
            bytes_accessed=8 * n * half * rows * width * dim,
            transcendentals=size * size * half * width // LANE,
        ),
        name="column_forward",
    )(chunks)


def column_backward_kernel(scale, chunk_ref, grad_ref, out_ref, bias):
    half, width = chunk_ref.shape[2], chunk_ref.shape[4]
    bias[...] = jnp.where(column_mask(bias.shape[0]), 0.0, -jnp.inf)
    blocks = width // LANE

    @pl.loop(0, half * blocks)
    def _(step):
        head, at = step // blocks, pl.multiple_of(step % blocks * LANE, LANE)
        q, k, v = (gathered(chunk_ref, (array, head), at) for array in range(3))
        grad = gathered(grad_ref, (head,), at)
        probs = column_probs(bias, q, k, scale)
        prob_grad = dot(grad, v, ((1,), (1,)))
        inner = jnp.sum(probs * prob_grad, axis=-1, keepdims=True)
        score_low = (probs * (prob_grad - inner)).astype(BF16)
        scattered(out_ref, (0, head), at, (dot(score_low, k, ((1,), (0,))) * scale).astype(BF16))
        scattered(out_ref, (1, head), at, (dot(score_low, q, ((0,), (0,))) * scale).astype(BF16))
        scattered(out_ref, (2, head), at, dot(probs.astype(BF16), grad, ((0,), (0,))).astype(BF16))


def column_backward(chunks, grads):
    n, _, half, rows, width, dim = chunks.shape
    size = n * rows * LANE
    return pl.pallas_call(
        functools.partial(column_backward_kernel, dim**-0.5),
        in_specs=[VMEM] * 2,
        out_specs=VMEM,
        out_shape=jax.ShapeDtypeStruct(chunks.shape, BF16),
        scratch_shapes=[pltpu.VMEM((size, size), F32)],
        compiler_params=params(24),
        cost_estimate=pl.CostEstimate(
            flops=10 * size * size * dim * half * width // LANE,
            bytes_accessed=14 * n * half * rows * width * dim,
            transcendentals=size * size * half * width // LANE,
        ),
        name="column_backward",
    )(chunks, grads)


PAIRS = [(0, 1), (1, 0), (2, 3), (3, 2)]
INWARD = [(0, 1), (3, 2)]
CROSS = [(1, 2), (2, 1)]
OUTWARD = [(1, 0), (2, 3)]


def after(value, *done):
    return lax.optimization_barrier((value, *done))[0]


class Links:
    def __init__(self, n, window):
        self.n, self.inner, self.window, self.sent = n, n // 4, window, []

    def send(self, value, pairs):
        over = len(self.sent) - self.window + 1
        if over > 0:
            value = after(value, *self.sent[max(0, over - self.window) : over])
        out = lax.ppermute(value, "ctx", pairs)
        self.sent.append(out)
        return out

    def along(self, value, pairs):
        return self.send(value, [(a * self.inner + y, b * self.inner + y) for a, b in pairs for y in range(self.inner)])

    def flip(self, value, d):
        return self.send(value, [(place, place ^ d) for place in range(self.n)])


def swap(chunks):
    return lax.all_to_all(chunks, "ctx", split_axis=0, concat_axis=0, tiled=True)


class LayerSum:
    def __init__(self, ids, flat, blocks, heads_n):
        self.ids, self.flat, self.blocks, self.heads_n = ids, flat, blocks, heads_n
        self.mine = lax.axis_index("head").astype(jnp.int32)
        self.per = len(blocks) // heads_n
        self.even = list(range(0, heads_n, 2))

    def part(self, offsets, extra, first):
        wanted = [(self.mine ^ g) * self.per + b for g in offsets for b in range(self.per)]
        wanted = jnp.stack(wanted).astype(jnp.int32)
        return layer_part(self.ids, self.flat, self.blocks, wanted, extra, first)

    def move(self, part, g):
        return lax.ppermute(part, "head", [(place, place ^ g) for place in range(self.heads_n)])

    def start(self):
        self.first = self.part([g + 1 for g in self.even], [], [])
        self.near = self.move(self.first, 1)

    def turn(self, done):
        self.flat = after(self.flat, done)
        self.parts = [self.part([g], [self.near], [g // 2 * self.per]) for g in self.even[1:]]
        self.far = [self.move(part, g) for part, g in zip(self.parts, self.even[1:])]

    def finish(self):
        return self.part([0], [self.near] + self.far, [0] * (1 + len(self.far)))


def on_device(queries, keys, values, out_grad, wo, *, n, heads_n):
    tokens, heads, dim = queries.shape
    half, depth, inner = heads // 2, wo.shape[1], n // 4
    me = lax.axis_index("ctx").astype(jnp.int32)
    line, spot = me // inner, me % inner
    middle, upper = (line == 1) | (line == 2), line < 2
    far, close = [jnp.where(upper, 2, 1), jnp.where(upper, 3, 0)], [line ^ 1, line]
    links = Links(n, 5)

    def around(block):
        return [block if e == 0 else links.flip(block, e) for e in range(inner)]

    def targets(owners, e):
        return jnp.stack([owner * inner + (spot ^ e) for owner in owners]).astype(jnp.int32)

    def leaving(flat, owners):
        return [proj_part(targets(owners, e), flat, out_grad, [], depth, dim, 0)[0] for e in range(1, inner)]

    def exchanged(parts):
        return [links.flip(part, e + 1) for e, part in enumerate(parts)]

    def summed(flat, owners, theirs, lead):
        return proj_part(targets(owners, 0), flat, out_grad, theirs, depth, dim, lead)

    def add(*terms):
        return sum(term.astype(F32) for term in terms).astype(BF16)

    near = links.along(wo, PAIRS)
    cross_own = links.along(wo, CROSS)
    own_blocks = around(wo)
    chunks, by_head = split_inputs(queries, keys, values, n)
    row_out = row_forward(*by_head)
    row_far, row_close = leaving(row_out, far), leaving(row_out, close)
    near = after(near, chunks, *own_blocks[1:])
    near_blocks = around(near)
    cross_near = links.along(near, CROSS)
    out_own = links.along(cross_own, OUTWARD)
    chunks = swap(after(chunks, *near_blocks, cross_near, out_own, *row_far, *row_close))
    out_near = links.along(cross_near, OUTWARD)
    far_own = jnp.where(middle, cross_own, out_own)
    far_own_blocks = around(far_own)
    far_near = jnp.where(middle, cross_near, out_near)
    far_near_blocks = around(far_near)
    blocks = own_blocks + near_blocks + far_own_blocks + far_near_blocks
    ids = [owner * inner + (spot ^ e) for owner in (line, line ^ 1, *far) for e in range(inner)]
    ids = jnp.stack(ids).astype(jnp.int32)
    early = n - inner

    outs = column_forward(after(chunks, *far_own_blocks))
    column_part = swap(outs)
    so_far = attn_grad(ids[:early], after(out_grad, outs), blocks[:early], None, dim)
    grad_row, grads = attn_grad(ids[early:], out_grad, blocks[early:], so_far, dim)
    row_far = exchanged([after(part, so_far, *far_near_blocks) for part in row_far])
    row_close = exchanged(row_close)
    grads = swap(after(grads, column_part, *row_far))
    (row_far,) = summed(after(row_out, outs), far, row_far, 0)
    row_far_in = links.along(row_far, INWARD)
    column_out, flat = collect(row_out, after(column_part, row_far))
    column_far, column_close = leaving(column_out, far), leaving(column_out, close)
    column_far = exchanged(column_far)
    gradients = column_backward(chunks, after(grads, *column_close, row_far))
    column_grads = swap(after(gradients, *column_far, row_far_in, *row_close))

    layer = LayerSum(ids, after(flat, gradients), blocks, heads_n)
    layer.start()
    column_close = exchanged(column_close)
    (column_far,) = summed(after(column_out, gradients), far, column_far, 0)
    column_far_in = links.along(column_far, INWARD)
    row_cross = links.along(add(row_far, row_far_in), CROSS)
    row_near, row_own = summed(after(row_out, gradients), close, row_close, 1)
    row_near_in = links.along(row_near[0], INWARD)
    row_grads = row_backward(*by_head, after(grad_row, column_far))
    column_near, column_own = summed(after(column_out, gradients), close, column_close, 1)
    column_near_in = links.along(column_near[0], INWARD)
    layer.turn(gradients)
    first = after(column_far_in, row_grads[0], row_near[0], column_near[0], *layer.parts)
    column_cross = links.along(add(column_far, first), CROSS)
    row_back = links.along(add(row_near[0], after(row_cross, row_near_in)[1]), OUTWARD)
    gradients = join_gradients(column_grads, row_grads)
    layer_out = layer.finish()
    last = after(column_cross, column_near_in, gradients[0], layer_out)
    column_back = links.along(add(column_near[0], last[1]), OUTWARD)

    proj_row = add(row_own[0], row_near_in, row_cross[0], row_back)
    proj_column = add(column_own[0], column_near_in, column_cross[0], column_back)
    shape = (half, dim, depth)
    proj_grad = jnp.stack([proj_row.reshape(shape), proj_column.reshape(shape)], axis=1)
    return (layer_out, *gradients, proj_grad.reshape(heads * dim, depth))


def solution(mesh):
    in_specs = (
        P("ctx", "head", None),
        P("ctx", "head", None),
        P("ctx", "head", None),
        P("ctx", None),
        P("head", "ctx"),
    )
    out_specs = (
        P("ctx", "head"),
        P("ctx", "head", None),
        P("ctx", "head", None),
        P("ctx", "head", None),
        P("head", "ctx"),
    )
    return jax.shard_map(
        functools.partial(on_device, n=mesh.shape["ctx"], heads_n=mesh.shape["head"]),
        mesh=mesh,
        in_specs=in_specs,
        out_specs=out_specs,
        check_vma=False,
    )
```

```python
import functools

import jax
import jax.numpy as jnp
from jax import lax
from jax.experimental import pallas as pl
from jax.experimental.pallas import tpu as pltpu
from jax.sharding import PartitionSpec as P

C = 512
LANE = 16
VMEM = pl.BlockSpec(memory_space=pltpu.VMEM)
BF16 = jnp.bfloat16
F32 = jnp.float32


def params(mib):
    return pltpu.CompilerParams(vmem_limit_bytes=mib * 1024 * 1024)


def dot(a, b, dims):
    return lax.dot_general(a, b, (dims, ((), ())), preferred_element_type=F32)


def softmax(scores):
    highest = jnp.max(scores, axis=-1, keepdims=True)
    lifted = jnp.exp(scores - highest)
    return lifted * (1.0 / jnp.sum(lifted, axis=-1, keepdims=True))


def split_kernel(q_ref, k_ref, v_ref, chunk_ref, *rest):
    row_refs, wide = rest[:3], rest[3]
    n, width = chunk_ref.shape[0], chunk_ref.shape[3]
    span, heads, dim = q_ref.shape
    for array, ref in enumerate((q_ref, k_ref, v_ref)):
        wide[...] = ref[...].astype(F32).reshape(span * heads, dim)
        for head in range(heads // 2):
            row_refs[array][head] = wide[pl.ds(2 * head, span, stride=heads), :].astype(BF16)
            for d in range(n):
                odd = wide[pl.ds(d * width * heads + 2 * head + 1, width, stride=heads), :]
                chunk_ref[d, array, head] = odd.astype(BF16)


def split_inputs(queries, keys, values, n):
    tokens, heads, dim = queries.shape
    rows, width, half = tokens // C, C // n, heads // 2
    by_head = jax.ShapeDtypeStruct((half, tokens, dim), BF16)
    out = pl.pallas_call(
        split_kernel,
        grid=(rows,),
        in_specs=[pl.BlockSpec((C, heads, dim), lambda r: (r, 0, 0))] * 3,
        out_specs=[pl.BlockSpec((n, 3, half, pl.squeezed, width, dim), lambda r: (0, 0, 0, r, 0, 0))]
        + [pl.BlockSpec((half, C, dim), lambda r: (0, r, 0))] * 3,
        scratch_shapes=[pltpu.VMEM((C * heads, dim), F32)],
        out_shape=[jax.ShapeDtypeStruct((n, 3, half, rows, width, dim), BF16)] + [by_head] * 3,
        compiler_params=params(60),
        name="split_inputs",
    )(queries, keys, values)
    return out[0], out[1:]


def join_kernel(chunk_ref, *refs):
    row_refs, outs, wide = refs[:3], refs[3:6], refs[6]
    n, width = chunk_ref.shape[0], chunk_ref.shape[3]
    span, heads, dim = outs[0].shape
    for array in range(3):
        for head in range(heads // 2):
            wide[pl.ds(2 * head, span, stride=heads), :] = row_refs[array][head].astype(F32)
            for d in range(n):
                part = chunk_ref[d, array, head].astype(F32)
                wide[pl.ds(d * width * heads + 2 * head + 1, width, stride=heads), :] = part
        outs[array][...] = wide[...].reshape(span, heads, dim).astype(BF16)


def join_gradients(chunks, by_head):
    n, _, half, rows, width, dim = chunks.shape
    tokens, heads = by_head[0].shape[1], 2 * half
    return pl.pallas_call(
        join_kernel,
        grid=(rows,),
        in_specs=[pl.BlockSpec((n, 3, half, pl.squeezed, width, dim), lambda r: (0, 0, 0, r, 0, 0))]
        + [pl.BlockSpec((half, C, dim), lambda r: (0, r, 0))] * 3,
        out_specs=[pl.BlockSpec((C, heads, dim), lambda r: (r, 0, 0))] * 3,
        scratch_shapes=[pltpu.VMEM((C * heads, dim), F32)],
        out_shape=[jax.ShapeDtypeStruct((tokens, heads, dim), BF16)] * 3,
        compiler_params=params(60),
        name="join_gradients",
    )(chunks, *by_head)


def collect_kernel(row_ref, chunk_ref, flat_ref, both_ref):
    n, half, rows, width, dim = chunk_ref.shape
    for head in range(half):
        both_ref[:, 2 * head * dim : (2 * head + 1) * dim] = row_ref[:, head * dim : (head + 1) * dim]
        for d in range(n):
            for row in range(rows):
                part = chunk_ref[d, head, row]
                at = row * C + d * width
                flat_ref[at : at + width, head * dim : (head + 1) * dim] = part
                both_ref[at : at + width, (2 * head + 1) * dim : (2 * head + 2) * dim] = part


def collect(row_out, chunks):
    n, half, rows, width, dim = chunks.shape
    return pl.pallas_call(
        collect_kernel,
        in_specs=[VMEM] * 2,
        out_specs=[VMEM] * 2,
        out_shape=[
            jax.ShapeDtypeStruct((rows * C, half * dim), BF16),
            jax.ShapeDtypeStruct((rows * C, 2 * half * dim), BF16),
        ],
        compiler_params=params(24),
        name="collect",
    )(row_out, chunks)


def attn_grad_kernel(n, dim, last, ids, grad_ref, *refs):
    blocks, refs = refs[:n], refs[n:]
    step = pl.program_id(0)
    if last:
        so_far, row_ref, chunk_ref, weight, sem, total = refs
    else:
        total, weight, sem = refs
    tokens = grad_ref.shape[0]
    tile = tokens // 4

    @pl.when(step == 0)
    def _():
        for d in range(n):
            pltpu.make_async_copy(blocks[d], weight.at[d], sem.at[d]).start()
        total[...] = so_far[...] if last else jnp.zeros_like(total)

    pltpu.make_async_copy(blocks[0], weight.at[step], sem.at[step]).wait()

    @pl.loop(0, tokens, step=tile)
    def _(at):
        at = pl.multiple_of(at, tile)
        total[pl.ds(at, tile)] += dot(grad_ref[pl.ds(at, tile)], weight[step], ((1,), (1,)))

    if last:

        @pl.when(step == n - 1)
        def _():
            places, half, rows, width, _ = chunk_ref.shape
            for head in range(half):
                row_ref[:, head * dim : (head + 1) * dim] = total[:, 2 * head * dim : (2 * head + 1) * dim].astype(BF16)
                for d in range(places):
                    for row in range(rows):
                        at = row * C + d * width
                        part = total[at : at + width, (2 * head + 1) * dim : (2 * head + 2) * dim]
                        chunk_ref[d, head, row] = part.astype(BF16)


def attn_grad(ids, out_grad, blocks, so_far, dim):
    m, (span, depth), last = len(blocks), blocks[0].shape, so_far is not None
    tokens, model = out_grad.shape
    n, half = model // depth, span // dim // 2
    total = jax.ShapeDtypeStruct((tokens, span), F32)
    whole = pl.BlockSpec((tokens, span), lambda b, ids: (0, 0))
    chunk = jax.ShapeDtypeStruct((n, half, tokens // C, C // n, dim), BF16)
    scratch = [pltpu.VMEM((m, span, depth), BF16), pltpu.SemaphoreType.DMA((m,))]
    return pl.pallas_call(
        functools.partial(attn_grad_kernel, m, dim, last),
        grid_spec=pltpu.PrefetchScalarGridSpec(
            num_scalar_prefetch=1,
            grid=(m,),
            in_specs=[pl.BlockSpec((tokens, depth), lambda b, ids: (0, ids[b]))]
            + [pl.BlockSpec(memory_space=pl.ANY)] * m
            + [whole] * last,
            out_specs=[
                pl.BlockSpec((tokens, half * dim), lambda b, ids: (0, 0)),
                pl.BlockSpec(chunk.shape, lambda b, ids: (0, 0, 0, 0, 0)),
            ]
            if last
            else whole,
            scratch_shapes=scratch + [pltpu.VMEM(total.shape, F32)] * last,
        ),
        out_shape=[jax.ShapeDtypeStruct((tokens, half * dim), BF16), chunk] if last else total,
        compiler_params=params(60),
        cost_estimate=pl.CostEstimate(
            flops=2 * tokens * span * depth * m,
            bytes_accessed=2 * m * depth * (tokens + span) + 4 * tokens * span,
            transcendentals=0,
        ),
        name="attn_grad",
    )(ids, out_grad, *blocks, *([so_far] if last else []))


def layer_kernel(n, count, adds, ids, wanted, flat_ref, *refs):
    blocks, extra, out_ref = refs[:n], refs[n : n + adds], refs[n + adds]
    weight, sem = refs[n + adds + 1 :]
    step = pl.program_id(0)
    tokens = flat_ref.shape[0]
    tile = tokens // 4

    @pl.when(step == 0)
    def _():
        for s in range(count):
            for d in range(n):

                @pl.when(ids[d] == wanted[s])
                def _():
                    pltpu.make_async_copy(blocks[d], weight.at[s], sem.at[s]).start()

    pltpu.make_async_copy(blocks[0], weight.at[step], sem.at[step]).wait()

    @pl.loop(0, tokens, step=tile)
    def _(at):
        at = pl.multiple_of(at, tile)
        value = dot(flat_ref[pl.ds(at, tile)], weight[step], ((1,), (0,)))
        for ref in extra:
            value = value + ref[pl.ds(at, tile)].astype(F32)
        out_ref[pl.ds(at, tile)] = value.astype(BF16)


def layer_part(ids, flat, blocks, wanted, extra, first):
    n, (span, depth) = len(blocks), blocks[0].shape
    tokens, count = flat.shape[0], wanted.shape[0]
    by_column = pl.BlockSpec((tokens, depth), lambda s, ids, wanted: (0, s))
    return pl.pallas_call(
        functools.partial(layer_kernel, n, count, len(extra)),
        grid_spec=pltpu.PrefetchScalarGridSpec(
            num_scalar_prefetch=2,
            grid=(count,),
            in_specs=[pl.BlockSpec((tokens, span), lambda s, ids, wanted: (0, 0))]
            + [pl.BlockSpec(memory_space=pl.ANY)] * n
            + [pl.BlockSpec((tokens, depth), functools.partial(lambda f, s, ids, wanted: (0, s + f), f)) for f in first],
            out_specs=by_column,
            scratch_shapes=[pltpu.VMEM((count, span, depth), BF16), pltpu.SemaphoreType.DMA((count,))],
        ),
        out_shape=jax.ShapeDtypeStruct((tokens, count * depth), BF16),
        compiler_params=params(60),
        cost_estimate=pl.CostEstimate(
            flops=2 * tokens * span * depth * count,
            bytes_accessed=2 * (count * depth * (tokens + span) + tokens * span),
            transcendentals=0,
        ),
        name="layer_part",
    )(ids, wanted, flat, *blocks, *extra)


def proj_kernel(lead, adds, dim, order, flat_ref, grad_ref, *refs):
    extra, outs, turned = refs[:adds], refs[adds:-1], refs[-1]
    step = pl.program_id(0)
    span = flat_ref.shape[1]

    @pl.when(step == 0)
    def _():
        for at in range(0, span, dim):
            turned[at : at + dim] = flat_ref[:, at : at + dim].T

    def value(at):
        out = dot(turned[at : at + dim], grad_ref[...], ((1,), (0,)))
        for ref in extra:
            out = out + ref[at : at + dim].astype(F32)
        return out.astype(BF16)

    @pl.when(step < lead)
    def _():
        for at in range(0, span, dim):
            outs[0][at : at + dim] = value(at)

    @pl.when(step >= lead)
    def _():
        for at in range(0, span, dim):
            outs[-1][at : at + dim] = value(at)


def proj_part(order, flat, out_grad, extra, depth, dim, lead):
    tokens, span = flat.shape
    count = order.shape[0]
    sizes = [size for size in (lead, count - lead) if size]
    places = [lambda s, order: (jnp.minimum(s, lead - 1), 0, 0), lambda s, order: (jnp.maximum(s - lead, 0), 0, 0)]
    return pl.pallas_call(
        functools.partial(proj_kernel, lead, len(extra), dim),
        grid_spec=pltpu.PrefetchScalarGridSpec(
            num_scalar_prefetch=1,
            grid=(count,),
            in_specs=[
                pl.BlockSpec((tokens, span), lambda s, order: (0, 0)),
                pl.BlockSpec((tokens, depth), lambda s, order: (0, order[s])),
            ]
            + [pl.BlockSpec((pl.squeezed, span, depth), lambda s, order: (s, 0, 0))] * len(extra),
            out_specs=[pl.BlockSpec((pl.squeezed, span, depth), place) for place in places[-len(sizes) :]],
            scratch_shapes=[pltpu.VMEM((span, tokens), BF16)],
        ),
        out_shape=[jax.ShapeDtypeStruct((size, span, depth), BF16) for size in sizes],
        compiler_params=params(60),
        cost_estimate=pl.CostEstimate(
            flops=2 * tokens * span * depth * count,
            bytes_accessed=2 * (count * depth * (tokens + span * (1 + len(extra))) + tokens * span),
            transcendentals=0,
        ),
        name="proj_part",
    )(order, flat, out_grad, *extra)


def row_blocks(length):
    step = length // 2
    return [(start, step) for start in range(0, length, step)]


def row_probs(q, k, start, step, scale):
    scores = dot(q, k, ((1,), (1,))) * scale
    place = lax.broadcasted_iota(jnp.int32, scores.shape, 0) + start
    seen = lax.broadcasted_iota(jnp.int32, scores.shape, 1)
    return softmax(jnp.where(place >= seen, scores, -jnp.inf))


def row_forward_kernel(scale, q_ref, k_ref, v_ref, o_ref):
    for start, step in row_blocks(q_ref.shape[0]):
        stop = start + step
        probs = row_probs(q_ref[start:stop], k_ref[:stop], start, step, scale)
        o_ref[start:stop] = dot(probs.astype(BF16), v_ref[:stop], ((1,), (0,))).astype(BF16)


def row_forward(q, k, v):
    half, tokens, dim = q.shape
    by_head = pl.BlockSpec((pl.squeezed, C, dim), lambda r, h: (h, r, 0))
    return pl.pallas_call(
        functools.partial(row_forward_kernel, dim**-0.5),
        grid=(tokens // C, half),
        in_specs=[by_head] * 3,
        out_specs=pl.BlockSpec((C, dim), lambda r, h: (r, h)),
        out_shape=jax.ShapeDtypeStruct((tokens, half * dim), BF16),
        compiler_params=params(60),
        cost_estimate=pl.CostEstimate(
            flops=4 * tokens * C * half * dim, bytes_accessed=8 * tokens * half * dim, transcendentals=tokens * C * half
        ),
        name="row_forward",
    )(q, k, v)


def row_backward_kernel(scale, q_ref, k_ref, v_ref, g_ref, dq_ref, dk_ref, dv_ref, k_sum, v_sum):
    k_sum[...] = jnp.zeros_like(k_sum)
    v_sum[...] = jnp.zeros_like(v_sum)
    for start, step in row_blocks(q_ref.shape[0]):
        stop = start + step
        q, k, grad = q_ref[start:stop], k_ref[:stop], g_ref[start:stop]
        probs = row_probs(q, k, start, step, scale)
        prob_grad = dot(grad, v_ref[:stop], ((1,), (1,)))
        inner = jnp.sum(probs * prob_grad, axis=-1, keepdims=True)
        score_low = (probs * (prob_grad - inner)).astype(BF16)
        dq_ref[start:stop] = (dot(score_low, k, ((1,), (0,))) * scale).astype(BF16)
        k_sum[:stop] += dot(score_low, q, ((0,), (0,)))
        v_sum[:stop] += dot(probs.astype(BF16), grad, ((0,), (0,)))
    dk_ref[...] = (k_sum[...] * scale).astype(BF16)
    dv_ref[...] = v_sum[...].astype(BF16)


def row_backward(q, k, v, grad):
    half, tokens, dim = q.shape
    by_head = pl.BlockSpec((pl.squeezed, C, dim), lambda r, h: (h, r, 0))
    return pl.pallas_call(
        functools.partial(row_backward_kernel, dim**-0.5),
        grid=(tokens // C, half),
        in_specs=[by_head] * 3 + [pl.BlockSpec((C, dim), lambda r, h: (r, h))],
        out_specs=[by_head] * 3,
        out_shape=[jax.ShapeDtypeStruct(q.shape, BF16)] * 3,
        scratch_shapes=[pltpu.VMEM((C, dim), F32)] * 2,
        compiler_params=params(60),
        cost_estimate=pl.CostEstimate(
            flops=10 * tokens * C * half * dim, bytes_accessed=14 * tokens * half * dim, transcendentals=tokens * C * half
        ),
        name="row_backward",
    )(q, k, v, grad)


def column_mask(size):
    def parts(axis):
        place = lax.broadcasted_iota(jnp.int32, (size, size), axis)
        return place // LANE, place % LANE

    row_q, column_q = parts(0)
    row_k, column_k = parts(1)
    return (column_q == column_k) & (row_q >= row_k)


def gathered(ref, index, at):
    n, rows = ref.shape[0], ref.shape[-3]
    return jnp.concatenate([ref[(d, *index, row, pl.ds(at, LANE))] for d in range(n) for row in range(rows)], axis=0)


def scattered(ref, index, at, value):
    n, rows = ref.shape[0], ref.shape[-3]
    for d in range(n):
        for row in range(rows):
            line = d * rows + row
            ref[(d, *index, row, pl.ds(at, LANE))] = value[line * LANE : (line + 1) * LANE]


def column_probs(bias, q, k, scale):
    return softmax(dot(q, k, ((1,), (1,))) * scale + bias[...])


def column_forward_kernel(scale, chunk_ref, out_ref, bias):
    half, width = chunk_ref.shape[2], chunk_ref.shape[4]
    bias[...] = jnp.where(column_mask(bias.shape[0]), 0.0, -jnp.inf)
    blocks = width // LANE

    @pl.loop(0, half * blocks)
    def _(step):
        head, at = step // blocks, pl.multiple_of(step % blocks * LANE, LANE)
        q, k, v = (gathered(chunk_ref, (array, head), at) for array in range(3))
        probs = column_probs(bias, q, k, scale)
        scattered(out_ref, (head,), at, dot(probs.astype(BF16), v, ((1,), (0,))).astype(BF16))


def column_forward(chunks):
    n, _, half, rows, width, dim = chunks.shape
    size = n * rows * LANE
    return pl.pallas_call(
        functools.partial(column_forward_kernel, dim**-0.5),
        in_specs=[VMEM],
        out_specs=VMEM,
        out_shape=jax.ShapeDtypeStruct((n, half, rows, width, dim), BF16),
        scratch_shapes=[pltpu.VMEM((size, size), F32)],
        compiler_params=params(24),
        cost_estimate=pl.CostEstimate(
            flops=4 * size * size * dim * half * width // LANE,
            bytes_accessed=8 * n * half * rows * width * dim,
            transcendentals=size * size * half * width // LANE,
        ),
        name="column_forward",
    )(chunks)


def column_backward_kernel(scale, chunk_ref, grad_ref, out_ref, bias):
    half, width = chunk_ref.shape[2], chunk_ref.shape[4]
    bias[...] = jnp.where(column_mask(bias.shape[0]), 0.0, -jnp.inf)
    blocks = width // LANE

    @pl.loop(0, half * blocks)
    def _(step):
        head, at = step // blocks, pl.multiple_of(step % blocks * LANE, LANE)
        q, k, v = (gathered(chunk_ref, (array, head), at) for array in range(3))
        grad = gathered(grad_ref, (head,), at)
        probs = column_probs(bias, q, k, scale)
        prob_grad = dot(grad, v, ((1,), (1,)))
        inner = jnp.sum(probs * prob_grad, axis=-1, keepdims=True)
        score_low = (probs * (prob_grad - inner)).astype(BF16)
        scattered(out_ref, (0, head), at, (dot(score_low, k, ((1,), (0,))) * scale).astype(BF16))
        scattered(out_ref, (1, head), at, (dot(score_low, q, ((0,), (0,))) * scale).astype(BF16))
        scattered(out_ref, (2, head), at, dot(probs.astype(BF16), grad, ((0,), (0,))).astype(BF16))


def column_backward(chunks, grads):
    n, _, half, rows, width, dim = chunks.shape
    size = n * rows * LANE
    return pl.pallas_call(
        functools.partial(column_backward_kernel, dim**-0.5),
        in_specs=[VMEM] * 2,
        out_specs=VMEM,
        out_shape=jax.ShapeDtypeStruct(chunks.shape, BF16),
        scratch_shapes=[pltpu.VMEM((size, size), F32)],
        compiler_params=params(24),
        cost_estimate=pl.CostEstimate(
            flops=10 * size * size * dim * half * width // LANE,
            bytes_accessed=14 * n * half * rows * width * dim,
            transcendentals=size * size * half * width // LANE,
        ),
        name="column_backward",
    )(chunks, grads)


PAIRS = [(0, 1), (1, 0), (2, 3), (3, 2)]
INWARD = [(0, 1), (3, 2)]
CROSS = [(1, 2), (2, 1)]
OUTWARD = [(1, 0), (2, 3)]


def after(value, *done):
    return lax.optimization_barrier((value, *done))[0]


class Links:
    def __init__(self, n, window):
        self.n, self.inner, self.window, self.sent = n, n // 4, window, []

    def send(self, value, pairs):
        over = len(self.sent) - self.window + 1
        if over > 0:
            value = after(value, *self.sent[max(0, over - self.window) : over])
        out = lax.ppermute(value, "ctx", pairs)
        self.sent.append(out)
        return out

    def along(self, value, pairs):
        return self.send(value, [(a * self.inner + y, b * self.inner + y) for a, b in pairs for y in range(self.inner)])

    def flip(self, value, d):
        return self.send(value, [(place, place ^ d) for place in range(self.n)])


def swap(chunks):
    return lax.all_to_all(chunks, "ctx", split_axis=0, concat_axis=0, tiled=True)


class LayerSum:
    def __init__(self, ids, flat, blocks, heads_n):
        self.ids, self.flat, self.blocks, self.heads_n = ids, flat, blocks, heads_n
        self.mine = lax.axis_index("head").astype(jnp.int32)
        self.per = len(blocks) // heads_n
        self.even = list(range(0, heads_n, 2))

    def part(self, offsets, extra, first):
        wanted = [(self.mine ^ g) * self.per + b for g in offsets for b in range(self.per)]
        wanted = jnp.stack(wanted).astype(jnp.int32)
        return layer_part(self.ids, self.flat, self.blocks, wanted, extra, first)

    def move(self, part, g):
        return lax.ppermute(part, "head", [(place, place ^ g) for place in range(self.heads_n)])

    def start(self):
        self.first = self.part([g + 1 for g in self.even], [], [])
        self.near = self.move(self.first, 1)

    def turn(self, done):
        self.flat = after(self.flat, done)
        self.parts = [self.part([g], [self.near], [g // 2 * self.per]) for g in self.even[1:]]
        self.far = [self.move(part, g) for part, g in zip(self.parts, self.even[1:])]

    def finish(self):
        return self.part([0], [self.near] + self.far, [0] * (1 + len(self.far)))


def on_device(queries, keys, values, out_grad, wo, *, n, heads_n):
    tokens, heads, dim = queries.shape
    half, depth, inner = heads // 2, wo.shape[1], n // 4
    me = lax.axis_index("ctx").astype(jnp.int32)
    line, spot = me // inner, me % inner
    middle, upper = (line == 1) | (line == 2), line < 2
    far, close = [jnp.where(upper, 2, 1), jnp.where(upper, 3, 0)], [line ^ 1, line]
    links = Links(n, 5)

    def around(block):
        return [block if e == 0 else links.flip(block, e) for e in range(inner)]

    def targets(owners, e):
        return jnp.stack([owner * inner + (spot ^ e) for owner in owners]).astype(jnp.int32)

    def leaving(flat, owners):
        return [proj_part(targets(owners, e), flat, out_grad, [], depth, dim, 0)[0] for e in range(1, inner)]

    def exchanged(parts):
        return [links.flip(part, e + 1) for e, part in enumerate(parts)]

    def summed(flat, owners, theirs, lead):
        return proj_part(targets(owners, 0), flat, out_grad, theirs, depth, dim, lead)

    def add(*terms):
        return sum(term.astype(F32) for term in terms).astype(BF16)

    near = links.along(wo, PAIRS)
    cross_own = links.along(wo, CROSS)
    own_blocks = around(wo)
    chunks, by_head = split_inputs(queries, keys, values, n)
    row_out = row_forward(*by_head)
    row_far, row_close = leaving(row_out, far), leaving(row_out, close)
    near = after(near, chunks, *own_blocks[1:])
    near_blocks = around(near)
    cross_near = links.along(near, CROSS)
    out_own = links.along(cross_own, OUTWARD)
    chunks = swap(after(chunks, *near_blocks, cross_near, out_own, *row_far, *row_close))
    out_near = links.along(cross_near, OUTWARD)
    far_own = jnp.where(middle, cross_own, out_own)
    far_own_blocks = around(far_own)
    far_near = jnp.where(middle, cross_near, out_near)
    far_near_blocks = around(far_near)
    blocks = own_blocks + near_blocks + far_own_blocks + far_near_blocks
    ids = [owner * inner + (spot ^ e) for owner in (line, line ^ 1, *far) for e in range(inner)]
    ids = jnp.stack(ids).astype(jnp.int32)
    early = n - inner

    outs = column_forward(after(chunks, *far_own_blocks))
    column_part = swap(outs)
    so_far = attn_grad(ids[:early], after(out_grad, outs), blocks[:early], None, dim)
    grad_row, grads = attn_grad(ids[early:], out_grad, blocks[early:], so_far, dim)
    row_far = exchanged([after(part, so_far, *far_near_blocks) for part in row_far])
    grads = swap(after(grads, column_part))
    column_out, flat = collect(row_out, column_part)
    column_far, column_close = leaving(column_out, far), leaving(column_out, close)
    column_far = exchanged(column_far)
    (row_far,) = summed(after(row_out, *column_close), far, row_far, 0)
    row_far_in = links.along(row_far, INWARD)
    gradients = column_backward(chunks, after(grads, *column_close, row_far))
    column_grads = swap(after(gradients, *column_far, row_far_in))

    layer = LayerSum(ids, after(flat, gradients), blocks, heads_n)
    layer.start()
    row_close, column_close = exchanged(row_close), exchanged(column_close)
    (column_far,) = summed(after(column_out, gradients), far, column_far, 0)
    column_far_in = links.along(column_far, INWARD)
    row_cross = links.along(add(row_far, row_far_in), CROSS)
    row_near, row_own = summed(after(row_out, gradients), close, row_close, 1)
    row_near_in = links.along(row_near[0], INWARD)
    row_grads = row_backward(*by_head, after(grad_row, column_far))
    column_near, column_own = summed(after(column_out, gradients), close, column_close, 1)
    column_near_in = links.along(column_near[0], INWARD)
    layer.turn(gradients)
    first = after(column_far_in, row_grads[0], row_near[0], column_near[0], *layer.parts)
    column_cross = links.along(add(column_far, first), CROSS)
    gradients = join_gradients(column_grads, row_grads)
    layer_out = layer.finish()
    row_back = links.along(add(row_near[0], after(row_cross, gradients[0], layer_out)[1]), OUTWARD)
    column_back = links.along(add(column_near[0], after(column_cross, gradients[0], layer_out)[1]), OUTWARD)

    proj_row = add(row_own[0], row_near_in, row_cross[0], row_back)
    proj_column = add(column_own[0], column_near_in, column_cross[0], column_back)
    shape = (half, dim, depth)
    proj_grad = jnp.stack([proj_row.reshape(shape), proj_column.reshape(shape)], axis=1)
    return (layer_out, *gradients, proj_grad.reshape(heads * dim, depth))


def solution(mesh):
    in_specs = (
        P("ctx", "head", None),
        P("ctx", "head", None),
        P("ctx", "head", None),
        P("ctx", None),
        P("head", "ctx"),
    )
    out_specs = (
        P("ctx", "head"),
        P("ctx", "head", None),
        P("ctx", "head", None),
        P("ctx", "head", None),
        P("head", "ctx"),
    )
    return jax.shard_map(
        functools.partial(on_device, n=mesh.shape["ctx"], heads_n=mesh.shape["head"]),
        mesh=mesh,
        in_specs=in_specs,
        out_specs=out_specs,
        check_vma=False,
    )
```

```python
import functools

import jax
import jax.numpy as jnp
from jax import lax
from jax.experimental import pallas as pl
from jax.experimental.pallas import tpu as pltpu
from jax.sharding import PartitionSpec as P

C = 512
LANE = 16
VMEM = pl.BlockSpec(memory_space=pltpu.VMEM)
BF16 = jnp.bfloat16
F32 = jnp.float32


def params(mib):
    return pltpu.CompilerParams(vmem_limit_bytes=mib * 1024 * 1024)


def dot(a, b, dims):
    return lax.dot_general(a, b, (dims, ((), ())), preferred_element_type=F32)


def softmax(scores):
    highest = jnp.max(scores, axis=-1, keepdims=True)
    lifted = jnp.exp(scores - highest)
    return lifted * (1.0 / jnp.sum(lifted, axis=-1, keepdims=True))


def split_kernel(q_ref, k_ref, v_ref, chunk_ref, *rest):
    row_refs, wide = rest[:3], rest[3]
    n, width = chunk_ref.shape[0], chunk_ref.shape[3]
    span, heads, dim = q_ref.shape
    for array, ref in enumerate((q_ref, k_ref, v_ref)):
        wide[...] = ref[...].astype(F32).reshape(span * heads, dim)
        for head in range(heads // 2):
            row_refs[array][head] = wide[pl.ds(2 * head, span, stride=heads), :].astype(BF16)
            for d in range(n):
                odd = wide[pl.ds(d * width * heads + 2 * head + 1, width, stride=heads), :]
                chunk_ref[d, array, head] = odd.astype(BF16)


def split_inputs(queries, keys, values, n):
    tokens, heads, dim = queries.shape
    rows, width, half = tokens // C, C // n, heads // 2
    by_head = jax.ShapeDtypeStruct((half, tokens, dim), BF16)
    out = pl.pallas_call(
        split_kernel,
        grid=(rows,),
        in_specs=[pl.BlockSpec((C, heads, dim), lambda r: (r, 0, 0))] * 3,
        out_specs=[pl.BlockSpec((n, 3, half, pl.squeezed, width, dim), lambda r: (0, 0, 0, r, 0, 0))]
        + [pl.BlockSpec((half, C, dim), lambda r: (0, r, 0))] * 3,
        scratch_shapes=[pltpu.VMEM((C * heads, dim), F32)],
        out_shape=[jax.ShapeDtypeStruct((n, 3, half, rows, width, dim), BF16)] + [by_head] * 3,
        compiler_params=params(60),
        name="split_inputs",
    )(queries, keys, values)
    return out[0], out[1:]


def join_kernel(chunk_ref, *refs):
    row_refs, outs, wide = refs[:3], refs[3:6], refs[6]
    n, width = chunk_ref.shape[0], chunk_ref.shape[3]
    span, heads, dim = outs[0].shape
    for array in range(3):
        for head in range(heads // 2):
            wide[pl.ds(2 * head, span, stride=heads), :] = row_refs[array][head].astype(F32)
            for d in range(n):
                part = chunk_ref[d, array, head].astype(F32)
                wide[pl.ds(d * width * heads + 2 * head + 1, width, stride=heads), :] = part
        outs[array][...] = wide[...].reshape(span, heads, dim).astype(BF16)


def join_gradients(chunks, by_head):
    n, _, half, rows, width, dim = chunks.shape
    tokens, heads = by_head[0].shape[1], 2 * half
    return pl.pallas_call(
        join_kernel,
        grid=(rows,),
        in_specs=[pl.BlockSpec((n, 3, half, pl.squeezed, width, dim), lambda r: (0, 0, 0, r, 0, 0))]
        + [pl.BlockSpec((half, C, dim), lambda r: (0, r, 0))] * 3,
        out_specs=[pl.BlockSpec((C, heads, dim), lambda r: (r, 0, 0))] * 3,
        scratch_shapes=[pltpu.VMEM((C * heads, dim), F32)],
        out_shape=[jax.ShapeDtypeStruct((tokens, heads, dim), BF16)] * 3,
        compiler_params=params(60),
        name="join_gradients",
    )(chunks, *by_head)


def collect_kernel(row_ref, chunk_ref, flat_ref, both_ref):
    n, half, rows, width, dim = chunk_ref.shape
    for head in range(half):
        both_ref[:, 2 * head * dim : (2 * head + 1) * dim] = row_ref[:, head * dim : (head + 1) * dim]
        for d in range(n):
            for row in range(rows):
                part = chunk_ref[d, head, row]
                at = row * C + d * width
                flat_ref[at : at + width, head * dim : (head + 1) * dim] = part
                both_ref[at : at + width, (2 * head + 1) * dim : (2 * head + 2) * dim] = part


def collect(row_out, chunks):
    n, half, rows, width, dim = chunks.shape
    return pl.pallas_call(
        collect_kernel,
        in_specs=[VMEM] * 2,
        out_specs=[VMEM] * 2,
        out_shape=[
            jax.ShapeDtypeStruct((rows * C, half * dim), BF16),
            jax.ShapeDtypeStruct((rows * C, 2 * half * dim), BF16),
        ],
        compiler_params=params(24),
        name="collect",
    )(row_out, chunks)


def attn_grad_kernel(n, dim, last, ids, grad_ref, *refs):
    blocks, refs = refs[:n], refs[n:]
    step = pl.program_id(0)
    if last:
        so_far, row_ref, chunk_ref, weight, sem, total = refs
    else:
        total, weight, sem = refs
    tokens = grad_ref.shape[0]
    tile = tokens // 4

    @pl.when(step == 0)
    def _():
        for d in range(n):
            pltpu.make_async_copy(blocks[d], weight.at[d], sem.at[d]).start()
        total[...] = so_far[...] if last else jnp.zeros_like(total)

    pltpu.make_async_copy(blocks[0], weight.at[step], sem.at[step]).wait()

    @pl.loop(0, tokens, step=tile)
    def _(at):
        at = pl.multiple_of(at, tile)
        total[pl.ds(at, tile)] += dot(grad_ref[pl.ds(at, tile)], weight[step], ((1,), (1,)))

    if last:

        @pl.when(step == n - 1)
        def _():
            places, half, rows, width, _ = chunk_ref.shape
            for head in range(half):
                row_ref[:, head * dim : (head + 1) * dim] = total[:, 2 * head * dim : (2 * head + 1) * dim].astype(BF16)
                for d in range(places):
                    for row in range(rows):
                        at = row * C + d * width
                        part = total[at : at + width, (2 * head + 1) * dim : (2 * head + 2) * dim]
                        chunk_ref[d, head, row] = part.astype(BF16)


def attn_grad(ids, out_grad, blocks, so_far, dim):
    m, (span, depth), last = len(blocks), blocks[0].shape, so_far is not None
    tokens, model = out_grad.shape
    n, half = model // depth, span // dim // 2
    total = jax.ShapeDtypeStruct((tokens, span), F32)
    whole = pl.BlockSpec((tokens, span), lambda b, ids: (0, 0))
    chunk = jax.ShapeDtypeStruct((n, half, tokens // C, C // n, dim), BF16)
    scratch = [pltpu.VMEM((m, span, depth), BF16), pltpu.SemaphoreType.DMA((m,))]
    return pl.pallas_call(
        functools.partial(attn_grad_kernel, m, dim, last),
        grid_spec=pltpu.PrefetchScalarGridSpec(
            num_scalar_prefetch=1,
            grid=(m,),
            in_specs=[pl.BlockSpec((tokens, depth), lambda b, ids: (0, ids[b]))]
            + [pl.BlockSpec(memory_space=pl.ANY)] * m
            + [whole] * last,
            out_specs=[
                pl.BlockSpec((tokens, half * dim), lambda b, ids: (0, 0)),
                pl.BlockSpec(chunk.shape, lambda b, ids: (0, 0, 0, 0, 0)),
            ]
            if last
            else whole,
            scratch_shapes=scratch + [pltpu.VMEM(total.shape, F32)] * last,
        ),
        out_shape=[jax.ShapeDtypeStruct((tokens, half * dim), BF16), chunk] if last else total,
        compiler_params=params(60),
        cost_estimate=pl.CostEstimate(
            flops=2 * tokens * span * depth * m,
            bytes_accessed=2 * m * depth * (tokens + span) + 4 * tokens * span,
            transcendentals=0,
        ),
        name="attn_grad",
    )(ids, out_grad, *blocks, *([so_far] if last else []))


def layer_kernel(n, count, adds, ids, wanted, flat_ref, *refs):
    blocks, extra, out_ref = refs[:n], refs[n : n + adds], refs[n + adds]
    weight, sem = refs[n + adds + 1 :]
    step = pl.program_id(0)
    tokens = flat_ref.shape[0]
    tile = tokens // 4

    @pl.when(step == 0)
    def _():
        for s in range(count):
            for d in range(n):

                @pl.when(ids[d] == wanted[s])
                def _():
                    pltpu.make_async_copy(blocks[d], weight.at[s], sem.at[s]).start()

    pltpu.make_async_copy(blocks[0], weight.at[step], sem.at[step]).wait()

    @pl.loop(0, tokens, step=tile)
    def _(at):
        at = pl.multiple_of(at, tile)
        value = dot(flat_ref[pl.ds(at, tile)], weight[step], ((1,), (0,)))
        for ref in extra:
            value = value + ref[pl.ds(at, tile)].astype(F32)
        out_ref[pl.ds(at, tile)] = value.astype(BF16)


def layer_part(ids, flat, blocks, wanted, extra, first):
    n, (span, depth) = len(blocks), blocks[0].shape
    tokens, count = flat.shape[0], wanted.shape[0]
    by_column = pl.BlockSpec((tokens, depth), lambda s, ids, wanted: (0, s))
    return pl.pallas_call(
        functools.partial(layer_kernel, n, count, len(extra)),
        grid_spec=pltpu.PrefetchScalarGridSpec(
            num_scalar_prefetch=2,
            grid=(count,),
            in_specs=[pl.BlockSpec((tokens, span), lambda s, ids, wanted: (0, 0))]
            + [pl.BlockSpec(memory_space=pl.ANY)] * n
            + [pl.BlockSpec((tokens, depth), functools.partial(lambda f, s, ids, wanted: (0, s + f), f)) for f in first],
            out_specs=by_column,
            scratch_shapes=[pltpu.VMEM((count, span, depth), BF16), pltpu.SemaphoreType.DMA((count,))],
        ),
        out_shape=jax.ShapeDtypeStruct((tokens, count * depth), BF16),
        compiler_params=params(60),
        cost_estimate=pl.CostEstimate(
            flops=2 * tokens * span * depth * count,
            bytes_accessed=2 * (count * depth * (tokens + span) + tokens * span),
            transcendentals=0,
        ),
        name="layer_part",
    )(ids, wanted, flat, *blocks, *extra)


def proj_kernel(lead, adds, dim, order, flat_ref, grad_ref, *refs):
    extra, outs, turned = refs[:adds], refs[adds:-1], refs[-1]
    step = pl.program_id(0)
    span = flat_ref.shape[1]

    @pl.when(step == 0)
    def _():
        for at in range(0, span, dim):
            turned[at : at + dim] = flat_ref[:, at : at + dim].T

    def value(at):
        out = dot(turned[at : at + dim], grad_ref[...], ((1,), (0,)))
        for ref in extra:
            out = out + ref[at : at + dim].astype(F32)
        return out.astype(BF16)

    @pl.when(step < lead)
    def _():
        for at in range(0, span, dim):
            outs[0][at : at + dim] = value(at)

    @pl.when(step >= lead)
    def _():
        for at in range(0, span, dim):
            outs[-1][at : at + dim] = value(at)


def proj_part(order, flat, out_grad, extra, depth, dim, lead):
    tokens, span = flat.shape
    count = order.shape[0]
    sizes = [size for size in (lead, count - lead) if size]
    places = [lambda s, order: (jnp.minimum(s, lead - 1), 0, 0), lambda s, order: (jnp.maximum(s - lead, 0), 0, 0)]
    return pl.pallas_call(
        functools.partial(proj_kernel, lead, len(extra), dim),
        grid_spec=pltpu.PrefetchScalarGridSpec(
            num_scalar_prefetch=1,
            grid=(count,),
            in_specs=[
                pl.BlockSpec((tokens, span), lambda s, order: (0, 0)),
                pl.BlockSpec((tokens, depth), lambda s, order: (0, order[s])),
            ]
            + [pl.BlockSpec((pl.squeezed, span, depth), lambda s, order: (s, 0, 0))] * len(extra),
            out_specs=[pl.BlockSpec((pl.squeezed, span, depth), place) for place in places[-len(sizes) :]],
            scratch_shapes=[pltpu.VMEM((span, tokens), BF16)],
        ),
        out_shape=[jax.ShapeDtypeStruct((size, span, depth), BF16) for size in sizes],
        compiler_params=params(60),
        cost_estimate=pl.CostEstimate(
            flops=2 * tokens * span * depth * count,
            bytes_accessed=2 * (count * depth * (tokens + span * (1 + len(extra))) + tokens * span),
            transcendentals=0,
        ),
        name="proj_part",
    )(order, flat, out_grad, *extra)


def row_blocks(length):
    step = length // 2
    return [(start, step) for start in range(0, length, step)]


def row_probs(q, k, start, step, scale):
    scores = dot(q, k, ((1,), (1,))) * scale
    place = lax.broadcasted_iota(jnp.int32, scores.shape, 0) + start
    seen = lax.broadcasted_iota(jnp.int32, scores.shape, 1)
    return softmax(jnp.where(place >= seen, scores, -jnp.inf))


def row_forward_kernel(scale, q_ref, k_ref, v_ref, o_ref):
    for start, step in row_blocks(q_ref.shape[0]):
        stop = start + step
        probs = row_probs(q_ref[start:stop], k_ref[:stop], start, step, scale)
        o_ref[start:stop] = dot(probs.astype(BF16), v_ref[:stop], ((1,), (0,))).astype(BF16)


def row_forward(q, k, v):
    half, tokens, dim = q.shape
    by_head = pl.BlockSpec((pl.squeezed, C, dim), lambda r, h: (h, r, 0))
    return pl.pallas_call(
        functools.partial(row_forward_kernel, dim**-0.5),
        grid=(tokens // C, half),
        in_specs=[by_head] * 3,
        out_specs=pl.BlockSpec((C, dim), lambda r, h: (r, h)),
        out_shape=jax.ShapeDtypeStruct((tokens, half * dim), BF16),
        compiler_params=params(60),
        cost_estimate=pl.CostEstimate(
            flops=4 * tokens * C * half * dim, bytes_accessed=8 * tokens * half * dim, transcendentals=tokens * C * half
        ),
        name="row_forward",
    )(q, k, v)


def row_backward_kernel(scale, q_ref, k_ref, v_ref, g_ref, dq_ref, dk_ref, dv_ref, k_sum, v_sum):
    k_sum[...] = jnp.zeros_like(k_sum)
    v_sum[...] = jnp.zeros_like(v_sum)
    for start, step in row_blocks(q_ref.shape[0]):
        stop = start + step
        q, k, grad = q_ref[start:stop], k_ref[:stop], g_ref[start:stop]
        probs = row_probs(q, k, start, step, scale)
        prob_grad = dot(grad, v_ref[:stop], ((1,), (1,)))
        inner = jnp.sum(probs * prob_grad, axis=-1, keepdims=True)
        score_low = (probs * (prob_grad - inner)).astype(BF16)
        dq_ref[start:stop] = (dot(score_low, k, ((1,), (0,))) * scale).astype(BF16)
        k_sum[:stop] += dot(score_low, q, ((0,), (0,)))
        v_sum[:stop] += dot(probs.astype(BF16), grad, ((0,), (0,)))
    dk_ref[...] = (k_sum[...] * scale).astype(BF16)
    dv_ref[...] = v_sum[...].astype(BF16)


def row_backward(q, k, v, grad):
    half, tokens, dim = q.shape
    by_head = pl.BlockSpec((pl.squeezed, C, dim), lambda r, h: (h, r, 0))
    return pl.pallas_call(
        functools.partial(row_backward_kernel, dim**-0.5),
        grid=(tokens // C, half),
        in_specs=[by_head] * 3 + [pl.BlockSpec((C, dim), lambda r, h: (r, h))],
        out_specs=[by_head] * 3,
        out_shape=[jax.ShapeDtypeStruct(q.shape, BF16)] * 3,
        scratch_shapes=[pltpu.VMEM((C, dim), F32)] * 2,
        compiler_params=params(60),
        cost_estimate=pl.CostEstimate(
            flops=10 * tokens * C * half * dim, bytes_accessed=14 * tokens * half * dim, transcendentals=tokens * C * half
        ),
        name="row_backward",
    )(q, k, v, grad)


def column_mask(size):
    def parts(axis):
        place = lax.broadcasted_iota(jnp.int32, (size, size), axis)
        return place // LANE, place % LANE

    row_q, column_q = parts(0)
    row_k, column_k = parts(1)
    return (column_q == column_k) & (row_q >= row_k)


def gathered(ref, index, at):
    n, rows = ref.shape[0], ref.shape[-3]
    return jnp.concatenate([ref[(d, *index, row, pl.ds(at, LANE))] for d in range(n) for row in range(rows)], axis=0)


def scattered(ref, index, at, value):
    n, rows = ref.shape[0], ref.shape[-3]
    for d in range(n):
        for row in range(rows):
            line = d * rows + row
            ref[(d, *index, row, pl.ds(at, LANE))] = value[line * LANE : (line + 1) * LANE]


def column_probs(bias, q, k, scale):
    return softmax(dot(q, k, ((1,), (1,))) * scale + bias[...])


def column_forward_kernel(scale, chunk_ref, out_ref, bias):
    half, width = chunk_ref.shape[2], chunk_ref.shape[4]
    bias[...] = jnp.where(column_mask(bias.shape[0]), 0.0, -jnp.inf)
    blocks = width // LANE

    @pl.loop(0, half * blocks)
    def _(step):
        head, at = step // blocks, pl.multiple_of(step % blocks * LANE, LANE)
        q, k, v = (gathered(chunk_ref, (array, head), at) for array in range(3))
        probs = column_probs(bias, q, k, scale)
        scattered(out_ref, (head,), at, dot(probs.astype(BF16), v, ((1,), (0,))).astype(BF16))


def column_forward(chunks):
    n, _, half, rows, width, dim = chunks.shape
    size = n * rows * LANE
    return pl.pallas_call(
        functools.partial(column_forward_kernel, dim**-0.5),
        in_specs=[VMEM],
        out_specs=VMEM,
        out_shape=jax.ShapeDtypeStruct((n, half, rows, width, dim), BF16),
        scratch_shapes=[pltpu.VMEM((size, size), F32)],
        compiler_params=params(24),
        cost_estimate=pl.CostEstimate(
            flops=4 * size * size * dim * half * width // LANE,
            bytes_accessed=8 * n * half * rows * width * dim,
            transcendentals=size * size * half * width // LANE,
        ),
        name="column_forward",
    )(chunks)


def column_backward_kernel(scale, chunk_ref, grad_ref, out_ref, bias):
    half, width = chunk_ref.shape[2], chunk_ref.shape[4]
    bias[...] = jnp.where(column_mask(bias.shape[0]), 0.0, -jnp.inf)
    blocks = width // LANE

    @pl.loop(0, half * blocks)
    def _(step):
        head, at = step // blocks, pl.multiple_of(step % blocks * LANE, LANE)
        q, k, v = (gathered(chunk_ref, (array, head), at) for array in range(3))
        grad = gathered(grad_ref, (head,), at)
        probs = column_probs(bias, q, k, scale)
        prob_grad = dot(grad, v, ((1,), (1,)))
        inner = jnp.sum(probs * prob_grad, axis=-1, keepdims=True)
        score_low = (probs * (prob_grad - inner)).astype(BF16)
        scattered(out_ref, (0, head), at, (dot(score_low, k, ((1,), (0,))) * scale).astype(BF16))
        scattered(out_ref, (1, head), at, (dot(score_low, q, ((0,), (0,))) * scale).astype(BF16))
        scattered(out_ref, (2, head), at, dot(probs.astype(BF16), grad, ((0,), (0,))).astype(BF16))


def column_backward(chunks, grads):
    n, _, half, rows, width, dim = chunks.shape
    size = n * rows * LANE
    return pl.pallas_call(
        functools.partial(column_backward_kernel, dim**-0.5),
        in_specs=[VMEM] * 2,
        out_specs=VMEM,
        out_shape=jax.ShapeDtypeStruct(chunks.shape, BF16),
        scratch_shapes=[pltpu.VMEM((size, size), F32)],
        compiler_params=params(24),
        cost_estimate=pl.CostEstimate(
            flops=10 * size * size * dim * half * width // LANE,
            bytes_accessed=14 * n * half * rows * width * dim,
            transcendentals=size * size * half * width // LANE,
        ),
        name="column_backward",
    )(chunks, grads)


PAIRS = [(0, 1), (1, 0), (2, 3), (3, 2)]
INWARD = [(0, 1), (3, 2)]
CROSS = [(1, 2), (2, 1)]
OUTWARD = [(1, 0), (2, 3)]


def after(value, *done):
    return lax.optimization_barrier((value, *done))[0]


class Links:
    def __init__(self, n, window):
        self.n, self.inner, self.window, self.sent = n, n // 4, window, []

    def send(self, value, pairs):
        over = len(self.sent) - self.window + 1
        if over > 0:
            value = after(value, *self.sent[max(0, over - self.window) : over])
        out = lax.ppermute(value, "ctx", pairs)
        self.sent.append(out)
        return out

    def along(self, value, pairs):
        return self.send(value, [(a * self.inner + y, b * self.inner + y) for a, b in pairs for y in range(self.inner)])

    def flip(self, value, d):
        return self.send(value, [(place, place ^ d) for place in range(self.n)])


def swap(chunks):
    return lax.all_to_all(chunks, "ctx", split_axis=0, concat_axis=0, tiled=True)


class LayerSum:
    def __init__(self, ids, flat, blocks, heads_n):
        self.ids, self.flat, self.blocks, self.heads_n = ids, flat, blocks, heads_n
        self.mine = lax.axis_index("head").astype(jnp.int32)
        self.per = len(blocks) // heads_n
        self.even = list(range(0, heads_n, 2))

    def part(self, offsets, extra, first):
        wanted = [(self.mine ^ g) * self.per + b for g in offsets for b in range(self.per)]
        wanted = jnp.stack(wanted).astype(jnp.int32)
        return layer_part(self.ids, self.flat, self.blocks, wanted, extra, first)

    def move(self, part, g):
        return lax.ppermute(part, "head", [(place, place ^ g) for place in range(self.heads_n)])

    def start(self):
        self.first = self.part([g + 1 for g in self.even], [], [])
        self.near = self.move(self.first, 1)

    def turn(self, done):
        self.flat = after(self.flat, done)
        self.parts = [self.part([g], [self.near], [g // 2 * self.per]) for g in self.even[1:]]
        self.far = [self.move(part, g) for part, g in zip(self.parts, self.even[1:])]

    def finish(self):
        return self.part([0], [self.near] + self.far, [0] * (1 + len(self.far)))


def on_device(queries, keys, values, out_grad, wo, *, n, heads_n):
    tokens, heads, dim = queries.shape
    half, depth, inner = heads // 2, wo.shape[1], n // 4
    me = lax.axis_index("ctx").astype(jnp.int32)
    line, spot = me // inner, me % inner
    middle, upper = (line == 1) | (line == 2), line < 2
    far, close = [jnp.where(upper, 2, 1), jnp.where(upper, 3, 0)], [line ^ 1, line]
    links = Links(n, 5)

    def around(block):
        return [block if e == 0 else links.flip(block, e) for e in range(inner)]

    def targets(owners, e):
        return jnp.stack([owner * inner + (spot ^ e) for owner in owners]).astype(jnp.int32)

    def leaving(flat, owners):
        return [proj_part(targets(owners, e), flat, out_grad, [], depth, dim, 0)[0] for e in range(1, inner)]

    def exchanged(parts):
        return [links.flip(part, e + 1) for e, part in enumerate(parts)]

    def summed(flat, owners, theirs, lead):
        return proj_part(targets(owners, 0), flat, out_grad, theirs, depth, dim, lead)

    def add(*terms):
        return sum(term.astype(F32) for term in terms).astype(BF16)

    near = links.along(wo, PAIRS)
    cross_own = links.along(wo, CROSS)
    own_blocks = around(wo)
    chunks, by_head = split_inputs(queries, keys, values, n)
    row_out = row_forward(*by_head)
    row_far, row_close = leaving(row_out, far), leaving(row_out, close)
    near = after(near, chunks, *own_blocks[1:])
    near_blocks = around(near)
    cross_near = links.along(near, CROSS)
    out_own = links.along(cross_own, OUTWARD)
    chunks = swap(after(chunks, *near_blocks, cross_near, out_own, *row_far, *row_close))
    out_near = links.along(cross_near, OUTWARD)
    far_own = jnp.where(middle, cross_own, out_own)
    far_own_blocks = around(far_own)
    far_near = jnp.where(middle, cross_near, out_near)
    far_near_blocks = around(far_near)
    blocks = own_blocks + near_blocks + far_own_blocks + far_near_blocks
    ids = [owner * inner + (spot ^ e) for owner in (line, line ^ 1, *far) for e in range(inner)]
    ids = jnp.stack(ids).astype(jnp.int32)
    early = n - inner

    outs = column_forward(after(chunks, *far_own_blocks))
    column_part = swap(outs)
    so_far = attn_grad(ids[:early], after(out_grad, outs), blocks[:early], None, dim)
    grad_row, grads = attn_grad(ids[early:], out_grad, blocks[early:], so_far, dim)
    row_far = exchanged([after(part, so_far, *far_near_blocks) for part in row_far])
    column_out, flat = collect(row_out, column_part)
    column_far, column_close = leaving(column_out, far), leaving(column_out, close)
    grads = swap(after(grads, column_part, *row_far, *column_far, *column_close))
    column_far = exchanged(column_far)
    (row_far,) = summed(after(row_out, *column_close), far, row_far, 0)
    row_far_in = links.along(row_far, INWARD)
    layer = LayerSum(ids, after(flat, row_far), blocks, heads_n)
    layer.start()
    row_close = exchanged([after(part, *column_far) for part in row_close])
    (column_far,) = summed(column_out, far, column_far, 0)
    column_far_in = links.along(column_far, INWARD)
    row_middle = add(row_far, row_far_in)
    row_cross = links.along(row_middle, CROSS)
    gradients = column_backward(chunks, after(grads, column_far, row_middle, layer.first))
    column_close = exchanged(column_close)
    column_cross = links.along(add(column_far, column_far_in), CROSS)
    column_grads = swap(after(gradients, row_cross, column_cross, *row_close, *column_close))

    layer.turn(gradients)
    row_near, row_own = summed(after(row_out, gradients), close, row_close, 1)
    row_near_in = links.along(row_near[0], INWARD)
    column_near, column_own = summed(after(column_out, gradients), close, column_close, 1)
    column_near_in = links.along(column_near[0], INWARD)
    row_grads = row_backward(*by_head, after(grad_row, gradients))
    row_back = links.along(add(row_near[0], row_cross[1]), OUTWARD)
    column_back = links.along(add(column_near[0], column_cross[1]), OUTWARD)
    layer_out = layer.finish()
    ahead = after(row_grads[0], layer_out, row_back, column_back, row_near_in, column_near_in)
    gradients = join_gradients(column_grads, [ahead, *row_grads[1:]])

    proj_row = add(row_own[0], row_near_in, row_cross[0], row_back)
    proj_column = add(column_own[0], column_near_in, column_cross[0], column_back)
    shape = (half, dim, depth)
    proj_grad = jnp.stack([proj_row.reshape(shape), proj_column.reshape(shape)], axis=1)
    return (layer_out, *gradients, proj_grad.reshape(heads * dim, depth))


def solution(mesh):
    in_specs = (
        P("ctx", "head", None),
        P("ctx", "head", None),
        P("ctx", "head", None),
        P("ctx", None),
        P("head", "ctx"),
    )
    out_specs = (
        P("ctx", "head"),
        P("ctx", "head", None),
        P("ctx", "head", None),
        P("ctx", "head", None),
        P("head", "ctx"),
    )
    return jax.shard_map(
        functools.partial(on_device, n=mesh.shape["ctx"], heads_n=mesh.shape["head"]),
        mesh=mesh,
        in_specs=in_specs,
        out_specs=out_specs,
        check_vma=False,
    )
```

```python
import functools

import jax
import jax.numpy as jnp
from jax import lax
from jax.experimental import pallas as pl
from jax.experimental.pallas import tpu as pltpu
from jax.sharding import PartitionSpec as P

C = 512
LANE = 16
VMEM = pl.BlockSpec(memory_space=pltpu.VMEM)
BF16 = jnp.bfloat16
F32 = jnp.float32


def params(mib):
    return pltpu.CompilerParams(vmem_limit_bytes=mib * 1024 * 1024)


def dot(a, b, dims):
    return lax.dot_general(a, b, (dims, ((), ())), preferred_element_type=F32)


def softmax(scores):
    highest = jnp.max(scores, axis=-1, keepdims=True)
    lifted = jnp.exp(scores - highest)
    return lifted * (1.0 / jnp.sum(lifted, axis=-1, keepdims=True))


def split_kernel(q_ref, k_ref, v_ref, chunk_ref, *rest):
    row_refs, wide = rest[:3], rest[3]
    n, width = chunk_ref.shape[0], chunk_ref.shape[3]
    span, heads, dim = q_ref.shape
    for array, ref in enumerate((q_ref, k_ref, v_ref)):
        wide[...] = ref[...].astype(F32).reshape(span * heads, dim)
        for head in range(heads // 2):
            row_refs[array][head] = wide[pl.ds(2 * head, span, stride=heads), :].astype(BF16)
            for d in range(n):
                odd = wide[pl.ds(d * width * heads + 2 * head + 1, width, stride=heads), :]
                chunk_ref[d, array, head] = odd.astype(BF16)


def split_inputs(queries, keys, values, n):
    tokens, heads, dim = queries.shape
    rows, width, half = tokens // C, C // n, heads // 2
    by_head = jax.ShapeDtypeStruct((half, tokens, dim), BF16)
    out = pl.pallas_call(
        split_kernel,
        grid=(rows,),
        in_specs=[pl.BlockSpec((C, heads, dim), lambda r: (r, 0, 0))] * 3,
        out_specs=[pl.BlockSpec((n, 3, half, pl.squeezed, width, dim), lambda r: (0, 0, 0, r, 0, 0))]
        + [pl.BlockSpec((half, C, dim), lambda r: (0, r, 0))] * 3,
        scratch_shapes=[pltpu.VMEM((C * heads, dim), F32)],
        out_shape=[jax.ShapeDtypeStruct((n, 3, half, rows, width, dim), BF16)] + [by_head] * 3,
        compiler_params=params(60),
        name="split_inputs",
    )(queries, keys, values)
    return out[0], out[1:]


def join_kernel(chunk_ref, *refs):
    row_refs, outs, wide = refs[:3], refs[3:6], refs[6]
    n, width = chunk_ref.shape[0], chunk_ref.shape[3]
    span, heads, dim = outs[0].shape
    for array in range(3):
        for head in range(heads // 2):
            wide[pl.ds(2 * head, span, stride=heads), :] = row_refs[array][head].astype(F32)
            for d in range(n):
                part = chunk_ref[d, array, head].astype(F32)
                wide[pl.ds(d * width * heads + 2 * head + 1, width, stride=heads), :] = part
        outs[array][...] = wide[...].reshape(span, heads, dim).astype(BF16)


def join_gradients(chunks, by_head):
    n, _, half, rows, width, dim = chunks.shape
    tokens, heads = by_head[0].shape[1], 2 * half
    return pl.pallas_call(
        join_kernel,
        grid=(rows,),
        in_specs=[pl.BlockSpec((n, 3, half, pl.squeezed, width, dim), lambda r: (0, 0, 0, r, 0, 0))]
        + [pl.BlockSpec((half, C, dim), lambda r: (0, r, 0))] * 3,
        out_specs=[pl.BlockSpec((C, heads, dim), lambda r: (r, 0, 0))] * 3,
        scratch_shapes=[pltpu.VMEM((C * heads, dim), F32)],
        out_shape=[jax.ShapeDtypeStruct((tokens, heads, dim), BF16)] * 3,
        compiler_params=params(60),
        name="join_gradients",
    )(chunks, *by_head)


def collect_kernel(row_ref, chunk_ref, flat_ref, both_ref):
    n, half, rows, width, dim = chunk_ref.shape
    for head in range(half):
        both_ref[:, 2 * head * dim : (2 * head + 1) * dim] = row_ref[:, head * dim : (head + 1) * dim]
        for d in range(n):
            for row in range(rows):
                part = chunk_ref[d, head, row]
                at = row * C + d * width
                flat_ref[at : at + width, head * dim : (head + 1) * dim] = part
                both_ref[at : at + width, (2 * head + 1) * dim : (2 * head + 2) * dim] = part


def collect(row_out, chunks):
    n, half, rows, width, dim = chunks.shape
    return pl.pallas_call(
        collect_kernel,
        in_specs=[VMEM] * 2,
        out_specs=[VMEM] * 2,
        out_shape=[
            jax.ShapeDtypeStruct((rows * C, half * dim), BF16),
            jax.ShapeDtypeStruct((rows * C, 2 * half * dim), BF16),
        ],
        compiler_params=params(24),
        name="collect",
    )(row_out, chunks)


def attn_grad_kernel(n, dim, last, ids, grad_ref, *refs):
    blocks, refs = refs[:n], refs[n:]
    step = pl.program_id(0)
    if last:
        so_far, row_ref, chunk_ref, weight, sem, total = refs
    else:
        total, weight, sem = refs
    tokens = grad_ref.shape[0]
    tile = tokens // 4

    @pl.when(step == 0)
    def _():
        for d in range(n):
            pltpu.make_async_copy(blocks[d], weight.at[d], sem.at[d]).start()
        total[...] = so_far[...] if last else jnp.zeros_like(total)

    pltpu.make_async_copy(blocks[0], weight.at[step], sem.at[step]).wait()

    @pl.loop(0, tokens, step=tile)
    def _(at):
        at = pl.multiple_of(at, tile)
        total[pl.ds(at, tile)] += dot(grad_ref[pl.ds(at, tile)], weight[step], ((1,), (1,)))

    if last:

        @pl.when(step == n - 1)
        def _():
            places, half, rows, width, _ = chunk_ref.shape
            for head in range(half):
                row_ref[:, head * dim : (head + 1) * dim] = total[:, 2 * head * dim : (2 * head + 1) * dim].astype(BF16)
                for d in range(places):
                    for row in range(rows):
                        at = row * C + d * width
                        part = total[at : at + width, (2 * head + 1) * dim : (2 * head + 2) * dim]
                        chunk_ref[d, head, row] = part.astype(BF16)


def attn_grad(ids, out_grad, blocks, so_far, dim):
    m, (span, depth), last = len(blocks), blocks[0].shape, so_far is not None
    tokens, model = out_grad.shape
    n, half = model // depth, span // dim // 2
    total = jax.ShapeDtypeStruct((tokens, span), F32)
    whole = pl.BlockSpec((tokens, span), lambda b, ids: (0, 0))
    chunk = jax.ShapeDtypeStruct((n, half, tokens // C, C // n, dim), BF16)
    scratch = [pltpu.VMEM((m, span, depth), BF16), pltpu.SemaphoreType.DMA((m,))]
    return pl.pallas_call(
        functools.partial(attn_grad_kernel, m, dim, last),
        grid_spec=pltpu.PrefetchScalarGridSpec(
            num_scalar_prefetch=1,
            grid=(m,),
            in_specs=[pl.BlockSpec((tokens, depth), lambda b, ids: (0, ids[b]))]
            + [pl.BlockSpec(memory_space=pl.ANY)] * m
            + [whole] * last,
            out_specs=[
                pl.BlockSpec((tokens, half * dim), lambda b, ids: (0, 0)),
                pl.BlockSpec(chunk.shape, lambda b, ids: (0, 0, 0, 0, 0)),
            ]
            if last
            else whole,
            scratch_shapes=scratch + [pltpu.VMEM(total.shape, F32)] * last,
        ),
        out_shape=[jax.ShapeDtypeStruct((tokens, half * dim), BF16), chunk] if last else total,
        compiler_params=params(60),
        cost_estimate=pl.CostEstimate(
            flops=2 * tokens * span * depth * m,
            bytes_accessed=2 * m * depth * (tokens + span) + 4 * tokens * span,
            transcendentals=0,
        ),
        name="attn_grad",
    )(ids, out_grad, *blocks, *([so_far] if last else []))


def layer_kernel(n, count, adds, ids, wanted, flat_ref, *refs):
    blocks, extra, out_ref = refs[:n], refs[n : n + adds], refs[n + adds]
    weight, sem = refs[n + adds + 1 :]
    step = pl.program_id(0)
    tokens = flat_ref.shape[0]
    tile = tokens // 4

    @pl.when(step == 0)
    def _():
        for s in range(count):
            for d in range(n):

                @pl.when(ids[d] == wanted[s])
                def _():
                    pltpu.make_async_copy(blocks[d], weight.at[s], sem.at[s]).start()

    pltpu.make_async_copy(blocks[0], weight.at[step], sem.at[step]).wait()

    @pl.loop(0, tokens, step=tile)
    def _(at):
        at = pl.multiple_of(at, tile)
        value = dot(flat_ref[pl.ds(at, tile)], weight[step], ((1,), (0,)))
        for ref in extra:
            value = value + ref[pl.ds(at, tile)].astype(F32)
        out_ref[pl.ds(at, tile)] = value.astype(BF16)


def layer_part(ids, flat, blocks, wanted, extra, first):
    n, (span, depth) = len(blocks), blocks[0].shape
    tokens, count = flat.shape[0], wanted.shape[0]
    by_column = pl.BlockSpec((tokens, depth), lambda s, ids, wanted: (0, s))
    return pl.pallas_call(
        functools.partial(layer_kernel, n, count, len(extra)),
        grid_spec=pltpu.PrefetchScalarGridSpec(
            num_scalar_prefetch=2,
            grid=(count,),
            in_specs=[pl.BlockSpec((tokens, span), lambda s, ids, wanted: (0, 0))]
            + [pl.BlockSpec(memory_space=pl.ANY)] * n
            + [pl.BlockSpec((tokens, depth), functools.partial(lambda f, s, ids, wanted: (0, s + f), f)) for f in first],
            out_specs=by_column,
            scratch_shapes=[pltpu.VMEM((count, span, depth), BF16), pltpu.SemaphoreType.DMA((count,))],
        ),
        out_shape=jax.ShapeDtypeStruct((tokens, count * depth), BF16),
        compiler_params=params(60),
        cost_estimate=pl.CostEstimate(
            flops=2 * tokens * span * depth * count,
            bytes_accessed=2 * (count * depth * (tokens + span) + tokens * span),
            transcendentals=0,
        ),
        name="layer_part",
    )(ids, wanted, flat, *blocks, *extra)


def proj_kernel(lead, adds, dim, order, flat_ref, grad_ref, *refs):
    extra, outs, turned = refs[:adds], refs[adds:-1], refs[-1]
    step = pl.program_id(0)
    span = flat_ref.shape[1]

    @pl.when(step == 0)
    def _():
        for at in range(0, span, dim):
            turned[at : at + dim] = flat_ref[:, at : at + dim].T

    def value(at):
        out = dot(turned[at : at + dim], grad_ref[...], ((1,), (0,)))
        for ref in extra:
            out = out + ref[at : at + dim].astype(F32)
        return out.astype(BF16)

    @pl.when(step < lead)
    def _():
        for at in range(0, span, dim):
            outs[0][at : at + dim] = value(at)

    @pl.when(step >= lead)
    def _():
        for at in range(0, span, dim):
            outs[-1][at : at + dim] = value(at)


def proj_part(order, flat, out_grad, extra, depth, dim, lead):
    tokens, span = flat.shape
    count = order.shape[0]
    sizes = [size for size in (lead, count - lead) if size]
    places = [lambda s, order: (jnp.minimum(s, lead - 1), 0, 0), lambda s, order: (jnp.maximum(s - lead, 0), 0, 0)]
    return pl.pallas_call(
        functools.partial(proj_kernel, lead, len(extra), dim),
        grid_spec=pltpu.PrefetchScalarGridSpec(
            num_scalar_prefetch=1,
            grid=(count,),
            in_specs=[
                pl.BlockSpec((tokens, span), lambda s, order: (0, 0)),
                pl.BlockSpec((tokens, depth), lambda s, order: (0, order[s])),
            ]
            + [pl.BlockSpec((pl.squeezed, span, depth), lambda s, order: (s, 0, 0))] * len(extra),
            out_specs=[pl.BlockSpec((pl.squeezed, span, depth), place) for place in places[-len(sizes) :]],
            scratch_shapes=[pltpu.VMEM((span, tokens), BF16)],
        ),
        out_shape=[jax.ShapeDtypeStruct((size, span, depth), BF16) for size in sizes],
        compiler_params=params(60),
        cost_estimate=pl.CostEstimate(
            flops=2 * tokens * span * depth * count,
            bytes_accessed=2 * (count * depth * (tokens + span * (1 + len(extra))) + tokens * span),
            transcendentals=0,
        ),
        name="proj_part",
    )(order, flat, out_grad, *extra)


def row_blocks(length):
    step = length // 2
    return [(start, step) for start in range(0, length, step)]


def row_probs(q, k, start, step, scale):
    scores = dot(q, k, ((1,), (1,))) * scale
    place = lax.broadcasted_iota(jnp.int32, scores.shape, 0) + start
    seen = lax.broadcasted_iota(jnp.int32, scores.shape, 1)
    return softmax(jnp.where(place >= seen, scores, -jnp.inf))


def row_forward_kernel(scale, q_ref, k_ref, v_ref, o_ref):
    for start, step in row_blocks(q_ref.shape[0]):
        stop = start + step
        probs = row_probs(q_ref[start:stop], k_ref[:stop], start, step, scale)
        o_ref[start:stop] = dot(probs.astype(BF16), v_ref[:stop], ((1,), (0,))).astype(BF16)


def row_forward(q, k, v):
    half, tokens, dim = q.shape
    by_head = pl.BlockSpec((pl.squeezed, C, dim), lambda r, h: (h, r, 0))
    return pl.pallas_call(
        functools.partial(row_forward_kernel, dim**-0.5),
        grid=(tokens // C, half),
        in_specs=[by_head] * 3,
        out_specs=pl.BlockSpec((C, dim), lambda r, h: (r, h)),
        out_shape=jax.ShapeDtypeStruct((tokens, half * dim), BF16),
        compiler_params=params(60),
        cost_estimate=pl.CostEstimate(
            flops=4 * tokens * C * half * dim, bytes_accessed=8 * tokens * half * dim, transcendentals=tokens * C * half
        ),
        name="row_forward",
    )(q, k, v)


def row_backward_kernel(scale, q_ref, k_ref, v_ref, g_ref, dq_ref, dk_ref, dv_ref, k_sum, v_sum):
    k_sum[...] = jnp.zeros_like(k_sum)
    v_sum[...] = jnp.zeros_like(v_sum)
    for start, step in row_blocks(q_ref.shape[0]):
        stop = start + step
        q, k, grad = q_ref[start:stop], k_ref[:stop], g_ref[start:stop]
        probs = row_probs(q, k, start, step, scale)
        prob_grad = dot(grad, v_ref[:stop], ((1,), (1,)))
        inner = jnp.sum(probs * prob_grad, axis=-1, keepdims=True)
        score_low = (probs * (prob_grad - inner)).astype(BF16)
        dq_ref[start:stop] = (dot(score_low, k, ((1,), (0,))) * scale).astype(BF16)
        k_sum[:stop] += dot(score_low, q, ((0,), (0,)))
        v_sum[:stop] += dot(probs.astype(BF16), grad, ((0,), (0,)))
    dk_ref[...] = (k_sum[...] * scale).astype(BF16)
    dv_ref[...] = v_sum[...].astype(BF16)


def row_backward(q, k, v, grad):
    half, tokens, dim = q.shape
    by_head = pl.BlockSpec((pl.squeezed, C, dim), lambda r, h: (h, r, 0))
    return pl.pallas_call(
        functools.partial(row_backward_kernel, dim**-0.5),
        grid=(tokens // C, half),
        in_specs=[by_head] * 3 + [pl.BlockSpec((C, dim), lambda r, h: (r, h))],
        out_specs=[by_head] * 3,
        out_shape=[jax.ShapeDtypeStruct(q.shape, BF16)] * 3,
        scratch_shapes=[pltpu.VMEM((C, dim), F32)] * 2,
        compiler_params=params(60),
        cost_estimate=pl.CostEstimate(
            flops=10 * tokens * C * half * dim, bytes_accessed=14 * tokens * half * dim, transcendentals=tokens * C * half
        ),
        name="row_backward",
    )(q, k, v, grad)


def column_mask(size):
    def parts(axis):
        place = lax.broadcasted_iota(jnp.int32, (size, size), axis)
        return place // LANE, place % LANE

    row_q, column_q = parts(0)
    row_k, column_k = parts(1)
    return (column_q == column_k) & (row_q >= row_k)


def gathered(ref, index, at):
    n, rows = ref.shape[0], ref.shape[-3]
    return jnp.concatenate([ref[(d, *index, row, pl.ds(at, LANE))] for d in range(n) for row in range(rows)], axis=0)


def scattered(ref, index, at, value):
    n, rows = ref.shape[0], ref.shape[-3]
    for d in range(n):
        for row in range(rows):
            line = d * rows + row
            ref[(d, *index, row, pl.ds(at, LANE))] = value[line * LANE : (line + 1) * LANE]


def column_probs(bias, q, k, scale):
    return softmax(dot(q, k, ((1,), (1,))) * scale + bias[...])


def column_forward_kernel(scale, chunk_ref, out_ref, bias):
    half, width = chunk_ref.shape[2], chunk_ref.shape[4]
    bias[...] = jnp.where(column_mask(bias.shape[0]), 0.0, -jnp.inf)
    blocks = width // LANE

    @pl.loop(0, half * blocks)
    def _(step):
        head, at = step // blocks, pl.multiple_of(step % blocks * LANE, LANE)
        q, k, v = (gathered(chunk_ref, (array, head), at) for array in range(3))
        probs = column_probs(bias, q, k, scale)
        scattered(out_ref, (head,), at, dot(probs.astype(BF16), v, ((1,), (0,))).astype(BF16))


def column_forward(chunks):
    n, _, half, rows, width, dim = chunks.shape
    size = n * rows * LANE
    return pl.pallas_call(
        functools.partial(column_forward_kernel, dim**-0.5),
        in_specs=[VMEM],
        out_specs=VMEM,
        out_shape=jax.ShapeDtypeStruct((n, half, rows, width, dim), BF16),
        scratch_shapes=[pltpu.VMEM((size, size), F32)],
        compiler_params=params(24),
        cost_estimate=pl.CostEstimate(
            flops=4 * size * size * dim * half * width // LANE,
            bytes_accessed=8 * n * half * rows * width * dim,
            transcendentals=size * size * half * width // LANE,
        ),
        name="column_forward",
    )(chunks)


def column_backward_kernel(scale, chunk_ref, grad_ref, out_ref, bias):
    half, width = chunk_ref.shape[2], chunk_ref.shape[4]
    bias[...] = jnp.where(column_mask(bias.shape[0]), 0.0, -jnp.inf)
    blocks = width // LANE

    @pl.loop(0, half * blocks)
    def _(step):
        head, at = step // blocks, pl.multiple_of(step % blocks * LANE, LANE)
        q, k, v = (gathered(chunk_ref, (array, head), at) for array in range(3))
        grad = gathered(grad_ref, (head,), at)
        probs = column_probs(bias, q, k, scale)
        prob_grad = dot(grad, v, ((1,), (1,)))
        inner = jnp.sum(probs * prob_grad, axis=-1, keepdims=True)
        score_low = (probs * (prob_grad - inner)).astype(BF16)
        scattered(out_ref, (0, head), at, (dot(score_low, k, ((1,), (0,))) * scale).astype(BF16))
        scattered(out_ref, (1, head), at, (dot(score_low, q, ((0,), (0,))) * scale).astype(BF16))
        scattered(out_ref, (2, head), at, dot(probs.astype(BF16), grad, ((0,), (0,))).astype(BF16))


def column_backward(chunks, grads):
    n, _, half, rows, width, dim = chunks.shape
    size = n * rows * LANE
    return pl.pallas_call(
        functools.partial(column_backward_kernel, dim**-0.5),
        in_specs=[VMEM] * 2,
        out_specs=VMEM,
        out_shape=jax.ShapeDtypeStruct(chunks.shape, BF16),
        scratch_shapes=[pltpu.VMEM((size, size), F32)],
        compiler_params=params(24),
        cost_estimate=pl.CostEstimate(
            flops=10 * size * size * dim * half * width // LANE,
            bytes_accessed=14 * n * half * rows * width * dim,
            transcendentals=size * size * half * width // LANE,
        ),
        name="column_backward",
    )(chunks, grads)


PAIRS = [(0, 1), (1, 0), (2, 3), (3, 2)]
INWARD = [(0, 1), (3, 2)]
CROSS = [(1, 2), (2, 1)]
OUTWARD = [(1, 0), (2, 3)]


def after(value, *done):
    return lax.optimization_barrier((value, *done))[0]


class Links:
    def __init__(self, n, window):
        self.n, self.inner, self.window, self.sent = n, n // 4, window, []

    def send(self, value, pairs):
        over = len(self.sent) - self.window + 1
        if over > 0:
            value = after(value, *self.sent[max(0, over - self.window) : over])
        out = lax.ppermute(value, "ctx", pairs)
        self.sent.append(out)
        return out

    def along(self, value, pairs):
        return self.send(value, [(a * self.inner + y, b * self.inner + y) for a, b in pairs for y in range(self.inner)])

    def flip(self, value, d):
        return self.send(value, [(place, place ^ d) for place in range(self.n)])


def swap(chunks):
    return lax.all_to_all(chunks, "ctx", split_axis=0, concat_axis=0, tiled=True)


class LayerSum:
    def __init__(self, ids, flat, blocks, heads_n):
        self.ids, self.flat, self.blocks, self.heads_n = ids, flat, blocks, heads_n
        self.mine = lax.axis_index("head").astype(jnp.int32)
        self.per = len(blocks) // heads_n
        self.even = list(range(0, heads_n, 2))

    def part(self, offsets, extra, first):
        wanted = [(self.mine ^ g) * self.per + b for g in offsets for b in range(self.per)]
        wanted = jnp.stack(wanted).astype(jnp.int32)
        return layer_part(self.ids, self.flat, self.blocks, wanted, extra, first)

    def move(self, part, g):
        return lax.ppermute(part, "head", [(place, place ^ g) for place in range(self.heads_n)])

    def start(self):
        self.first = self.part([g + 1 for g in self.even], [], [])
        self.near = self.move(self.first, 1)

    def turn(self, done):
        self.flat = after(self.flat, done)
        self.parts = [self.part([g], [self.near], [g // 2 * self.per]) for g in self.even[1:]]
        self.far = [self.move(part, g) for part, g in zip(self.parts, self.even[1:])]

    def finish(self):
        return self.part([0], [self.near] + self.far, [0] * (1 + len(self.far)))


def on_device(queries, keys, values, out_grad, wo, *, n, heads_n):
    tokens, heads, dim = queries.shape
    half, depth, inner = heads // 2, wo.shape[1], n // 4
    me = lax.axis_index("ctx").astype(jnp.int32)
    line, spot = me // inner, me % inner
    middle, upper = (line == 1) | (line == 2), line < 2
    far, close = [jnp.where(upper, 2, 1), jnp.where(upper, 3, 0)], [line ^ 1, line]
    links = Links(n, 5)

    def around(block):
        return [block if e == 0 else links.flip(block, e) for e in range(inner)]

    def targets(owners, e):
        return jnp.stack([owner * inner + (spot ^ e) for owner in owners]).astype(jnp.int32)

    def leaving(flat, owners):
        return [proj_part(targets(owners, e), flat, out_grad, [], depth, dim, 0)[0] for e in range(1, inner)]

    def exchanged(parts):
        return [links.flip(part, e + 1) for e, part in enumerate(parts)]

    def summed(flat, owners, theirs, lead):
        return proj_part(targets(owners, 0), flat, out_grad, theirs, depth, dim, lead)

    def add(*terms):
        return sum(term.astype(F32) for term in terms).astype(BF16)

    near = links.along(wo, PAIRS)
    cross_own = links.along(wo, CROSS)
    own_blocks = around(wo)
    chunks, by_head = split_inputs(queries, keys, values, n)
    row_out = row_forward(*by_head)
    row_far, row_close = leaving(row_out, far), leaving(row_out, close)
    near = after(near, chunks, *own_blocks[1:])
    near_blocks = around(near)
    cross_near = links.along(near, CROSS)
    out_own = links.along(cross_own, OUTWARD)
    chunks = swap(after(chunks, *near_blocks, cross_near, out_own, *row_far, *row_close))
    out_near = links.along(cross_near, OUTWARD)
    far_own = jnp.where(middle, cross_own, out_own)
    far_own_blocks = around(far_own)
    far_near = jnp.where(middle, cross_near, out_near)
    far_near_blocks = around(far_near)
    blocks = own_blocks + near_blocks + far_own_blocks + far_near_blocks
    ids = [owner * inner + (spot ^ e) for owner in (line, line ^ 1, *far) for e in range(inner)]
    ids = jnp.stack(ids).astype(jnp.int32)
    early = n - inner

    outs = column_forward(after(chunks, *far_own_blocks))
    column_part = swap(outs)
    so_far = attn_grad(ids[:early], after(out_grad, outs), blocks[:early], None, dim)
    grad_row, grads = attn_grad(ids[early:], out_grad, blocks[early:], so_far, dim)
    row_far = exchanged([after(part, so_far, *far_near_blocks) for part in row_far])
    column_out, flat = collect(row_out, after(column_part, grads))
    column_far, column_close = leaving(column_out, far), leaving(column_out, close)
    grads = swap(after(grads, column_part, *row_far, *column_far, *column_close))
    column_far = exchanged(column_far)
    (row_far,) = summed(after(row_out, *column_close), far, row_far, 0)
    row_far_in = links.along(row_far, INWARD)
    row_close = exchanged([after(part, *column_far) for part in row_close])
    (column_far,) = summed(column_out, far, column_far, 0)
    column_far_in = links.along(column_far, INWARD)
    row_middle = add(row_far, row_far_in)
    row_cross = links.along(row_middle, CROSS)
    gradients = column_backward(chunks, after(grads, column_far, row_middle))
    layer = LayerSum(ids, after(flat, gradients), blocks, heads_n)
    layer.start()
    column_close = exchanged(column_close)
    column_cross = links.along(add(column_far, column_far_in), CROSS)
    column_grads = swap(after(gradients, row_cross, column_cross, *row_close, *column_close))

    layer.turn(gradients)
    row_near, row_own = summed(after(row_out, gradients), close, row_close, 1)
    row_near_in = links.along(row_near[0], INWARD)
    column_near, column_own = summed(after(column_out, gradients), close, column_close, 1)
    column_near_in = links.along(column_near[0], INWARD)
    row_grads = row_backward(*by_head, after(grad_row, gradients))
    row_back = links.along(add(row_near[0], row_cross[1]), OUTWARD)
    column_back = links.along(add(column_near[0], column_cross[1]), OUTWARD)
    layer_out = layer.finish()
    ahead = after(row_grads[0], layer_out, row_back, column_back, row_near_in, column_near_in)
    gradients = join_gradients(column_grads, [ahead, *row_grads[1:]])

    proj_row = add(row_own[0], row_near_in, row_cross[0], row_back)
    proj_column = add(column_own[0], column_near_in, column_cross[0], column_back)
    shape = (half, dim, depth)
    proj_grad = jnp.stack([proj_row.reshape(shape), proj_column.reshape(shape)], axis=1)
    return (layer_out, *gradients, proj_grad.reshape(heads * dim, depth))


def solution(mesh):
    in_specs = (
        P("ctx", "head", None),
        P("ctx", "head", None),
        P("ctx", "head", None),
        P("ctx", None),
        P("head", "ctx"),
    )
    out_specs = (
        P("ctx", "head"),
        P("ctx", "head", None),
        P("ctx", "head", None),
        P("ctx", "head", None),
        P("head", "ctx"),
    )
    return jax.shard_map(
        functools.partial(on_device, n=mesh.shape["ctx"], heads_n=mesh.shape["head"]),
        mesh=mesh,
        in_specs=in_specs,
        out_specs=out_specs,
        check_vma=False,
    )
```

```python
import functools

import jax
import jax.numpy as jnp
from jax import lax
from jax.experimental import pallas as pl
from jax.experimental.pallas import tpu as pltpu
from jax.sharding import PartitionSpec as P

C = 512
LANE = 16
VMEM = pl.BlockSpec(memory_space=pltpu.VMEM)
BF16 = jnp.bfloat16
F32 = jnp.float32


def params(mib):
    return pltpu.CompilerParams(vmem_limit_bytes=mib * 1024 * 1024)


def dot(a, b, dims):
    return lax.dot_general(a, b, (dims, ((), ())), preferred_element_type=F32)


def softmax(scores):
    highest = jnp.max(scores, axis=-1, keepdims=True)
    lifted = jnp.exp(scores - highest)
    return lifted * (1.0 / jnp.sum(lifted, axis=-1, keepdims=True))


def split_kernel(q_ref, k_ref, v_ref, chunk_ref, *rest):
    row_refs, wide = rest[:3], rest[3]
    n, width = chunk_ref.shape[0], chunk_ref.shape[3]
    span, heads, dim = q_ref.shape
    for array, ref in enumerate((q_ref, k_ref, v_ref)):
        wide[...] = ref[...].astype(F32).reshape(span * heads, dim)
        for head in range(heads // 2):
            row_refs[array][head] = wide[pl.ds(2 * head, span, stride=heads), :].astype(BF16)
            for d in range(n):
                odd = wide[pl.ds(d * width * heads + 2 * head + 1, width, stride=heads), :]
                chunk_ref[d, array, head] = odd.astype(BF16)


def split_inputs(queries, keys, values, n):
    tokens, heads, dim = queries.shape
    rows, width, half = tokens // C, C // n, heads // 2
    by_head = jax.ShapeDtypeStruct((half, tokens, dim), BF16)
    out = pl.pallas_call(
        split_kernel,
        grid=(rows,),
        in_specs=[pl.BlockSpec((C, heads, dim), lambda r: (r, 0, 0))] * 3,
        out_specs=[pl.BlockSpec((n, 3, half, pl.squeezed, width, dim), lambda r: (0, 0, 0, r, 0, 0))]
        + [pl.BlockSpec((half, C, dim), lambda r: (0, r, 0))] * 3,
        scratch_shapes=[pltpu.VMEM((C * heads, dim), F32)],
        out_shape=[jax.ShapeDtypeStruct((n, 3, half, rows, width, dim), BF16)] + [by_head] * 3,
        compiler_params=params(60),
        name="split_inputs",
    )(queries, keys, values)
    return out[0], out[1:]


def join_kernel(chunk_ref, *refs):
    row_refs, outs, wide = refs[:3], refs[3:6], refs[6]
    n, width = chunk_ref.shape[0], chunk_ref.shape[3]
    span, heads, dim = outs[0].shape
    for array in range(3):
        for head in range(heads // 2):
            wide[pl.ds(2 * head, span, stride=heads), :] = row_refs[array][head].astype(F32)
            for d in range(n):
                part = chunk_ref[d, array, head].astype(F32)
                wide[pl.ds(d * width * heads + 2 * head + 1, width, stride=heads), :] = part
        outs[array][...] = wide[...].reshape(span, heads, dim).astype(BF16)


def join_gradients(chunks, by_head):
    n, _, half, rows, width, dim = chunks.shape
    tokens, heads = by_head[0].shape[1], 2 * half
    return pl.pallas_call(
        join_kernel,
        grid=(rows,),
        in_specs=[pl.BlockSpec((n, 3, half, pl.squeezed, width, dim), lambda r: (0, 0, 0, r, 0, 0))]
        + [pl.BlockSpec((half, C, dim), lambda r: (0, r, 0))] * 3,
        out_specs=[pl.BlockSpec((C, heads, dim), lambda r: (r, 0, 0))] * 3,
        scratch_shapes=[pltpu.VMEM((C * heads, dim), F32)],
        out_shape=[jax.ShapeDtypeStruct((tokens, heads, dim), BF16)] * 3,
        compiler_params=params(60),
        name="join_gradients",
    )(chunks, *by_head)


def collect_kernel(row_ref, chunk_ref, flat_ref, both_ref):
    n, half, rows, width, dim = chunk_ref.shape
    for head in range(half):
        both_ref[:, 2 * head * dim : (2 * head + 1) * dim] = row_ref[:, head * dim : (head + 1) * dim]
        for d in range(n):
            for row in range(rows):
                part = chunk_ref[d, head, row]
                at = row * C + d * width
                flat_ref[at : at + width, head * dim : (head + 1) * dim] = part
                both_ref[at : at + width, (2 * head + 1) * dim : (2 * head + 2) * dim] = part


def collect(row_out, chunks):
    n, half, rows, width, dim = chunks.shape
    return pl.pallas_call(
        collect_kernel,
        in_specs=[VMEM] * 2,
        out_specs=[VMEM] * 2,
        out_shape=[
            jax.ShapeDtypeStruct((rows * C, half * dim), BF16),
            jax.ShapeDtypeStruct((rows * C, 2 * half * dim), BF16),
        ],
        compiler_params=params(24),
        name="collect",
    )(row_out, chunks)


def attn_grad_kernel(n, dim, last, ids, grad_ref, *refs):
    blocks, refs = refs[:n], refs[n:]
    step = pl.program_id(0)
    if last:
        so_far, row_ref, chunk_ref, weight, sem, total = refs
    else:
        total, weight, sem = refs
    tokens = grad_ref.shape[0]
    tile = tokens // 4

    @pl.when(step == 0)
    def _():
        for d in range(n):
            pltpu.make_async_copy(blocks[d], weight.at[d], sem.at[d]).start()
        total[...] = so_far[...] if last else jnp.zeros_like(total)

    pltpu.make_async_copy(blocks[0], weight.at[step], sem.at[step]).wait()

    @pl.loop(0, tokens, step=tile)
    def _(at):
        at = pl.multiple_of(at, tile)
        total[pl.ds(at, tile)] += dot(grad_ref[pl.ds(at, tile)], weight[step], ((1,), (1,)))

    if last:

        @pl.when(step == n - 1)
        def _():
            places, half, rows, width, _ = chunk_ref.shape
            for head in range(half):
                row_ref[:, head * dim : (head + 1) * dim] = total[:, 2 * head * dim : (2 * head + 1) * dim].astype(BF16)
                for d in range(places):
                    for row in range(rows):
                        at = row * C + d * width
                        part = total[at : at + width, (2 * head + 1) * dim : (2 * head + 2) * dim]
                        chunk_ref[d, head, row] = part.astype(BF16)


def attn_grad(ids, out_grad, blocks, so_far, dim):
    m, (span, depth), last = len(blocks), blocks[0].shape, so_far is not None
    tokens, model = out_grad.shape
    n, half = model // depth, span // dim // 2
    total = jax.ShapeDtypeStruct((tokens, span), F32)
    whole = pl.BlockSpec((tokens, span), lambda b, ids: (0, 0))
    chunk = jax.ShapeDtypeStruct((n, half, tokens // C, C // n, dim), BF16)
    scratch = [pltpu.VMEM((m, span, depth), BF16), pltpu.SemaphoreType.DMA((m,))]
    return pl.pallas_call(
        functools.partial(attn_grad_kernel, m, dim, last),
        grid_spec=pltpu.PrefetchScalarGridSpec(
            num_scalar_prefetch=1,
            grid=(m,),
            in_specs=[pl.BlockSpec((tokens, depth), lambda b, ids: (0, ids[b]))]
            + [pl.BlockSpec(memory_space=pl.ANY)] * m
            + [whole] * last,
            out_specs=[
                pl.BlockSpec((tokens, half * dim), lambda b, ids: (0, 0)),
                pl.BlockSpec(chunk.shape, lambda b, ids: (0, 0, 0, 0, 0)),
            ]
            if last
            else whole,
            scratch_shapes=scratch + [pltpu.VMEM(total.shape, F32)] * last,
        ),
        out_shape=[jax.ShapeDtypeStruct((tokens, half * dim), BF16), chunk] if last else total,
        compiler_params=params(60),
        cost_estimate=pl.CostEstimate(
            flops=2 * tokens * span * depth * m,
            bytes_accessed=2 * m * depth * (tokens + span) + 4 * tokens * span,
            transcendentals=0,
        ),
        name="attn_grad",
    )(ids, out_grad, *blocks, *([so_far] if last else []))


def layer_kernel(n, count, adds, ids, wanted, flat_ref, *refs):
    blocks, extra, out_ref = refs[:n], refs[n : n + adds], refs[n + adds]
    weight, sem = refs[n + adds + 1 :]
    step = pl.program_id(0)
    tokens = flat_ref.shape[0]
    tile = tokens // 4

    @pl.when(step == 0)
    def _():
        for s in range(count):
            for d in range(n):

                @pl.when(ids[d] == wanted[s])
                def _():
                    pltpu.make_async_copy(blocks[d], weight.at[s], sem.at[s]).start()

    pltpu.make_async_copy(blocks[0], weight.at[step], sem.at[step]).wait()

    @pl.loop(0, tokens, step=tile)
    def _(at):
        at = pl.multiple_of(at, tile)
        value = dot(flat_ref[pl.ds(at, tile)], weight[step], ((1,), (0,)))
        for ref in extra:
            value = value + ref[pl.ds(at, tile)].astype(F32)
        out_ref[pl.ds(at, tile)] = value.astype(BF16)


def layer_part(ids, flat, blocks, wanted, extra, first):
    n, (span, depth) = len(blocks), blocks[0].shape
    tokens, count = flat.shape[0], wanted.shape[0]
    by_column = pl.BlockSpec((tokens, depth), lambda s, ids, wanted: (0, s))
    return pl.pallas_call(
        functools.partial(layer_kernel, n, count, len(extra)),
        grid_spec=pltpu.PrefetchScalarGridSpec(
            num_scalar_prefetch=2,
            grid=(count,),
            in_specs=[pl.BlockSpec((tokens, span), lambda s, ids, wanted: (0, 0))]
            + [pl.BlockSpec(memory_space=pl.ANY)] * n
            + [pl.BlockSpec((tokens, depth), functools.partial(lambda f, s, ids, wanted: (0, s + f), f)) for f in first],
            out_specs=by_column,
            scratch_shapes=[pltpu.VMEM((count, span, depth), BF16), pltpu.SemaphoreType.DMA((count,))],
        ),
        out_shape=jax.ShapeDtypeStruct((tokens, count * depth), BF16),
        compiler_params=params(60),
        cost_estimate=pl.CostEstimate(
            flops=2 * tokens * span * depth * count,
            bytes_accessed=2 * (count * depth * (tokens + span) + tokens * span),
            transcendentals=0,
        ),
        name="layer_part",
    )(ids, wanted, flat, *blocks, *extra)


def proj_kernel(lead, adds, dim, order, flat_ref, grad_ref, *refs):
    extra, outs, turned = refs[:adds], refs[adds:-1], refs[-1]
    step = pl.program_id(0)
    span = flat_ref.shape[1]

    @pl.when(step == 0)
    def _():
        for at in range(0, span, dim):
            turned[at : at + dim] = flat_ref[:, at : at + dim].T

    def value(at):
        out = dot(turned[at : at + dim], grad_ref[...], ((1,), (0,)))
        for ref in extra:
            out = out + ref[at : at + dim].astype(F32)
        return out.astype(BF16)

    @pl.when(step < lead)
    def _():
        for at in range(0, span, dim):
            outs[0][at : at + dim] = value(at)

    @pl.when(step >= lead)
    def _():
        for at in range(0, span, dim):
            outs[-1][at : at + dim] = value(at)


def proj_part(order, flat, out_grad, extra, depth, dim, lead):
    tokens, span = flat.shape
    count = order.shape[0]
    sizes = [size for size in (lead, count - lead) if size]
    places = [lambda s, order: (jnp.minimum(s, lead - 1), 0, 0), lambda s, order: (jnp.maximum(s - lead, 0), 0, 0)]
    return pl.pallas_call(
        functools.partial(proj_kernel, lead, len(extra), dim),
        grid_spec=pltpu.PrefetchScalarGridSpec(
            num_scalar_prefetch=1,
            grid=(count,),
            in_specs=[
                pl.BlockSpec((tokens, span), lambda s, order: (0, 0)),
                pl.BlockSpec((tokens, depth), lambda s, order: (0, order[s])),
            ]
            + [pl.BlockSpec((pl.squeezed, span, depth), lambda s, order: (s, 0, 0))] * len(extra),
            out_specs=[pl.BlockSpec((pl.squeezed, span, depth), place) for place in places[-len(sizes) :]],
            scratch_shapes=[pltpu.VMEM((span, tokens), BF16)],
        ),
        out_shape=[jax.ShapeDtypeStruct((size, span, depth), BF16) for size in sizes],
        compiler_params=params(60),
        cost_estimate=pl.CostEstimate(
            flops=2 * tokens * span * depth * count,
            bytes_accessed=2 * (count * depth * (tokens + span * (1 + len(extra))) + tokens * span),
            transcendentals=0,
        ),
        name="proj_part",
    )(order, flat, out_grad, *extra)


def row_blocks(length):
    step = length // 2
    return [(start, step) for start in range(0, length, step)]


def row_probs(q, k, start, step, scale):
    scores = dot(q, k, ((1,), (1,))) * scale
    place = lax.broadcasted_iota(jnp.int32, scores.shape, 0) + start
    seen = lax.broadcasted_iota(jnp.int32, scores.shape, 1)
    return softmax(jnp.where(place >= seen, scores, -jnp.inf))


def row_forward_kernel(scale, q_ref, k_ref, v_ref, o_ref):
    for start, step in row_blocks(q_ref.shape[0]):
        stop = start + step
        probs = row_probs(q_ref[start:stop], k_ref[:stop], start, step, scale)
        o_ref[start:stop] = dot(probs.astype(BF16), v_ref[:stop], ((1,), (0,))).astype(BF16)


def row_forward(q, k, v):
    half, tokens, dim = q.shape
    by_head = pl.BlockSpec((pl.squeezed, C, dim), lambda r, h: (h, r, 0))
    return pl.pallas_call(
        functools.partial(row_forward_kernel, dim**-0.5),
        grid=(tokens // C, half),
        in_specs=[by_head] * 3,
        out_specs=pl.BlockSpec((C, dim), lambda r, h: (r, h)),
        out_shape=jax.ShapeDtypeStruct((tokens, half * dim), BF16),
        compiler_params=params(60),
        cost_estimate=pl.CostEstimate(
            flops=4 * tokens * C * half * dim, bytes_accessed=8 * tokens * half * dim, transcendentals=tokens * C * half
        ),
        name="row_forward",
    )(q, k, v)


def row_backward_kernel(scale, q_ref, k_ref, v_ref, g_ref, dq_ref, dk_ref, dv_ref, k_sum, v_sum):
    k_sum[...] = jnp.zeros_like(k_sum)
    v_sum[...] = jnp.zeros_like(v_sum)
    for start, step in row_blocks(q_ref.shape[0]):
        stop = start + step
        q, k, grad = q_ref[start:stop], k_ref[:stop], g_ref[start:stop]
        probs = row_probs(q, k, start, step, scale)
        prob_grad = dot(grad, v_ref[:stop], ((1,), (1,)))
        inner = jnp.sum(probs * prob_grad, axis=-1, keepdims=True)
        score_low = (probs * (prob_grad - inner)).astype(BF16)
        dq_ref[start:stop] = (dot(score_low, k, ((1,), (0,))) * scale).astype(BF16)
        k_sum[:stop] += dot(score_low, q, ((0,), (0,)))
        v_sum[:stop] += dot(probs.astype(BF16), grad, ((0,), (0,)))
    dk_ref[...] = (k_sum[...] * scale).astype(BF16)
    dv_ref[...] = v_sum[...].astype(BF16)


def row_backward(q, k, v, grad):
    half, tokens, dim = q.shape
    by_head = pl.BlockSpec((pl.squeezed, C, dim), lambda r, h: (h, r, 0))
    return pl.pallas_call(
        functools.partial(row_backward_kernel, dim**-0.5),
        grid=(tokens // C, half),
        in_specs=[by_head] * 3 + [pl.BlockSpec((C, dim), lambda r, h: (r, h))],
        out_specs=[by_head] * 3,
        out_shape=[jax.ShapeDtypeStruct(q.shape, BF16)] * 3,
        scratch_shapes=[pltpu.VMEM((C, dim), F32)] * 2,
        compiler_params=params(60),
        cost_estimate=pl.CostEstimate(
            flops=10 * tokens * C * half * dim, bytes_accessed=14 * tokens * half * dim, transcendentals=tokens * C * half
        ),
        name="row_backward",
    )(q, k, v, grad)


def column_mask(size):
    def parts(axis):
        place = lax.broadcasted_iota(jnp.int32, (size, size), axis)
        return place // LANE, place % LANE

    row_q, column_q = parts(0)
    row_k, column_k = parts(1)
    return (column_q == column_k) & (row_q >= row_k)


def gathered(ref, index, at):
    n, rows = ref.shape[0], ref.shape[-3]
    return jnp.concatenate([ref[(d, *index, row, pl.ds(at, LANE))] for d in range(n) for row in range(rows)], axis=0)


def scattered(ref, index, at, value):
    n, rows = ref.shape[0], ref.shape[-3]
    for d in range(n):
        for row in range(rows):
            line = d * rows + row
            ref[(d, *index, row, pl.ds(at, LANE))] = value[line * LANE : (line + 1) * LANE]


def column_probs(bias, q, k, scale):
    return softmax(dot(q, k, ((1,), (1,))) * scale + bias[...])


def column_forward_kernel(scale, chunk_ref, out_ref, bias):
    half, width = chunk_ref.shape[2], chunk_ref.shape[4]
    bias[...] = jnp.where(column_mask(bias.shape[0]), 0.0, -jnp.inf)
    blocks = width // LANE

    @pl.loop(0, half * blocks)
    def _(step):
        head, at = step // blocks, pl.multiple_of(step % blocks * LANE, LANE)
        q, k, v = (gathered(chunk_ref, (array, head), at) for array in range(3))
        probs = column_probs(bias, q, k, scale)
        scattered(out_ref, (head,), at, dot(probs.astype(BF16), v, ((1,), (0,))).astype(BF16))


def column_forward(chunks):
    n, _, half, rows, width, dim = chunks.shape
    size = n * rows * LANE
    return pl.pallas_call(
        functools.partial(column_forward_kernel, dim**-0.5),
        in_specs=[VMEM],
        out_specs=VMEM,
        out_shape=jax.ShapeDtypeStruct((n, half, rows, width, dim), BF16),
        scratch_shapes=[pltpu.VMEM((size, size), F32)],
        compiler_params=params(24),
        cost_estimate=pl.CostEstimate(
            flops=4 * size * size * dim * half * width // LANE,
            bytes_accessed=8 * n * half * rows * width * dim,
            transcendentals=size * size * half * width // LANE,
        ),
        name="column_forward",
    )(chunks)


def column_backward_kernel(scale, chunk_ref, grad_ref, out_ref, bias):
    half, width = chunk_ref.shape[2], chunk_ref.shape[4]
    bias[...] = jnp.where(column_mask(bias.shape[0]), 0.0, -jnp.inf)
    blocks = width // LANE

    @pl.loop(0, half * blocks)
    def _(step):
        head, at = step // blocks, pl.multiple_of(step % blocks * LANE, LANE)
        q, k, v = (gathered(chunk_ref, (array, head), at) for array in range(3))
        grad = gathered(grad_ref, (head,), at)
        probs = column_probs(bias, q, k, scale)
        prob_grad = dot(grad, v, ((1,), (1,)))
        inner = jnp.sum(probs * prob_grad, axis=-1, keepdims=True)
        score_low = (probs * (prob_grad - inner)).astype(BF16)
        scattered(out_ref, (0, head), at, (dot(score_low, k, ((1,), (0,))) * scale).astype(BF16))
        scattered(out_ref, (1, head), at, (dot(score_low, q, ((0,), (0,))) * scale).astype(BF16))
        scattered(out_ref, (2, head), at, dot(probs.astype(BF16), grad, ((0,), (0,))).astype(BF16))


def column_backward(chunks, grads):
    n, _, half, rows, width, dim = chunks.shape
    size = n * rows * LANE
    return pl.pallas_call(
        functools.partial(column_backward_kernel, dim**-0.5),
        in_specs=[VMEM] * 2,
        out_specs=VMEM,
        out_shape=jax.ShapeDtypeStruct(chunks.shape, BF16),
        scratch_shapes=[pltpu.VMEM((size, size), F32)],
        compiler_params=params(24),
        cost_estimate=pl.CostEstimate(
            flops=10 * size * size * dim * half * width // LANE,
            bytes_accessed=14 * n * half * rows * width * dim,
            transcendentals=size * size * half * width // LANE,
        ),
        name="column_backward",
    )(chunks, grads)


PAIRS = [(0, 1), (1, 0), (2, 3), (3, 2)]
INWARD = [(0, 1), (3, 2)]
CROSS = [(1, 2), (2, 1)]
OUTWARD = [(1, 0), (2, 3)]


def after(value, *done):
    return lax.optimization_barrier((value, *done))[0]


class Links:
    def __init__(self, n, window):
        self.n, self.inner, self.window, self.sent = n, n // 4, window, []

    def send(self, value, pairs):
        over = len(self.sent) - self.window + 1
        if over > 0:
            value = after(value, *self.sent[max(0, over - self.window) : over])
        out = lax.ppermute(value, "ctx", pairs)
        self.sent.append(out)
        return out

    def along(self, value, pairs):
        return self.send(value, [(a * self.inner + y, b * self.inner + y) for a, b in pairs for y in range(self.inner)])

    def flip(self, value, d):
        return self.send(value, [(place, place ^ d) for place in range(self.n)])


def swap(chunks):
    return lax.all_to_all(chunks, "ctx", split_axis=0, concat_axis=0, tiled=True)


class LayerSum:
    def __init__(self, ids, flat, blocks, heads_n):
        self.ids, self.flat, self.blocks, self.heads_n = ids, flat, blocks, heads_n
        self.mine = lax.axis_index("head").astype(jnp.int32)
        self.per = len(blocks) // heads_n
        self.even = list(range(0, heads_n, 2))

    def part(self, offsets, extra, first):
        wanted = [(self.mine ^ g) * self.per + b for g in offsets for b in range(self.per)]
        wanted = jnp.stack(wanted).astype(jnp.int32)
        return layer_part(self.ids, self.flat, self.blocks, wanted, extra, first)

    def move(self, part, g):
        return lax.ppermute(part, "head", [(place, place ^ g) for place in range(self.heads_n)])

    def start(self):
        self.first = self.part([g + 1 for g in self.even], [], [])
        self.near = self.move(self.first, 1)

    def turn(self, done):
        self.flat = after(self.flat, done)
        self.parts = [self.part([g], [self.near], [g // 2 * self.per]) for g in self.even[1:]]
        self.far = [self.move(part, g) for part, g in zip(self.parts, self.even[1:])]

    def finish(self):
        return self.part([0], [self.near] + self.far, [0] * (1 + len(self.far)))


def on_device(queries, keys, values, out_grad, wo, *, n, heads_n):
    tokens, heads, dim = queries.shape
    half, depth, inner = heads // 2, wo.shape[1], n // 4
    me = lax.axis_index("ctx").astype(jnp.int32)
    line, spot = me // inner, me % inner
    middle, upper = (line == 1) | (line == 2), line < 2
    far, close = [jnp.where(upper, 2, 1), jnp.where(upper, 3, 0)], [line ^ 1, line]
    links = Links(n, 5)

    def around(block):
        return [block if e == 0 else links.flip(block, e) for e in range(inner)]

    def targets(owners, e):
        return jnp.stack([owner * inner + (spot ^ e) for owner in owners]).astype(jnp.int32)

    def leaving(flat, owners):
        return [proj_part(targets(owners, e), flat, out_grad, [], depth, dim, 0)[0] for e in range(1, inner)]

    def exchanged(parts):
        return [links.flip(part, e + 1) for e, part in enumerate(parts)]

    def summed(flat, owners, theirs, lead):
        return proj_part(targets(owners, 0), flat, out_grad, theirs, depth, dim, lead)

    def add(*terms):
        return sum(term.astype(F32) for term in terms).astype(BF16)

    near = links.along(wo, PAIRS)
    cross_own = links.along(wo, CROSS)
    own_blocks = around(wo)
    chunks, by_head = split_inputs(queries, keys, values, n)
    row_out = row_forward(*by_head)
    row_far, row_close = leaving(row_out, far), leaving(row_out, close)
    near = after(near, chunks, *own_blocks[1:])
    near_blocks = around(near)
    cross_near = links.along(near, CROSS)
    out_own = links.along(cross_own, OUTWARD)
    chunks = swap(after(chunks, *near_blocks, cross_near, out_own, *row_far, *row_close))
    out_near = links.along(cross_near, OUTWARD)
    far_own = jnp.where(middle, cross_own, out_own)
    far_own_blocks = around(far_own)
    far_near = jnp.where(middle, cross_near, out_near)
    far_near_blocks = around(far_near)
    blocks = own_blocks + near_blocks + far_own_blocks + far_near_blocks
    ids = [owner * inner + (spot ^ e) for owner in (line, line ^ 1, *far) for e in range(inner)]
    ids = jnp.stack(ids).astype(jnp.int32)
    early = n - inner

    outs = column_forward(after(chunks, *far_own_blocks))
    column_part = swap(outs)
    so_far = attn_grad(ids[:early], after(out_grad, outs), blocks[:early], None, dim)
    grad_row, grads = attn_grad(ids[early:], out_grad, blocks[early:], so_far, dim)
    row_far = exchanged([after(part, so_far, *far_near_blocks) for part in row_far])
    column_out, flat = collect(row_out, after(column_part, grads))
    column_far, column_close = leaving(column_out, far), leaving(column_out, close)
    grads = swap(after(grads, column_part, *row_far, *column_far, *column_close))
    column_far = exchanged(column_far)
    (row_far,) = summed(after(row_out, *column_close), far, row_far, 0)
    row_far_in = links.along(row_far, INWARD)
    row_close = exchanged([after(part, *column_far) for part in row_close])
    (column_far,) = summed(column_out, far, column_far, 0)
    column_far_in = links.along(column_far, INWARD)
    row_middle = add(row_far, row_far_in)
    row_cross = links.along(row_middle, CROSS)
    gradients = column_backward(chunks, after(grads, row_far))
    layer = LayerSum(ids, after(flat, gradients), blocks, heads_n)
    layer.start()
    column_close = exchanged(column_close)
    column_cross = links.along(add(column_far, column_far_in), CROSS)
    row_near, row_own = summed(after(row_out, gradients), close, row_close, 1)
    row_near_in = links.along(row_near[0], INWARD)
    row_back = links.along(add(row_near[0], row_cross[1]), OUTWARD)
    column_grads = swap(after(gradients, column_cross, *column_close, row_near_in, row_back))

    layer.turn(gradients)
    column_near, column_own = summed(after(column_out, gradients), close, column_close, 1)
    column_near_in = links.along(column_near[0], INWARD)
    row_grads = row_backward(*by_head, after(grad_row, gradients))
    column_back = links.along(add(column_near[0], column_cross[1]), OUTWARD)
    layer_out = layer.finish()
    ahead = after(row_grads[0], layer_out)
    gradients = join_gradients(column_grads, [ahead, *row_grads[1:]])

    proj_row = add(row_own[0], row_near_in, row_cross[0], row_back)
    proj_column = add(column_own[0], after(column_near_in, layer_out), column_cross[0], column_back)
    shape = (half, dim, depth)
    proj_grad = jnp.stack([proj_row.reshape(shape), proj_column.reshape(shape)], axis=1)
    return (layer_out, *gradients, proj_grad.reshape(heads * dim, depth))


def solution(mesh):
    in_specs = (
        P("ctx", "head", None),
        P("ctx", "head", None),
        P("ctx", "head", None),
        P("ctx", None),
        P("head", "ctx"),
    )
    out_specs = (
        P("ctx", "head"),
        P("ctx", "head", None),
        P("ctx", "head", None),
        P("ctx", "head", None),
        P("head", "ctx"),
    )
    return jax.shard_map(
        functools.partial(on_device, n=mesh.shape["ctx"], heads_n=mesh.shape["head"]),
        mesh=mesh,
        in_specs=in_specs,
        out_specs=out_specs,
        check_vma=False,
    )
```

```python
import functools

import jax
import jax.numpy as jnp
from jax import lax
from jax.experimental import pallas as pl
from jax.experimental.pallas import tpu as pltpu
from jax.sharding import PartitionSpec as P

C = 512
LANE = 16
VMEM = pl.BlockSpec(memory_space=pltpu.VMEM)
BF16 = jnp.bfloat16
F32 = jnp.float32


def params(mib):
    return pltpu.CompilerParams(vmem_limit_bytes=mib * 1024 * 1024)


def dot(a, b, dims):
    return lax.dot_general(a, b, (dims, ((), ())), preferred_element_type=F32)


def softmax(scores):
    highest = jnp.max(scores, axis=-1, keepdims=True)
    lifted = jnp.exp(scores - highest)
    return lifted * (1.0 / jnp.sum(lifted, axis=-1, keepdims=True))


def split_kernel(q_ref, k_ref, v_ref, chunk_ref, *rest):
    row_refs, wide = rest[:3], rest[3]
    n, width = chunk_ref.shape[0], chunk_ref.shape[3]
    span, heads, dim = q_ref.shape
    for array, ref in enumerate((q_ref, k_ref, v_ref)):
        wide[...] = ref[...].astype(F32).reshape(span * heads, dim)
        for head in range(heads // 2):
            row_refs[array][head] = wide[pl.ds(2 * head, span, stride=heads), :].astype(BF16)
            for d in range(n):
                odd = wide[pl.ds(d * width * heads + 2 * head + 1, width, stride=heads), :]
                chunk_ref[d, array, head] = odd.astype(BF16)


def split_inputs(queries, keys, values, n):
    tokens, heads, dim = queries.shape
    rows, width, half = tokens // C, C // n, heads // 2
    by_head = jax.ShapeDtypeStruct((half, tokens, dim), BF16)
    out = pl.pallas_call(
        split_kernel,
        grid=(rows,),
        in_specs=[pl.BlockSpec((C, heads, dim), lambda r: (r, 0, 0))] * 3,
        out_specs=[pl.BlockSpec((n, 3, half, pl.squeezed, width, dim), lambda r: (0, 0, 0, r, 0, 0))]
        + [pl.BlockSpec((half, C, dim), lambda r: (0, r, 0))] * 3,
        scratch_shapes=[pltpu.VMEM((C * heads, dim), F32)],
        out_shape=[jax.ShapeDtypeStruct((n, 3, half, rows, width, dim), BF16)] + [by_head] * 3,
        compiler_params=params(60),
        name="split_inputs",
    )(queries, keys, values)
    return out[0], out[1:]


def join_kernel(chunk_ref, *refs):
    row_refs, outs, wide = refs[:3], refs[3:6], refs[6]
    n, width = chunk_ref.shape[0], chunk_ref.shape[3]
    span, heads, dim = outs[0].shape
    for array in range(3):
        for head in range(heads // 2):
            wide[pl.ds(2 * head, span, stride=heads), :] = row_refs[array][head].astype(F32)
            for d in range(n):
                part = chunk_ref[d, array, head].astype(F32)
                wide[pl.ds(d * width * heads + 2 * head + 1, width, stride=heads), :] = part
        outs[array][...] = wide[...].reshape(span, heads, dim).astype(BF16)


def join_gradients(chunks, by_head):
    n, _, half, rows, width, dim = chunks.shape
    tokens, heads = by_head[0].shape[1], 2 * half
    return pl.pallas_call(
        join_kernel,
        grid=(rows,),
        in_specs=[pl.BlockSpec((n, 3, half, pl.squeezed, width, dim), lambda r: (0, 0, 0, r, 0, 0))]
        + [pl.BlockSpec((half, C, dim), lambda r: (0, r, 0))] * 3,
        out_specs=[pl.BlockSpec((C, heads, dim), lambda r: (r, 0, 0))] * 3,
        scratch_shapes=[pltpu.VMEM((C * heads, dim), F32)],
        out_shape=[jax.ShapeDtypeStruct((tokens, heads, dim), BF16)] * 3,
        compiler_params=params(60),
        name="join_gradients",
    )(chunks, *by_head)


def collect_kernel(row_ref, chunk_ref, flat_ref, both_ref):
    n, half, rows, width, dim = chunk_ref.shape
    for head in range(half):
        both_ref[:, 2 * head * dim : (2 * head + 1) * dim] = row_ref[:, head * dim : (head + 1) * dim]
        for d in range(n):
            for row in range(rows):
                part = chunk_ref[d, head, row]
                at = row * C + d * width
                flat_ref[at : at + width, head * dim : (head + 1) * dim] = part
                both_ref[at : at + width, (2 * head + 1) * dim : (2 * head + 2) * dim] = part


def collect(row_out, chunks):
    n, half, rows, width, dim = chunks.shape
    return pl.pallas_call(
        collect_kernel,
        in_specs=[VMEM] * 2,
        out_specs=[VMEM] * 2,
        out_shape=[
            jax.ShapeDtypeStruct((rows * C, half * dim), BF16),
            jax.ShapeDtypeStruct((rows * C, 2 * half * dim), BF16),
        ],
        compiler_params=params(24),
        name="collect",
    )(row_out, chunks)


def attn_grad_kernel(n, dim, last, ids, grad_ref, *refs):
    blocks, refs = refs[:n], refs[n:]
    step = pl.program_id(0)
    if last:
        so_far, row_ref, chunk_ref, weight, sem, total = refs
    else:
        total, weight, sem = refs
    tokens = grad_ref.shape[0]
    tile = tokens // 4

    @pl.when(step == 0)
    def _():
        for d in range(n):
            pltpu.make_async_copy(blocks[d], weight.at[d], sem.at[d]).start()
        total[...] = so_far[...] if last else jnp.zeros_like(total)

    pltpu.make_async_copy(blocks[0], weight.at[step], sem.at[step]).wait()

    @pl.loop(0, tokens, step=tile)
    def _(at):
        at = pl.multiple_of(at, tile)
        total[pl.ds(at, tile)] += dot(grad_ref[pl.ds(at, tile)], weight[step], ((1,), (1,)))

    if last:

        @pl.when(step == n - 1)
        def _():
            places, half, rows, width, _ = chunk_ref.shape
            for head in range(half):
                row_ref[:, head * dim : (head + 1) * dim] = total[:, 2 * head * dim : (2 * head + 1) * dim].astype(BF16)
                for d in range(places):
                    for row in range(rows):
                        at = row * C + d * width
                        part = total[at : at + width, (2 * head + 1) * dim : (2 * head + 2) * dim]
                        chunk_ref[d, head, row] = part.astype(BF16)


def attn_grad(ids, out_grad, blocks, so_far, dim):
    m, (span, depth), last = len(blocks), blocks[0].shape, so_far is not None
    tokens, model = out_grad.shape
    n, half = model // depth, span // dim // 2
    total = jax.ShapeDtypeStruct((tokens, span), F32)
    whole = pl.BlockSpec((tokens, span), lambda b, ids: (0, 0))
    chunk = jax.ShapeDtypeStruct((n, half, tokens // C, C // n, dim), BF16)
    scratch = [pltpu.VMEM((m, span, depth), BF16), pltpu.SemaphoreType.DMA((m,))]
    return pl.pallas_call(
        functools.partial(attn_grad_kernel, m, dim, last),
        grid_spec=pltpu.PrefetchScalarGridSpec(
            num_scalar_prefetch=1,
            grid=(m,),
            in_specs=[pl.BlockSpec((tokens, depth), lambda b, ids: (0, ids[b]))]
            + [pl.BlockSpec(memory_space=pl.ANY)] * m
            + [whole] * last,
            out_specs=[
                pl.BlockSpec((tokens, half * dim), lambda b, ids: (0, 0)),
                pl.BlockSpec(chunk.shape, lambda b, ids: (0, 0, 0, 0, 0)),
            ]
            if last
            else whole,
            scratch_shapes=scratch + [pltpu.VMEM(total.shape, F32)] * last,
        ),
        out_shape=[jax.ShapeDtypeStruct((tokens, half * dim), BF16), chunk] if last else total,
        compiler_params=params(60),
        cost_estimate=pl.CostEstimate(
            flops=2 * tokens * span * depth * m,
            bytes_accessed=2 * m * depth * (tokens + span) + 4 * tokens * span,
            transcendentals=0,
        ),
        name="attn_grad",
    )(ids, out_grad, *blocks, *([so_far] if last else []))


def layer_kernel(n, count, adds, ids, wanted, flat_ref, *refs):
    blocks, extra, out_ref = refs[:n], refs[n : n + adds], refs[n + adds]
    weight, sem = refs[n + adds + 1 :]
    step = pl.program_id(0)
    tokens = flat_ref.shape[0]
    tile = tokens // 4

    @pl.when(step == 0)
    def _():
        for s in range(count):
            for d in range(n):

                @pl.when(ids[d] == wanted[s])
                def _():
                    pltpu.make_async_copy(blocks[d], weight.at[s], sem.at[s]).start()

    pltpu.make_async_copy(blocks[0], weight.at[step], sem.at[step]).wait()

    @pl.loop(0, tokens, step=tile)
    def _(at):
        at = pl.multiple_of(at, tile)
        value = dot(flat_ref[pl.ds(at, tile)], weight[step], ((1,), (0,)))
        for ref in extra:
            value = value + ref[pl.ds(at, tile)].astype(F32)
        out_ref[pl.ds(at, tile)] = value.astype(BF16)


def layer_part(ids, flat, blocks, wanted, extra, first):
    n, (span, depth) = len(blocks), blocks[0].shape
    tokens, count = flat.shape[0], wanted.shape[0]
    by_column = pl.BlockSpec((tokens, depth), lambda s, ids, wanted: (0, s))
    return pl.pallas_call(
        functools.partial(layer_kernel, n, count, len(extra)),
        grid_spec=pltpu.PrefetchScalarGridSpec(
            num_scalar_prefetch=2,
            grid=(count,),
            in_specs=[pl.BlockSpec((tokens, span), lambda s, ids, wanted: (0, 0))]
            + [pl.BlockSpec(memory_space=pl.ANY)] * n
            + [pl.BlockSpec((tokens, depth), functools.partial(lambda f, s, ids, wanted: (0, s + f), f)) for f in first],
            out_specs=by_column,
            scratch_shapes=[pltpu.VMEM((count, span, depth), BF16), pltpu.SemaphoreType.DMA((count,))],
        ),
        out_shape=jax.ShapeDtypeStruct((tokens, count * depth), BF16),
        compiler_params=params(60),
        cost_estimate=pl.CostEstimate(
            flops=2 * tokens * span * depth * count,
            bytes_accessed=2 * (count * depth * (tokens + span) + tokens * span),
            transcendentals=0,
        ),
        name="layer_part",
    )(ids, wanted, flat, *blocks, *extra)


def proj_kernel(lead, adds, dim, order, flat_ref, grad_ref, *refs):
    extra, outs, turned = refs[:adds], refs[adds:-1], refs[-1]
    step = pl.program_id(0)
    span = flat_ref.shape[1]

    @pl.when(step == 0)
    def _():
        for at in range(0, span, dim):
            turned[at : at + dim] = flat_ref[:, at : at + dim].T

    def value(at):
        out = dot(turned[at : at + dim], grad_ref[...], ((1,), (0,)))
        for ref in extra:
            out = out + ref[at : at + dim].astype(F32)
        return out.astype(BF16)

    @pl.when(step < lead)
    def _():
        for at in range(0, span, dim):
            outs[0][at : at + dim] = value(at)

    @pl.when(step >= lead)
    def _():
        for at in range(0, span, dim):
            outs[-1][at : at + dim] = value(at)


def proj_part(order, flat, out_grad, extra, depth, dim, lead):
    tokens, span = flat.shape
    count = order.shape[0]
    sizes = [size for size in (lead, count - lead) if size]
    places = [lambda s, order: (jnp.minimum(s, lead - 1), 0, 0), lambda s, order: (jnp.maximum(s - lead, 0), 0, 0)]
    return pl.pallas_call(
        functools.partial(proj_kernel, lead, len(extra), dim),
        grid_spec=pltpu.PrefetchScalarGridSpec(
            num_scalar_prefetch=1,
            grid=(count,),
            in_specs=[
                pl.BlockSpec((tokens, span), lambda s, order: (0, 0)),
                pl.BlockSpec((tokens, depth), lambda s, order: (0, order[s])),
            ]
            + [pl.BlockSpec((pl.squeezed, span, depth), lambda s, order: (s, 0, 0))] * len(extra),
            out_specs=[pl.BlockSpec((pl.squeezed, span, depth), place) for place in places[-len(sizes) :]],
            scratch_shapes=[pltpu.VMEM((span, tokens), BF16)],
        ),
        out_shape=[jax.ShapeDtypeStruct((size, span, depth), BF16) for size in sizes],
        compiler_params=params(60),
        cost_estimate=pl.CostEstimate(
            flops=2 * tokens * span * depth * count,
            bytes_accessed=2 * (count * depth * (tokens + span * (1 + len(extra))) + tokens * span),
            transcendentals=0,
        ),
        name="proj_part",
    )(order, flat, out_grad, *extra)


def row_blocks(length):
    step = length // 2
    return [(start, step) for start in range(0, length, step)]


def row_probs(q, k, start, step, scale):
    scores = dot(q, k, ((1,), (1,))) * scale
    place = lax.broadcasted_iota(jnp.int32, scores.shape, 0) + start
    seen = lax.broadcasted_iota(jnp.int32, scores.shape, 1)
    return softmax(jnp.where(place >= seen, scores, -jnp.inf))


def row_forward_kernel(scale, q_ref, k_ref, v_ref, o_ref):
    for start, step in row_blocks(q_ref.shape[0]):
        stop = start + step
        probs = row_probs(q_ref[start:stop], k_ref[:stop], start, step, scale)
        o_ref[start:stop] = dot(probs.astype(BF16), v_ref[:stop], ((1,), (0,))).astype(BF16)


def row_forward(q, k, v):
    half, tokens, dim = q.shape
    by_head = pl.BlockSpec((pl.squeezed, C, dim), lambda r, h: (h, r, 0))
    return pl.pallas_call(
        functools.partial(row_forward_kernel, dim**-0.5),
        grid=(tokens // C, half),
        in_specs=[by_head] * 3,
        out_specs=pl.BlockSpec((C, dim), lambda r, h: (r, h)),
        out_shape=jax.ShapeDtypeStruct((tokens, half * dim), BF16),
        compiler_params=params(60),
        cost_estimate=pl.CostEstimate(
            flops=4 * tokens * C * half * dim, bytes_accessed=8 * tokens * half * dim, transcendentals=tokens * C * half
        ),
        name="row_forward",
    )(q, k, v)


def row_backward_kernel(scale, q_ref, k_ref, v_ref, g_ref, dq_ref, dk_ref, dv_ref, k_sum, v_sum):
    k_sum[...] = jnp.zeros_like(k_sum)
    v_sum[...] = jnp.zeros_like(v_sum)
    for start, step in row_blocks(q_ref.shape[0]):
        stop = start + step
        q, k, grad = q_ref[start:stop], k_ref[:stop], g_ref[start:stop]
        probs = row_probs(q, k, start, step, scale)
        prob_grad = dot(grad, v_ref[:stop], ((1,), (1,)))
        inner = jnp.sum(probs * prob_grad, axis=-1, keepdims=True)
        score_low = (probs * (prob_grad - inner)).astype(BF16)
        dq_ref[start:stop] = (dot(score_low, k, ((1,), (0,))) * scale).astype(BF16)
        k_sum[:stop] += dot(score_low, q, ((0,), (0,)))
        v_sum[:stop] += dot(probs.astype(BF16), grad, ((0,), (0,)))
    dk_ref[...] = (k_sum[...] * scale).astype(BF16)
    dv_ref[...] = v_sum[...].astype(BF16)


def row_backward(q, k, v, grad):
    half, tokens, dim = q.shape
    by_head = pl.BlockSpec((pl.squeezed, C, dim), lambda r, h: (h, r, 0))
    return pl.pallas_call(
        functools.partial(row_backward_kernel, dim**-0.5),
        grid=(tokens // C, half),
        in_specs=[by_head] * 3 + [pl.BlockSpec((C, dim), lambda r, h: (r, h))],
        out_specs=[by_head] * 3,
        out_shape=[jax.ShapeDtypeStruct(q.shape, BF16)] * 3,
        scratch_shapes=[pltpu.VMEM((C, dim), F32)] * 2,
        compiler_params=params(60),
        cost_estimate=pl.CostEstimate(
            flops=10 * tokens * C * half * dim, bytes_accessed=14 * tokens * half * dim, transcendentals=tokens * C * half
        ),
        name="row_backward",
    )(q, k, v, grad)


def column_mask(size):
    def parts(axis):
        place = lax.broadcasted_iota(jnp.int32, (size, size), axis)
        return place // LANE, place % LANE

    row_q, column_q = parts(0)
    row_k, column_k = parts(1)
    return (column_q == column_k) & (row_q >= row_k)


def gathered(ref, index, at):
    n, rows = ref.shape[0], ref.shape[-3]
    return jnp.concatenate([ref[(d, *index, row, pl.ds(at, LANE))] for d in range(n) for row in range(rows)], axis=0)


def scattered(ref, index, at, value):
    n, rows = ref.shape[0], ref.shape[-3]
    for d in range(n):
        for row in range(rows):
            line = d * rows + row
            ref[(d, *index, row, pl.ds(at, LANE))] = value[line * LANE : (line + 1) * LANE]


def column_probs(bias, q, k, scale):
    return softmax(dot(q, k, ((1,), (1,))) * scale + bias[...])


def column_forward_kernel(scale, chunk_ref, out_ref, bias):
    half, width = chunk_ref.shape[2], chunk_ref.shape[4]
    bias[...] = jnp.where(column_mask(bias.shape[0]), 0.0, -jnp.inf)
    blocks = width // LANE

    @pl.loop(0, half * blocks)
    def _(step):
        head, at = step // blocks, pl.multiple_of(step % blocks * LANE, LANE)
        q, k, v = (gathered(chunk_ref, (array, head), at) for array in range(3))
        probs = column_probs(bias, q, k, scale)
        scattered(out_ref, (head,), at, dot(probs.astype(BF16), v, ((1,), (0,))).astype(BF16))


def column_forward(chunks):
    n, _, half, rows, width, dim = chunks.shape
    size = n * rows * LANE
    return pl.pallas_call(
        functools.partial(column_forward_kernel, dim**-0.5),
        in_specs=[VMEM],
        out_specs=VMEM,
        out_shape=jax.ShapeDtypeStruct((n, half, rows, width, dim), BF16),
        scratch_shapes=[pltpu.VMEM((size, size), F32)],
        compiler_params=params(24),
        cost_estimate=pl.CostEstimate(
            flops=4 * size * size * dim * half * width // LANE,
            bytes_accessed=8 * n * half * rows * width * dim,
            transcendentals=size * size * half * width // LANE,
        ),
        name="column_forward",
    )(chunks)


def column_backward_kernel(scale, chunk_ref, grad_ref, out_ref, bias):
    half, width = chunk_ref.shape[2], chunk_ref.shape[4]
    bias[...] = jnp.where(column_mask(bias.shape[0]), 0.0, -jnp.inf)
    blocks = width // LANE

    @pl.loop(0, half * blocks)
    def _(step):
        head, at = step // blocks, pl.multiple_of(step % blocks * LANE, LANE)
        q, k, v = (gathered(chunk_ref, (array, head), at) for array in range(3))
        grad = gathered(grad_ref, (head,), at)
        probs = column_probs(bias, q, k, scale)
        prob_grad = dot(grad, v, ((1,), (1,)))
        inner = jnp.sum(probs * prob_grad, axis=-1, keepdims=True)
        score_low = (probs * (prob_grad - inner)).astype(BF16)
        scattered(out_ref, (0, head), at, (dot(score_low, k, ((1,), (0,))) * scale).astype(BF16))
        scattered(out_ref, (1, head), at, (dot(score_low, q, ((0,), (0,))) * scale).astype(BF16))
        scattered(out_ref, (2, head), at, dot(probs.astype(BF16), grad, ((0,), (0,))).astype(BF16))


def column_backward(chunks, grads):
    n, _, half, rows, width, dim = chunks.shape
    size = n * rows * LANE
    return pl.pallas_call(
        functools.partial(column_backward_kernel, dim**-0.5),
        in_specs=[VMEM] * 2,
        out_specs=VMEM,
        out_shape=jax.ShapeDtypeStruct(chunks.shape, BF16),
        scratch_shapes=[pltpu.VMEM((size, size), F32)],
        compiler_params=params(24),
        cost_estimate=pl.CostEstimate(
            flops=10 * size * size * dim * half * width // LANE,
            bytes_accessed=14 * n * half * rows * width * dim,
            transcendentals=size * size * half * width // LANE,
        ),
        name="column_backward",
    )(chunks, grads)


PAIRS = [(0, 1), (1, 0), (2, 3), (3, 2)]
INWARD = [(0, 1), (3, 2)]
CROSS = [(1, 2), (2, 1)]
OUTWARD = [(1, 0), (2, 3)]


def after(value, *done):
    return lax.optimization_barrier((value, *done))[0]


class Links:
    def __init__(self, n, window):
        self.n, self.inner, self.window, self.sent = n, n // 4, window, []

    def send(self, value, pairs):
        over = len(self.sent) - self.window + 1
        if over > 0:
            value = after(value, *self.sent[max(0, over - self.window) : over])
        out = lax.ppermute(value, "ctx", pairs)
        self.sent.append(out)
        return out

    def along(self, value, pairs):
        return self.send(value, [(a * self.inner + y, b * self.inner + y) for a, b in pairs for y in range(self.inner)])

    def flip(self, value, d):
        return self.send(value, [(place, place ^ d) for place in range(self.n)])


def swap(chunks):
    return lax.all_to_all(chunks, "ctx", split_axis=0, concat_axis=0, tiled=True)


class LayerSum:
    def __init__(self, ids, flat, blocks, heads_n):
        self.ids, self.flat, self.blocks, self.heads_n = ids, flat, blocks, heads_n
        self.mine = lax.axis_index("head").astype(jnp.int32)
        self.per = len(blocks) // heads_n
        self.even = list(range(0, heads_n, 2))

    def part(self, offsets, extra, first):
        wanted = [(self.mine ^ g) * self.per + b for g in offsets for b in range(self.per)]
        wanted = jnp.stack(wanted).astype(jnp.int32)
        return layer_part(self.ids, self.flat, self.blocks, wanted, extra, first)

    def move(self, part, g):
        return lax.ppermute(part, "head", [(place, place ^ g) for place in range(self.heads_n)])

    def start(self):
        self.first = self.part([g + 1 for g in self.even], [], [])
        self.near = self.move(self.first, 1)

    def turn(self, done):
        self.flat = after(self.flat, done)
        self.parts = [self.part([g], [self.near], [g // 2 * self.per]) for g in self.even[1:]]
        self.far = [self.move(part, g) for part, g in zip(self.parts, self.even[1:])]

    def finish(self):
        return self.part([0], [self.near] + self.far, [0] * (1 + len(self.far)))


def on_device(queries, keys, values, out_grad, wo, *, n, heads_n):
    tokens, heads, dim = queries.shape
    half, depth, inner = heads // 2, wo.shape[1], n // 4
    me = lax.axis_index("ctx").astype(jnp.int32)
    line, spot = me // inner, me % inner
    middle, upper = (line == 1) | (line == 2), line < 2
    far, close = [jnp.where(upper, 2, 1), jnp.where(upper, 3, 0)], [line ^ 1, line]
    links = Links(n, 5)

    def around(block):
        return [block if e == 0 else links.flip(block, e) for e in range(inner)]

    def targets(owners, e):
        return jnp.stack([owner * inner + (spot ^ e) for owner in owners]).astype(jnp.int32)

    def leaving(flat, owners):
        return [proj_part(targets(owners, e), flat, out_grad, [], depth, dim, 0)[0] for e in range(1, inner)]

    def exchanged(parts):
        return [links.flip(part, e + 1) for e, part in enumerate(parts)]

    def summed(flat, owners, theirs, lead):
        return proj_part(targets(owners, 0), flat, out_grad, theirs, depth, dim, lead)

    def add(*terms):
        return sum(term.astype(F32) for term in terms).astype(BF16)

    near = links.along(wo, PAIRS)
    cross_own = links.along(wo, CROSS)
    own_blocks = around(wo)
    chunks, by_head = split_inputs(queries, keys, values, n)
    row_out = row_forward(*by_head)
    row_far, row_close = leaving(row_out, far), leaving(row_out, close)
    near = after(near, chunks, *own_blocks[1:])
    near_blocks = around(near)
    cross_near = links.along(near, CROSS)
    out_own = links.along(cross_own, OUTWARD)
    chunks = swap(after(chunks, *near_blocks, cross_near, out_own, *row_far, *row_close))
    out_near = links.along(cross_near, OUTWARD)
    far_own = jnp.where(middle, cross_own, out_own)
    far_own_blocks = around(far_own)
    far_near = jnp.where(middle, cross_near, out_near)
    far_near_blocks = around(far_near)
    blocks = own_blocks + near_blocks + far_own_blocks + far_near_blocks
    ids = [owner * inner + (spot ^ e) for owner in (line, line ^ 1, *far) for e in range(inner)]
    ids = jnp.stack(ids).astype(jnp.int32)
    early = n - inner

    outs = column_forward(after(chunks, *far_own_blocks))
    column_part = swap(outs)
    so_far = attn_grad(ids[:early], after(out_grad, outs), blocks[:early], None, dim)
    grad_row, grads = attn_grad(ids[early:], out_grad, blocks[early:], so_far, dim)
    row_far = exchanged([after(part, so_far, *far_near_blocks) for part in row_far])
    column_out, flat = collect(row_out, after(column_part, grads))
    column_far, column_close = leaving(column_out, far), leaving(column_out, close)
    grads = swap(after(grads, column_part, *row_far, *column_far, *column_close))
    column_far = exchanged(column_far)
    (row_far,) = summed(after(row_out, *column_close), far, row_far, 0)
    row_far_in = links.along(row_far, INWARD)
    row_close = exchanged([after(part, *column_far) for part in row_close])
    gradients = column_backward(chunks, after(grads, row_far))
    (column_far,) = summed(after(column_out, gradients), far, column_far, 0)
    column_far_in = links.along(column_far, INWARD)
    row_cross = links.along(add(row_far, row_far_in), CROSS)
    layer = LayerSum(ids, after(flat, gradients), blocks, heads_n)
    layer.start()
    column_close = exchanged(column_close)
    column_cross = links.along(add(column_far, column_far_in), CROSS)
    row_near, row_own = summed(after(row_out, gradients), close, row_close, 1)
    row_near_in = links.along(row_near[0], INWARD)
    row_back = links.along(add(row_near[0], row_cross[1]), OUTWARD)
    layer.turn(gradients)
    column_grads = swap(after(gradients, *layer.parts, column_cross, *column_close, row_near_in, row_back))

    column_near, column_own = summed(after(column_out, gradients), close, column_close, 1)
    column_near_in = links.along(column_near[0], INWARD)
    row_grads = row_backward(*by_head, after(grad_row, gradients))
    column_back = links.along(add(column_near[0], column_cross[1]), OUTWARD)
    layer_out = layer.finish()
    ahead = after(row_grads[0], layer_out)
    gradients = join_gradients(column_grads, [ahead, *row_grads[1:]])

    proj_row = add(row_own[0], row_near_in, row_cross[0], row_back)
    proj_column = add(column_own[0], after(column_near_in, layer_out), column_cross[0], column_back)
    shape = (half, dim, depth)
    proj_grad = jnp.stack([proj_row.reshape(shape), proj_column.reshape(shape)], axis=1)
    return (layer_out, *gradients, proj_grad.reshape(heads * dim, depth))


def solution(mesh):
    in_specs = (
        P("ctx", "head", None),
        P("ctx", "head", None),
        P("ctx", "head", None),
        P("ctx", None),
        P("head", "ctx"),
    )
    out_specs = (
        P("ctx", "head"),
        P("ctx", "head", None),
        P("ctx", "head", None),
        P("ctx", "head", None),
        P("head", "ctx"),
    )
    return jax.shard_map(
        functools.partial(on_device, n=mesh.shape["ctx"], heads_n=mesh.shape["head"]),
        mesh=mesh,
        in_specs=in_specs,
        out_specs=out_specs,
        check_vma=False,
    )
```
